32 devices in a mesh: row: 4 (over x, core), col: 8 (over z, y).
Axes of the slice: x: 2, y: 2, z: 4, core: 2. Of those that a mesh axis runs over, the one named last changes fastest.
Arguments:
- pair: bfloat16 [64, 64, 128], P('row', 'col'), may hold values from -6 to 6
- pair_mask: int32 [64, 64], P('row', 'col'), may hold values 0 or 1
- contact_mask: int32 [64, 64], P('row', 'col'), may hold values 0 or 1
- dilations: int32 [2], replicated, may hold values from 1 to 8, as said below
- w_proj: bfloat16 [128, 512], replicated, may hold values from -0.5 to 0.5
- w_gate: bfloat16 [128, 128], replicated, may hold values from -0.5 to 0.5
- w_out: bfloat16 [128, 128], replicated, may hold values from -0.5 to 0.5
- conv_one: bfloat16 [9, 128, 128], replicated, may hold values from -0.1875 to 0.1875
- conv_two: bfloat16 [9, 128, 128], replicated, may hold values from -0.1875 to 0.1875
- cotangent: bfloat16 [64, 64, 128], P('row', 'col'), may hold values from -6 to 6
Outputs:
- output: bfloat16 [64, 64, 128], P('row', 'col')
- grad_pair: bfloat16 [64, 64, 128], P('row', 'col')
- grad_one: float32 [9, 128, 128], replicated
- grad_two: float32 [9, 128, 128], replicated
The draws below stay inside these ranges and needn't reach their ends.
Inputs may be any that keep to these rules, and one draw needn't show every extreme that they name: `dilations`: one of the two rates equals 8, the other is smaller.
All inputs are finite; a program needn't handle non-finite values. No bound on the sum of `pair_mask` or of `contact_mask` on one device may be relied on, other than what follows from the above.
Results may differ from the reference program's by a relative error of at most 0.015.
Values may be sent and summed in bfloat16 or wider, within the bound.
No kernel may reach another device: no remote copies, remote signals or barrier semaphores. Data moves between devices by JAX's collectives and lax.ppermute only.
A program may use at most 64 MiB of HBM per device.

```python
import jax
import jax.numpy as jnp
from jax import lax

C = 128
H = 128
DMAX = 8
N = 64


def draw_dilations(key, part):
    key = jax.random.fold_in(key, 7)
    other = jax.random.randint(jax.random.fold_in(key, 11), (), 1, DMAX)
    which = jax.random.randint(jax.random.fold_in(key, 12), (), 0, 2)
    return jnp.where(jnp.arange(2) == which, DMAX, other).astype(jnp.int32)


def place_ends(entries, stream_key, smallest, high):
    extent = entries.shape
    spot = [jax.random.randint(jax.random.fold_in(stream_key, axis), (), 0, extent[axis]) for axis in range(len(extent))]
    entries = entries.at[tuple(spot)].set(smallest)
    longest = extent.index(max(extent))
    spot[longest] = (spot[longest] + 1) % extent[longest]
    return entries.at[tuple(spot)].set(high)


def shard_levels(stream_key, dims, cuts, low, largest):
    def one(axis_at, parts):
        steps = jax.random.uniform(jax.random.fold_in(jax.random.fold_in(stream_key, 6), axis_at), (parts,), jnp.float32, low / len(cuts), largest / len(cuts))
        return jnp.repeat(jnp.exp(steps), dims[axis_at] // parts).reshape((-1,) + (1,) * (len(dims) - axis_at - 1))

    gain = one(*cuts[0])
    for cut in cuts[1:]:
        gain = gain * one(*cut)
    return gain


def gaussian(rng, shape, deviation, most, pieces=(), dtype=jnp.bfloat16):
    array = deviation * jax.random.normal(rng, shape, jnp.float32)
    if pieces:
        array = array * shard_levels(rng, shape, pieces, -0.22, 0.18)
    return jnp.clip(array, -most, most).astype(dtype)


def setup_inputs(seed: int = 0) -> dict:
    key_list = jax.random.split(jax.random.key(seed), 11)
    return {
        "pair": gaussian(key_list[0], (N, N, C), 1.0, 6.0, ((0, 4), (1, 8))),
        "pair_mask": place_ends((jax.random.randint(key_list[1], (N, N), 0, 4) < 3).astype(jnp.int32), jax.random.fold_in(key_list[1], 1), 0, 1),
        "contact_mask": place_ends((jax.random.randint(key_list[2], (N, N), 0, 2) < 1).astype(jnp.int32), jax.random.fold_in(key_list[2], 1), 0, 1),
        "dilations": draw_dilations(jax.random.fold_in(key_list[10], 71), 0),
        "w_proj": gaussian(key_list[4], (C, 4 * H), C ** -0.5, 0.5),
        "w_gate": gaussian(key_list[5], (C, C), C ** -0.5, 0.5),
        "w_out": gaussian(key_list[6], (H, C), H ** -0.5, 0.5),
        "conv_one": gaussian(key_list[7], (9, C, C), (9 * C) ** -0.5, 0.1875),
        "conv_two": gaussian(key_list[8], (9, C, C), (9 * C) ** -0.5, 0.1875),
        "cotangent": gaussian(key_list[9], (N, N, C), 1.0, 6.0, ((0, 4), (1, 8))),
    }


EPSILON = 1e-05

def layer_norm(values):
    centre = values - lax.optimization_barrier(jnp.mean(values, axis=-1, keepdims=True))
    spread = lax.optimization_barrier(jnp.mean(centre * centre, axis=-1, keepdims=True))
    return centre * lax.rsqrt(spread + EPSILON)

def pad_border(field):
    return jnp.pad(field, ((DMAX, DMAX), (DMAX, DMAX), (0, 0)))

def window(padded, dilation, row_tap, col_tap, height, breadth):
    row_start = (DMAX + (row_tap - 1) * dilation).astype(jnp.int32)
    col_start = (DMAX + (col_tap - 1) * dilation).astype(jnp.int32)
    return lax.dynamic_slice(padded, (row_start, col_start, jnp.int32(0)), (height, breadth, padded.shape[2]))

def conv_forward(field, weights, dilation):
    height, breadth, channels = field.shape
    padded = pad_border(field)
    result = jnp.zeros((height * breadth, weights.shape[2]), jnp.float32)
    for tap_index in range(9):
        shifted = window(padded, dilation, tap_index // 3, tap_index % 3, height, breadth)
        result = result + jnp.dot(shifted.reshape(-1, channels), weights[tap_index], preferred_element_type=jnp.float32)
    return result

def conv_transpose(field, weights, dilation):
    height, breadth, channels = field.shape
    padded = pad_border(field)
    result = jnp.zeros((height * breadth, weights.shape[1]), jnp.float32)
    for tap_index in range(9):
        shifted = window(padded, dilation, 2 - tap_index // 3, 2 - tap_index % 3, height, breadth)
        result = result + jnp.dot(shifted.reshape(-1, channels), weights[tap_index].T, preferred_element_type=jnp.float32)
    return result

def weight_grad(field, upstream, dilation):
    height, breadth, channels = field.shape
    padded = pad_border(field)
    upstream_flat = upstream.reshape(height * breadth, -1)
    grads = []
    for tap_index in range(9):
        shifted = window(padded, dilation, tap_index // 3, tap_index % 3, height, breadth)
        grads.append(lax.dot_general(shifted.reshape(-1, channels), upstream_flat, (((0,), (0,)), ((), ())), preferred_element_type=jnp.float32))
    return jnp.stack(grads, axis=0)

def reference(pair, pair_mask, contact_mask, dilations, w_proj, w_gate, w_out, conv_one, conv_two, cotangent):
    total, _, channels = pair.shape
    hidden = w_out.shape[0]
    pair_flat = pair.astype(jnp.float32).reshape(-1, channels)
    normed = layer_norm(pair_flat).astype(jnp.bfloat16)
    projected = jnp.dot(normed, w_proj, preferred_element_type=jnp.float32)
    mask_col = pair_mask.reshape(-1, 1).astype(jnp.float32)
    left_side = (mask_col * jax.nn.sigmoid(projected[:, hidden:2 * hidden]) * projected[:, :hidden]).astype(jnp.bfloat16)
    right_side = (mask_col * jax.nn.sigmoid(projected[:, 3 * hidden:]) * projected[:, 2 * hidden:3 * hidden]).astype(jnp.bfloat16)
    left_full = left_side.reshape(total, total, hidden).astype(jnp.float32)
    right_full = right_side.reshape(total, total, hidden).astype(jnp.float32)
    products = jnp.einsum('ikh,jkh->ijh', left_full, right_full)
    product_norm = layer_norm(products.reshape(-1, hidden)).astype(jnp.bfloat16)
    gating = jax.nn.sigmoid(jnp.dot(normed, w_gate, preferred_element_type=jnp.float32))
    updated = (pair_flat + gating * jnp.dot(product_norm, w_out, preferred_element_type=jnp.float32)).astype(jnp.bfloat16)
    updated_f = updated.astype(jnp.float32)
    centre = updated_f - lax.optimization_barrier(jnp.mean(updated_f, axis=-1, keepdims=True))
    inv_spread = lax.rsqrt(lax.optimization_barrier(jnp.mean(centre * centre, axis=-1, keepdims=True)) + EPSILON)
    scaled = centre * inv_spread
    contact = contact_mask.reshape(-1, 1).astype(jnp.float32)
    first_in = (scaled * contact).astype(jnp.bfloat16).reshape(total, total, channels)
    first_pre = conv_forward(first_in, conv_one, dilations[0])
    sigma = jax.nn.sigmoid(first_pre)
    second_in = (first_pre * sigma).astype(jnp.bfloat16).reshape(total, total, channels)
    second_pre = conv_forward(second_in, conv_two, dilations[1])
    output = (updated_f + second_pre).astype(jnp.bfloat16).reshape(total, total, channels)
    grad_two = weight_grad(second_in, cotangent, dilations[1]) / total
    grad_hidden = conv_transpose(cotangent, conv_two, dilations[1])
    grad_pre = (grad_hidden * sigma * (1.0 + first_pre * (1.0 - sigma))).astype(jnp.bfloat16).reshape(total, total, channels)
    grad_one = weight_grad(first_in, grad_pre, dilations[0]) / total
    grad_input = conv_transpose(grad_pre, conv_one, dilations[0]) * contact
    grad_norm = inv_spread * (grad_input - lax.optimization_barrier(jnp.mean(grad_input, axis=-1, keepdims=True)) - scaled * lax.optimization_barrier(jnp.mean(grad_input * scaled, axis=-1, keepdims=True)))
    grad_pair = (cotangent.astype(jnp.float32).reshape(-1, channels) + grad_norm).astype(jnp.bfloat16).reshape(total, total, channels)
    return (output, grad_pair, grad_one, grad_two)
```

```python
import functools

import jax
import jax.numpy as jnp
from jax import lax
from jax.experimental import pallas as pl
from jax.experimental.pallas import tpu as pltpu
from jax.sharding import PartitionSpec as P

DMAX = 8
MASK_ROWS = 16
VMEM_LIMIT = 56 * 1024 * 1024


EPSILON = 1e-05


def with_halo(block, sides, width):
    for axis, dim in sides:
        count = lax.axis_size(axis)
        forward = [(i, i + 1) for i in range(count - 1)]
        backward = [(target, source) for source, target in forward]
        low = lax.ppermute(
            lax.slice_in_dim(block, block.shape[dim] - width, None, axis=dim), axis, forward
        )
        high = lax.ppermute(lax.slice_in_dim(block, 0, width, axis=dim), axis, backward)
        block = jnp.concatenate([low, block, high], axis=dim)
    return block


def broadcast(x, axis, root):
    mine = lax.axis_index(axis) == root
    return lax.psum(jnp.where(mine, x, jnp.zeros_like(x)), axis)


def layer_norm(values):
    centre = values - jnp.mean(values, axis=-1, keepdims=True)
    spread = jnp.mean(centre * centre, axis=-1, keepdims=True)
    return centre * lax.rsqrt(spread + EPSILON)


def with_rim(field):
    return with_halo(field, (("row", 0), ("col", 1)), DMAX)


def gather_taps(padded, dilation, mirrored, height, breadth):
    windows = []
    for tap_index in range(9):
        row_tap = tap_index // 3
        col_tap = tap_index % 3
        if mirrored:
            row_tap = 2 - row_tap
            col_tap = 2 - col_tap
        row_start = DMAX + (row_tap - 1) * dilation
        col_start = DMAX + (col_tap - 1) * dilation
        windows.append(
            lax.dynamic_slice(
                padded, (row_start, col_start, jnp.int32(0)), (height, breadth, padded.shape[2])
            )
        )
    return jnp.concatenate(windows, axis=2).reshape(height * breadth, -1)


def sharded(
    pair, pair_mask, contact_mask, dilations, w_proj, w_gate, w_out, conv_one, conv_two, cotangent
):
    height, breadth, channels = pair.shape
    hidden = w_out.shape[0]
    row_count = lax.axis_size("row")
    col_count = lax.axis_size("col")
    ratio = col_count // row_count
    row_place = lax.axis_index("row")
    col_place = lax.axis_index("col")
    tokens = breadth * col_count
    pixels = height * breadth
    pair_flat = pair.astype(jnp.float32).reshape(pixels, channels)
    normed = layer_norm(pair_flat).astype(jnp.bfloat16)
    projected = jnp.dot(normed, w_proj, preferred_element_type=jnp.float32)
    mask_col = pair_mask.reshape(pixels, 1).astype(jnp.float32)
    left_side = (
        (mask_col * jax.nn.sigmoid(projected[:, hidden : 2 * hidden]) * projected[:, :hidden])
        .astype(jnp.bfloat16)
        .reshape(height, breadth, hidden)
    )
    right_side = (
        (
            mask_col
            * jax.nn.sigmoid(projected[:, 3 * hidden :])
            * projected[:, 2 * hidden : 3 * hidden]
        )
        .astype(jnp.bfloat16)
        .reshape(height, breadth, hidden)
    )
    right_all = lax.all_gather(right_side, "col", axis=1, tiled=True)
    offset = jnp.clip(col_place * breadth - row_place * height, 0, height - breadth)
    right_local = lax.dynamic_slice_in_dim(right_all, offset, breadth, 0)
    right_rows = broadcast(right_local, "row", col_place // ratio)
    products = jnp.einsum(
        "ikh,jkh->ijh",
        lax.all_gather(left_side, "col", axis=1, tiled=True),
        right_rows,
        preferred_element_type=jnp.float32,
    )
    product_norm = layer_norm(products.reshape(pixels, hidden)).astype(jnp.bfloat16)
    gating = jax.nn.sigmoid(jnp.dot(normed, w_gate, preferred_element_type=jnp.float32))
    updated = (
        pair_flat + gating * jnp.dot(product_norm, w_out, preferred_element_type=jnp.float32)
    ).astype(jnp.bfloat16)
    updated_f = updated.astype(jnp.float32)
    centre = updated_f - jnp.mean(updated_f, axis=-1, keepdims=True)
    inv_spread = lax.rsqrt(jnp.mean(centre * centre, axis=-1, keepdims=True) + EPSILON)
    scaled = centre * inv_spread
    contact = contact_mask.reshape(pixels, 1).astype(jnp.float32)
    first_in = (scaled * contact).astype(jnp.bfloat16).reshape(height, breadth, channels)
    rate_one = dilations[0]
    rate_two = dilations[1]
    first_taps = gather_taps(with_rim(first_in), rate_one, False, height, breadth)
    first_pre = jnp.dot(
        first_taps, conv_one.reshape(9 * channels, channels), preferred_element_type=jnp.float32
    )
    sigma = jax.nn.sigmoid(first_pre)
    second_in = (first_pre * sigma).astype(jnp.bfloat16).reshape(height, breadth, channels)
    second_taps = gather_taps(with_rim(second_in), rate_two, False, height, breadth)
    second_pre = jnp.dot(
        second_taps, conv_two.reshape(9 * channels, channels), preferred_element_type=jnp.float32
    )
    output = (updated_f + second_pre).astype(jnp.bfloat16).reshape(height, breadth, channels)
    cot_flat = cotangent.reshape(pixels, channels)
    grad_two = (
        lax.dot_general(
            second_taps, cot_flat, (((0,), (0,)), ((), ())), preferred_element_type=jnp.float32
        ).reshape(9, channels, channels)
        / tokens
    )
    cot_taps = gather_taps(with_rim(cotangent), rate_two, True, height, breadth)
    grad_hidden = jnp.dot(
        cot_taps,
        conv_two.transpose(0, 2, 1).reshape(9 * channels, channels),
        preferred_element_type=jnp.float32,
    )
    grad_pre = (grad_hidden * sigma * (1.0 + first_pre * (1.0 - sigma))).astype(jnp.bfloat16)
    grad_one = (
        lax.dot_general(
            first_taps, grad_pre, (((0,), (0,)), ((), ())), preferred_element_type=jnp.float32
        ).reshape(9, channels, channels)
        / tokens
    )
    grad_taps = gather_taps(
        with_rim(grad_pre.reshape(height, breadth, channels)), rate_one, True, height, breadth
    )
    grad_input = (
        jnp.dot(
            grad_taps,
            conv_one.transpose(0, 2, 1).reshape(9 * channels, channels),
            preferred_element_type=jnp.float32,
        )
        * contact
    )
    grad_norm = inv_spread * (
        grad_input
        - jnp.mean(grad_input, axis=-1, keepdims=True)
        - scaled * jnp.mean(grad_input * scaled, axis=-1, keepdims=True)
    )
    grad_pair = (
        (cot_flat.astype(jnp.float32) + grad_norm)
        .astype(jnp.bfloat16)
        .reshape(height, breadth, channels)
    )
    grad_one, grad_two = lax.psum((grad_one, grad_two), ("row", "col"))
    return (output, grad_pair, grad_one, grad_two)


def exchange_plan(row_count, col_count):
    rounds = []
    distance = col_count // 2
    while distance:
        rounds.append(("col", distance))
        distance //= 2
    distance = row_count // 2
    while distance:
        rounds.append(("row", distance))
        distance //= 2
    return rounds


def gather_blocks(block, rounds):
    held = block[None]
    for step, (axis, distance) in enumerate(rounds):
        pairs = [(i, i ^ distance) for i in range(lax.axis_size(axis))]
        other = lax.ppermute(held, axis, pairs)
        if step < len(rounds) - 1:
            held = jnp.concatenate([held, other], axis=0)
    return held, other


def place_of(position, rounds, row_place, col_place):
    row, col = row_place, col_place
    for step, (axis, distance) in enumerate(rounds):
        bit = ((position >> step) & 1) * distance
        if axis == "row":
            row = row ^ bit
        else:
            col = col ^ bit
    return row, col


def sigmoid(values):
    return 1.0 / (1.0 + jnp.exp(-values))


def matmul(left, right):
    return jnp.dot(left, right, preferred_element_type=jnp.float32)


def block_kernel(
    rounds,
    height,
    breadth,
    tokens,
    scalars,
    near,
    far,
    cot_all,
    w_all,
    w_out,
    one,
    one_t,
    two,
    two_t,
    output,
    grad_pair,
    grad_one,
    grad_two,
    left,
    right,
    gating,
    start,
    contact,
    updated,
    field,
    wide,
    wide_cot,
    second,
    factor,
    grad_pre,
    flipped,
    flipped_two,
    sum_one,
    sum_two,
):
    channels = w_out.shape[1]
    hidden = w_out.shape[0]
    pixels = height * breadth
    row_place, col_place = scalars[0], scalars[1]
    rate_one, rate_two = scalars[2], scalars[3]
    half = near.shape[0]
    line = tokens + 2 * DMAX

    rim = jnp.zeros((tokens, DMAX, channels), jnp.float32)
    field[:, 0:DMAX, :] = rim
    field[:, DMAX + tokens :, :] = rim
    edge = jnp.zeros((DMAX, tokens, 3 * channels), jnp.bfloat16)
    for target in (wide, wide_cot):
        target[0:DMAX] = edge
        target[DMAX + tokens :] = edge
    border = jnp.zeros((DMAX, line, channels), jnp.float32)
    side = jnp.zeros((tokens, DMAX, channels), jnp.float32)
    for target in (second, grad_pre):
        target[0:DMAX] = border
        target[DMAX + tokens :] = border
        target[DMAX : DMAX + tokens, 0:DMAX, :] = side
        target[DMAX : DMAX + tokens, DMAX + tokens :, :] = side

    pick_rows = lax.broadcasted_iota(jnp.int32, (MASK_ROWS, 2 * channels), 0)
    pick_lanes = lax.broadcasted_iota(jnp.int32, (MASK_ROWS, 2 * channels), 1)
    pick = jnp.where(pick_rows == pick_lanes // channels, 1.0, 0.0).astype(jnp.bfloat16)

    def project(source, base):
        def body(slot, carry):
            row, col = place_of(base + slot, rounds, row_place, col_place)
            rows = pl.ds(row * height, height)
            cols = pl.ds(pl.multiple_of(col * breadth, breadth), breadth)
            values = source[slot, 0:pixels, :].astype(jnp.float32)
            masks = lax.dot_general(
                source[slot, pixels:, :],
                pick,
                (((0,), (0,)), ((), ())),
                preferred_element_type=jnp.float32,
            )
            normed = layer_norm(values).astype(jnp.bfloat16)
            projected = matmul(normed, w_all[...])
            shape = (height, breadth, hidden)
            mask = masks[:, :hidden]
            left[rows, cols, :] = (
                mask * sigmoid(projected[:, hidden : 2 * hidden]) * projected[:, :hidden]
            ).reshape(shape)
            right_side = (
                mask
                * sigmoid(projected[:, 3 * hidden : 4 * hidden])
                * projected[:, 2 * hidden : 3 * hidden]
            ).reshape(shape)
            right[cols, pl.ds(pl.multiple_of(row * height, height), height), :] = jnp.swapaxes(
                right_side, 0, 1
            )
            gating[rows, cols, :] = sigmoid(projected[:, 4 * hidden :]).reshape(shape)
            start[rows, cols, :] = values.reshape(shape)
            contact[rows, cols, :] = masks[:, channels:].reshape(shape)
            return carry

        lax.fori_loop(0, half, body, 0)

    project(near, 0)
    project(far, half)

    def spread(rows, rate, target):
        for tap in range(3):
            moved = field[rows, pl.ds(DMAX + (tap - 1) * rate, tokens), :]
            target[
                pl.ds(DMAX + rows.start, rows.size), :, tap * channels : (tap + 1) * channels
            ] = moved.astype(jnp.bfloat16)

    def taps(source, first, count, rate):
        views = [
            source[pl.ds(DMAX + first + (tap - 1) * rate, count)].reshape(count * tokens, -1)
            for tap in range(3)
        ]
        return jnp.concatenate(views, axis=1)

    def place_cot(slot, carry):
        row, col = cot_place(slot)
        cols = pl.ds(pl.multiple_of(DMAX + col * breadth, breadth), breadth)
        field[pl.ds(row * height, height), cols, :] = (
            cot_all[slot].astype(jnp.float32).reshape(height, breadth, channels)
        )
        return carry

    def cot_place(slot):
        col_count = tokens // breadth
        return slot // col_count, slot % col_count

    lax.fori_loop(0, 2 * half, place_cot, 0)
    lax.fori_loop(
        0, tokens // 4, lambda i, c: (spread(pl.ds(i * 4, 4), -rate_two, wide_cot), c)[1], 0
    )

    group = 4

    def triangle(step, carry):
        rows = pl.ds(step * group, group)

        def inner(part, sums):
            base = part * 8
            for k in range(8):
                others = right[base + k]
                sums = tuple(
                    total + left[step * group + i, pl.ds(base + k, 1), :] * others
                    for i, total in enumerate(sums)
                )
            return sums

        sums = lax.fori_loop(
            0,
            tokens // 8,
            inner,
            tuple(jnp.zeros((tokens, hidden), jnp.float32) for _ in range(group)),
        )
        product_norm = layer_norm(jnp.concatenate(sums, axis=0)).astype(jnp.bfloat16)
        change = matmul(product_norm, w_out[...]).reshape(group, tokens, channels)
        fresh = (start[rows] + gating[rows] * change).astype(jnp.bfloat16).astype(jnp.float32)
        updated[rows] = fresh
        first_in = layer_norm(fresh) * contact[rows]
        field[rows, DMAX : DMAX + tokens, :] = first_in
        spread(rows, rate_one, wide)
        flat = first_in.reshape(group * tokens, channels)
        flipped[:, pl.ds(pl.multiple_of(step * group * tokens, group * tokens), group * tokens)] = (
            flat.T.astype(jnp.bfloat16)
        )
        return carry

    lax.fori_loop(0, tokens // group, triangle, 0)

    chunk = 8
    size = chunk * tokens

    def first_conv(step, carry):
        first = step * chunk
        pre = matmul(taps(wide, first, chunk, rate_one), one[...])
        sigma = sigmoid(pre)
        second_in = pre * sigma
        factor[pl.ds(first, chunk)] = (sigma * (1.0 + pre * (1.0 - sigma))).reshape(
            chunk, tokens, channels
        )
        second[pl.ds(DMAX + first, chunk), DMAX : DMAX + tokens, :] = second_in.reshape(
            chunk, tokens, channels
        )
        flipped_two[:, pl.ds(pl.multiple_of(step * size, size), size)] = second_in.T.astype(
            jnp.bfloat16
        )
        return carry

    lax.fori_loop(0, tokens // chunk, first_conv, 0)

    sum_two[...] = jnp.zeros_like(sum_two)

    def back_two(step, carry):
        first = step * chunk
        shifted = taps(wide_cot, first, chunk, -rate_two)
        sum_two[...] += matmul(
            flipped_two[:, pl.ds(pl.multiple_of(step * size, size), size)], shifted
        )
        rows = pl.ds(first, chunk)
        pre = matmul(shifted, two_t[...]).reshape(chunk, tokens, channels) * factor[rows]
        pre = pre.astype(jnp.bfloat16).astype(jnp.float32)
        grad_pre[pl.ds(DMAX + first, chunk), DMAX : DMAX + tokens, :] = pre
        return carry

    lax.fori_loop(0, tokens // chunk, back_two, 0)

    def spread_pre(step, carry):
        rows = pl.ds(DMAX + step * 4, 4)
        for tap in range(3):
            moved = grad_pre[rows, pl.ds(DMAX - (tap - 1) * rate_one, tokens), :]
            wide[rows, :, tap * channels : (tap + 1) * channels] = moved.astype(jnp.bfloat16)
        return carry

    lax.fori_loop(0, tokens // 4, spread_pre, 0)

    sum_one[...] = jnp.zeros_like(sum_one)

    def back_one(step, carry):
        shifted = taps(wide, step * chunk, chunk, -rate_one)
        sum_one[...] += matmul(
            flipped[:, pl.ds(pl.multiple_of(step * size, size), size)], shifted
        )
        return carry

    lax.fori_loop(0, tokens // chunk, back_one, 0)
    for tap in range(9):
        lanes = slice(tap * channels, (tap + 1) * channels)
        grad_one[tap] = sum_one[:, lanes] * (1.0 / tokens)
        grad_two[tap] = sum_two[:, lanes] * (1.0 / tokens)

    row_start, col_start = row_place * height, col_place * breadth

    def windows(source, rate):
        views = [
            source[
                pl.ds(row_start + DMAX + (tap // 3 - 1) * rate, height),
                pl.ds(col_start + DMAX + (tap % 3 - 1) * rate, breadth),
                :,
            ].reshape(pixels, channels)
            for tap in range(9)
        ]
        return jnp.concatenate(views, axis=1).astype(jnp.bfloat16)

    rows = pl.ds(row_start, height)
    cols = pl.ds(pl.multiple_of(col_start, breadth), breadth)
    mine = updated[rows, cols, :].reshape(pixels, channels)
    second_pre = matmul(windows(second, rate_two), two[...])
    output[...] = (mine + second_pre).astype(jnp.bfloat16)
    grad_input = matmul(windows(grad_pre, -rate_one), one_t[...]) * contact[rows, cols, :].reshape(
        pixels, channels
    )
    centre = mine - jnp.mean(mine, axis=-1, keepdims=True)
    inv_spread = lax.rsqrt(jnp.mean(centre * centre, axis=-1, keepdims=True) + EPSILON)
    scaled = centre * inv_spread
    grad_norm = inv_spread * (
        grad_input
        - jnp.mean(grad_input, axis=-1, keepdims=True)
        - scaled * jnp.mean(grad_input * scaled, axis=-1, keepdims=True)
    )
    own = row_place * (tokens // breadth) + col_place
    grad_pair[...] = (cot_all[own].astype(jnp.float32) + grad_norm).astype(jnp.bfloat16)


def replicated(
    pair, pair_mask, contact_mask, dilations, w_proj, w_gate, w_out, conv_one, conv_two, cotangent
):
    height, breadth, channels = pair.shape
    hidden = w_out.shape[0]
    row_count, col_count = lax.axis_size("row"), lax.axis_size("col")
    tokens = height * row_count
    pixels = height * breadth
    rounds = exchange_plan(row_count, col_count)
    masks = [
        mask.reshape(1, pixels).astype(jnp.bfloat16) for mask in (pair_mask, contact_mask)
    ]
    filler = jnp.zeros((MASK_ROWS - 2, channels), jnp.bfloat16)
    packed = jnp.concatenate([pair.reshape(pixels, channels), *masks, filler], axis=0)
    near, far = gather_blocks(packed, rounds)
    cot_all = lax.all_gather(cotangent.reshape(pixels, channels), ("row", "col"), axis=0)
    scalars = jnp.concatenate(
        [
            jnp.stack([lax.axis_index("row"), lax.axis_index("col")]).astype(jnp.int32),
            dilations,
        ]
    )
    f32, bf16 = jnp.float32, jnp.bfloat16
    line = tokens + 2 * DMAX
    in_vmem = pl.BlockSpec(memory_space=pltpu.VMEM)
    output, grad_pair, grad_one, grad_two = pl.pallas_call(
        functools.partial(block_kernel, rounds, height, breadth, tokens),
        in_specs=[pl.BlockSpec(memory_space=pltpu.SMEM)] + [in_vmem] * 9,
        out_specs=[in_vmem] * 4,
        out_shape=[
            jax.ShapeDtypeStruct((pixels, channels), bf16),
            jax.ShapeDtypeStruct((pixels, channels), bf16),
            jax.ShapeDtypeStruct((9, channels, channels), f32),
            jax.ShapeDtypeStruct((9, channels, channels), f32),
        ],
        scratch_shapes=[
            pltpu.VMEM((tokens, tokens, hidden), f32),
            pltpu.VMEM((tokens, tokens, hidden), f32),
            pltpu.VMEM((tokens, tokens, channels), f32),
            pltpu.VMEM((tokens, tokens, channels), f32),
            pltpu.VMEM((tokens, tokens, channels), f32),
            pltpu.VMEM((tokens, tokens, channels), f32),
            pltpu.VMEM((tokens, line, channels), f32),
            pltpu.VMEM((line, tokens, 3 * channels), bf16),
            pltpu.VMEM((line, tokens, 3 * channels), bf16),
            pltpu.VMEM((line, line, channels), f32),
            pltpu.VMEM((tokens, tokens, channels), f32),
            pltpu.VMEM((line, line, channels), f32),
            pltpu.VMEM((channels, tokens * tokens), bf16),
            pltpu.VMEM((channels, tokens * tokens), bf16),
            pltpu.VMEM((channels, 9 * channels), f32),
            pltpu.VMEM((channels, 9 * channels), f32),
        ],
        compiler_params=pltpu.CompilerParams(vmem_limit_bytes=VMEM_LIMIT),
    )(
        scalars,
        near,
        far,
        cot_all,
        jnp.concatenate([w_proj, w_gate], axis=1),
        w_out,
        conv_one.reshape(9 * channels, channels),
        conv_one.transpose(0, 2, 1).reshape(9 * channels, channels),
        conv_two.reshape(9 * channels, channels),
        conv_two.transpose(0, 2, 1).reshape(9 * channels, channels),
    )
    block = (height, breadth, channels)
    return output.reshape(block), grad_pair.reshape(block), grad_one, grad_two


def fits(pair, w_out, row_count, col_count):
    height, breadth, channels = pair.shape
    tokens = height * row_count
    powers = all(count & (count - 1) == 0 for count in (row_count, col_count))
    whole = (tokens + 2 * DMAX) ** 2 * channels
    return (
        powers
        and height * breadth == channels == w_out.shape[0]
        and whole * 60 <= VMEM_LIMIT
    )


def local(*arguments):
    pair, w_out = arguments[0], arguments[6]
    if fits(pair, w_out, lax.axis_size("row"), lax.axis_size("col")):
        return replicated(*arguments)
    return sharded(*arguments)


def solution(mesh):
    in_specs = (
        P("row", "col", None),
        P("row", "col"),
        P("row", "col"),
        P(),
        P(),
        P(),
        P(),
        P(),
        P(),
        P("row", "col", None),
    )
    out_specs = (P("row", "col", None), P("row", "col", None), P(), P())
    return jax.shard_map(local, mesh=mesh, in_specs=in_specs, out_specs=out_specs, check_vma=False)
```

```python
import functools

import jax
import jax.numpy as jnp
from jax import lax
from jax.experimental import pallas as pl
from jax.experimental.pallas import tpu as pltpu
from jax.sharding import PartitionSpec as P

DMAX = 8
VMEM_LIMIT = 56 * 1024 * 1024


EPSILON = 1e-05


def with_halo(block, sides, width):
    for axis, dim in sides:
        count = lax.axis_size(axis)
        forward = [(i, i + 1) for i in range(count - 1)]
        backward = [(target, source) for source, target in forward]
        low = lax.ppermute(
            lax.slice_in_dim(block, block.shape[dim] - width, None, axis=dim), axis, forward
        )
        high = lax.ppermute(lax.slice_in_dim(block, 0, width, axis=dim), axis, backward)
        block = jnp.concatenate([low, block, high], axis=dim)
    return block


def broadcast(x, axis, root):
    mine = lax.axis_index(axis) == root
    return lax.psum(jnp.where(mine, x, jnp.zeros_like(x)), axis)


def layer_norm(values):
    centre = values - jnp.mean(values, axis=-1, keepdims=True)
    spread = jnp.mean(centre * centre, axis=-1, keepdims=True)
    return centre * lax.rsqrt(spread + EPSILON)


def with_rim(field):
    return with_halo(field, (("row", 0), ("col", 1)), DMAX)


def gather_taps(padded, dilation, mirrored, height, breadth):
    windows = []
    for tap_index in range(9):
        row_tap = tap_index // 3
        col_tap = tap_index % 3
        if mirrored:
            row_tap = 2 - row_tap
            col_tap = 2 - col_tap
        row_start = DMAX + (row_tap - 1) * dilation
        col_start = DMAX + (col_tap - 1) * dilation
        windows.append(
            lax.dynamic_slice(
                padded, (row_start, col_start, jnp.int32(0)), (height, breadth, padded.shape[2])
            )
        )
    return jnp.concatenate(windows, axis=2).reshape(height * breadth, -1)


def sharded(
    pair, pair_mask, contact_mask, dilations, w_proj, w_gate, w_out, conv_one, conv_two, cotangent
):
    height, breadth, channels = pair.shape
    hidden = w_out.shape[0]
    row_count = lax.axis_size("row")
    col_count = lax.axis_size("col")
    ratio = col_count // row_count
    row_place = lax.axis_index("row")
    col_place = lax.axis_index("col")
    tokens = breadth * col_count
    pixels = height * breadth
    pair_flat = pair.astype(jnp.float32).reshape(pixels, channels)
    normed = layer_norm(pair_flat).astype(jnp.bfloat16)
    projected = jnp.dot(normed, w_proj, preferred_element_type=jnp.float32)
    mask_col = pair_mask.reshape(pixels, 1).astype(jnp.float32)
    left_side = (
        (mask_col * jax.nn.sigmoid(projected[:, hidden : 2 * hidden]) * projected[:, :hidden])
        .astype(jnp.bfloat16)
        .reshape(height, breadth, hidden)
    )
    right_side = (
        (
            mask_col
            * jax.nn.sigmoid(projected[:, 3 * hidden :])
            * projected[:, 2 * hidden : 3 * hidden]
        )
        .astype(jnp.bfloat16)
        .reshape(height, breadth, hidden)
    )
    right_all = lax.all_gather(right_side, "col", axis=1, tiled=True)
    offset = jnp.clip(col_place * breadth - row_place * height, 0, height - breadth)
    right_local = lax.dynamic_slice_in_dim(right_all, offset, breadth, 0)
    right_rows = broadcast(right_local, "row", col_place // ratio)
    products = jnp.einsum(
        "ikh,jkh->ijh",
        lax.all_gather(left_side, "col", axis=1, tiled=True),
        right_rows,
        preferred_element_type=jnp.float32,
    )
    product_norm = layer_norm(products.reshape(pixels, hidden)).astype(jnp.bfloat16)
    gating = jax.nn.sigmoid(jnp.dot(normed, w_gate, preferred_element_type=jnp.float32))
    updated = (
        pair_flat + gating * jnp.dot(product_norm, w_out, preferred_element_type=jnp.float32)
    ).astype(jnp.bfloat16)
    updated_f = updated.astype(jnp.float32)
    centre = updated_f - jnp.mean(updated_f, axis=-1, keepdims=True)
    inv_spread = lax.rsqrt(jnp.mean(centre * centre, axis=-1, keepdims=True) + EPSILON)
    scaled = centre * inv_spread
    contact = contact_mask.reshape(pixels, 1).astype(jnp.float32)
    first_in = (scaled * contact).astype(jnp.bfloat16).reshape(height, breadth, channels)
    rate_one = dilations[0]
    rate_two = dilations[1]
    first_taps = gather_taps(with_rim(first_in), rate_one, False, height, breadth)
    first_pre = jnp.dot(
        first_taps, conv_one.reshape(9 * channels, channels), preferred_element_type=jnp.float32
    )
    sigma = jax.nn.sigmoid(first_pre)
    second_in = (first_pre * sigma).astype(jnp.bfloat16).reshape(height, breadth, channels)
    second_taps = gather_taps(with_rim(second_in), rate_two, False, height, breadth)
    second_pre = jnp.dot(
        second_taps, conv_two.reshape(9 * channels, channels), preferred_element_type=jnp.float32
    )
    output = (updated_f + second_pre).astype(jnp.bfloat16).reshape(height, breadth, channels)
    cot_flat = cotangent.reshape(pixels, channels)
    grad_two = (
        lax.dot_general(
            second_taps, cot_flat, (((0,), (0,)), ((), ())), preferred_element_type=jnp.float32
        ).reshape(9, channels, channels)
        / tokens
    )
    cot_taps = gather_taps(with_rim(cotangent), rate_two, True, height, breadth)
    grad_hidden = jnp.dot(
        cot_taps,
        conv_two.transpose(0, 2, 1).reshape(9 * channels, channels),
        preferred_element_type=jnp.float32,
    )
    grad_pre = (grad_hidden * sigma * (1.0 + first_pre * (1.0 - sigma))).astype(jnp.bfloat16)
    grad_one = (
        lax.dot_general(
            first_taps, grad_pre, (((0,), (0,)), ((), ())), preferred_element_type=jnp.float32
        ).reshape(9, channels, channels)
        / tokens
    )
    grad_taps = gather_taps(
        with_rim(grad_pre.reshape(height, breadth, channels)), rate_one, True, height, breadth
    )
    grad_input = (
        jnp.dot(
            grad_taps,
            conv_one.transpose(0, 2, 1).reshape(9 * channels, channels),
            preferred_element_type=jnp.float32,
        )
        * contact
    )
    grad_norm = inv_spread * (
        grad_input
        - jnp.mean(grad_input, axis=-1, keepdims=True)
        - scaled * jnp.mean(grad_input * scaled, axis=-1, keepdims=True)
    )
    grad_pair = (
        (cot_flat.astype(jnp.float32) + grad_norm)
        .astype(jnp.bfloat16)
        .reshape(height, breadth, channels)
    )
    grad_one, grad_two = lax.psum((grad_one, grad_two), ("row", "col"))
    return (output, grad_pair, grad_one, grad_two)


def halvings(axis, count):
    return [(axis, count >> step) for step in range(1, count.bit_length())]


def exchange_plan(row_count, col_count):
    rows, cols = halvings("row", row_count), halvings("col", col_count)
    return cols + rows, rows[:-1] + cols + rows[-1:]


def gather_blocks(block, rounds):
    held = block[None]
    for step, (axis, distance) in enumerate(rounds):
        pairs = [(i, i ^ distance) for i in range(lax.axis_size(axis))]
        other = lax.ppermute(held, axis, pairs)
        if step < len(rounds) - 1:
            held = jnp.concatenate([held, other], axis=0)
    return held, other


def place_of(position, rounds, row_place, col_place):
    row, col = row_place, col_place
    for step, (axis, distance) in enumerate(rounds):
        bit = ((position >> step) & 1) * distance
        if axis == "row":
            row = row ^ bit
        else:
            col = col ^ bit
    return row, col


def sigmoid(values):
    return 0.5 + 0.5 * jnp.tanh(0.5 * values)


def matmul(left, right):
    return jnp.dot(left, right, preferred_element_type=jnp.float32)


def block_kernel(
    rounds,
    cot_rounds,
    height,
    breadth,
    tokens,
    scalars,
    near,
    far,
    cot_near,
    cot_far,
    w_all,
    w_out,
    one,
    one_t,
    two,
    two_t,
    output,
    grad_pair,
    grad_one,
    grad_two,
    left,
    right,
    gating,
    start,
    contact,
    updated,
    field,
    wide,
    wide_cot,
    second,
    factor,
    grad_pre,
    flipped,
    flipped_two,
    sum_one,
    sum_two,
):
    channels = w_out.shape[1]
    hidden = w_out.shape[0]
    pixels = height * breadth
    row_place, col_place = scalars[0], scalars[1]
    rate_one, rate_two = scalars[2], scalars[3]
    half = near.shape[0]
    line = tokens + 2 * DMAX

    rim = jnp.zeros((tokens, DMAX, channels), jnp.float32)
    field[:, 0:DMAX, :] = rim
    field[:, DMAX + tokens :, :] = rim
    edge = jnp.zeros((DMAX, tokens, 3 * channels), jnp.bfloat16)
    for target in (wide, wide_cot):
        target[0:DMAX] = edge
        target[DMAX + tokens :] = edge
    border = jnp.zeros((DMAX, line, channels), jnp.float32)
    side = jnp.zeros((tokens, DMAX, channels), jnp.float32)
    for target in (second, grad_pre):
        target[0:DMAX] = border
        target[DMAX + tokens :] = border
        target[DMAX : DMAX + tokens, 0:DMAX, :] = side
        target[DMAX : DMAX + tokens, DMAX + tokens :, :] = side

    lane = lax.broadcasted_iota(jnp.int32, (breadth, channels), 1)
    place = lax.broadcasted_iota(jnp.int32, (breadth, channels), 0)
    own_lane = jnp.where((lane % breadth == place) & (lane < 2 * breadth), 1.0, 0.0)
    pick_lane = lax.broadcasted_iota(jnp.int32, (channels, 2 * channels), 0)
    pick_half = lax.broadcasted_iota(jnp.int32, (channels, 2 * channels), 1) // channels
    pick = jnp.where(pick_lane // breadth == pick_half, 1.0, 0.0).astype(jnp.bfloat16)
    several = 4

    def project(source, base):
        def body(step, carry):
            first = step * several
            masks = jnp.concatenate(
                [
                    (
                        source[first + i, pixels:, :].astype(jnp.float32)[:, None, :]
                        * own_lane[None]
                    ).reshape(pixels, channels)
                    for i in range(several)
                ],
                axis=0,
            ).astype(jnp.bfloat16)
            masks = matmul(masks, pick)
            values = jnp.concatenate(
                [source[first + i, 0:pixels, :] for i in range(several)], axis=0
            ).astype(jnp.float32)
            normed = layer_norm(values).astype(jnp.bfloat16)
            projected = matmul(normed, w_all[...])
            mask = masks[:, :hidden]
            left_side = (
                mask * sigmoid(projected[:, hidden : 2 * hidden]) * projected[:, :hidden]
            )
            right_side = (
                mask
                * sigmoid(projected[:, 3 * hidden : 4 * hidden])
                * projected[:, 2 * hidden : 3 * hidden]
            )
            gates = sigmoid(projected[:, 4 * hidden :])
            shape = (height, breadth, channels)
            for i in range(several):
                row, col = place_of(base + first + i, rounds, row_place, col_place)
                rows = pl.ds(pl.multiple_of(row * height, height), height)
                cols = pl.ds(pl.multiple_of(col * breadth, breadth), breadth)
                part = slice(i * pixels, (i + 1) * pixels)
                left[rows, cols, :] = left_side[part].reshape(shape)
                right[cols, rows, :] = jnp.swapaxes(right_side[part].reshape(shape), 0, 1)
                gating[rows, cols, :] = gates[part].reshape(shape)
                start[rows, cols, :] = values[part].reshape(shape)
                contact[rows, cols, :] = masks[part, channels:].reshape(shape)
            return carry

        lax.fori_loop(0, half // several, body, 0)

    project(near, 0)
    project(far, half)

    def spread(rows, rate, target):
        for tap in range(3):
            moved = field[rows, pl.ds(DMAX + (tap - 1) * rate, tokens), :]
            target[
                pl.ds(DMAX + rows.start, rows.size), :, tap * channels : (tap + 1) * channels
            ] = moved.astype(jnp.bfloat16)

    def taps(source, first, count, rate):
        views = [
            source[pl.ds(DMAX + first + (tap - 1) * rate, count)].reshape(count * tokens, -1)
            for tap in range(3)
        ]
        return jnp.concatenate(views, axis=1)

    def place_cot(source, base):
        def body(step, carry):
            for i in range(several):
                slot = step * several + i
                row, col = place_of(base + slot, cot_rounds, row_place, col_place)
                cols = pl.ds(pl.multiple_of(DMAX + col * breadth, breadth), breadth)
                field[pl.ds(row * height, height), cols, :] = (
                    source[slot].astype(jnp.float32).reshape(height, breadth, channels)
                )
            return carry

        lax.fori_loop(0, half // several, body, 0)

    chunk = 8
    size = chunk * tokens
    steps = tokens // chunk
    place_cot(cot_near, 0)
    place_cot(cot_far, half)
    lax.fori_loop(
        0, steps, lambda i, c: (spread(pl.ds(i * chunk, chunk), -rate_two, wide_cot), c)[1], 0
    )

    group = 4

    def triangle(step, carry):
        def inner(part, sums):
            base = pl.multiple_of(part * 8, 8)
            for k in range(8):
                others = right[base + k]
                sums = tuple(
                    total + left[step * group + i, pl.ds(base + k, 1), :] * others
                    for i, total in enumerate(sums)
                )
            return sums

        sums = lax.fori_loop(
            0,
            tokens // 8,
            inner,
            tuple(jnp.zeros((tokens, hidden), jnp.float32) for _ in range(group)),
        )
        for i, total in enumerate(sums):
            left[step * group + i] = total
        return carry

    lax.fori_loop(0, tokens // group, triangle, 0)

    def update(step, carry):
        rows = pl.ds(step * chunk, chunk)
        products = left[rows].reshape(size, hidden)
        product_norm = layer_norm(products).astype(jnp.bfloat16)
        change = matmul(product_norm, w_out[...]).reshape(chunk, tokens, channels)
        fresh = (start[rows] + gating[rows] * change).astype(jnp.bfloat16).astype(jnp.float32)
        updated[rows] = fresh
        first_in = layer_norm(fresh) * contact[rows]
        field[rows, DMAX : DMAX + tokens, :] = first_in
        spread(rows, rate_one, wide)
        flipped[:, pl.ds(pl.multiple_of(step * size, size), size)] = (
            first_in.reshape(size, channels).astype(jnp.bfloat16).T
        )
        return carry

    lax.fori_loop(0, steps, update, 0)

    def first_conv(step, carry):
        first = step * chunk
        pre = matmul(taps(wide, first, chunk, rate_one), one[...])
        sigma = sigmoid(pre)
        second_in = pre * sigma
        factor[pl.ds(first, chunk)] = (sigma * (1.0 + pre * (1.0 - sigma))).reshape(
            chunk, tokens, channels
        )
        second[pl.ds(DMAX + first, chunk), DMAX : DMAX + tokens, :] = second_in.reshape(
            chunk, tokens, channels
        )
        flipped_two[:, pl.ds(pl.multiple_of(step * size, size), size)] = second_in.astype(
            jnp.bfloat16
        ).T
        return carry

    lax.fori_loop(0, steps, first_conv, 0)

    sum_two[...] = jnp.zeros_like(sum_two)

    def back_two(step, carry):
        first = step * chunk
        shifted = taps(wide_cot, first, chunk, -rate_two)
        sum_two[...] += matmul(
            flipped_two[:, pl.ds(pl.multiple_of(step * size, size), size)], shifted
        )
        rows = pl.ds(first, chunk)
        pre = matmul(shifted, two_t[...]).reshape(chunk, tokens, channels) * factor[rows]
        pre = pre.astype(jnp.bfloat16).astype(jnp.float32)
        grad_pre[pl.ds(DMAX + first, chunk), DMAX : DMAX + tokens, :] = pre
        return carry

    lax.fori_loop(0, steps, back_two, 0)

    def spread_pre(step, carry):
        rows = pl.ds(DMAX + step * chunk, chunk)
        for tap in range(3):
            moved = grad_pre[rows, pl.ds(DMAX - (tap - 1) * rate_one, tokens), :]
            wide[rows, :, tap * channels : (tap + 1) * channels] = moved.astype(jnp.bfloat16)
        return carry

    lax.fori_loop(0, steps, spread_pre, 0)

    sum_one[...] = jnp.zeros_like(sum_one)

    def back_one(step, carry):
        shifted = taps(wide, step * chunk, chunk, -rate_one)
        sum_one[...] += matmul(
            flipped[:, pl.ds(pl.multiple_of(step * size, size), size)], shifted
        )
        return carry

    lax.fori_loop(0, steps, back_one, 0)
    for tap in range(9):
        lanes = slice(tap * channels, (tap + 1) * channels)
        grad_one[tap] = sum_one[:, lanes] * (1.0 / tokens)
        grad_two[tap] = sum_two[:, lanes] * (1.0 / tokens)

    row_start, col_start = row_place * height, col_place * breadth

    def windows(source, rate):
        views = [
            source[
                pl.ds(row_start + DMAX + (tap // 3 - 1) * rate, height),
                pl.ds(col_start + DMAX + (tap % 3 - 1) * rate, breadth),
                :,
            ].reshape(pixels, channels)
            for tap in range(9)
        ]
        return jnp.concatenate(views, axis=1).astype(jnp.bfloat16)

    rows = pl.ds(row_start, height)
    cols = pl.ds(pl.multiple_of(col_start, breadth), breadth)
    mine = updated[rows, cols, :].reshape(pixels, channels)
    second_pre = matmul(windows(second, rate_two), two[...])
    output[...] = (mine + second_pre).astype(jnp.bfloat16)
    grad_input = matmul(windows(grad_pre, -rate_one), one_t[...]) * contact[rows, cols, :].reshape(
        pixels, channels
    )
    centre = mine - jnp.mean(mine, axis=-1, keepdims=True)
    inv_spread = lax.rsqrt(jnp.mean(centre * centre, axis=-1, keepdims=True) + EPSILON)
    scaled = centre * inv_spread
    grad_norm = inv_spread * (
        grad_input
        - jnp.mean(grad_input, axis=-1, keepdims=True)
        - scaled * jnp.mean(grad_input * scaled, axis=-1, keepdims=True)
    )
    grad_pair[...] = (cot_near[0].astype(jnp.float32) + grad_norm).astype(jnp.bfloat16)


def replicated(
    pair, pair_mask, contact_mask, dilations, w_proj, w_gate, w_out, conv_one, conv_two, cotangent
):
    height, breadth, channels = pair.shape
    hidden = w_out.shape[0]
    row_count, col_count = lax.axis_size("row"), lax.axis_size("col")
    tokens = height * row_count
    pixels = height * breadth
    rounds, cot_rounds = exchange_plan(row_count, col_count)
    masks = jnp.concatenate(
        [
            pair_mask.astype(jnp.bfloat16),
            contact_mask.astype(jnp.bfloat16),
            jnp.zeros((height, channels - 2 * breadth), jnp.bfloat16),
        ],
        axis=1,
    )
    packed = jnp.concatenate([pair.reshape(pixels, channels), masks], axis=0)
    near, far = gather_blocks(packed, rounds)
    cot_near, cot_far = gather_blocks(cotangent.reshape(pixels, channels), cot_rounds)
    scalars = jnp.concatenate(
        [
            jnp.stack([lax.axis_index("row"), lax.axis_index("col")]).astype(jnp.int32),
            dilations,
        ]
    )
    f32, bf16 = jnp.float32, jnp.bfloat16
    line = tokens + 2 * DMAX
    in_vmem = pl.BlockSpec(memory_space=pltpu.VMEM)
    output, grad_pair, grad_one, grad_two = pl.pallas_call(
        functools.partial(block_kernel, rounds, cot_rounds, height, breadth, tokens),
        in_specs=[pl.BlockSpec(memory_space=pltpu.SMEM)] + [in_vmem] * 10,
        out_specs=[in_vmem] * 4,
        out_shape=[
            jax.ShapeDtypeStruct((pixels, channels), bf16),
            jax.ShapeDtypeStruct((pixels, channels), bf16),
            jax.ShapeDtypeStruct((9, channels, channels), f32),
            jax.ShapeDtypeStruct((9, channels, channels), f32),
        ],
        scratch_shapes=[
            pltpu.VMEM((tokens, tokens, hidden), f32),
            pltpu.VMEM((tokens, tokens, hidden), f32),
            pltpu.VMEM((tokens, tokens, channels), f32),
            pltpu.VMEM((tokens, tokens, channels), f32),
            pltpu.VMEM((tokens, tokens, channels), f32),
            pltpu.VMEM((tokens, tokens, channels), f32),
            pltpu.VMEM((tokens, line, channels), f32),
            pltpu.VMEM((line, tokens, 3 * channels), bf16),
            pltpu.VMEM((line, tokens, 3 * channels), bf16),
            pltpu.VMEM((line, line, channels), f32),
            pltpu.VMEM((tokens, tokens, channels), f32),
            pltpu.VMEM((line, line, channels), f32),
            pltpu.VMEM((channels, tokens * tokens), bf16),
            pltpu.VMEM((channels, tokens * tokens), bf16),
            pltpu.VMEM((channels, 9 * channels), f32),
            pltpu.VMEM((channels, 9 * channels), f32),
        ],
        compiler_params=pltpu.CompilerParams(vmem_limit_bytes=VMEM_LIMIT),
    )(
        scalars,
        near,
        far,
        cot_near,
        cot_far,
        jnp.concatenate([w_proj, w_gate], axis=1),
        w_out,
        conv_one.reshape(9 * channels, channels),
        conv_one.transpose(0, 2, 1).reshape(9 * channels, channels),
        conv_two.reshape(9 * channels, channels),
        conv_two.transpose(0, 2, 1).reshape(9 * channels, channels),
    )
    block = (height, breadth, channels)
    return output.reshape(block), grad_pair.reshape(block), grad_one, grad_two


def fits(pair, w_out, row_count, col_count):
    height, breadth, channels = pair.shape
    tokens = height * row_count
    powers = all(count & (count - 1) == 0 for count in (row_count, col_count))
    whole = (tokens + 2 * DMAX) ** 2 * channels
    return (
        powers
        and row_count * col_count >= 8
        and height * breadth == channels == w_out.shape[0]
        and whole * 60 <= VMEM_LIMIT
    )


def local(*arguments):
    pair, w_out = arguments[0], arguments[6]
    if fits(pair, w_out, lax.axis_size("row"), lax.axis_size("col")):
        return replicated(*arguments)
    return sharded(*arguments)


def solution(mesh):
    in_specs = (
        P("row", "col", None),
        P("row", "col"),
        P("row", "col"),
        P(),
        P(),
        P(),
        P(),
        P(),
        P(),
        P("row", "col", None),
    )
    out_specs = (P("row", "col", None), P("row", "col", None), P(), P())
    return jax.shard_map(local, mesh=mesh, in_specs=in_specs, out_specs=out_specs, check_vma=False)
```

```python
import functools

import jax
import jax.numpy as jnp
from jax import lax
from jax.experimental import pallas as pl
from jax.experimental.pallas import tpu as pltpu
from jax.sharding import PartitionSpec as P

DMAX = 8
VMEM_LIMIT = 48 * 1024 * 1024


EPSILON = 1e-05


def with_halo(block, sides, width):
    for axis, dim in sides:
        count = lax.axis_size(axis)
        forward = [(i, i + 1) for i in range(count - 1)]
        backward = [(target, source) for source, target in forward]
        low = lax.ppermute(
            lax.slice_in_dim(block, block.shape[dim] - width, None, axis=dim), axis, forward
        )
        high = lax.ppermute(lax.slice_in_dim(block, 0, width, axis=dim), axis, backward)
        block = jnp.concatenate([low, block, high], axis=dim)
    return block


def broadcast(x, axis, root):
    mine = lax.axis_index(axis) == root
    return lax.psum(jnp.where(mine, x, jnp.zeros_like(x)), axis)


def layer_norm(values):
    centre = values - jnp.mean(values, axis=-1, keepdims=True)
    spread = jnp.mean(centre * centre, axis=-1, keepdims=True)
    return centre * lax.rsqrt(spread + EPSILON)


def with_rim(field):
    return with_halo(field, (("row", 0), ("col", 1)), DMAX)


def gather_taps(padded, dilation, mirrored, height, breadth):
    windows = []
    for tap_index in range(9):
        row_tap = tap_index // 3
        col_tap = tap_index % 3
        if mirrored:
            row_tap = 2 - row_tap
            col_tap = 2 - col_tap
        row_start = DMAX + (row_tap - 1) * dilation
        col_start = DMAX + (col_tap - 1) * dilation
        windows.append(
            lax.dynamic_slice(
                padded, (row_start, col_start, jnp.int32(0)), (height, breadth, padded.shape[2])
            )
        )
    return jnp.concatenate(windows, axis=2).reshape(height * breadth, -1)


def sharded(
    pair, pair_mask, contact_mask, dilations, w_proj, w_gate, w_out, conv_one, conv_two, cotangent
):
    height, breadth, channels = pair.shape
    hidden = w_out.shape[0]
    row_count = lax.axis_size("row")
    col_count = lax.axis_size("col")
    ratio = col_count // row_count
    row_place = lax.axis_index("row")
    col_place = lax.axis_index("col")
    tokens = breadth * col_count
    pixels = height * breadth
    pair_flat = pair.astype(jnp.float32).reshape(pixels, channels)
    normed = layer_norm(pair_flat).astype(jnp.bfloat16)
    projected = jnp.dot(normed, w_proj, preferred_element_type=jnp.float32)
    mask_col = pair_mask.reshape(pixels, 1).astype(jnp.float32)
    left_side = (
        (mask_col * jax.nn.sigmoid(projected[:, hidden : 2 * hidden]) * projected[:, :hidden])
        .astype(jnp.bfloat16)
        .reshape(height, breadth, hidden)
    )
    right_side = (
        (
            mask_col
            * jax.nn.sigmoid(projected[:, 3 * hidden :])
            * projected[:, 2 * hidden : 3 * hidden]
        )
        .astype(jnp.bfloat16)
        .reshape(height, breadth, hidden)
    )
    right_all = lax.all_gather(right_side, "col", axis=1, tiled=True)
    offset = jnp.clip(col_place * breadth - row_place * height, 0, height - breadth)
    right_local = lax.dynamic_slice_in_dim(right_all, offset, breadth, 0)
    right_rows = broadcast(right_local, "row", col_place // ratio)
    products = jnp.einsum(
        "ikh,jkh->ijh",
        lax.all_gather(left_side, "col", axis=1, tiled=True),
        right_rows,
        preferred_element_type=jnp.float32,
    )
    product_norm = layer_norm(products.reshape(pixels, hidden)).astype(jnp.bfloat16)
    gating = jax.nn.sigmoid(jnp.dot(normed, w_gate, preferred_element_type=jnp.float32))
    updated = (
        pair_flat + gating * jnp.dot(product_norm, w_out, preferred_element_type=jnp.float32)
    ).astype(jnp.bfloat16)
    updated_f = updated.astype(jnp.float32)
    centre = updated_f - jnp.mean(updated_f, axis=-1, keepdims=True)
    inv_spread = lax.rsqrt(jnp.mean(centre * centre, axis=-1, keepdims=True) + EPSILON)
    scaled = centre * inv_spread
    contact = contact_mask.reshape(pixels, 1).astype(jnp.float32)
    first_in = (scaled * contact).astype(jnp.bfloat16).reshape(height, breadth, channels)
    rate_one = dilations[0]
    rate_two = dilations[1]
    first_taps = gather_taps(with_rim(first_in), rate_one, False, height, breadth)
    first_pre = jnp.dot(
        first_taps, conv_one.reshape(9 * channels, channels), preferred_element_type=jnp.float32
    )
    sigma = jax.nn.sigmoid(first_pre)
    second_in = (first_pre * sigma).astype(jnp.bfloat16).reshape(height, breadth, channels)
    second_taps = gather_taps(with_rim(second_in), rate_two, False, height, breadth)
    second_pre = jnp.dot(
        second_taps, conv_two.reshape(9 * channels, channels), preferred_element_type=jnp.float32
    )
    output = (updated_f + second_pre).astype(jnp.bfloat16).reshape(height, breadth, channels)
    cot_flat = cotangent.reshape(pixels, channels)
    grad_two = (
        lax.dot_general(
            second_taps, cot_flat, (((0,), (0,)), ((), ())), preferred_element_type=jnp.float32
        ).reshape(9, channels, channels)
        / tokens
    )
    cot_taps = gather_taps(with_rim(cotangent), rate_two, True, height, breadth)
    grad_hidden = jnp.dot(
        cot_taps,
        conv_two.transpose(0, 2, 1).reshape(9 * channels, channels),
        preferred_element_type=jnp.float32,
    )
    grad_pre = (grad_hidden * sigma * (1.0 + first_pre * (1.0 - sigma))).astype(jnp.bfloat16)
    grad_one = (
        lax.dot_general(
            first_taps, grad_pre, (((0,), (0,)), ((), ())), preferred_element_type=jnp.float32
        ).reshape(9, channels, channels)
        / tokens
    )
    grad_taps = gather_taps(
        with_rim(grad_pre.reshape(height, breadth, channels)), rate_one, True, height, breadth
    )
    grad_input = (
        jnp.dot(
            grad_taps,
            conv_one.transpose(0, 2, 1).reshape(9 * channels, channels),
            preferred_element_type=jnp.float32,
        )
        * contact
    )
    grad_norm = inv_spread * (
        grad_input
        - jnp.mean(grad_input, axis=-1, keepdims=True)
        - scaled * jnp.mean(grad_input * scaled, axis=-1, keepdims=True)
    )
    grad_pair = (
        (cot_flat.astype(jnp.float32) + grad_norm)
        .astype(jnp.bfloat16)
        .reshape(height, breadth, channels)
    )
    grad_one, grad_two = lax.psum((grad_one, grad_two), ("row", "col"))
    return (output, grad_pair, grad_one, grad_two)


def halvings(axis, count):
    return [(axis, count >> step) for step in range(1, count.bit_length())]


def exchange_plan(row_count, col_count):
    rows, cols = halvings("row", row_count), halvings("col", col_count)
    return cols + rows, rows[:-1] + cols + rows[-1:]


def gather_blocks(block, rounds):
    held = block[None]
    for step, (axis, distance) in enumerate(rounds):
        pairs = [(i, i ^ distance) for i in range(lax.axis_size(axis))]
        other = lax.ppermute(held, axis, pairs)
        if step < len(rounds) - 1:
            held = jnp.concatenate([held, other], axis=0)
    return held, other


def place_of(position, rounds, row_place, col_place):
    row, col = row_place, col_place
    for step, (axis, distance) in enumerate(rounds):
        bit = ((position >> step) & 1) * distance
        if axis == "row":
            row = row ^ bit
        else:
            col = col ^ bit
    return row, col


def same_place(position, rounds, others):
    moved = 0
    for step, hop in enumerate(rounds):
        moved = moved | (((position >> step) & 1) << others.index(hop))
    return moved


def sigmoid(values):
    return 0.5 + 0.5 * jnp.tanh(0.5 * values)


def matmul(left, right):
    return jnp.dot(left, right, preferred_element_type=jnp.float32)


def block_kernel(
    rounds,
    cot_rounds,
    height,
    breadth,
    tokens,
    dilations,
    near,
    far,
    cot_near,
    cot_far,
    w_proj,
    w_gate,
    w_out,
    one,
    two,
    output,
    grad_pair,
    grad_one,
    grad_two,
    left,
    right,
    gating,
    start,
    contact,
    updated,
    products,
    field,
    cot_field,
    wide,
    wide_cot,
    wide_pre,
    second,
    hidden_grad,
    grad_pre,
    flipped,
    flipped_two,
    sum_one,
    sum_two,
    two_t,
):
    channels = w_out.shape[1]
    hidden = w_out.shape[0]
    pixels = height * breadth
    row_place, col_place = lax.axis_index("row"), lax.axis_index("col")
    rate_one, rate_two = dilations[0], dilations[1]
    half = near.shape[0]
    line = tokens + 2 * DMAX
    inside = slice(DMAX, DMAX + tokens)

    rim = jnp.zeros((tokens, DMAX, channels), jnp.float32)
    edge = jnp.zeros((DMAX, tokens, 3 * channels), jnp.bfloat16)
    border = jnp.zeros((DMAX, line, channels), jnp.float32)
    for target in (field, cot_field):
        target[:, 0:DMAX, :] = rim
        target[:, DMAX + tokens :, :] = rim
    for target in (wide, wide_cot, wide_pre):
        target[0:DMAX] = edge
        target[DMAX + tokens :] = edge
    for target in (second, grad_pre):
        target[0:DMAX] = border
        target[DMAX + tokens :] = border
        target[inside, 0:DMAX, :] = rim
        target[inside, DMAX + tokens :, :] = rim
    for tap in range(9):
        two_t[tap * channels : (tap + 1) * channels] = two[tap].T

    lane = lax.broadcasted_iota(jnp.int32, (breadth, channels), 1)
    place = lax.broadcasted_iota(jnp.int32, (breadth, channels), 0)
    own_lane = jnp.where((lane % breadth == place) & (lane < 2 * breadth), 1.0, 0.0)
    pick_lane = lax.broadcasted_iota(jnp.int32, (channels, 2 * channels), 0)
    pick_half = lax.broadcasted_iota(jnp.int32, (channels, 2 * channels), 1) // channels
    pick = jnp.where(pick_lane // breadth == pick_half, 1.0, 0.0).astype(jnp.bfloat16)
    several = 4

    def project(source, cot_source, base):
        def body(step, carry):
            first = step * several
            partners = [
                same_place(first + i, rounds[:-1], cot_rounds[:-1]) for i in range(several)
            ]
            masks = jnp.concatenate(
                [
                    (
                        cot_source[partner, pixels:, :].astype(jnp.float32)[:, None, :]
                        * own_lane[None]
                    ).reshape(pixels, channels)
                    for partner in partners
                ],
                axis=0,
            ).astype(jnp.bfloat16)
            masks = matmul(masks, pick)
            values = (
                source[pl.ds(first, several)]
                .reshape(several * pixels, channels)
                .astype(jnp.float32)
            )
            normed = layer_norm(values).astype(jnp.bfloat16)
            projected = matmul(normed, w_proj[...])
            mask = masks[:, :hidden]
            left_side = (
                mask * sigmoid(projected[:, hidden : 2 * hidden]) * projected[:, :hidden]
            )
            right_side = (
                mask
                * sigmoid(projected[:, 3 * hidden :])
                * projected[:, 2 * hidden : 3 * hidden]
            )
            gates = sigmoid(matmul(normed, w_gate[...]))
            shape = (height, breadth, channels)
            for i in range(several):
                row, col = place_of(base + first + i, rounds, row_place, col_place)
                rows = pl.ds(pl.multiple_of(row * height, height), height)
                cols = pl.ds(pl.multiple_of(col * breadth, breadth), breadth)
                padded = pl.ds(pl.multiple_of(DMAX + col * breadth, breadth), breadth)
                part = slice(i * pixels, (i + 1) * pixels)
                left[rows, cols, :] = left_side[part].reshape(shape)
                right[cols, rows, :] = jnp.swapaxes(right_side[part].reshape(shape), 0, 1)
                gating[rows, cols, :] = gates[part].reshape(shape)
                start[rows, cols, :] = values[part].reshape(shape)
                contact[rows, cols, :] = masks[part, channels:].reshape(shape)
                cot_field[rows, padded, :] = (
                    cot_source[partners[i], 0:pixels, :].astype(jnp.float32).reshape(shape)
                )
            return carry

        lax.fori_loop(0, half // several, body, 0)

    project(near, cot_near, 0)
    project(far, cot_far, half)

    def spread(source, rows, pad, rate, target):
        for tap in range(3):
            moved = source[
                pl.ds(pad + rows.start, rows.size), pl.ds(DMAX + (tap - 1) * rate, tokens), :
            ]
            target[
                pl.ds(DMAX + rows.start, rows.size), :, tap * channels : (tap + 1) * channels
            ] = moved.astype(jnp.bfloat16)

    def taps(source, first, count, rate):
        views = [
            source[pl.ds(DMAX + first + (tap - 1) * rate, count)].reshape(count * tokens, -1)
            for tap in range(3)
        ]
        return jnp.concatenate(views, axis=1)

    def lanes(step, size):
        return pl.ds(pl.multiple_of(step * size, size), size)

    chunk = 8
    size = chunk * tokens
    steps = tokens // chunk

    def spread_cot(step, carry):
        spread(cot_field, pl.ds(step * chunk, chunk), 0, -rate_two, wide_cot)
        return carry

    lax.fori_loop(0, steps, spread_cot, 0)

    group = 4

    def triangle(step):
        sums = [jnp.zeros((tokens, hidden), jnp.float32)] * group
        for k in range(tokens):
            others = right[k]
            sums = [
                total + left[step * group + i, k : k + 1, :] * others
                for i, total in enumerate(sums)
            ]
        for i, total in enumerate(sums):
            products[step * group + i] = total

    def hidden_conv(step):
        hidden_grad[pl.ds(step * group, group)] = matmul(
            taps(wide_cot, step * group, group, -rate_two), two_t[...]
        ).reshape(group, tokens, channels)

    def update(step):
        rows = pl.ds(step * group, group)
        flat = products[rows].reshape(group * tokens, hidden)
        product_norm = layer_norm(flat).astype(jnp.bfloat16)
        change = matmul(product_norm, w_out[...]).reshape(group, tokens, channels)
        fresh = (start[rows] + gating[rows] * change).astype(jnp.bfloat16).astype(jnp.float32)
        updated[rows] = fresh
        first_in = layer_norm(fresh) * contact[rows]
        field[rows, inside, :] = first_in
        spread(field, rows, 0, rate_one, wide)
        flipped[:, lanes(step, group * tokens)] = (
            first_in.reshape(group * tokens, channels).astype(jnp.bfloat16).T
        )

    def early(step, carry):
        triangle(step)
        hidden_conv(step)
        update(step - 1)
        return carry

    triangle(0)
    hidden_conv(0)
    lax.fori_loop(1, tokens // group, early, 0)
    update(tokens // group - 1)

    def first_conv(step):
        first = step * chunk
        rows = pl.ds(DMAX + first, chunk)
        shape = (chunk, tokens, channels)
        pre = matmul(taps(wide, first, chunk, rate_one), one[...])
        sigma = sigmoid(pre)
        second_in = pre * sigma
        second[rows, inside, :] = second_in.reshape(shape)
        flipped_two[:, lanes(step, size)] = second_in.astype(jnp.bfloat16).T
        factor = (sigma * (1.0 + pre * (1.0 - sigma))).reshape(shape)
        grad_pre[rows, inside, :] = (
            (hidden_grad[pl.ds(first, chunk)] * factor).astype(jnp.bfloat16).astype(jnp.float32)
        )

    def after_conv(step):
        sum_two[...] += matmul(
            flipped_two[:, lanes(step, size)], taps(wide_cot, step * chunk, chunk, -rate_two)
        )
        spread(grad_pre, pl.ds(step * chunk, chunk), DMAX, -rate_one, wide_pre)

    def middle(step, carry):
        first_conv(step)
        after_conv(step - 1)
        return carry

    sum_two[...] = jnp.zeros_like(sum_two)
    first_conv(0)
    lax.fori_loop(1, steps, middle, 0)
    after_conv(steps - 1)

    sum_one[...] = jnp.zeros_like(sum_one)

    def back_one(step, carry):
        sum_one[...] += matmul(
            flipped[:, lanes(step, size)], taps(wide_pre, step * chunk, chunk, -rate_one)
        )
        return carry

    lax.fori_loop(0, steps, back_one, 0)
    for tap in range(9):
        columns = slice(tap * channels, (tap + 1) * channels)
        grad_one[tap] = sum_one[:, columns] * (1.0 / tokens)
        grad_two[tap] = sum_two[:, columns] * (1.0 / tokens)

    row_start, col_start = row_place * height, col_place * breadth

    def windows(source, rate):
        views = [
            source[
                pl.ds(row_start + DMAX + (tap // 3 - 1) * rate, height),
                pl.ds(col_start + DMAX + (tap % 3 - 1) * rate, breadth),
                :,
            ].reshape(pixels, channels)
            for tap in range(9)
        ]
        return jnp.concatenate(views, axis=1).astype(jnp.bfloat16)

    rows = pl.ds(row_start, height)
    cols = pl.ds(pl.multiple_of(col_start, breadth), breadth)
    mine = updated[rows, cols, :].reshape(pixels, channels)
    second_pre = matmul(windows(second, rate_two), two[...].reshape(9 * channels, channels))
    output[...] = (mine + second_pre).astype(jnp.bfloat16)
    one_rows = [one[tap * channels : (tap + 1) * channels] for tap in range(9)]
    grad_input = lax.dot_general(
        windows(grad_pre, -rate_one),
        jnp.concatenate(one_rows, axis=1),
        (((1,), (1,)), ((), ())),
        preferred_element_type=jnp.float32,
    ) * contact[rows, cols, :].reshape(pixels, channels)
    centre = mine - jnp.mean(mine, axis=-1, keepdims=True)
    inv_spread = lax.rsqrt(jnp.mean(centre * centre, axis=-1, keepdims=True) + EPSILON)
    scaled = centre * inv_spread
    grad_norm = inv_spread * (
        grad_input
        - jnp.mean(grad_input, axis=-1, keepdims=True)
        - scaled * jnp.mean(grad_input * scaled, axis=-1, keepdims=True)
    )
    grad_pair[...] = (cot_near[0, 0:pixels, :].astype(jnp.float32) + grad_norm).astype(
        jnp.bfloat16
    )


def replicated(
    pair, pair_mask, contact_mask, dilations, w_proj, w_gate, w_out, conv_one, conv_two, cotangent
):
    height, breadth, channels = pair.shape
    hidden = w_out.shape[0]
    row_count, col_count = lax.axis_size("row"), lax.axis_size("col")
    tokens = height * row_count
    pixels = height * breadth
    rounds, cot_rounds = exchange_plan(row_count, col_count)
    masks = jnp.concatenate(
        [
            pair_mask.astype(jnp.bfloat16),
            contact_mask.astype(jnp.bfloat16),
            jnp.zeros((height, channels - 2 * breadth), jnp.bfloat16),
        ],
        axis=1,
    )
    packed = jnp.concatenate([cotangent.reshape(pixels, channels), masks], axis=0)
    near, far = gather_blocks(pair.reshape(pixels, channels), rounds)
    cot_near, cot_far = gather_blocks(packed, cot_rounds)
    f32, bf16 = jnp.float32, jnp.bfloat16
    line = tokens + 2 * DMAX
    in_vmem = pl.BlockSpec(memory_space=pltpu.VMEM)
    whole = pltpu.VMEM((tokens, tokens, channels), f32)
    padded = pltpu.VMEM((tokens, line, channels), f32)
    bordered = pltpu.VMEM((line, line, channels), f32)
    tripled = pltpu.VMEM((line, tokens, 3 * channels), bf16)
    turned = pltpu.VMEM((channels, tokens * tokens), bf16)
    sums = pltpu.VMEM((channels, 9 * channels), f32)
    output, grad_pair, grad_one, grad_two = pl.pallas_call(
        functools.partial(block_kernel, rounds, cot_rounds, height, breadth, tokens),
        in_specs=[pl.BlockSpec(memory_space=pltpu.SMEM)] + [in_vmem] * 9,
        out_specs=[in_vmem] * 4,
        out_shape=[
            jax.ShapeDtypeStruct((pixels, channels), bf16),
            jax.ShapeDtypeStruct((pixels, channels), bf16),
            jax.ShapeDtypeStruct((9, channels, channels), f32),
            jax.ShapeDtypeStruct((9, channels, channels), f32),
        ],
        scratch_shapes=[whole] * 7
        + [padded] * 2
        + [tripled] * 3
        + [bordered, whole, bordered]
        + [turned] * 2
        + [sums] * 2
        + [pltpu.VMEM((9 * channels, channels), bf16)],
        compiler_params=pltpu.CompilerParams(vmem_limit_bytes=VMEM_LIMIT),
    )(
        dilations,
        near,
        far,
        cot_near,
        cot_far,
        w_proj,
        w_gate,
        w_out,
        conv_one.reshape(9 * channels, channels),
        conv_two,
    )
    block = (height, breadth, channels)
    return output.reshape(block), grad_pair.reshape(block), grad_one, grad_two


def fits(pair, w_out, row_count, col_count):
    height, breadth, channels = pair.shape
    tokens = height * row_count
    powers = all(count & (count - 1) == 0 for count in (row_count, col_count))
    whole = (tokens + 2 * DMAX) ** 2 * channels
    return (
        powers
        and row_count * col_count >= 8
        and height * breadth == channels == w_out.shape[0]
        and whole * 60 <= VMEM_LIMIT
    )


def local(*arguments):
    pair, w_out = arguments[0], arguments[6]
    if fits(pair, w_out, lax.axis_size("row"), lax.axis_size("col")):
        return replicated(*arguments)
    return sharded(*arguments)


def solution(mesh):
    in_specs = (
        P("row", "col", None),
        P("row", "col"),
        P("row", "col"),
        P(),
        P(),
        P(),
        P(),
        P(),
        P(),
        P("row", "col", None),
    )
    out_specs = (P("row", "col", None), P("row", "col", None), P(), P())
    return jax.shard_map(local, mesh=mesh, in_specs=in_specs, out_specs=out_specs, check_vma=False)
```

```python
import functools

import jax
import jax.numpy as jnp
from jax import lax
from jax.experimental import pallas as pl
from jax.experimental.pallas import tpu as pltpu
from jax.sharding import PartitionSpec as P

DMAX = 8
VMEM_LIMIT = 48 * 1024 * 1024


EPSILON = 1e-05


def with_halo(block, sides, width):
    for axis, dim in sides:
        count = lax.axis_size(axis)
        forward = [(i, i + 1) for i in range(count - 1)]
        backward = [(target, source) for source, target in forward]
        low = lax.ppermute(
            lax.slice_in_dim(block, block.shape[dim] - width, None, axis=dim), axis, forward
        )
        high = lax.ppermute(lax.slice_in_dim(block, 0, width, axis=dim), axis, backward)
        block = jnp.concatenate([low, block, high], axis=dim)
    return block


def broadcast(x, axis, root):
    mine = lax.axis_index(axis) == root
    return lax.psum(jnp.where(mine, x, jnp.zeros_like(x)), axis)


def layer_norm(values, axis=-1):
    centre = values - jnp.mean(values, axis=axis, keepdims=True)
    spread = jnp.mean(centre * centre, axis=axis, keepdims=True)
    return centre * lax.rsqrt(spread + EPSILON)


def with_rim(field):
    return with_halo(field, (("row", 0), ("col", 1)), DMAX)


def gather_taps(padded, dilation, mirrored, height, breadth):
    windows = []
    for tap_index in range(9):
        row_tap = tap_index // 3
        col_tap = tap_index % 3
        if mirrored:
            row_tap = 2 - row_tap
            col_tap = 2 - col_tap
        row_start = DMAX + (row_tap - 1) * dilation
        col_start = DMAX + (col_tap - 1) * dilation
        windows.append(
            lax.dynamic_slice(
                padded, (row_start, col_start, jnp.int32(0)), (height, breadth, padded.shape[2])
            )
        )
    return jnp.concatenate(windows, axis=2).reshape(height * breadth, -1)


def sharded(
    pair, pair_mask, contact_mask, dilations, w_proj, w_gate, w_out, conv_one, conv_two, cotangent
):
    height, breadth, channels = pair.shape
    hidden = w_out.shape[0]
    row_count = lax.axis_size("row")
    col_count = lax.axis_size("col")
    ratio = col_count // row_count
    row_place = lax.axis_index("row")
    col_place = lax.axis_index("col")
    tokens = breadth * col_count
    pixels = height * breadth
    pair_flat = pair.astype(jnp.float32).reshape(pixels, channels)
    normed = layer_norm(pair_flat).astype(jnp.bfloat16)
    projected = jnp.dot(normed, w_proj, preferred_element_type=jnp.float32)
    mask_col = pair_mask.reshape(pixels, 1).astype(jnp.float32)
    left_side = (
        (mask_col * jax.nn.sigmoid(projected[:, hidden : 2 * hidden]) * projected[:, :hidden])
        .astype(jnp.bfloat16)
        .reshape(height, breadth, hidden)
    )
    right_side = (
        (
            mask_col
            * jax.nn.sigmoid(projected[:, 3 * hidden :])
            * projected[:, 2 * hidden : 3 * hidden]
        )
        .astype(jnp.bfloat16)
        .reshape(height, breadth, hidden)
    )
    right_all = lax.all_gather(right_side, "col", axis=1, tiled=True)
    offset = jnp.clip(col_place * breadth - row_place * height, 0, height - breadth)
    right_local = lax.dynamic_slice_in_dim(right_all, offset, breadth, 0)
    right_rows = broadcast(right_local, "row", col_place // ratio)
    products = jnp.einsum(
        "ikh,jkh->ijh",
        lax.all_gather(left_side, "col", axis=1, tiled=True),
        right_rows,
        preferred_element_type=jnp.float32,
    )
    product_norm = layer_norm(products.reshape(pixels, hidden)).astype(jnp.bfloat16)
    gating = jax.nn.sigmoid(jnp.dot(normed, w_gate, preferred_element_type=jnp.float32))
    updated = (
        pair_flat + gating * jnp.dot(product_norm, w_out, preferred_element_type=jnp.float32)
    ).astype(jnp.bfloat16)
    updated_f = updated.astype(jnp.float32)
    centre = updated_f - jnp.mean(updated_f, axis=-1, keepdims=True)
    inv_spread = lax.rsqrt(jnp.mean(centre * centre, axis=-1, keepdims=True) + EPSILON)
    scaled = centre * inv_spread
    contact = contact_mask.reshape(pixels, 1).astype(jnp.float32)
    first_in = (scaled * contact).astype(jnp.bfloat16).reshape(height, breadth, channels)
    rate_one = dilations[0]
    rate_two = dilations[1]
    first_taps = gather_taps(with_rim(first_in), rate_one, False, height, breadth)
    first_pre = jnp.dot(
        first_taps, conv_one.reshape(9 * channels, channels), preferred_element_type=jnp.float32
    )
    sigma = jax.nn.sigmoid(first_pre)
    second_in = (first_pre * sigma).astype(jnp.bfloat16).reshape(height, breadth, channels)
    second_taps = gather_taps(with_rim(second_in), rate_two, False, height, breadth)
    second_pre = jnp.dot(
        second_taps, conv_two.reshape(9 * channels, channels), preferred_element_type=jnp.float32
    )
    output = (updated_f + second_pre).astype(jnp.bfloat16).reshape(height, breadth, channels)
    cot_flat = cotangent.reshape(pixels, channels)
    grad_two = (
        lax.dot_general(
            second_taps, cot_flat, (((0,), (0,)), ((), ())), preferred_element_type=jnp.float32
        ).reshape(9, channels, channels)
        / tokens
    )
    cot_taps = gather_taps(with_rim(cotangent), rate_two, True, height, breadth)
    grad_hidden = jnp.dot(
        cot_taps,
        conv_two.transpose(0, 2, 1).reshape(9 * channels, channels),
        preferred_element_type=jnp.float32,
    )
    grad_pre = (grad_hidden * sigma * (1.0 + first_pre * (1.0 - sigma))).astype(jnp.bfloat16)
    grad_one = (
        lax.dot_general(
            first_taps, grad_pre, (((0,), (0,)), ((), ())), preferred_element_type=jnp.float32
        ).reshape(9, channels, channels)
        / tokens
    )
    grad_taps = gather_taps(
        with_rim(grad_pre.reshape(height, breadth, channels)), rate_one, True, height, breadth
    )
    grad_input = (
        jnp.dot(
            grad_taps,
            conv_one.transpose(0, 2, 1).reshape(9 * channels, channels),
            preferred_element_type=jnp.float32,
        )
        * contact
    )
    grad_norm = inv_spread * (
        grad_input
        - jnp.mean(grad_input, axis=-1, keepdims=True)
        - scaled * jnp.mean(grad_input * scaled, axis=-1, keepdims=True)
    )
    grad_pair = (
        (cot_flat.astype(jnp.float32) + grad_norm)
        .astype(jnp.bfloat16)
        .reshape(height, breadth, channels)
    )
    grad_one, grad_two = lax.psum((grad_one, grad_two), ("row", "col"))
    return (output, grad_pair, grad_one, grad_two)


def halvings(axis, count):
    return [(axis, count >> step) for step in range(1, count.bit_length())]


def exchange_plan(row_count, col_count):
    rows, cols = halvings("row", row_count), halvings("col", col_count)
    return cols + rows, rows[:-1] + cols + rows[-1:]


def gather_blocks(block, rounds):
    held = block[None]
    for step, (axis, distance) in enumerate(rounds):
        pairs = [(i, i ^ distance) for i in range(lax.axis_size(axis))]
        other = lax.ppermute(held, axis, pairs)
        if step < len(rounds) - 1:
            held = jnp.concatenate([held, other], axis=0)
    return held, other


def place_of(position, rounds, row_place, col_place):
    row, col = row_place, col_place
    for step, (axis, distance) in enumerate(rounds):
        bit = ((position >> step) & 1) * distance
        if axis == "row":
            row = row ^ bit
        else:
            col = col ^ bit
    return row, col


def slot_of(row_change, col_change, rounds):
    slot = 0
    for step, (axis, distance) in enumerate(rounds[:-1]):
        change = row_change if axis == "row" else col_change
        slot = slot | (((change // distance) & 1) << step)
    return slot


def sigmoid(values):
    return 0.5 + 0.5 * jnp.tanh(0.5 * values)


def matmul(left, right):
    return jnp.dot(left, right, preferred_element_type=jnp.float32)


def matmul_nt(left, right):
    return lax.dot_general(
        left, right, (((1,), (1,)), ((), ())), preferred_element_type=jnp.float32
    )


def project_half(
    plan, core, pairs, cots, w_proj, w_gate, left, right, swapped, gating, contact, start, turned
):
    rounds, cot_rounds, height, breadth, tokens = plan
    channels, hidden = w_gate.shape[0], w_gate.shape[1]
    col_count, chips = tokens // breadth, tokens // height // 2
    row_place, col_place = lax.axis_index("row"), lax.axis_index("col")
    lane = lax.broadcasted_iota(jnp.int32, (breadth, channels), 1)
    place = lax.broadcasted_iota(jnp.int32, (breadth, channels), 0)
    own_lane = jnp.where((lane % breadth == place) & (lane < 2 * breadth), 1.0, 0.0)
    pick_lane = lax.broadcasted_iota(jnp.int32, (channels, 2 * channels), 0)
    pick_half = lax.broadcasted_iota(jnp.int32, (channels, 2 * channels), 1) // channels
    pick = jnp.where(pick_lane // breadth == pick_half, 1.0, 0.0).astype(jnp.bfloat16)
    pixels = height * breadth
    rows = 8
    for first in range(0, height, rows):
        values, masks = [], []
        for chip in range(chips):
            row_change = (chip * 2 + core) ^ row_place
            blocks, marks = [], []
            for col in range(col_count):
                col_change = col_place ^ col
                slot = slot_of(row_change, col_change, rounds)
                cot_slot = slot_of(row_change, col_change, cot_rounds)
                blocks.append(
                    pairs[slot, first * breadth : (first + rows) * breadth, :]
                    .astype(jnp.float32)
                    .reshape(rows, breadth, channels)
                )
                mark = cots[cot_slot, pixels:, :].astype(jnp.float32)[first : first + rows]
                marks.append(mark[:, None, :] * own_lane[None])
            values.append(jnp.concatenate(blocks, axis=1).reshape(rows * tokens, channels))
            masks.append(jnp.concatenate(marks, axis=1).reshape(rows * tokens, channels))
        values = jnp.concatenate(values, axis=0)
        masks = matmul(jnp.concatenate(masks, axis=0).astype(jnp.bfloat16), pick)
        normed = layer_norm(values)
        gates = sigmoid(matmul(normed.astype(jnp.bfloat16), w_gate[...]))
        masked = (normed * masks[:, :channels]).astype(jnp.bfloat16)
        projected = matmul(masked, w_proj[...])
        sides = [
            sigmoid(projected[:, (2 * side + 1) * hidden : (2 * side + 2) * hidden])
            * projected[:, 2 * side * hidden : (2 * side + 1) * hidden]
            for side in range(2)
        ]
        for side, target in zip(sides, turned):
            side = side.reshape(chips, rows, tokens, hidden)
            for row in range(rows):
                strip = jnp.concatenate([side[chip, row] for chip in range(chips)], axis=0)
                target[pl.ds(first + row, hidden, stride=height), :] = strip.T
        shape = (chips, rows, tokens, channels)
        span = slice(first, first + rows)
        gating[:, span] = gates.reshape(shape)
        contact[:, span] = masks[:, channels:].astype(jnp.bfloat16).reshape(shape)
        start[:, span] = values.astype(jnp.bfloat16).reshape(shape)
    shape = (hidden, height, chips * tokens)
    left[...] = turned[0][...].reshape(shape).astype(jnp.bfloat16)
    other = turned[1][...]
    right[...] = other.reshape(shape).astype(jnp.bfloat16)
    swapped[...] = pltpu.roll(other, tokens, 1).reshape(shape).astype(jnp.bfloat16)


def near_kernel(
    plan,
    near,
    cot_near,
    w_proj,
    w_gate,
    two,
    left,
    right,
    swapped,
    gating,
    contact,
    start,
    two_t,
    turned_left,
    turned_right,
):
    core = lax.axis_index("row") % 2
    channels = two.shape[1]
    for tap in range(9):
        two_t[tap * channels : (tap + 1) * channels] = two[tap].T
    project_half(
        plan,
        core,
        near,
        cot_near,
        w_proj,
        w_gate,
        left,
        right,
        swapped,
        gating,
        contact,
        start,
        (turned_left, turned_right),
    )


def map_kernel(
    plan,
    dilations,
    far,
    cot_near,
    cot_far,
    w_proj,
    w_gate,
    w_out,
    one,
    two,
    near_left,
    near_right,
    near_swapped,
    near_gating,
    near_contact,
    near_start,
    two_t,
    output,
    grad_pair,
    grad_one,
    grad_two,
    left,
    right,
    swapped,
    gating,
    contact,
    start,
    turned_left,
    turned_right,
    products,
    updated,
    hidden_grad,
    field,
    wide,
    wide_cot,
    wide_pre,
    second,
    grad_pre,
    flipped,
    flipped_two,
    sum_one,
    sum_two,
):
    rounds, cot_rounds, height, breadth, tokens = plan
    hidden, channels = w_out.shape
    pixels = height * breadth
    chips = tokens // height // 2
    row_place, col_place = lax.axis_index("row"), lax.axis_index("col")
    core = row_place % 2
    rate_one, rate_two = dilations[0], dilations[1]
    half = far.shape[0]
    line = tokens + 2 * DMAX
    inside = slice(DMAX, DMAX + tokens)

    rim = jnp.zeros((tokens, DMAX, channels), jnp.float32)
    edge = jnp.zeros((DMAX, tokens, 3 * channels), jnp.bfloat16)
    border = jnp.zeros((DMAX, line, channels), jnp.float32)
    field[:, 0:DMAX, :] = rim
    field[:, DMAX + tokens :, :] = rim
    for target in (wide, wide_cot, wide_pre):
        target[0:DMAX] = edge
        target[DMAX + tokens :] = edge
    for target in (second, grad_pre):
        target[0:DMAX] = border
        target[DMAX + tokens :] = border
        target[inside, 0:DMAX, :] = rim
        target[inside, DMAX + tokens :, :] = rim

    for whole, part in (
        (left, near_left),
        (right, near_right),
        (swapped, near_swapped),
        (gating, near_gating),
        (contact, near_contact),
        (start, near_start),
    ):
        whole[core] = part[...]
    targets = [
        whole.at[1 - core] for whole in (left, right, swapped, gating, contact, start)
    ]
    project_half(
        plan,
        1 - core,
        far,
        cot_far,
        w_proj,
        w_gate,
        *targets,
        (turned_left, turned_right),
    )

    several = 4

    def place_cot(source, base):
        def body(step, carry):
            for i in range(several):
                slot = step * several + i
                row, col = place_of(base + slot, cot_rounds, row_place, col_place)
                cols = pl.ds(pl.multiple_of(DMAX + col * breadth, breadth), breadth)
                field[pl.ds(row * height, height), cols, :] = (
                    source[slot, 0:pixels, :]
                    .astype(jnp.float32)
                    .reshape(height, breadth, channels)
                )
            return carry

        lax.fori_loop(0, half // several, body, 0)

    place_cot(cot_near, 0)
    place_cot(cot_far, half)

    def spread(source, rows, pad, rate, target):
        for tap in range(3):
            moved = source[
                pl.ds(pad + rows.start, rows.size), pl.ds(DMAX + (tap - 1) * rate, tokens), :
            ]
            target[
                pl.ds(DMAX + rows.start, rows.size), :, tap * channels : (tap + 1) * channels
            ] = moved.astype(jnp.bfloat16)

    def taps(source, first, count, rate):
        views = [
            source[pl.ds(DMAX + first + (tap - 1) * rate, count)].reshape(count * tokens, -1)
            for tap in range(3)
        ]
        return jnp.concatenate(views, axis=1)

    def lanes(step, size):
        return pl.ds(pl.multiple_of(step * size, size), size)

    chunk = 8
    size = chunk * tokens
    steps = tokens // chunk

    def spread_cot(step, carry):
        spread(field, pl.ds(step * chunk, chunk), 0, -rate_two, wide_cot)
        return carry

    lax.fori_loop(0, steps, spread_cot, 0)

    lane = lax.broadcasted_iota(jnp.int32, (height, chips * tokens), 1)
    low = jnp.where(lane < tokens, 1.0, 0.0).astype(jnp.bfloat16)
    high = jnp.where(lane < tokens, 0.0, 1.0).astype(jnp.bfloat16)
    batch = 8

    def multiply(step, carry):
        for part in range(batch):
            h = step * batch + part
            ahead = [right[0, h], right[1, h]]
            back = [swapped[0, h], swapped[1, h]]
            strips = [strip * low for strip in ahead + back]
            strips += [strip * high for strip in back + ahead]
            mine = jnp.concatenate([left[0, h], left[1, h]], axis=0)
            products[pl.ds(pl.multiple_of(h * 2 * height, 2 * height), 2 * height), :] = (
                matmul_nt(mine, jnp.concatenate(strips, axis=0))
            )
        return carry

    lax.fori_loop(0, hidden // batch, multiply, 0)

    def update(step, carry):
        side, first = step // (height // chunk), (step % (height // chunk)) * chunk
        turned = []
        for row in range(chunk):
            strip = products[pl.ds(side * height + first + row, hidden, stride=2 * height), :]
            turned.append(layer_norm(strip, axis=0).astype(jnp.bfloat16).T)
        product_norm = jnp.concatenate(
            [
                strip[chip * tokens : (chip + 1) * tokens]
                for chip in range(chips)
                for strip in turned
            ],
            axis=0,
        )
        shape = (chips, chunk, tokens, channels)
        change = matmul(product_norm, w_out[...]).reshape(shape)
        rows = pl.ds(first, chunk)
        fresh = start[side, :, rows].astype(jnp.float32) + gating[side, :, rows] * change
        fresh = fresh.astype(jnp.bfloat16).astype(jnp.float32)
        first_in = layer_norm(fresh) * contact[side, :, rows].astype(jnp.float32)
        for chip in range(chips):
            base = (chip * 2 + side) * height + first
            rows = pl.ds(base, chunk)
            updated[rows] = fresh[chip]
            field[rows, inside, :] = first_in[chip]
            spread(field, rows, 0, rate_one, wide)
            flipped[:, pl.ds(pl.multiple_of(base * tokens, size), size)] = (
                first_in[chip].reshape(size, channels).astype(jnp.bfloat16).T
            )
            hidden_grad[rows] = matmul(
                taps(wide_cot, base, chunk, -rate_two), two_t[...]
            ).reshape(chunk, tokens, channels)
        return carry

    lax.fori_loop(0, 2 * (height // chunk), update, 0)

    def first_conv(step):
        first = step * chunk
        rows = pl.ds(DMAX + first, chunk)
        shape = (chunk, tokens, channels)
        pre = matmul(taps(wide, first, chunk, rate_one), one[...])
        sigma = sigmoid(pre)
        second_in = pre * sigma
        second[rows, inside, :] = second_in.reshape(shape)
        flipped_two[:, lanes(step, size)] = second_in.astype(jnp.bfloat16).T
        factor = (sigma * (1.0 + pre * (1.0 - sigma))).reshape(shape)
        grad_pre[rows, inside, :] = (
            (hidden_grad[pl.ds(first, chunk)] * factor).astype(jnp.bfloat16).astype(jnp.float32)
        )

    def after_conv(step):
        sum_two[...] += matmul(
            flipped_two[:, lanes(step, size)], taps(wide_cot, step * chunk, chunk, -rate_two)
        )
        spread(grad_pre, pl.ds(step * chunk, chunk), DMAX, -rate_one, wide_pre)

    def middle(step, carry):
        first_conv(step)
        after_conv(step - 1)
        return carry

    sum_two[...] = jnp.zeros_like(sum_two)
    first_conv(0)
    lax.fori_loop(1, steps, middle, 0)
    after_conv(steps - 1)

    sum_one[...] = jnp.zeros_like(sum_one)

    def back_one(step, carry):
        sum_one[...] += matmul(
            flipped[:, lanes(step, size)], taps(wide_pre, step * chunk, chunk, -rate_one)
        )
        return carry

    lax.fori_loop(0, steps, back_one, 0)
    for tap in range(9):
        columns = slice(tap * channels, (tap + 1) * channels)
        grad_one[tap] = sum_one[:, columns] * (1.0 / tokens)
        grad_two[tap] = sum_two[:, columns] * (1.0 / tokens)

    row_start, col_start = row_place * height, col_place * breadth

    def windows(source, rate):
        views = [
            source[
                pl.ds(row_start + DMAX + (tap // 3 - 1) * rate, height),
                pl.ds(col_start + DMAX + (tap % 3 - 1) * rate, breadth),
                :,
            ].reshape(pixels, channels)
            for tap in range(9)
        ]
        return jnp.concatenate(views, axis=1).astype(jnp.bfloat16)

    rows = pl.ds(row_start, height)
    cols = pl.ds(pl.multiple_of(col_start, breadth), breadth)
    mine = updated[rows, cols, :].reshape(pixels, channels)
    second_pre = matmul(windows(second, rate_two), two[...].reshape(9 * channels, channels))
    output[...] = (mine + second_pre).astype(jnp.bfloat16)
    own_contact = contact[core, row_place // 2].astype(jnp.float32)
    own_contact = own_contact.reshape(height, tokens, channels)
    place_col = lax.broadcasted_iota(jnp.int32, (tokens, channels), 0) // breadth
    own_contact = jnp.where((place_col == col_place)[None], own_contact, 0.0)
    own_contact = own_contact.reshape(height, tokens // breadth, breadth, channels)
    own_contact = jnp.sum(own_contact, axis=1).reshape(pixels, channels)
    one_rows = [one[tap * channels : (tap + 1) * channels] for tap in range(9)]
    grad_input = lax.dot_general(
        windows(grad_pre, -rate_one),
        jnp.concatenate(one_rows, axis=1),
        (((1,), (1,)), ((), ())),
        preferred_element_type=jnp.float32,
    ) * own_contact
    centre = mine - jnp.mean(mine, axis=-1, keepdims=True)
    inv_spread = lax.rsqrt(jnp.mean(centre * centre, axis=-1, keepdims=True) + EPSILON)
    scaled = centre * inv_spread
    grad_norm = inv_spread * (
        grad_input
        - jnp.mean(grad_input, axis=-1, keepdims=True)
        - scaled * jnp.mean(grad_input * scaled, axis=-1, keepdims=True)
    )
    grad_pair[...] = (cot_near[0, 0:pixels, :].astype(jnp.float32) + grad_norm).astype(
        jnp.bfloat16
    )


def replicated(
    pair, pair_mask, contact_mask, dilations, w_proj, w_gate, w_out, conv_one, conv_two, cotangent
):
    height, breadth, channels = pair.shape
    hidden = w_out.shape[0]
    row_count, col_count = lax.axis_size("row"), lax.axis_size("col")
    tokens = height * row_count
    pixels = height * breadth
    rounds, cot_rounds = exchange_plan(row_count, col_count)
    masks = jnp.concatenate(
        [
            pair_mask.astype(jnp.bfloat16),
            contact_mask.astype(jnp.bfloat16),
            jnp.zeros((height, channels - 2 * breadth), jnp.bfloat16),
        ],
        axis=1,
    )
    packed = jnp.concatenate([cotangent.reshape(pixels, channels), masks], axis=0)
    near, far = gather_blocks(pair.reshape(pixels, channels), rounds)
    cot_near, cot_far = gather_blocks(packed, cot_rounds)
    f32, bf16 = jnp.float32, jnp.bfloat16
    plan = (rounds, cot_rounds, height, breadth, tokens)
    chips = row_count // 2
    line = tokens + 2 * DMAX
    in_vmem = pl.BlockSpec(memory_space=pltpu.VMEM)
    side = ((hidden, height, chips * tokens), bf16)
    rows = (chips, height, tokens, channels)
    halves = [side] * 3 + [(rows, f32), (rows, bf16), (rows, bf16)]
    turned = pltpu.VMEM((hidden * height, chips * tokens), f32)
    near_parts = pl.pallas_call(
        functools.partial(near_kernel, plan),
        in_specs=[in_vmem] * 5,
        out_specs=[in_vmem] * 7,
        out_shape=[
            jax.ShapeDtypeStruct(shape, dtype)
            for shape, dtype in halves + [((9 * channels, channels), bf16)]
        ],
        scratch_shapes=[turned] * 2,
        compiler_params=pltpu.CompilerParams(vmem_limit_bytes=VMEM_LIMIT // 3),
        cost_estimate=pl.CostEstimate(
            flops=tokens * tokens * channels * 5 * hidden,
            bytes_accessed=8 * tokens * tokens * channels,
            transcendentals=3 * tokens * tokens * channels // 2,
        ),
    )(near, cot_near, w_proj, w_gate, conv_two)
    whole = pltpu.VMEM((tokens, tokens, channels), f32)
    padded = pltpu.VMEM((tokens, line, channels), f32)
    bordered = pltpu.VMEM((line, line, channels), f32)
    tripled = pltpu.VMEM((line, tokens, 3 * channels), bf16)
    flat = pltpu.VMEM((channels, tokens * tokens), bf16)
    sums = pltpu.VMEM((channels, 9 * channels), f32)
    output, grad_pair, grad_one, grad_two = pl.pallas_call(
        functools.partial(map_kernel, plan),
        in_specs=[pl.BlockSpec(memory_space=pltpu.SMEM)] + [in_vmem] * 15,
        out_specs=[in_vmem] * 4,
        out_shape=[
            jax.ShapeDtypeStruct((pixels, channels), bf16),
            jax.ShapeDtypeStruct((pixels, channels), bf16),
            jax.ShapeDtypeStruct((9, channels, channels), f32),
            jax.ShapeDtypeStruct((9, channels, channels), f32),
        ],
        scratch_shapes=[pltpu.VMEM((2,) + shape, dtype) for shape, dtype in halves]
        + [turned] * 2
        + [pltpu.VMEM((hidden * 2 * height, chips * tokens), f32)]
        + [whole] * 2
        + [padded]
        + [tripled] * 3
        + [bordered] * 2
        + [flat] * 2
        + [sums] * 2,
        compiler_params=pltpu.CompilerParams(vmem_limit_bytes=VMEM_LIMIT),
    )(
        dilations,
        far,
        cot_near,
        cot_far,
        w_proj,
        w_gate,
        w_out,
        conv_one.reshape(9 * channels, channels),
        conv_two,
        *near_parts,
    )
    block = (height, breadth, channels)
    return output.reshape(block), grad_pair.reshape(block), grad_one, grad_two


def fits(pair, w_out, row_count, col_count):
    height, breadth, channels = pair.shape
    tokens = height * row_count
    powers = all(count & (count - 1) == 0 for count in (row_count, col_count))
    whole = (tokens + 2 * DMAX) ** 2 * channels
    return (
        powers
        and row_count * col_count >= 8
        and height * breadth == channels == w_out.shape[0]
        and row_count // 2 * tokens == channels
        and whole * 60 <= VMEM_LIMIT
    )


def local(*arguments):
    pair, w_out = arguments[0], arguments[6]
    if fits(pair, w_out, lax.axis_size("row"), lax.axis_size("col")):
        return replicated(*arguments)
    return sharded(*arguments)


def solution(mesh):
    in_specs = (
        P("row", "col", None),
        P("row", "col"),
        P("row", "col"),
        P(),
        P(),
        P(),
        P(),
        P(),
        P(),
        P("row", "col", None),
    )
    out_specs = (P("row", "col", None), P("row", "col", None), P(), P())
    return jax.shard_map(local, mesh=mesh, in_specs=in_specs, out_specs=out_specs, check_vma=False)
```

```python
import functools

import jax
import jax.numpy as jnp
from jax import lax
from jax.experimental import pallas as pl
from jax.experimental.pallas import tpu as pltpu
from jax.sharding import PartitionSpec as P

DMAX = 8
VMEM_LIMIT = 48 * 1024 * 1024
FORWARD_VMEM = 36 * 1024 * 1024
BACKWARD_VMEM = 28 * 1024 * 1024


EPSILON = 1e-05


def with_halo(block, sides, width):
    for axis, dim in sides:
        count = lax.axis_size(axis)
        forward = [(i, i + 1) for i in range(count - 1)]
        backward = [(target, source) for source, target in forward]
        low = lax.ppermute(
            lax.slice_in_dim(block, block.shape[dim] - width, None, axis=dim), axis, forward
        )
        high = lax.ppermute(lax.slice_in_dim(block, 0, width, axis=dim), axis, backward)
        block = jnp.concatenate([low, block, high], axis=dim)
    return block


def broadcast(x, axis, root):
    mine = lax.axis_index(axis) == root
    return lax.psum(jnp.where(mine, x, jnp.zeros_like(x)), axis)


def layer_norm(values, axis=-1):
    centre = values - jnp.mean(values, axis=axis, keepdims=True)
    spread = jnp.mean(centre * centre, axis=axis, keepdims=True)
    return centre * lax.rsqrt(spread + EPSILON)


def with_rim(field):
    return with_halo(field, (("row", 0), ("col", 1)), DMAX)


def gather_taps(padded, dilation, mirrored, height, breadth):
    windows = []
    for tap_index in range(9):
        row_tap = tap_index // 3
        col_tap = tap_index % 3
        if mirrored:
            row_tap = 2 - row_tap
            col_tap = 2 - col_tap
        row_start = DMAX + (row_tap - 1) * dilation
        col_start = DMAX + (col_tap - 1) * dilation
        windows.append(
            lax.dynamic_slice(
                padded, (row_start, col_start, jnp.int32(0)), (height, breadth, padded.shape[2])
            )
        )
    return jnp.concatenate(windows, axis=2).reshape(height * breadth, -1)


def sharded(
    pair, pair_mask, contact_mask, dilations, w_proj, w_gate, w_out, conv_one, conv_two, cotangent
):
    height, breadth, channels = pair.shape
    hidden = w_out.shape[0]
    row_count = lax.axis_size("row")
    col_count = lax.axis_size("col")
    ratio = col_count // row_count
    row_place = lax.axis_index("row")
    col_place = lax.axis_index("col")
    tokens = breadth * col_count
    pixels = height * breadth
    pair_flat = pair.astype(jnp.float32).reshape(pixels, channels)
    normed = layer_norm(pair_flat).astype(jnp.bfloat16)
    projected = jnp.dot(normed, w_proj, preferred_element_type=jnp.float32)
    mask_col = pair_mask.reshape(pixels, 1).astype(jnp.float32)
    left_side = (
        (mask_col * jax.nn.sigmoid(projected[:, hidden : 2 * hidden]) * projected[:, :hidden])
        .astype(jnp.bfloat16)
        .reshape(height, breadth, hidden)
    )
    right_side = (
        (
            mask_col
            * jax.nn.sigmoid(projected[:, 3 * hidden :])
            * projected[:, 2 * hidden : 3 * hidden]
        )
        .astype(jnp.bfloat16)
        .reshape(height, breadth, hidden)
    )
    right_all = lax.all_gather(right_side, "col", axis=1, tiled=True)
    offset = jnp.clip(col_place * breadth - row_place * height, 0, height - breadth)
    right_local = lax.dynamic_slice_in_dim(right_all, offset, breadth, 0)
    right_rows = broadcast(right_local, "row", col_place // ratio)
    products = jnp.einsum(
        "ikh,jkh->ijh",
        lax.all_gather(left_side, "col", axis=1, tiled=True),
        right_rows,
        preferred_element_type=jnp.float32,
    )
    product_norm = layer_norm(products.reshape(pixels, hidden)).astype(jnp.bfloat16)
    gating = jax.nn.sigmoid(jnp.dot(normed, w_gate, preferred_element_type=jnp.float32))
    updated = (
        pair_flat + gating * jnp.dot(product_norm, w_out, preferred_element_type=jnp.float32)
    ).astype(jnp.bfloat16)
    updated_f = updated.astype(jnp.float32)
    centre = updated_f - jnp.mean(updated_f, axis=-1, keepdims=True)
    inv_spread = lax.rsqrt(jnp.mean(centre * centre, axis=-1, keepdims=True) + EPSILON)
    scaled = centre * inv_spread
    contact = contact_mask.reshape(pixels, 1).astype(jnp.float32)
    first_in = (scaled * contact).astype(jnp.bfloat16).reshape(height, breadth, channels)
    rate_one = dilations[0]
    rate_two = dilations[1]
    first_taps = gather_taps(with_rim(first_in), rate_one, False, height, breadth)
    first_pre = jnp.dot(
        first_taps, conv_one.reshape(9 * channels, channels), preferred_element_type=jnp.float32
    )
    sigma = jax.nn.sigmoid(first_pre)
    second_in = (first_pre * sigma).astype(jnp.bfloat16).reshape(height, breadth, channels)
    second_taps = gather_taps(with_rim(second_in), rate_two, False, height, breadth)
    second_pre = jnp.dot(
        second_taps, conv_two.reshape(9 * channels, channels), preferred_element_type=jnp.float32
    )
    output = (updated_f + second_pre).astype(jnp.bfloat16).reshape(height, breadth, channels)
    cot_flat = cotangent.reshape(pixels, channels)
    grad_two = (
        lax.dot_general(
            second_taps, cot_flat, (((0,), (0,)), ((), ())), preferred_element_type=jnp.float32
        ).reshape(9, channels, channels)
        / tokens
    )
    cot_taps = gather_taps(with_rim(cotangent), rate_two, True, height, breadth)
    grad_hidden = jnp.dot(
        cot_taps,
        conv_two.transpose(0, 2, 1).reshape(9 * channels, channels),
        preferred_element_type=jnp.float32,
    )
    grad_pre = (grad_hidden * sigma * (1.0 + first_pre * (1.0 - sigma))).astype(jnp.bfloat16)
    grad_one = (
        lax.dot_general(
            first_taps, grad_pre, (((0,), (0,)), ((), ())), preferred_element_type=jnp.float32
        ).reshape(9, channels, channels)
        / tokens
    )
    grad_taps = gather_taps(
        with_rim(grad_pre.reshape(height, breadth, channels)), rate_one, True, height, breadth
    )
    grad_input = (
        jnp.dot(
            grad_taps,
            conv_one.transpose(0, 2, 1).reshape(9 * channels, channels),
            preferred_element_type=jnp.float32,
        )
        * contact
    )
    grad_norm = inv_spread * (
        grad_input
        - jnp.mean(grad_input, axis=-1, keepdims=True)
        - scaled * jnp.mean(grad_input * scaled, axis=-1, keepdims=True)
    )
    grad_pair = (
        (cot_flat.astype(jnp.float32) + grad_norm)
        .astype(jnp.bfloat16)
        .reshape(height, breadth, channels)
    )
    grad_one, grad_two = lax.psum((grad_one, grad_two), ("row", "col"))
    return (output, grad_pair, grad_one, grad_two)


def halvings(axis, count):
    return [(axis, count >> step) for step in range(1, count.bit_length())]


def exchange_plan(row_count, col_count):
    rows, cols = halvings("row", row_count), halvings("col", col_count)
    return cols + rows, rows[:-1] + cols + rows[-1:]


def gather_blocks(block, rounds, early=None):
    held = block[None]
    for step, (axis, distance) in enumerate(rounds):
        if step == 2 and early is not None:
            held, early = lax.optimization_barrier((held, early))
        pairs = [(i, i ^ distance) for i in range(lax.axis_size(axis))]
        other = lax.ppermute(held, axis, pairs)
        if step < len(rounds) - 1:
            held = jnp.concatenate([held, other], axis=0)
    return held, other, early


def place_of(position, rounds, row_place, col_place):
    row, col = row_place, col_place
    for step, (axis, distance) in enumerate(rounds):
        bit = ((position >> step) & 1) * distance
        if axis == "row":
            row = row ^ bit
        else:
            col = col ^ bit
    return row, col


def slot_of(row_change, col_change, rounds):
    slot = 0
    for step, (axis, distance) in enumerate(rounds[:-1]):
        change = row_change if axis == "row" else col_change
        slot = slot | (((change // distance) & 1) << step)
    return slot


def sigmoid(values):
    return 0.5 + 0.5 * jnp.tanh(0.5 * values)


def matmul(left, right):
    return jnp.dot(left, right, preferred_element_type=jnp.float32)


def matmul_nt(left, right):
    return lax.dot_general(
        left, right, (((1,), (1,)), ((), ())), preferred_element_type=jnp.float32
    )


def project_half(
    plan, core, pairs, w_proj, w_gate, left, right, swapped, gating, contact, start, turned
):
    rounds, _, height, breadth, tokens = plan
    channels, hidden = w_gate.shape[0], w_gate.shape[1]
    col_count, chips = tokens // breadth, tokens // height // 2
    row_place, col_place = lax.axis_index("row"), lax.axis_index("col")
    lane = lax.broadcasted_iota(jnp.int32, (breadth, channels), 1)
    place = lax.broadcasted_iota(jnp.int32, (breadth, channels), 0)
    own_lane = jnp.where((lane % breadth == place) & (lane < 2 * breadth), 1.0, 0.0)
    pick_lane = lax.broadcasted_iota(jnp.int32, (channels, 2 * channels), 0)
    pick_half = lax.broadcasted_iota(jnp.int32, (channels, 2 * channels), 1) // channels
    pick = jnp.where(pick_lane // breadth == pick_half, 1.0, 0.0).astype(jnp.bfloat16)
    pixels = height * breadth
    rows = 8
    for first in range(0, height, rows):
        values, masks = [], []
        for chip in range(chips):
            row_change = (chip * 2 + core) ^ row_place
            blocks, marks = [], []
            for col in range(col_count):
                col_change = col_place ^ col
                slot = slot_of(row_change, col_change, rounds)
                blocks.append(
                    pairs[slot, first * breadth : (first + rows) * breadth, :]
                    .astype(jnp.float32)
                    .reshape(rows, breadth, channels)
                )
                mark = pairs[slot, pixels:, :].astype(jnp.float32)[first : first + rows]
                marks.append(mark[:, None, :] * own_lane[None])
            values.append(jnp.concatenate(blocks, axis=1).reshape(rows * tokens, channels))
            masks.append(jnp.concatenate(marks, axis=1).reshape(rows * tokens, channels))
        values = jnp.concatenate(values, axis=0)
        masks = matmul(jnp.concatenate(masks, axis=0).astype(jnp.bfloat16), pick)
        normed = layer_norm(values)
        gates = sigmoid(matmul(normed.astype(jnp.bfloat16), w_gate[...]))
        masked = (normed * masks[:, :channels]).astype(jnp.bfloat16)
        projected = matmul(masked, w_proj[...])
        sides = [
            sigmoid(projected[:, (2 * side + 1) * hidden : (2 * side + 2) * hidden])
            * projected[:, 2 * side * hidden : (2 * side + 1) * hidden]
            for side in range(2)
        ]
        for side, target in zip(sides, turned):
            side = side.reshape(chips, rows, tokens, hidden)
            for row in range(rows):
                strip = jnp.concatenate([side[chip, row] for chip in range(chips)], axis=0)
                target[pl.ds(first + row, hidden, stride=height), :] = strip.T
        shape = (chips, rows, tokens, channels)
        span = slice(first, first + rows)
        gating[:, span] = gates.astype(jnp.bfloat16).reshape(shape)
        contact[:, span] = masks[:, channels:].astype(jnp.bfloat16).reshape(shape)
        start[:, span] = values.astype(jnp.bfloat16).reshape(shape)
    shape = (hidden, height, chips * tokens)
    left[...] = turned[0][...].reshape(shape).astype(jnp.bfloat16)
    other = turned[1][...]
    right[...] = other.reshape(shape).astype(jnp.bfloat16)
    swapped[...] = pltpu.roll(other, tokens, 1).reshape(shape).astype(jnp.bfloat16)


def near_kernel(
    plan,
    near,
    w_proj,
    w_gate,
    two,
    left,
    right,
    swapped,
    gating,
    contact,
    start,
    two_t,
    turned_left,
    turned_right,
):
    core = lax.axis_index("row") % 2
    channels = two.shape[1]
    for tap in range(9):
        two_t[tap * channels : (tap + 1) * channels] = two[tap].T
    project_half(
        plan,
        core,
        near,
        w_proj,
        w_gate,
        left,
        right,
        swapped,
        gating,
        contact,
        start,
        (turned_left, turned_right),
    )


def spread(source, rows, pad, rate, target):
    tokens, channels = target.shape[1], source.shape[2]
    for tap in range(3):
        moved = source[
            pl.ds(pad + rows.start, rows.size), pl.ds(DMAX + (tap - 1) * rate, tokens), :
        ]
        target[pl.ds(DMAX + rows.start, rows.size), :, tap * channels : (tap + 1) * channels] = (
            moved.astype(jnp.bfloat16)
        )


def taps(source, first, count, rate):
    tokens = source.shape[1]
    views = [
        source[pl.ds(DMAX + first + (tap - 1) * rate, count)].reshape(count * tokens, -1)
        for tap in range(3)
    ]
    return jnp.concatenate(views, axis=1)


def windows(source, rate, row_start, col_start, height, breadth):
    views = [
        source[
            pl.ds(row_start + DMAX + (tap // 3 - 1) * rate, height),
            pl.ds(col_start + DMAX + (tap % 3 - 1) * rate, breadth),
            :,
        ].reshape(height * breadth, -1)
        for tap in range(9)
    ]
    return jnp.concatenate(views, axis=1).astype(jnp.bfloat16)


def lanes(step, size):
    return pl.ds(pl.multiple_of(step * size, size), size)


def clear_border(target, tokens):
    line, channels = target.shape[1], target.shape[2]
    border = jnp.zeros((DMAX, line, channels), target.dtype)
    rim = jnp.zeros((tokens, DMAX, channels), target.dtype)
    if target.shape[0] > tokens:
        target[0:DMAX] = border
        target[DMAX + tokens :] = border
    if line > tokens:
        rows = slice(target.shape[0] - tokens - DMAX, target.shape[0] - DMAX)
        if target.shape[0] == tokens:
            rows = slice(0, tokens)
        target[rows, 0:DMAX, :] = rim
        target[rows, DMAX + tokens :, :] = rim


def forward_kernel(
    plan,
    dilations,
    far,
    w_proj,
    w_gate,
    w_out,
    one,
    two,
    near_left,
    near_right,
    near_swapped,
    near_gating,
    near_contact,
    near_start,
    output,
    flipped,
    flipped_two,
    factor,
    mine,
    own_contact,
    far_left,
    right,
    swapped,
    far_gating,
    far_contact,
    far_start,
    turned_left,
    turned_right,
    products,
    updated,
    field,
    wide,
    second,
):
    _, _, height, breadth, tokens = plan
    hidden, channels = w_out.shape
    pixels = height * breadth
    chips = tokens // height // 2
    row_place, col_place = lax.axis_index("row"), lax.axis_index("col")
    core = row_place % 2
    rate_one, rate_two = dilations[0], dilations[1]
    inside = slice(DMAX, DMAX + tokens)
    for target in (field, wide, second):
        clear_border(target, tokens)

    right[core] = near_right[...]
    swapped[core] = near_swapped[...]
    project_half(
        plan,
        1 - core,
        far,
        w_proj,
        w_gate,
        far_left,
        right.at[1 - core],
        swapped.at[1 - core],
        far_gating,
        far_contact,
        far_start,
        (turned_left, turned_right),
    )

    lane = lax.broadcasted_iota(jnp.int32, (height, chips * tokens), 1)
    low = jnp.where(lane < tokens, 1.0, 0.0).astype(jnp.bfloat16)
    high = jnp.where(lane < tokens, 0.0, 1.0).astype(jnp.bfloat16)
    batch = 8

    def multiply(step, carry):
        for part in range(batch):
            h = step * batch + part
            ahead = [right[0, h], right[1, h]]
            back = [swapped[0, h], swapped[1, h]]
            strips = [strip * low for strip in ahead + back]
            strips += [strip * high for strip in back + ahead]
            mine = jnp.concatenate([near_left[h], far_left[h]], axis=0)
            products[pl.ds(pl.multiple_of(h * 2 * height, 2 * height), 2 * height), :] = (
                matmul_nt(mine, jnp.concatenate(strips, axis=0))
            )
        return carry

    lax.fori_loop(0, hidden // batch, multiply, 0)

    chunk = 8
    size = chunk * tokens

    def update(step, half, side, gating, contact, start):
        first = step * chunk
        turned = []
        for row in range(chunk):
            strip = products[pl.ds(half * height + first + row, hidden, stride=2 * height), :]
            turned.append(layer_norm(strip, axis=0).astype(jnp.bfloat16).T)
        product_norm = jnp.concatenate(
            [
                strip[chip * tokens : (chip + 1) * tokens]
                for chip in range(chips)
                for strip in turned
            ],
            axis=0,
        )
        change = matmul(product_norm, w_out[...]).reshape(chips, chunk, tokens, channels)
        rows = pl.ds(first, chunk)
        fresh = start[:, rows].astype(jnp.float32) + gating[:, rows].astype(jnp.float32) * change
        fresh = fresh.astype(jnp.bfloat16).astype(jnp.float32)
        first_in = layer_norm(fresh) * contact[:, rows].astype(jnp.float32)
        for chip in range(chips):
            base = (chip * 2 + side) * height + first
            rows = pl.ds(base, chunk)
            updated[rows] = fresh[chip]
            field[rows, inside, :] = first_in[chip]
            spread(field, rows, 0, rate_one, wide)
            flipped[:, pl.ds(pl.multiple_of(base * tokens, size), size)] = (
                first_in[chip].reshape(size, channels).astype(jnp.bfloat16).T
            )

    halves = (
        (core, near_gating, near_contact, near_start),
        (1 - core, far_gating, far_contact, far_start),
    )
    for half, parts in enumerate(halves):
        lax.fori_loop(0, height // chunk, lambda i, c: (update(i, half, *parts), c)[1], 0)

    def first_conv(step, carry):
        first = step * chunk
        shape = (chunk, tokens, channels)
        pre = matmul(taps(wide, first, chunk, rate_one), one[...])
        sigma = sigmoid(pre)
        second_in = pre * sigma
        second[pl.ds(DMAX + first, chunk), inside, :] = second_in.reshape(shape)
        flipped_two[:, lanes(step, size)] = second_in.astype(jnp.bfloat16).T
        factor[pl.ds(first, chunk)] = (sigma * (1.0 + pre * (1.0 - sigma))).reshape(shape)
        return carry

    lax.fori_loop(0, tokens // chunk, first_conv, 0)

    row_start, col_start = row_place * height, col_place * breadth
    cols = pl.ds(pl.multiple_of(col_start, breadth), breadth)
    fresh = updated[pl.ds(row_start, height), cols, :].reshape(pixels, channels)
    mine[...] = fresh
    second_pre = matmul(
        windows(second, rate_two, row_start, col_start, height, breadth),
        two[...].reshape(9 * channels, channels),
    )
    output[...] = (fresh + second_pre).astype(jnp.bfloat16)
    marks = near_contact[row_place // 2].astype(jnp.float32)
    place_col = lax.broadcasted_iota(jnp.int32, (tokens, channels), 0) // breadth
    marks = jnp.where((place_col == col_place)[None], marks, 0.0)
    marks = marks.reshape(height, tokens // breadth, breadth, channels)
    own_contact[...] = jnp.sum(marks, axis=1).reshape(pixels, channels)


def backward_kernel(
    plan,
    dilations,
    cot_near,
    cot_far,
    one,
    two_t,
    flipped,
    flipped_two,
    factor,
    mine,
    own_contact,
    grad_pair,
    grad_one,
    grad_two,
    field,
    wide_cot,
    wide_pre,
    grad_pre,
    sum_one,
    sum_two,
):
    _, cot_rounds, height, breadth, tokens = plan
    channels = one.shape[1]
    pixels = height * breadth
    row_place, col_place = lax.axis_index("row"), lax.axis_index("col")
    rate_one, rate_two = dilations[0], dilations[1]
    half = cot_far.shape[0]
    inside = slice(DMAX, DMAX + tokens)
    for target in (field, wide_cot, wide_pre, grad_pre):
        clear_border(target, tokens)

    several = 4

    def place_cot(source, base):
        def body(step, carry):
            for i in range(several):
                slot = step * several + i
                row, col = place_of(base + slot, cot_rounds, row_place, col_place)
                cols = pl.ds(pl.multiple_of(DMAX + col * breadth, breadth), breadth)
                field[pl.ds(row * height, height), cols, :] = (
                    source[slot]
                    .astype(jnp.float32)
                    .reshape(height, breadth, channels)
                )
            return carry

        lax.fori_loop(0, half // several, body, 0)

    place_cot(cot_near, 0)
    place_cot(cot_far, half)

    chunk = 8
    size = chunk * tokens
    steps = tokens // chunk

    def spread_cot(step, carry):
        spread(field, pl.ds(step * chunk, chunk), 0, -rate_two, wide_cot)
        return carry

    lax.fori_loop(0, steps, spread_cot, 0)

    sum_two[...] = jnp.zeros_like(sum_two)

    def back_two(step, carry):
        first = step * chunk
        shifted = taps(wide_cot, first, chunk, -rate_two)
        before = matmul(shifted, two_t[...]).reshape(chunk, tokens, channels)
        before = (before * factor[pl.ds(first, chunk)]).astype(jnp.bfloat16).astype(jnp.float32)
        grad_pre[pl.ds(DMAX + first, chunk), inside, :] = before
        sum_two[...] += matmul(flipped_two[:, lanes(step, size)], shifted)
        spread(grad_pre, pl.ds(first, chunk), DMAX, -rate_one, wide_pre)
        return carry

    lax.fori_loop(0, steps, back_two, 0)

    sum_one[...] = jnp.zeros_like(sum_one)

    def back_one(step, carry):
        sum_one[...] += matmul(
            flipped[:, lanes(step, size)], taps(wide_pre, step * chunk, chunk, -rate_one)
        )
        return carry

    lax.fori_loop(0, steps, back_one, 0)
    for tap in range(9):
        columns = slice(tap * channels, (tap + 1) * channels)
        grad_one[tap] = sum_one[:, columns] * (1.0 / tokens)
        grad_two[tap] = sum_two[:, columns] * (1.0 / tokens)

    one_rows = [one[tap * channels : (tap + 1) * channels] for tap in range(9)]
    grad_input = own_contact[...] * matmul_nt(
        windows(
            grad_pre, -rate_one, row_place * height, col_place * breadth, height, breadth
        ),
        jnp.concatenate(one_rows, axis=1),
    )
    centre = mine[...] - jnp.mean(mine[...], axis=-1, keepdims=True)
    inv_spread = lax.rsqrt(jnp.mean(centre * centre, axis=-1, keepdims=True) + EPSILON)
    scaled = centre * inv_spread
    grad_norm = inv_spread * (
        grad_input
        - jnp.mean(grad_input, axis=-1, keepdims=True)
        - scaled * jnp.mean(grad_input * scaled, axis=-1, keepdims=True)
    )
    grad_pair[...] = (cot_near[0].astype(jnp.float32) + grad_norm).astype(jnp.bfloat16)


def replicated(
    pair, pair_mask, contact_mask, dilations, w_proj, w_gate, w_out, conv_one, conv_two, cotangent
):
    height, breadth, channels = pair.shape
    hidden = w_out.shape[0]
    row_count, col_count = lax.axis_size("row"), lax.axis_size("col")
    tokens = height * row_count
    pixels = height * breadth
    rounds, cot_rounds = exchange_plan(row_count, col_count)
    free = channels - 2 * breadth
    masks = jnp.pad(pair_mask, ((0, 0), (0, breadth + free))) + jnp.pad(
        contact_mask, ((0, 0), (breadth, free))
    )
    packed = jnp.concatenate(
        [pair.reshape(pixels, channels), masks.astype(jnp.bfloat16)], axis=0
    )
    rates = jnp.clip(dilations, 1, DMAX)
    near, far, rates = gather_blocks(packed, rounds, rates)
    cot_near, cot_far, _ = gather_blocks(cotangent.reshape(pixels, channels), cot_rounds)
    f32, bf16 = jnp.float32, jnp.bfloat16
    plan = (rounds, cot_rounds, height, breadth, tokens)
    chips = row_count // 2
    line = tokens + 2 * DMAX
    in_vmem = pl.BlockSpec(memory_space=pltpu.VMEM)
    side = ((hidden, height, chips * tokens), bf16)
    rows = (chips, height, tokens, channels)
    halves = [side] * 3 + [(rows, bf16)] * 3
    turned = pltpu.VMEM((hidden * height, chips * tokens), f32)
    stat = ((pixels, channels), f32)

    def shapes(*entries):
        return [jax.ShapeDtypeStruct(shape, dtype) for shape, dtype in entries]

    *near_parts, two_t = pl.pallas_call(
        functools.partial(near_kernel, plan),
        in_specs=[in_vmem] * 4,
        out_specs=[in_vmem] * 7,
        out_shape=shapes(*halves, ((9 * channels, channels), bf16)),
        scratch_shapes=[turned] * 2,
        compiler_params=pltpu.CompilerParams(vmem_limit_bytes=VMEM_LIMIT // 3),
        cost_estimate=pl.CostEstimate(
            flops=tokens * tokens * channels * 5 * hidden,
            bytes_accessed=8 * tokens * tokens * channels,
            transcendentals=3 * tokens * tokens * channels // 2,
        ),
    )(near, w_proj, w_gate, conv_two)
    whole = pltpu.VMEM((tokens, tokens, channels), f32)
    padded = pltpu.VMEM((tokens, line, channels), f32)
    bordered = pltpu.VMEM((line, line, channels), f32)
    tripled = pltpu.VMEM((line, tokens, 3 * channels), bf16)
    both = pltpu.VMEM((2,) + side[0], bf16)
    alone = pltpu.VMEM(rows, bf16)
    flat = ((channels, tokens * tokens), bf16)
    sums = pltpu.VMEM((channels, 9 * channels), f32)
    in_smem = pl.BlockSpec(memory_space=pltpu.SMEM)
    output, *held = pl.pallas_call(
        functools.partial(forward_kernel, plan),
        in_specs=[in_smem] + [in_vmem] * 12,
        out_specs=[in_vmem] * 6,
        out_shape=shapes(
            ((pixels, channels), bf16),
            flat,
            flat,
            ((tokens, tokens, channels), f32),
            stat,
            stat,
        ),
        scratch_shapes=[pltpu.VMEM(*side), both, both, alone, alone, alone]
        + [turned] * 2
        + [pltpu.VMEM((hidden * 2 * height, chips * tokens), f32)]
        + [whole, padded, tripled, bordered],
        compiler_params=pltpu.CompilerParams(vmem_limit_bytes=FORWARD_VMEM),
        cost_estimate=pl.CostEstimate(
            flops=tokens * tokens * channels * 40 * hidden,
            bytes_accessed=40 * tokens * tokens * channels,
            transcendentals=4 * tokens * tokens * channels,
        ),
    )(
        rates,
        far,
        w_proj,
        w_gate,
        w_out,
        conv_one.reshape(9 * channels, channels),
        conv_two,
        *near_parts,
    )
    grad_pair, grad_one, grad_two = pl.pallas_call(
        functools.partial(backward_kernel, plan),
        in_specs=[in_smem] + [in_vmem] * 9,
        out_specs=[in_vmem] * 3,
        out_shape=shapes(
            ((pixels, channels), bf16),
            ((9, channels, channels), f32),
            ((9, channels, channels), f32),
        ),
        scratch_shapes=[padded, tripled, tripled, bordered, sums, sums],
        compiler_params=pltpu.CompilerParams(vmem_limit_bytes=BACKWARD_VMEM),
    )(
        rates,
        cot_near,
        cot_far,
        conv_one.reshape(9 * channels, channels),
        two_t,
        *held,
    )
    block = (height, breadth, channels)
    return output.reshape(block), grad_pair.reshape(block), grad_one, grad_two


def fits(pair, w_out, row_count, col_count):
    height, breadth, channels = pair.shape
    tokens = height * row_count
    powers = all(count & (count - 1) == 0 for count in (row_count, col_count))
    whole = (tokens + 2 * DMAX) ** 2 * channels
    return (
        powers
        and row_count * col_count >= 8
        and height * breadth == channels == w_out.shape[0]
        and row_count // 2 * tokens == channels
        and whole * 60 <= VMEM_LIMIT
    )


def local(*arguments):
    pair, w_out = arguments[0], arguments[6]
    if fits(pair, w_out, lax.axis_size("row"), lax.axis_size("col")):
        return replicated(*arguments)
    return sharded(*arguments)


def solution(mesh):
    in_specs = (
        P("row", "col", None),
        P("row", "col"),
        P("row", "col"),
        P(),
        P(),
        P(),
        P(),
        P(),
        P(),
        P("row", "col", None),
    )
    out_specs = (P("row", "col", None), P("row", "col", None), P(), P())
    return jax.shard_map(local, mesh=mesh, in_specs=in_specs, out_specs=out_specs, check_vma=False)
```

```python
import functools

import jax
import jax.numpy as jnp
from jax import lax
from jax.experimental import pallas as pl
from jax.experimental.pallas import tpu as pltpu
from jax.sharding import PartitionSpec as P

DMAX = 8
VMEM_LIMIT = 48 * 1024 * 1024
FORWARD_VMEM = 36 * 1024 * 1024
BACKWARD_VMEM = 28 * 1024 * 1024


EPSILON = 1e-05


def with_halo(block, sides, width):
    for axis, dim in sides:
        count = lax.axis_size(axis)
        forward = [(i, i + 1) for i in range(count - 1)]
        backward = [(target, source) for source, target in forward]
        low = lax.ppermute(
            lax.slice_in_dim(block, block.shape[dim] - width, None, axis=dim), axis, forward
        )
        high = lax.ppermute(lax.slice_in_dim(block, 0, width, axis=dim), axis, backward)
        block = jnp.concatenate([low, block, high], axis=dim)
    return block


def broadcast(x, axis, root):
    mine = lax.axis_index(axis) == root
    return lax.psum(jnp.where(mine, x, jnp.zeros_like(x)), axis)


def layer_norm(values, axis=-1):
    centre = values - jnp.mean(values, axis=axis, keepdims=True)
    spread = jnp.mean(centre * centre, axis=axis, keepdims=True)
    return centre * lax.rsqrt(spread + EPSILON)


def with_rim(field):
    return with_halo(field, (("row", 0), ("col", 1)), DMAX)


def gather_taps(padded, dilation, mirrored, height, breadth):
    windows = []
    for tap_index in range(9):
        row_tap = tap_index // 3
        col_tap = tap_index % 3
        if mirrored:
            row_tap = 2 - row_tap
            col_tap = 2 - col_tap
        row_start = DMAX + (row_tap - 1) * dilation
        col_start = DMAX + (col_tap - 1) * dilation
        windows.append(
            lax.dynamic_slice(
                padded, (row_start, col_start, jnp.int32(0)), (height, breadth, padded.shape[2])
            )
        )
    return jnp.concatenate(windows, axis=2).reshape(height * breadth, -1)


def sharded(
    pair, pair_mask, contact_mask, dilations, w_proj, w_gate, w_out, conv_one, conv_two, cotangent
):
    height, breadth, channels = pair.shape
    hidden = w_out.shape[0]
    row_count = lax.axis_size("row")
    col_count = lax.axis_size("col")
    ratio = col_count // row_count
    row_place = lax.axis_index("row")
    col_place = lax.axis_index("col")
    tokens = breadth * col_count
    pixels = height * breadth
    pair_flat = pair.astype(jnp.float32).reshape(pixels, channels)
    normed = layer_norm(pair_flat).astype(jnp.bfloat16)
    projected = jnp.dot(normed, w_proj, preferred_element_type=jnp.float32)
    mask_col = pair_mask.reshape(pixels, 1).astype(jnp.float32)
    left_side = (
        (mask_col * jax.nn.sigmoid(projected[:, hidden : 2 * hidden]) * projected[:, :hidden])
        .astype(jnp.bfloat16)
        .reshape(height, breadth, hidden)
    )
    right_side = (
        (
            mask_col
            * jax.nn.sigmoid(projected[:, 3 * hidden :])
            * projected[:, 2 * hidden : 3 * hidden]
        )
        .astype(jnp.bfloat16)
        .reshape(height, breadth, hidden)
    )
    right_all = lax.all_gather(right_side, "col", axis=1, tiled=True)
    offset = jnp.clip(col_place * breadth - row_place * height, 0, height - breadth)
    right_local = lax.dynamic_slice_in_dim(right_all, offset, breadth, 0)
    right_rows = broadcast(right_local, "row", col_place // ratio)
    products = jnp.einsum(
        "ikh,jkh->ijh",
        lax.all_gather(left_side, "col", axis=1, tiled=True),
        right_rows,
        preferred_element_type=jnp.float32,
    )
    product_norm = layer_norm(products.reshape(pixels, hidden)).astype(jnp.bfloat16)
    gating = jax.nn.sigmoid(jnp.dot(normed, w_gate, preferred_element_type=jnp.float32))
    updated = (
        pair_flat + gating * jnp.dot(product_norm, w_out, preferred_element_type=jnp.float32)
    ).astype(jnp.bfloat16)
    updated_f = updated.astype(jnp.float32)
    centre = updated_f - jnp.mean(updated_f, axis=-1, keepdims=True)
    inv_spread = lax.rsqrt(jnp.mean(centre * centre, axis=-1, keepdims=True) + EPSILON)
    scaled = centre * inv_spread
    contact = contact_mask.reshape(pixels, 1).astype(jnp.float32)
    first_in = (scaled * contact).astype(jnp.bfloat16).reshape(height, breadth, channels)
    rate_one = dilations[0]
    rate_two = dilations[1]
    first_taps = gather_taps(with_rim(first_in), rate_one, False, height, breadth)
    first_pre = jnp.dot(
        first_taps, conv_one.reshape(9 * channels, channels), preferred_element_type=jnp.float32
    )
    sigma = jax.nn.sigmoid(first_pre)
    second_in = (first_pre * sigma).astype(jnp.bfloat16).reshape(height, breadth, channels)
    second_taps = gather_taps(with_rim(second_in), rate_two, False, height, breadth)
    second_pre = jnp.dot(
        second_taps, conv_two.reshape(9 * channels, channels), preferred_element_type=jnp.float32
    )
    output = (updated_f + second_pre).astype(jnp.bfloat16).reshape(height, breadth, channels)
    cot_flat = cotangent.reshape(pixels, channels)
    grad_two = (
        lax.dot_general(
            second_taps, cot_flat, (((0,), (0,)), ((), ())), preferred_element_type=jnp.float32
        ).reshape(9, channels, channels)
        / tokens
    )
    cot_taps = gather_taps(with_rim(cotangent), rate_two, True, height, breadth)
    grad_hidden = jnp.dot(
        cot_taps,
        conv_two.transpose(0, 2, 1).reshape(9 * channels, channels),
        preferred_element_type=jnp.float32,
    )
    grad_pre = (grad_hidden * sigma * (1.0 + first_pre * (1.0 - sigma))).astype(jnp.bfloat16)
    grad_one = (
        lax.dot_general(
            first_taps, grad_pre, (((0,), (0,)), ((), ())), preferred_element_type=jnp.float32
        ).reshape(9, channels, channels)
        / tokens
    )
    grad_taps = gather_taps(
        with_rim(grad_pre.reshape(height, breadth, channels)), rate_one, True, height, breadth
    )
    grad_input = (
        jnp.dot(
            grad_taps,
            conv_one.transpose(0, 2, 1).reshape(9 * channels, channels),
            preferred_element_type=jnp.float32,
        )
        * contact
    )
    grad_norm = inv_spread * (
        grad_input
        - jnp.mean(grad_input, axis=-1, keepdims=True)
        - scaled * jnp.mean(grad_input * scaled, axis=-1, keepdims=True)
    )
    grad_pair = (
        (cot_flat.astype(jnp.float32) + grad_norm)
        .astype(jnp.bfloat16)
        .reshape(height, breadth, channels)
    )
    grad_one, grad_two = lax.psum((grad_one, grad_two), ("row", "col"))
    return (output, grad_pair, grad_one, grad_two)


def halvings(axis, count):
    return [(axis, count >> step) for step in range(1, count.bit_length())]


def exchange_plan(row_count, col_count):
    rows, cols = halvings("row", row_count), halvings("col", col_count)
    return cols + rows, rows[:-1] + cols + rows[-1:]


def exchange(held, hop):
    axis, distance = hop
    return lax.ppermute(held, axis, [(i, i ^ distance) for i in range(lax.axis_size(axis))])


def place_of(position, rounds, row_place, col_place):
    row, col = row_place, col_place
    for step, (axis, distance) in enumerate(rounds):
        bit = ((position >> step) & 1) * distance
        if axis == "row":
            row = row ^ bit
        else:
            col = col ^ bit
    return row, col


def slot_of(row_change, col_change, rounds):
    slot = 0
    for step, (axis, distance) in enumerate(rounds[:-1]):
        change = row_change if axis == "row" else col_change
        slot = slot | (((change // distance) & 1) << step)
    return slot


def sigmoid(values):
    return 0.5 + 0.5 * jnp.tanh(0.5 * values)


def matmul(left, right):
    return jnp.dot(left, right, preferred_element_type=jnp.float32)


def matmul_nt(left, right):
    return lax.dot_general(
        left, right, (((1,), (1,)), ((), ())), preferred_element_type=jnp.float32
    )


def pack_kernel(dilations, pair, cotangent, pair_mask, contact_mask, packed, cot, rates):
    pixels, channels = pair.shape
    breadth, height = pair_mask.shape
    masks = jnp.concatenate(
        [
            pair_mask[...].astype(jnp.float32),
            contact_mask[...].astype(jnp.float32),
            jnp.zeros((breadth, channels - 2 * height), jnp.float32),
        ],
        axis=1,
    )
    tile = jnp.concatenate([masks, jnp.zeros_like(masks)], axis=0)
    packed[0, 0:pixels] = pair[...]
    packed[0, pixels:] = tile.astype(jnp.bfloat16)
    cot[0] = cotangent[...]
    for rate in range(2):
        rates[rate] = jnp.clip(dilations[rate], 1, DMAX)


def project_half(
    plan, core, pairs, w_proj, w_gate, left, right, swapped, gating, contact, start, turned
):
    rounds, _, height, breadth, tokens = plan
    channels, hidden = w_gate.shape[0], w_gate.shape[1]
    col_count, chips = tokens // breadth, tokens // height // 2
    row_place, col_place = lax.axis_index("row"), lax.axis_index("col")
    lane = lax.broadcasted_iota(jnp.int32, (height, breadth, channels), 2)
    place = lax.broadcasted_iota(jnp.int32, (height, breadth, channels), 0)
    own_lane = jnp.where((lane % height == place) & (lane < 2 * height), 1.0, 0.0)
    pick_lane = lax.broadcasted_iota(jnp.int32, (channels, 2 * channels), 0)
    pick_half = lax.broadcasted_iota(jnp.int32, (channels, 2 * channels), 1) // channels
    pick = jnp.where(pick_lane // height == pick_half, 1.0, 0.0).astype(jnp.bfloat16)
    pixels = height * breadth
    rows = 8
    for first in range(0, height, rows):
        values, masks = [], []
        for chip in range(chips):
            row_change = (chip * 2 + core) ^ row_place
            blocks, marks = [], []
            for col in range(col_count):
                col_change = col_place ^ col
                slot = slot_of(row_change, col_change, rounds)
                blocks.append(
                    pairs[slot, first * breadth : (first + rows) * breadth, :]
                    .astype(jnp.float32)
                    .reshape(rows, breadth, channels)
                )
                mark = pairs[slot, pixels:, :].astype(jnp.float32)[:breadth]
                marks.append(mark[None] * own_lane[first : first + rows])
            values.append(jnp.concatenate(blocks, axis=1).reshape(rows * tokens, channels))
            masks.append(jnp.concatenate(marks, axis=1).reshape(rows * tokens, channels))
        values = jnp.concatenate(values, axis=0)
        masks = matmul(jnp.concatenate(masks, axis=0).astype(jnp.bfloat16), pick)
        normed = layer_norm(values)
        gates = sigmoid(matmul(normed.astype(jnp.bfloat16), w_gate[...]))
        masked = (normed * masks[:, :channels]).astype(jnp.bfloat16)
        projected = matmul(masked, w_proj[...])
        sides = [
            sigmoid(projected[:, (2 * side + 1) * hidden : (2 * side + 2) * hidden])
            * projected[:, 2 * side * hidden : (2 * side + 1) * hidden]
            for side in range(2)
        ]
        for side, target in zip(sides, turned):
            side = side.reshape(chips, rows, tokens, hidden)
            for row in range(rows):
                strip = jnp.concatenate([side[chip, row] for chip in range(chips)], axis=0)
                target[pl.ds(first + row, hidden, stride=height), :] = strip.T
        shape = (chips, rows, tokens, channels)
        span = slice(first, first + rows)
        gating[:, span] = gates.astype(jnp.bfloat16).reshape(shape)
        contact[:, span] = masks[:, channels:].astype(jnp.bfloat16).reshape(shape)
        start[:, span] = values.astype(jnp.bfloat16).reshape(shape)
    shape = (hidden, height, chips * tokens)
    left[...] = turned[0][...].reshape(shape).astype(jnp.bfloat16)
    other = turned[1][...]
    right[...] = other.reshape(shape).astype(jnp.bfloat16)
    swapped[...] = pltpu.roll(other, tokens, 1).reshape(shape).astype(jnp.bfloat16)


def near_kernel(
    plan,
    near,
    w_proj,
    w_gate,
    two,
    left,
    right,
    swapped,
    gating,
    contact,
    start,
    two_t,
    turned_left,
    turned_right,
):
    core = lax.axis_index("row") % 2
    channels = two.shape[1]
    for tap in range(9):
        two_t[tap * channels : (tap + 1) * channels] = two[tap].T
    project_half(
        plan,
        core,
        near,
        w_proj,
        w_gate,
        left,
        right,
        swapped,
        gating,
        contact,
        start,
        (turned_left, turned_right),
    )


def spread(source, rows, pad, rate, target):
    tokens, channels = target.shape[1], source.shape[2]
    for tap in range(3):
        moved = source[
            pl.ds(pad + rows.start, rows.size), pl.ds(DMAX + (tap - 1) * rate, tokens), :
        ]
        target[pl.ds(DMAX + rows.start, rows.size), :, tap * channels : (tap + 1) * channels] = (
            moved.astype(jnp.bfloat16)
        )


def taps(source, first, count, rate):
    tokens = source.shape[1]
    views = [
        source[pl.ds(DMAX + first + (tap - 1) * rate, count)].reshape(count * tokens, -1)
        for tap in range(3)
    ]
    return jnp.concatenate(views, axis=1)


def windows(source, rate, row_start, col_start, height, breadth):
    views = [
        source[
            pl.ds(row_start + DMAX + (tap // 3 - 1) * rate, height),
            pl.ds(col_start + DMAX + (tap % 3 - 1) * rate, breadth),
            :,
        ].reshape(height * breadth, -1)
        for tap in range(9)
    ]
    return jnp.concatenate(views, axis=1).astype(jnp.bfloat16)


def lanes(step, size):
    return pl.ds(pl.multiple_of(step * size, size), size)


def clear_border(target, tokens):
    line, channels = target.shape[1], target.shape[2]
    border = jnp.zeros((DMAX, line, channels), target.dtype)
    rim = jnp.zeros((tokens, DMAX, channels), target.dtype)
    if target.shape[0] > tokens:
        target[0:DMAX] = border
        target[DMAX + tokens :] = border
    if line > tokens:
        rows = slice(target.shape[0] - tokens - DMAX, target.shape[0] - DMAX)
        if target.shape[0] == tokens:
            rows = slice(0, tokens)
        target[rows, 0:DMAX, :] = rim
        target[rows, DMAX + tokens :, :] = rim


def forward_kernel(
    plan,
    dilations,
    far,
    w_proj,
    w_gate,
    w_out,
    one,
    two,
    near_left,
    near_right,
    near_swapped,
    near_gating,
    near_contact,
    near_start,
    output,
    flipped,
    flipped_two,
    factor,
    mine,
    own_contact,
    far_left,
    right,
    swapped,
    far_gating,
    far_contact,
    far_start,
    turned_left,
    turned_right,
    products,
    updated,
    field,
    wide,
    second,
):
    _, _, height, breadth, tokens = plan
    hidden, channels = w_out.shape
    pixels = height * breadth
    chips = tokens // height // 2
    row_place, col_place = lax.axis_index("row"), lax.axis_index("col")
    core = row_place % 2
    rate_one, rate_two = dilations[0], dilations[1]
    inside = slice(DMAX, DMAX + tokens)
    for target in (field, wide, second):
        clear_border(target, tokens)

    right[core] = near_right[...]
    swapped[core] = near_swapped[...]
    project_half(
        plan,
        1 - core,
        far,
        w_proj,
        w_gate,
        far_left,
        right.at[1 - core],
        swapped.at[1 - core],
        far_gating,
        far_contact,
        far_start,
        (turned_left, turned_right),
    )

    lane = lax.broadcasted_iota(jnp.int32, (height, chips * tokens), 1)
    low = jnp.where(lane < tokens, 1.0, 0.0).astype(jnp.bfloat16)
    high = jnp.where(lane < tokens, 0.0, 1.0).astype(jnp.bfloat16)
    batch = 32

    def multiply(step, carry):
        for part in range(batch):
            h = step * batch + part
            ahead = [right[0, h], right[1, h]]
            back = [swapped[0, h], swapped[1, h]]
            strips = [strip * low for strip in ahead + back]
            strips += [strip * high for strip in back + ahead]
            mine = jnp.concatenate([near_left[h], far_left[h]], axis=0)
            products[pl.ds(pl.multiple_of(h * 2 * height, 2 * height), 2 * height), :] = (
                matmul_nt(mine, jnp.concatenate(strips, axis=0))
            )
        return carry

    lax.fori_loop(0, hidden // batch, multiply, 0)

    chunk = 8
    size = chunk * tokens

    def update(step, half, side, gating, contact, start):
        first = step * chunk
        turned = []
        for row in range(chunk):
            strip = products[pl.ds(half * height + first + row, hidden, stride=2 * height), :]
            turned.append(layer_norm(strip, axis=0).astype(jnp.bfloat16).T)
        product_norm = jnp.concatenate(
            [
                strip[chip * tokens : (chip + 1) * tokens]
                for chip in range(chips)
                for strip in turned
            ],
            axis=0,
        )
        change = matmul(product_norm, w_out[...]).reshape(chips, chunk, tokens, channels)
        rows = pl.ds(first, chunk)
        fresh = start[:, rows].astype(jnp.float32) + gating[:, rows].astype(jnp.float32) * change
        fresh = fresh.astype(jnp.bfloat16).astype(jnp.float32)
        first_in = layer_norm(fresh) * contact[:, rows].astype(jnp.float32)
        for chip in range(chips):
            base = (chip * 2 + side) * height + first
            rows = pl.ds(base, chunk)
            updated[rows] = fresh[chip]
            field[rows, inside, :] = first_in[chip]
            spread(field, rows, 0, rate_one, wide)
            flipped[:, pl.ds(pl.multiple_of(base * tokens, size), size)] = (
                first_in[chip].reshape(size, channels).astype(jnp.bfloat16).T
            )

    halves = (
        (core, near_gating, near_contact, near_start),
        (1 - core, far_gating, far_contact, far_start),
    )
    for half, parts in enumerate(halves):
        lax.fori_loop(0, height // chunk, lambda i, c: (update(i, half, *parts), c)[1], 0)

    def first_conv(step, carry):
        first = step * chunk
        shape = (chunk, tokens, channels)
        pre = matmul(taps(wide, first, chunk, rate_one), one[...])
        sigma = sigmoid(pre)
        second_in = pre * sigma
        second[pl.ds(DMAX + first, chunk), inside, :] = second_in.reshape(shape)
        flipped_two[:, lanes(step, size)] = second_in.astype(jnp.bfloat16).T
        factor[pl.ds(first, chunk)] = (sigma * (1.0 + pre * (1.0 - sigma))).reshape(shape)
        return carry

    lax.fori_loop(0, tokens // chunk, first_conv, 0)

    row_start, col_start = row_place * height, col_place * breadth
    cols = pl.ds(pl.multiple_of(col_start, breadth), breadth)
    fresh = updated[pl.ds(row_start, height), cols, :].reshape(pixels, channels)
    mine[...] = fresh
    second_pre = matmul(
        windows(second, rate_two, row_start, col_start, height, breadth),
        two[...].reshape(9 * channels, channels),
    )
    output[...] = (fresh + second_pre).astype(jnp.bfloat16)
    marks = near_contact[row_place // 2].astype(jnp.float32)
    place_col = lax.broadcasted_iota(jnp.int32, (tokens, channels), 0) // breadth
    marks = jnp.where((place_col == col_place)[None], marks, 0.0)
    marks = marks.reshape(height, tokens // breadth, breadth, channels)
    own_contact[...] = jnp.sum(marks, axis=1).reshape(pixels, channels)


def backward_kernel(
    plan,
    dilations,
    cot_near,
    cot_far,
    one,
    two_t,
    flipped,
    flipped_two,
    factor,
    mine,
    own_contact,
    grad_pair,
    grad_one,
    grad_two,
    field,
    wide_cot,
    wide_pre,
    grad_pre,
    sum_one,
    sum_two,
):
    _, cot_rounds, height, breadth, tokens = plan
    channels = one.shape[1]
    pixels = height * breadth
    row_place, col_place = lax.axis_index("row"), lax.axis_index("col")
    rate_one, rate_two = dilations[0], dilations[1]
    half = cot_far.shape[0]
    inside = slice(DMAX, DMAX + tokens)
    for target in (field, wide_cot, wide_pre, grad_pre):
        clear_border(target, tokens)

    several = 4

    def place_cot(source, base):
        def body(step, carry):
            for i in range(several):
                slot = step * several + i
                row, col = place_of(base + slot, cot_rounds, row_place, col_place)
                cols = pl.ds(pl.multiple_of(DMAX + col * breadth, breadth), breadth)
                field[pl.ds(row * height, height), cols, :] = (
                    source[slot]
                    .astype(jnp.float32)
                    .reshape(height, breadth, channels)
                )
            return carry

        lax.fori_loop(0, half // several, body, 0)

    place_cot(cot_near, 0)
    place_cot(cot_far, half)

    chunk = 8
    size = chunk * tokens
    steps = tokens // chunk

    def spread_cot(step, carry):
        spread(field, pl.ds(step * chunk, chunk), 0, -rate_two, wide_cot)
        return carry

    lax.fori_loop(0, steps, spread_cot, 0)

    sum_two[...] = jnp.zeros_like(sum_two)

    def back_two(step, carry):
        first = step * chunk
        shifted = taps(wide_cot, first, chunk, -rate_two)
        before = matmul(shifted, two_t[...]).reshape(chunk, tokens, channels)
        before = (before * factor[pl.ds(first, chunk)]).astype(jnp.bfloat16).astype(jnp.float32)
        grad_pre[pl.ds(DMAX + first, chunk), inside, :] = before
        sum_two[...] += matmul(flipped_two[:, lanes(step, size)], shifted)
        spread(grad_pre, pl.ds(first, chunk), DMAX, -rate_one, wide_pre)
        return carry

    lax.fori_loop(0, steps, back_two, 0)

    sum_one[...] = jnp.zeros_like(sum_one)

    def back_one(step, carry):
        sum_one[...] += matmul(
            flipped[:, lanes(step, size)], taps(wide_pre, step * chunk, chunk, -rate_one)
        )
        return carry

    lax.fori_loop(0, steps, back_one, 0)
    for tap in range(9):
        columns = slice(tap * channels, (tap + 1) * channels)
        grad_one[tap] = sum_one[:, columns] * (1.0 / tokens)
        grad_two[tap] = sum_two[:, columns] * (1.0 / tokens)

    one_rows = [one[tap * channels : (tap + 1) * channels] for tap in range(9)]
    grad_input = own_contact[...] * matmul_nt(
        windows(
            grad_pre, -rate_one, row_place * height, col_place * breadth, height, breadth
        ),
        jnp.concatenate(one_rows, axis=1),
    )
    centre = mine[...] - jnp.mean(mine[...], axis=-1, keepdims=True)
    inv_spread = lax.rsqrt(jnp.mean(centre * centre, axis=-1, keepdims=True) + EPSILON)
    scaled = centre * inv_spread
    grad_norm = inv_spread * (
        grad_input
        - jnp.mean(grad_input, axis=-1, keepdims=True)
        - scaled * jnp.mean(grad_input * scaled, axis=-1, keepdims=True)
    )
    grad_pair[...] = (cot_near[0].astype(jnp.float32) + grad_norm).astype(jnp.bfloat16)


def replicated(
    pair, pair_mask, contact_mask, dilations, w_proj, w_gate, w_out, conv_one, conv_two, cotangent
):
    height, breadth, channels = pair.shape
    hidden = w_out.shape[0]
    row_count, col_count = lax.axis_size("row"), lax.axis_size("col")
    tokens = height * row_count
    pixels = height * breadth
    rounds, cot_rounds = exchange_plan(row_count, col_count)
    f32, bf16 = jnp.float32, jnp.bfloat16
    plan = (rounds, cot_rounds, height, breadth, tokens)
    chips = row_count // 2
    line = tokens + 2 * DMAX
    in_vmem = pl.BlockSpec(memory_space=pltpu.VMEM)
    side = ((hidden, height, chips * tokens), bf16)
    rows = (chips, height, tokens, channels)
    halves = [side] * 3 + [(rows, bf16)] * 3
    turned = pltpu.VMEM((hidden * height, chips * tokens), f32)
    stat = ((pixels, channels), f32)

    def shapes(*entries):
        return [jax.ShapeDtypeStruct(shape, dtype) for shape, dtype in entries]

    in_smem = pl.BlockSpec(memory_space=pltpu.SMEM)
    held, cot_held, rates = pl.pallas_call(
        pack_kernel,
        in_specs=[in_smem] + [in_vmem] * 4,
        out_specs=[in_vmem, in_vmem, in_smem],
        out_shape=shapes(
            ((1, pixels + 2 * breadth, channels), bf16),
            ((1, pixels, channels), bf16),
            ((2,), jnp.int32),
        ),
    )(
        dilations,
        pair.reshape(pixels, channels),
        cotangent.reshape(pixels, channels),
        pair_mask.T,
        contact_mask.T,
    )
    for step, (hop, cot_hop) in enumerate(zip(rounds[:-1], cot_rounds[:-1])):
        held = jnp.concatenate([held, exchange(held, hop)], axis=0)
        cot_other = exchange(cot_held, cot_hop)
        if step < len(rounds) - 2:
            cot_held = jnp.concatenate([cot_held, cot_other], axis=0)
    near, far = held, exchange(held, rounds[-1])
    *near_parts, two_t = pl.pallas_call(
        functools.partial(near_kernel, plan),
        in_specs=[in_vmem] * 4,
        out_specs=[in_vmem] * 7,
        out_shape=shapes(*halves, ((9 * channels, channels), bf16)),
        scratch_shapes=[turned] * 2,
        compiler_params=pltpu.CompilerParams(vmem_limit_bytes=VMEM_LIMIT // 3),
        cost_estimate=pl.CostEstimate(
            flops=tokens * tokens * channels * 5 * hidden,
            bytes_accessed=8 * tokens * tokens * channels,
            transcendentals=3 * tokens * tokens * channels // 2,
        ),
    )(near, w_proj, w_gate, conv_two)
    cot_other, two_t = lax.optimization_barrier((cot_other, two_t))
    cot_near = jnp.concatenate([cot_held, cot_other], axis=0)
    cot_far = exchange(cot_near, cot_rounds[-1])
    whole = pltpu.VMEM((tokens, tokens, channels), f32)
    padded = pltpu.VMEM((tokens, line, channels), f32)
    bordered = pltpu.VMEM((line, line, channels), f32)
    tripled = pltpu.VMEM((line, tokens, 3 * channels), bf16)
    both = pltpu.VMEM((2,) + side[0], bf16)
    alone = pltpu.VMEM(rows, bf16)
    flat = ((channels, tokens * tokens), bf16)
    sums = pltpu.VMEM((channels, 9 * channels), f32)
    output, *held = pl.pallas_call(
        functools.partial(forward_kernel, plan),
        in_specs=[in_smem] + [in_vmem] * 12,
        out_specs=[in_vmem] * 6,
        out_shape=shapes(
            ((pixels, channels), bf16),
            flat,
            flat,
            ((tokens, tokens, channels), f32),
            stat,
            stat,
        ),
        scratch_shapes=[pltpu.VMEM(*side), both, both, alone, alone, alone]
        + [turned] * 2
        + [pltpu.VMEM((hidden * 2 * height, chips * tokens), f32)]
        + [whole, padded, tripled, bordered],
        compiler_params=pltpu.CompilerParams(vmem_limit_bytes=FORWARD_VMEM),
        cost_estimate=pl.CostEstimate(
            flops=tokens * tokens * channels * 40 * hidden,
            bytes_accessed=40 * tokens * tokens * channels,
            transcendentals=4 * tokens * tokens * channels,
        ),
    )(
        rates,
        far,
        w_proj,
        w_gate,
        w_out,
        conv_one.reshape(9 * channels, channels),
        conv_two,
        *near_parts,
    )
    grad_pair, grad_one, grad_two = pl.pallas_call(
        functools.partial(backward_kernel, plan),
        in_specs=[in_smem] + [in_vmem] * 9,
        out_specs=[in_vmem] * 3,
        out_shape=shapes(
            ((pixels, channels), bf16),
            ((9, channels, channels), f32),
            ((9, channels, channels), f32),
        ),
        scratch_shapes=[padded, tripled, tripled, bordered, sums, sums],
        compiler_params=pltpu.CompilerParams(vmem_limit_bytes=BACKWARD_VMEM),
    )(
        rates,
        cot_near,
        cot_far,
        conv_one.reshape(9 * channels, channels),
        two_t,
        *held,
    )
    block = (height, breadth, channels)
    return output.reshape(block), grad_pair.reshape(block), grad_one, grad_two


def fits(pair, w_out, row_count, col_count):
    height, breadth, channels = pair.shape
    tokens = height * row_count
    powers = all(count & (count - 1) == 0 for count in (row_count, col_count))
    whole = (tokens + 2 * DMAX) ** 2 * channels
    return (
        powers
        and row_count * col_count >= 8
        and height * breadth == channels == w_out.shape[0]
        and breadth == 8
        and row_count // 2 * tokens == channels
        and whole * 60 <= VMEM_LIMIT
    )


def local(*arguments):
    pair, w_out = arguments[0], arguments[6]
    if fits(pair, w_out, lax.axis_size("row"), lax.axis_size("col")):
        return replicated(*arguments)
    return sharded(*arguments)


def solution(mesh):
    in_specs = (
        P("row", "col", None),
        P("row", "col"),
        P("row", "col"),
        P(),
        P(),
        P(),
        P(),
        P(),
        P(),
        P("row", "col", None),
    )
    out_specs = (P("row", "col", None), P("row", "col", None), P(), P())
    return jax.shard_map(local, mesh=mesh, in_specs=in_specs, out_specs=out_specs, check_vma=False)
```

```python
import functools

import jax
import jax.numpy as jnp
from jax import lax
from jax.experimental import pallas as pl
from jax.experimental.pallas import tpu as pltpu
from jax.sharding import PartitionSpec as P

DMAX = 8
VMEM_LIMIT = 48 * 1024 * 1024
PACK_VMEM = 4 * 1024 * 1024
FORWARD_VMEM = 36 * 1024 * 1024
BACKWARD_VMEM = 28 * 1024 * 1024


EPSILON = 1e-05


def with_halo(block, sides, width):
    for axis, dim in sides:
        count = lax.axis_size(axis)
        forward = [(i, i + 1) for i in range(count - 1)]
        backward = [(target, source) for source, target in forward]
        low = lax.ppermute(
            lax.slice_in_dim(block, block.shape[dim] - width, None, axis=dim), axis, forward
        )
        high = lax.ppermute(lax.slice_in_dim(block, 0, width, axis=dim), axis, backward)
        block = jnp.concatenate([low, block, high], axis=dim)
    return block


def broadcast(x, axis, root):
    mine = lax.axis_index(axis) == root
    return lax.psum(jnp.where(mine, x, jnp.zeros_like(x)), axis)


def layer_norm(values, axis=-1):
    centre = values - jnp.mean(values, axis=axis, keepdims=True)
    spread = jnp.mean(centre * centre, axis=axis, keepdims=True)
    return centre * lax.rsqrt(spread + EPSILON)


def with_rim(field):
    return with_halo(field, (("row", 0), ("col", 1)), DMAX)


def gather_taps(padded, dilation, mirrored, height, breadth):
    windows = []
    for tap_index in range(9):
        row_tap = tap_index // 3
        col_tap = tap_index % 3
        if mirrored:
            row_tap = 2 - row_tap
            col_tap = 2 - col_tap
        row_start = DMAX + (row_tap - 1) * dilation
        col_start = DMAX + (col_tap - 1) * dilation
        windows.append(
            lax.dynamic_slice(
                padded, (row_start, col_start, jnp.int32(0)), (height, breadth, padded.shape[2])
            )
        )
    return jnp.concatenate(windows, axis=2).reshape(height * breadth, -1)


def sharded(
    pair, pair_mask, contact_mask, dilations, w_proj, w_gate, w_out, conv_one, conv_two, cotangent
):
    height, breadth, channels = pair.shape
    hidden = w_out.shape[0]
    row_count = lax.axis_size("row")
    col_count = lax.axis_size("col")
    ratio = col_count // row_count
    row_place = lax.axis_index("row")
    col_place = lax.axis_index("col")
    tokens = breadth * col_count
    pixels = height * breadth
    pair_flat = pair.astype(jnp.float32).reshape(pixels, channels)
    normed = layer_norm(pair_flat).astype(jnp.bfloat16)
    projected = jnp.dot(normed, w_proj, preferred_element_type=jnp.float32)
    mask_col = pair_mask.reshape(pixels, 1).astype(jnp.float32)
    left_side = (
        (mask_col * jax.nn.sigmoid(projected[:, hidden : 2 * hidden]) * projected[:, :hidden])
        .astype(jnp.bfloat16)
        .reshape(height, breadth, hidden)
    )
    right_side = (
        (
            mask_col
            * jax.nn.sigmoid(projected[:, 3 * hidden :])
            * projected[:, 2 * hidden : 3 * hidden]
        )
        .astype(jnp.bfloat16)
        .reshape(height, breadth, hidden)
    )
    right_all = lax.all_gather(right_side, "col", axis=1, tiled=True)
    offset = jnp.clip(col_place * breadth - row_place * height, 0, height - breadth)
    right_local = lax.dynamic_slice_in_dim(right_all, offset, breadth, 0)
    right_rows = broadcast(right_local, "row", col_place // ratio)
    products = jnp.einsum(
        "ikh,jkh->ijh",
        lax.all_gather(left_side, "col", axis=1, tiled=True),
        right_rows,
        preferred_element_type=jnp.float32,
    )
    product_norm = layer_norm(products.reshape(pixels, hidden)).astype(jnp.bfloat16)
    gating = jax.nn.sigmoid(jnp.dot(normed, w_gate, preferred_element_type=jnp.float32))
    updated = (
        pair_flat + gating * jnp.dot(product_norm, w_out, preferred_element_type=jnp.float32)
    ).astype(jnp.bfloat16)
    updated_f = updated.astype(jnp.float32)
    centre = updated_f - jnp.mean(updated_f, axis=-1, keepdims=True)
    inv_spread = lax.rsqrt(jnp.mean(centre * centre, axis=-1, keepdims=True) + EPSILON)
    scaled = centre * inv_spread
    contact = contact_mask.reshape(pixels, 1).astype(jnp.float32)
    first_in = (scaled * contact).astype(jnp.bfloat16).reshape(height, breadth, channels)
    rate_one = dilations[0]
    rate_two = dilations[1]
    first_taps = gather_taps(with_rim(first_in), rate_one, False, height, breadth)
    first_pre = jnp.dot(
        first_taps, conv_one.reshape(9 * channels, channels), preferred_element_type=jnp.float32
    )
    sigma = jax.nn.sigmoid(first_pre)
    second_in = (first_pre * sigma).astype(jnp.bfloat16).reshape(height, breadth, channels)
    second_taps = gather_taps(with_rim(second_in), rate_two, False, height, breadth)
    second_pre = jnp.dot(
        second_taps, conv_two.reshape(9 * channels, channels), preferred_element_type=jnp.float32
    )
    output = (updated_f + second_pre).astype(jnp.bfloat16).reshape(height, breadth, channels)
    cot_flat = cotangent.reshape(pixels, channels)
    grad_two = (
        lax.dot_general(
            second_taps, cot_flat, (((0,), (0,)), ((), ())), preferred_element_type=jnp.float32
        ).reshape(9, channels, channels)
        / tokens
    )
    cot_taps = gather_taps(with_rim(cotangent), rate_two, True, height, breadth)
    grad_hidden = jnp.dot(
        cot_taps,
        conv_two.transpose(0, 2, 1).reshape(9 * channels, channels),
        preferred_element_type=jnp.float32,
    )
    grad_pre = (grad_hidden * sigma * (1.0 + first_pre * (1.0 - sigma))).astype(jnp.bfloat16)
    grad_one = (
        lax.dot_general(
            first_taps, grad_pre, (((0,), (0,)), ((), ())), preferred_element_type=jnp.float32
        ).reshape(9, channels, channels)
        / tokens
    )
    grad_taps = gather_taps(
        with_rim(grad_pre.reshape(height, breadth, channels)), rate_one, True, height, breadth
    )
    grad_input = (
        jnp.dot(
            grad_taps,
            conv_one.transpose(0, 2, 1).reshape(9 * channels, channels),
            preferred_element_type=jnp.float32,
        )
        * contact
    )
    grad_norm = inv_spread * (
        grad_input
        - jnp.mean(grad_input, axis=-1, keepdims=True)
        - scaled * jnp.mean(grad_input * scaled, axis=-1, keepdims=True)
    )
    grad_pair = (
        (cot_flat.astype(jnp.float32) + grad_norm)
        .astype(jnp.bfloat16)
        .reshape(height, breadth, channels)
    )
    grad_one, grad_two = lax.psum((grad_one, grad_two), ("row", "col"))
    return (output, grad_pair, grad_one, grad_two)


def halvings(axis, count):
    return [(axis, count >> step) for step in range(1, count.bit_length())]


def exchange_plan(row_count, col_count):
    rows, cols = halvings("row", row_count), halvings("col", col_count)
    return cols + rows, rows[:-1] + cols + rows[-1:]


def exchange(held, hop):
    axis, distance = hop
    return lax.ppermute(held, axis, [(i, i ^ distance) for i in range(lax.axis_size(axis))])


def place_of(position, rounds, row_place, col_place):
    row, col = row_place, col_place
    for step, (axis, distance) in enumerate(rounds):
        bit = ((position >> step) & 1) * distance
        if axis == "row":
            row = row ^ bit
        else:
            col = col ^ bit
    return row, col


def slot_of(row_change, col_change, rounds):
    slot = 0
    for step, (axis, distance) in enumerate(rounds[:-1]):
        change = row_change if axis == "row" else col_change
        slot = slot | (((change // distance) & 1) << step)
    return slot


def sigmoid(values):
    return 0.5 + 0.5 * jnp.tanh(0.5 * values)


def matmul(left, right):
    return jnp.dot(left, right, preferred_element_type=jnp.float32)


def matmul_nt(left, right):
    return lax.dot_general(
        left, right, (((1,), (1,)), ((), ())), preferred_element_type=jnp.float32
    )


def pack_kernel(dilations, pair, cotangent, pair_mask, contact_mask, packed, cot, rates):
    pixels, channels = pair.shape
    breadth, height = pair_mask.shape
    masks = jnp.concatenate(
        [
            pair_mask[...].astype(jnp.float32),
            contact_mask[...].astype(jnp.float32),
            jnp.zeros((breadth, channels - 2 * height), jnp.float32),
        ],
        axis=1,
    )
    tile = jnp.concatenate([masks, jnp.zeros_like(masks)], axis=0)
    packed[0, 0:pixels] = pair[...]
    packed[0, pixels:] = tile.astype(jnp.bfloat16)
    cot[0] = cotangent[...]
    for rate in range(2):
        rates[rate] = jnp.clip(dilations[rate], 1, DMAX)


def project_half(
    plan, core, pairs, w_proj, w_gate, left, right, swapped, gating, contact, start, turned
):
    rounds, _, height, breadth, tokens = plan
    channels, hidden = w_gate.shape[0], w_gate.shape[1]
    col_count, chips = tokens // breadth, tokens // height // 2
    row_place, col_place = lax.axis_index("row"), lax.axis_index("col")
    lane = lax.broadcasted_iota(jnp.int32, (height, breadth, channels), 2)
    place = lax.broadcasted_iota(jnp.int32, (height, breadth, channels), 0)
    own_lane = jnp.where((lane % height == place) & (lane < 2 * height), 1.0, 0.0)
    pick_lane = lax.broadcasted_iota(jnp.int32, (channels, 2 * channels), 0)
    pick_half = lax.broadcasted_iota(jnp.int32, (channels, 2 * channels), 1) // channels
    pick = jnp.where(pick_lane // height == pick_half, 1.0, 0.0).astype(jnp.bfloat16)
    pixels = height * breadth
    rows = 8
    for first in range(0, height, rows):
        values, masks = [], []
        for chip in range(chips):
            row_change = (chip * 2 + core) ^ row_place
            blocks, marks = [], []
            for col in range(col_count):
                col_change = col_place ^ col
                slot = slot_of(row_change, col_change, rounds)
                blocks.append(
                    pairs[slot, first * breadth : (first + rows) * breadth, :]
                    .astype(jnp.float32)
                    .reshape(rows, breadth, channels)
                )
                mark = pairs[slot, pixels:, :].astype(jnp.float32)[:breadth]
                marks.append(mark[None] * own_lane[first : first + rows])
            values.append(jnp.concatenate(blocks, axis=1).reshape(rows * tokens, channels))
            masks.append(jnp.concatenate(marks, axis=1).reshape(rows * tokens, channels))
        values = jnp.concatenate(values, axis=0)
        masks = matmul(jnp.concatenate(masks, axis=0).astype(jnp.bfloat16), pick)
        normed = layer_norm(values)
        gates = sigmoid(matmul(normed.astype(jnp.bfloat16), w_gate[...]))
        masked = (normed * masks[:, :channels]).astype(jnp.bfloat16)
        projected = matmul(masked, w_proj[...])
        sides = [
            sigmoid(projected[:, (2 * side + 1) * hidden : (2 * side + 2) * hidden])
            * projected[:, 2 * side * hidden : (2 * side + 1) * hidden]
            for side in range(2)
        ]
        for side, target in zip(sides, turned):
            side = side.reshape(chips, rows, tokens, hidden)
            for row in range(rows):
                strip = jnp.concatenate([side[chip, row] for chip in range(chips)], axis=0)
                target[pl.ds(first + row, hidden, stride=height), :] = strip.T
        shape = (chips, rows, tokens, channels)
        span = slice(first, first + rows)
        gating[:, span] = gates.astype(jnp.bfloat16).reshape(shape)
        contact[:, span] = masks[:, channels:].astype(jnp.bfloat16).reshape(shape)
        start[:, span] = values.astype(jnp.bfloat16).reshape(shape)
    shape = (hidden, height, chips * tokens)
    left[...] = turned[0][...].reshape(shape).astype(jnp.bfloat16)
    other = turned[1][...]
    right[...] = other.reshape(shape).astype(jnp.bfloat16)
    swapped[...] = pltpu.roll(other, tokens, 1).reshape(shape).astype(jnp.bfloat16)


def near_kernel(
    plan,
    near,
    w_proj,
    w_gate,
    two,
    left,
    right,
    swapped,
    gating,
    contact,
    start,
    two_t,
    turned_left,
    turned_right,
):
    core = lax.axis_index("row") % 2
    channels = two.shape[1]
    for tap in range(9):
        two_t[tap * channels : (tap + 1) * channels] = two[tap].T
    project_half(
        plan,
        core,
        near,
        w_proj,
        w_gate,
        left,
        right,
        swapped,
        gating,
        contact,
        start,
        (turned_left, turned_right),
    )


def spread(source, rows, pad, rate, target):
    tokens, channels = target.shape[1], source.shape[2]
    for tap in range(3):
        moved = source[
            pl.ds(pad + rows.start, rows.size), pl.ds(DMAX + (tap - 1) * rate, tokens), :
        ]
        target[pl.ds(DMAX + rows.start, rows.size), :, tap * channels : (tap + 1) * channels] = (
            moved.astype(jnp.bfloat16)
        )


def taps(source, first, count, rate):
    tokens = source.shape[1]
    views = [
        source[pl.ds(DMAX + first + (tap - 1) * rate, count)].reshape(count * tokens, -1)
        for tap in range(3)
    ]
    return jnp.concatenate(views, axis=1)


def windows(source, rate, row_start, col_start, height, breadth):
    views = [
        source[
            pl.ds(row_start + DMAX + (tap // 3 - 1) * rate, height),
            pl.ds(col_start + DMAX + (tap % 3 - 1) * rate, breadth),
            :,
        ].reshape(height * breadth, -1)
        for tap in range(9)
    ]
    return jnp.concatenate(views, axis=1).astype(jnp.bfloat16)


def lanes(step, size):
    return pl.ds(pl.multiple_of(step * size, size), size)


def clear_border(target, tokens):
    line, channels = target.shape[1], target.shape[2]
    border = jnp.zeros((DMAX, line, channels), target.dtype)
    rim = jnp.zeros((tokens, DMAX, channels), target.dtype)
    if target.shape[0] > tokens:
        target[0:DMAX] = border
        target[DMAX + tokens :] = border
    if line > tokens:
        rows = slice(target.shape[0] - tokens - DMAX, target.shape[0] - DMAX)
        if target.shape[0] == tokens:
            rows = slice(0, tokens)
        target[rows, 0:DMAX, :] = rim
        target[rows, DMAX + tokens :, :] = rim


def forward_kernel(
    plan,
    dilations,
    far,
    w_proj,
    w_gate,
    w_out,
    one,
    two,
    near_left,
    near_right,
    near_swapped,
    near_gating,
    near_contact,
    near_start,
    output,
    flipped,
    flipped_two,
    factor,
    mine,
    own_contact,
    far_left,
    right,
    swapped,
    far_gating,
    far_contact,
    far_start,
    turned_left,
    turned_right,
    products,
    normed,
    updated,
    field,
    wide,
    second,
):
    _, _, height, breadth, tokens = plan
    hidden, channels = w_out.shape
    pixels = height * breadth
    chips = tokens // height // 2
    row_place, col_place = lax.axis_index("row"), lax.axis_index("col")
    core = row_place % 2
    rate_one, rate_two = dilations[0], dilations[1]
    inside = slice(DMAX, DMAX + tokens)
    for target in (field, wide, second):
        clear_border(target, tokens)

    right[core] = near_right[...]
    swapped[core] = near_swapped[...]
    project_half(
        plan,
        1 - core,
        far,
        w_proj,
        w_gate,
        far_left,
        right.at[1 - core],
        swapped.at[1 - core],
        far_gating,
        far_contact,
        far_start,
        (turned_left, turned_right),
    )

    lane = lax.broadcasted_iota(jnp.int32, (height, chips * tokens), 1)
    low = jnp.where(lane < tokens, 1.0, 0.0).astype(jnp.bfloat16)
    high = jnp.where(lane < tokens, 0.0, 1.0).astype(jnp.bfloat16)
    batch = 32

    def multiply(step, carry):
        for part in range(batch):
            h = step * batch + part
            ahead = [right[0, h], right[1, h]]
            back = [swapped[0, h], swapped[1, h]]
            strips = [strip * low for strip in ahead + back]
            strips += [strip * high for strip in back + ahead]
            mine = jnp.concatenate([near_left[h], far_left[h]], axis=0)
            products[pl.ds(pl.multiple_of(h * 2 * height, 2 * height), 2 * height), :] = (
                matmul_nt(mine, jnp.concatenate(strips, axis=0))
            )
        return carry

    lax.fori_loop(0, hidden // batch, multiply, 0)

    chunk = 8
    size = chunk * tokens

    halves = (
        (core, near_gating, near_contact, near_start),
        (1 - core, far_gating, far_contact, far_start),
    )
    parts = height // chunk

    def normalise(step):
        half, first = step // parts, step % parts * chunk
        for row in range(chunk):
            strip = products[pl.ds(half * height + first + row, hidden, stride=2 * height), :]
            strip = layer_norm(strip, axis=0).astype(jnp.bfloat16).T
            for chip in range(chips):
                normed[step, chip, row] = strip[chip * tokens : (chip + 1) * tokens]

    def update(step):
        first = step % parts * chunk
        side, gating, contact, start = halves[step // parts]
        change = matmul(normed[step].reshape(chips * size, hidden), w_out[...])
        change = change.reshape(chips, chunk, tokens, channels)
        rows = pl.ds(first, chunk)
        fresh = start[:, rows].astype(jnp.float32) + gating[:, rows].astype(jnp.float32) * change
        fresh = fresh.astype(jnp.bfloat16).astype(jnp.float32)
        first_in = layer_norm(fresh) * contact[:, rows].astype(jnp.float32)
        for chip in range(chips):
            base = (chip * 2 + side) * height + first
            rows = pl.ds(base, chunk)
            updated[rows] = fresh[chip]
            field[rows, inside, :] = first_in[chip]
            spread(field, rows, 0, rate_one, wide)
            flipped[:, pl.ds(pl.multiple_of(base * tokens, size), size)] = (
                first_in[chip].reshape(size, channels).astype(jnp.bfloat16).T
            )

    normalise(0)
    for step in range(1, 2 * parts):
        normalise(step)
        update(step - 1)
    update(2 * parts - 1)

    def first_conv(step):
        factor[pl.ds(step * chunk, chunk)] = matmul(
            taps(wide, step * chunk, chunk, rate_one), one[...]
        ).reshape(chunk, tokens, channels)

    def activate(step):
        rows = pl.ds(step * chunk, chunk)
        pre = factor[rows]
        sigma = sigmoid(pre)
        second_in = pre * sigma
        second[pl.ds(DMAX + step * chunk, chunk), inside, :] = second_in
        flipped_two[:, lanes(step, size)] = (
            second_in.reshape(size, channels).astype(jnp.bfloat16).T
        )
        factor[rows] = sigma * (1.0 + pre * (1.0 - sigma))

    def convolve(step, carry):
        activate(step - 1)
        first_conv(step)
        return carry

    first_conv(0)
    lax.fori_loop(1, tokens // chunk, convolve, 0)
    activate(tokens // chunk - 1)

    row_start, col_start = row_place * height, col_place * breadth
    cols = pl.ds(pl.multiple_of(col_start, breadth), breadth)
    fresh = updated[pl.ds(row_start, height), cols, :].reshape(pixels, channels)
    mine[...] = fresh
    second_pre = matmul(
        windows(second, rate_two, row_start, col_start, height, breadth),
        two[...].reshape(9 * channels, channels),
    )
    output[...] = (fresh + second_pre).astype(jnp.bfloat16)
    marks = near_contact[row_place // 2].astype(jnp.float32)
    place_col = lax.broadcasted_iota(jnp.int32, (tokens, channels), 0) // breadth
    marks = jnp.where((place_col == col_place)[None], marks, 0.0)
    marks = marks.reshape(height, tokens // breadth, breadth, channels)
    own_contact[...] = jnp.sum(marks, axis=1).reshape(pixels, channels)


def backward_kernel(
    plan,
    dilations,
    cot_near,
    cot_far,
    one,
    two_t,
    flipped,
    flipped_two,
    factor,
    mine,
    own_contact,
    grad_pair,
    grad_one,
    grad_two,
    field,
    wide_cot,
    wide_pre,
    grad_pre,
    sum_one,
    sum_two,
):
    _, cot_rounds, height, breadth, tokens = plan
    channels = one.shape[1]
    pixels = height * breadth
    row_place, col_place = lax.axis_index("row"), lax.axis_index("col")
    rate_one, rate_two = dilations[0], dilations[1]
    half = cot_far.shape[0]
    inside = slice(DMAX, DMAX + tokens)
    for target in (field, wide_cot, wide_pre, grad_pre):
        clear_border(target, tokens)

    several = 4

    def place_cot(source, base):
        def body(step, carry):
            for i in range(several):
                slot = step * several + i
                row, col = place_of(base + slot, cot_rounds, row_place, col_place)
                cols = pl.ds(pl.multiple_of(DMAX + col * breadth, breadth), breadth)
                field[pl.ds(row * height, height), cols, :] = (
                    source[slot]
                    .astype(jnp.float32)
                    .reshape(height, breadth, channels)
                )
            return carry

        lax.fori_loop(0, half // several, body, 0)

    place_cot(cot_near, 0)
    place_cot(cot_far, half)

    chunk = 8
    size = chunk * tokens
    steps = tokens // chunk

    def spread_cot(step, carry):
        spread(field, pl.ds(step * chunk, chunk), 0, -rate_two, wide_cot)
        return carry

    lax.fori_loop(0, steps, spread_cot, 0)

    sum_two[...] = jnp.zeros_like(sum_two)

    sum_one[...] = jnp.zeros_like(sum_one)

    def back_two(step):
        first = step * chunk
        shifted = taps(wide_cot, first, chunk, -rate_two)
        before = matmul(shifted, two_t[...]).reshape(chunk, tokens, channels)
        before = (before * factor[pl.ds(first, chunk)]).astype(jnp.bfloat16).astype(jnp.float32)
        grad_pre[pl.ds(DMAX + first, chunk), inside, :] = before
        sum_two[...] += matmul(flipped_two[:, lanes(step, size)], shifted)

    def spread_pre(step):
        spread(grad_pre, pl.ds(step * chunk, chunk), DMAX, -rate_one, wide_pre)

    def back_one(step):
        sum_one[...] += matmul(
            flipped[:, lanes(step, size)], taps(wide_pre, step * chunk, chunk, -rate_one)
        )

    def gradients(step, carry):
        back_one(step - 3)
        spread_pre(step - 1)
        back_two(step)
        return carry

    back_two(0)
    for step in (1, 2):
        spread_pre(step - 1)
        back_two(step)
    lax.fori_loop(3, steps, gradients, 0)
    spread_pre(steps - 1)
    lax.fori_loop(steps - 3, steps, lambda i, c: (back_one(i), c)[1], 0)
    for tap in range(9):
        columns = slice(tap * channels, (tap + 1) * channels)
        grad_one[tap] = sum_one[:, columns] * (1.0 / tokens)
        grad_two[tap] = sum_two[:, columns] * (1.0 / tokens)

    one_rows = [one[tap * channels : (tap + 1) * channels] for tap in range(9)]
    grad_input = own_contact[...] * matmul_nt(
        windows(
            grad_pre, -rate_one, row_place * height, col_place * breadth, height, breadth
        ),
        jnp.concatenate(one_rows, axis=1),
    )
    centre = mine[...] - jnp.mean(mine[...], axis=-1, keepdims=True)
    inv_spread = lax.rsqrt(jnp.mean(centre * centre, axis=-1, keepdims=True) + EPSILON)
    scaled = centre * inv_spread
    grad_norm = inv_spread * (
        grad_input
        - jnp.mean(grad_input, axis=-1, keepdims=True)
        - scaled * jnp.mean(grad_input * scaled, axis=-1, keepdims=True)
    )
    grad_pair[...] = (cot_near[0].astype(jnp.float32) + grad_norm).astype(jnp.bfloat16)


def replicated(
    pair, pair_mask, contact_mask, dilations, w_proj, w_gate, w_out, conv_one, conv_two, cotangent
):
    height, breadth, channels = pair.shape
    hidden = w_out.shape[0]
    row_count, col_count = lax.axis_size("row"), lax.axis_size("col")
    tokens = height * row_count
    pixels = height * breadth
    rounds, cot_rounds = exchange_plan(row_count, col_count)
    f32, bf16 = jnp.float32, jnp.bfloat16
    plan = (rounds, cot_rounds, height, breadth, tokens)
    chips = row_count // 2
    line = tokens + 2 * DMAX
    in_vmem = pl.BlockSpec(memory_space=pltpu.VMEM)
    side = ((hidden, height, chips * tokens), bf16)
    rows = (chips, height, tokens, channels)
    halves = [side] * 3 + [(rows, bf16)] * 3
    turned = pltpu.VMEM((hidden * height, chips * tokens), f32)
    stat = ((pixels, channels), f32)

    def shapes(*entries):
        return [jax.ShapeDtypeStruct(shape, dtype) for shape, dtype in entries]

    in_smem = pl.BlockSpec(memory_space=pltpu.SMEM)
    held, cot_held, rates = pl.pallas_call(
        pack_kernel,
        in_specs=[in_smem] + [in_vmem] * 4,
        out_specs=[in_vmem, in_vmem, in_smem],
        out_shape=shapes(
            ((1, pixels + 2 * breadth, channels), bf16),
            ((1, pixels, channels), bf16),
            ((2,), jnp.int32),
        ),
        compiler_params=pltpu.CompilerParams(vmem_limit_bytes=PACK_VMEM),
    )(
        dilations,
        pair.reshape(pixels, channels),
        cotangent.reshape(pixels, channels),
        pair_mask.T,
        contact_mask.T,
    )
    for step, (hop, cot_hop) in enumerate(zip(rounds[:-1], cot_rounds[:-1])):
        held = jnp.concatenate([held, exchange(held, hop)], axis=0)
        cot_other = exchange(cot_held, cot_hop)
        if step < len(rounds) - 2:
            cot_held = jnp.concatenate([cot_held, cot_other], axis=0)
    near, far = held, exchange(held, rounds[-1])
    *near_parts, two_t = pl.pallas_call(
        functools.partial(near_kernel, plan),
        in_specs=[in_vmem] * 4,
        out_specs=[in_vmem] * 7,
        out_shape=shapes(*halves, ((9 * channels, channels), bf16)),
        scratch_shapes=[turned] * 2,
        compiler_params=pltpu.CompilerParams(vmem_limit_bytes=VMEM_LIMIT // 3),
        cost_estimate=pl.CostEstimate(
            flops=tokens * tokens * channels * 5 * hidden,
            bytes_accessed=8 * tokens * tokens * channels,
            transcendentals=3 * tokens * tokens * channels // 2,
        ),
    )(near, w_proj, w_gate, conv_two)
    cot_other, two_t = lax.optimization_barrier((cot_other, two_t))
    cot_near = jnp.concatenate([cot_held, cot_other], axis=0)
    cot_far = exchange(cot_near, cot_rounds[-1])
    whole = pltpu.VMEM((tokens, tokens, channels), f32)
    padded = pltpu.VMEM((tokens, line, channels), f32)
    bordered = pltpu.VMEM((line, line, channels), f32)
    tripled = pltpu.VMEM((line, tokens, 3 * channels), bf16)
    both = pltpu.VMEM((2,) + side[0], bf16)
    alone = pltpu.VMEM(rows, bf16)
    flat = ((channels, tokens * tokens), bf16)
    sums = pltpu.VMEM((channels, 9 * channels), f32)
    output, *held = pl.pallas_call(
        functools.partial(forward_kernel, plan),
        in_specs=[in_smem] + [in_vmem] * 12,
        out_specs=[in_vmem] * 6,
        out_shape=shapes(
            ((pixels, channels), bf16),
            flat,
            flat,
            ((tokens, tokens, channels), f32),
            stat,
            stat,
        ),
        scratch_shapes=[pltpu.VMEM(*side), both, both, alone, alone, alone]
        + [turned] * 2
        + [pltpu.VMEM((hidden * 2 * height, chips * tokens), f32)]
        + [pltpu.VMEM((2 * height // 8, chips, 8, tokens, hidden), bf16)]
        + [whole, padded, tripled, bordered],
        compiler_params=pltpu.CompilerParams(vmem_limit_bytes=FORWARD_VMEM),
        cost_estimate=pl.CostEstimate(
            flops=tokens * tokens * channels * 40 * hidden,
            bytes_accessed=40 * tokens * tokens * channels,
            transcendentals=4 * tokens * tokens * channels,
        ),
    )(
        rates,
        far,
        w_proj,
        w_gate,
        w_out,
        conv_one.reshape(9 * channels, channels),
        conv_two,
        *near_parts,
    )
    grad_pair, grad_one, grad_two = pl.pallas_call(
        functools.partial(backward_kernel, plan),
        in_specs=[in_smem] + [in_vmem] * 9,
        out_specs=[in_vmem] * 3,
        out_shape=shapes(
            ((pixels, channels), bf16),
            ((9, channels, channels), f32),
            ((9, channels, channels), f32),
        ),
        scratch_shapes=[padded, tripled, tripled, bordered, sums, sums],
        compiler_params=pltpu.CompilerParams(vmem_limit_bytes=BACKWARD_VMEM),
    )(
        rates,
        cot_near,
        cot_far,
        conv_one.reshape(9 * channels, channels),
        two_t,
        *held,
    )
    block = (height, breadth, channels)
    return output.reshape(block), grad_pair.reshape(block), grad_one, grad_two


def fits(pair, w_out, row_count, col_count):
    height, breadth, channels = pair.shape
    tokens = height * row_count
    powers = all(count & (count - 1) == 0 for count in (row_count, col_count))
    whole = (tokens + 2 * DMAX) ** 2 * channels
    return (
        powers
        and row_count * col_count >= 8
        and height * breadth == channels == w_out.shape[0]
        and breadth == 8
        and row_count // 2 * tokens == channels
        and whole * 60 <= VMEM_LIMIT
    )


def local(*arguments):
    pair, w_out = arguments[0], arguments[6]
    if fits(pair, w_out, lax.axis_size("row"), lax.axis_size("col")):
        return replicated(*arguments)
    return sharded(*arguments)


def solution(mesh):
    in_specs = (
        P("row", "col", None),
        P("row", "col"),
        P("row", "col"),
        P(),
        P(),
        P(),
        P(),
        P(),
        P(),
        P("row", "col", None),
    )
    out_specs = (P("row", "col", None), P("row", "col", None), P(), P())
    return jax.shard_map(local, mesh=mesh, in_specs=in_specs, out_specs=out_specs, check_vma=False)
```

```python
import functools

import jax
import jax.numpy as jnp
from jax import lax
from jax.experimental import pallas as pl
from jax.experimental.pallas import tpu as pltpu
from jax.sharding import PartitionSpec as P

DMAX = 8
VMEM_LIMIT = 48 * 1024 * 1024
PITCH = 8
FORWARD_VMEM = 44 * 1024 * 1024
BACKWARD_VMEM = 28 * 1024 * 1024


EPSILON = 1e-05


def with_halo(block, sides, width):
    for axis, dim in sides:
        count = lax.axis_size(axis)
        forward = [(i, i + 1) for i in range(count - 1)]
        backward = [(target, source) for source, target in forward]
        low = lax.ppermute(
            lax.slice_in_dim(block, block.shape[dim] - width, None, axis=dim), axis, forward
        )
        high = lax.ppermute(lax.slice_in_dim(block, 0, width, axis=dim), axis, backward)
        block = jnp.concatenate([low, block, high], axis=dim)
    return block


def broadcast(x, axis, root):
    mine = lax.axis_index(axis) == root
    return lax.psum(jnp.where(mine, x, jnp.zeros_like(x)), axis)


def layer_norm(values, axis=-1):
    centre = values - jnp.mean(values, axis=axis, keepdims=True)
    spread = jnp.mean(centre * centre, axis=axis, keepdims=True)
    return centre * lax.rsqrt(spread + EPSILON)


def with_rim(field):
    return with_halo(field, (("row", 0), ("col", 1)), DMAX)


def gather_taps(padded, dilation, mirrored, height, breadth):
    windows = []
    for tap_index in range(9):
        row_tap = tap_index // 3
        col_tap = tap_index % 3
        if mirrored:
            row_tap = 2 - row_tap
            col_tap = 2 - col_tap
        row_start = DMAX + (row_tap - 1) * dilation
        col_start = DMAX + (col_tap - 1) * dilation
        windows.append(
            lax.dynamic_slice(
                padded, (row_start, col_start, jnp.int32(0)), (height, breadth, padded.shape[2])
            )
        )
    return jnp.concatenate(windows, axis=2).reshape(height * breadth, -1)


def sharded(
    pair, pair_mask, contact_mask, dilations, w_proj, w_gate, w_out, conv_one, conv_two, cotangent
):
    height, breadth, channels = pair.shape
    hidden = w_out.shape[0]
    row_count = lax.axis_size("row")
    col_count = lax.axis_size("col")
    ratio = col_count // row_count
    row_place = lax.axis_index("row")
    col_place = lax.axis_index("col")
    tokens = breadth * col_count
    pixels = height * breadth
    pair_flat = pair.astype(jnp.float32).reshape(pixels, channels)
    normed = layer_norm(pair_flat).astype(jnp.bfloat16)
    projected = jnp.dot(normed, w_proj, preferred_element_type=jnp.float32)
    mask_col = pair_mask.reshape(pixels, 1).astype(jnp.float32)
    left_side = (
        (mask_col * jax.nn.sigmoid(projected[:, hidden : 2 * hidden]) * projected[:, :hidden])
        .astype(jnp.bfloat16)
        .reshape(height, breadth, hidden)
    )
    right_side = (
        (
            mask_col
            * jax.nn.sigmoid(projected[:, 3 * hidden :])
            * projected[:, 2 * hidden : 3 * hidden]
        )
        .astype(jnp.bfloat16)
        .reshape(height, breadth, hidden)
    )
    right_all = lax.all_gather(right_side, "col", axis=1, tiled=True)
    offset = jnp.clip(col_place * breadth - row_place * height, 0, height - breadth)
    right_local = lax.dynamic_slice_in_dim(right_all, offset, breadth, 0)
    right_rows = broadcast(right_local, "row", col_place // ratio)
    products = jnp.einsum(
        "ikh,jkh->ijh",
        lax.all_gather(left_side, "col", axis=1, tiled=True),
        right_rows,
        preferred_element_type=jnp.float32,
    )
    product_norm = layer_norm(products.reshape(pixels, hidden)).astype(jnp.bfloat16)
    gating = jax.nn.sigmoid(jnp.dot(normed, w_gate, preferred_element_type=jnp.float32))
    updated = (
        pair_flat + gating * jnp.dot(product_norm, w_out, preferred_element_type=jnp.float32)
    ).astype(jnp.bfloat16)
    updated_f = updated.astype(jnp.float32)
    centre = updated_f - jnp.mean(updated_f, axis=-1, keepdims=True)
    inv_spread = lax.rsqrt(jnp.mean(centre * centre, axis=-1, keepdims=True) + EPSILON)
    scaled = centre * inv_spread
    contact = contact_mask.reshape(pixels, 1).astype(jnp.float32)
    first_in = (scaled * contact).astype(jnp.bfloat16).reshape(height, breadth, channels)
    rate_one = dilations[0]
    rate_two = dilations[1]
    first_taps = gather_taps(with_rim(first_in), rate_one, False, height, breadth)
    first_pre = jnp.dot(
        first_taps, conv_one.reshape(9 * channels, channels), preferred_element_type=jnp.float32
    )
    sigma = jax.nn.sigmoid(first_pre)
    second_in = (first_pre * sigma).astype(jnp.bfloat16).reshape(height, breadth, channels)
    second_taps = gather_taps(with_rim(second_in), rate_two, False, height, breadth)
    second_pre = jnp.dot(
        second_taps, conv_two.reshape(9 * channels, channels), preferred_element_type=jnp.float32
    )
    output = (updated_f + second_pre).astype(jnp.bfloat16).reshape(height, breadth, channels)
    cot_flat = cotangent.reshape(pixels, channels)
    grad_two = (
        lax.dot_general(
            second_taps, cot_flat, (((0,), (0,)), ((), ())), preferred_element_type=jnp.float32
        ).reshape(9, channels, channels)
        / tokens
    )
    cot_taps = gather_taps(with_rim(cotangent), rate_two, True, height, breadth)
    grad_hidden = jnp.dot(
        cot_taps,
        conv_two.transpose(0, 2, 1).reshape(9 * channels, channels),
        preferred_element_type=jnp.float32,
    )
    grad_pre = (grad_hidden * sigma * (1.0 + first_pre * (1.0 - sigma))).astype(jnp.bfloat16)
    grad_one = (
        lax.dot_general(
            first_taps, grad_pre, (((0,), (0,)), ((), ())), preferred_element_type=jnp.float32
        ).reshape(9, channels, channels)
        / tokens
    )
    grad_taps = gather_taps(
        with_rim(grad_pre.reshape(height, breadth, channels)), rate_one, True, height, breadth
    )
    grad_input = (
        jnp.dot(
            grad_taps,
            conv_one.transpose(0, 2, 1).reshape(9 * channels, channels),
            preferred_element_type=jnp.float32,
        )
        * contact
    )
    grad_norm = inv_spread * (
        grad_input
        - jnp.mean(grad_input, axis=-1, keepdims=True)
        - scaled * jnp.mean(grad_input * scaled, axis=-1, keepdims=True)
    )
    grad_pair = (
        (cot_flat.astype(jnp.float32) + grad_norm)
        .astype(jnp.bfloat16)
        .reshape(height, breadth, channels)
    )
    grad_one, grad_two = lax.psum((grad_one, grad_two), ("row", "col"))
    return (output, grad_pair, grad_one, grad_two)


def halvings(axis, count):
    return [(axis, count >> step) for step in range(1, count.bit_length())]


def exchange_plan(row_count, col_count):
    rows, cols = halvings("row", row_count), halvings("col", col_count)
    return cols + rows, rows[:-1] + cols + rows[-1:]


def exchange(held, hop):
    axis, distance = hop
    return lax.ppermute(held, axis, [(i, i ^ distance) for i in range(lax.axis_size(axis))])


def place_of(position, rounds, row_place, col_place):
    row, col = row_place, col_place
    for step, (axis, distance) in enumerate(rounds):
        bit = ((position >> step) & 1) * distance
        if axis == "row":
            row = row ^ bit
        else:
            col = col ^ bit
    return row, col


def slot_of(row_change, col_change, rounds):
    slot = 0
    for step, (axis, distance) in enumerate(rounds[:-1]):
        change = row_change if axis == "row" else col_change
        slot = slot | (((change // distance) & 1) << step)
    return slot


def sigmoid(values):
    return 0.5 + 0.5 * jnp.tanh(0.5 * values)


def matmul(left, right):
    return jnp.dot(left, right, preferred_element_type=jnp.float32)


def matmul_nt(left, right):
    return lax.dot_general(
        left, right, (((1,), (1,)), ((), ())), preferred_element_type=jnp.float32
    )


def project_half(
    plan, core, pairs, w_proj, w_gate, left, right, swapped, gating, contact, start, turned
):
    rounds, _, height, breadth, tokens = plan
    channels, hidden = w_gate.shape[0], w_gate.shape[1]
    col_count, chips = tokens // breadth, tokens // height // 2
    row_place, col_place = lax.axis_index("row"), lax.axis_index("col")
    lane = lax.broadcasted_iota(jnp.int32, (height, breadth, channels), 2)
    place = lax.broadcasted_iota(jnp.int32, (height, breadth, channels), 0)
    own_lane = jnp.where((lane % height == place) & (lane < 2 * height), 1.0, 0.0)
    pick_lane = lax.broadcasted_iota(jnp.int32, (channels, 2 * channels), 0)
    pick_half = lax.broadcasted_iota(jnp.int32, (channels, 2 * channels), 1) // channels
    pick = jnp.where(pick_lane // height == pick_half, 1.0, 0.0).astype(jnp.bfloat16)
    pixels = height * breadth
    rows = 8
    for first in range(0, height, rows):
        values, masks = [], []
        for chip in range(chips):
            row_change = (chip * 2 + core) ^ row_place
            blocks, marks = [], []
            for col in range(col_count):
                col_change = col_place ^ col
                slot = slot_of(row_change, col_change, rounds)
                blocks.append(
                    pairs[slot, first * breadth : (first + rows) * breadth, :]
                    .astype(jnp.float32)
                    .reshape(rows, breadth, channels)
                )
                mark = pairs[slot, pixels:, :].astype(jnp.float32)[:breadth]
                marks.append(mark[None] * own_lane[first : first + rows])
            values.append(jnp.concatenate(blocks, axis=1).reshape(rows * tokens, channels))
            masks.append(jnp.concatenate(marks, axis=1).reshape(rows * tokens, channels))
        values = jnp.concatenate(values, axis=0)
        masks = matmul(jnp.concatenate(masks, axis=0).astype(jnp.bfloat16), pick)
        normed = layer_norm(values)
        gates = sigmoid(matmul(normed.astype(jnp.bfloat16), w_gate[...]))
        masked = (normed * masks[:, :channels]).astype(jnp.bfloat16)
        projected = matmul(masked, w_proj[...])
        sides = [
            sigmoid(projected[:, (2 * side + 1) * hidden : (2 * side + 2) * hidden])
            * projected[:, 2 * side * hidden : (2 * side + 1) * hidden]
            for side in range(2)
        ]
        for side, target in zip(sides, turned):
            side = side.reshape(chips, rows, tokens, hidden)
            for row in range(rows):
                strip = jnp.concatenate([side[chip, row] for chip in range(chips)], axis=0)
                target[pl.ds(first + row, hidden, stride=height + PITCH), :] = strip.T
        shape = (chips, rows, tokens, channels)
        span = slice(first, first + rows)
        gating[:, span] = gates.astype(jnp.bfloat16).reshape(shape)
        contact[:, span] = masks[:, channels:].astype(jnp.bfloat16).reshape(shape)
        start[:, span] = values.astype(jnp.bfloat16).reshape(shape)
    shape = (hidden, height + PITCH, chips * tokens)
    mine, other = turned[0][...], turned[1][...]
    for target, source in (
        (left, mine),
        (right, other),
        (swapped, pltpu.roll(other, tokens, 1)),
    ):
        target[...] = source.reshape(shape)[:, :height].astype(jnp.bfloat16)


def near_kernel(
    plan,
    near,
    w_proj,
    w_gate,
    two,
    left,
    right,
    swapped,
    gating,
    contact,
    start,
    two_t,
    turned_left,
    turned_right,
):
    core = lax.axis_index("row") % 2
    channels = two.shape[1]
    for tap in range(9):
        two_t[tap * channels : (tap + 1) * channels] = two[tap].T
    project_half(
        plan,
        core,
        near,
        w_proj,
        w_gate,
        left,
        right,
        swapped,
        gating,
        contact,
        start,
        (turned_left, turned_right),
    )


def spread(source, rows, pad, rate, target):
    tokens, channels = target.shape[1], source.shape[2]
    for tap in range(3):
        first = DMAX + (tap - 1) * rate if tap != 1 else DMAX
        moved = source[pl.ds(pad + rows.start, rows.size), pl.ds(first, tokens), :]
        target[pl.ds(DMAX + rows.start, rows.size), :, tap * channels : (tap + 1) * channels] = (
            moved.astype(jnp.bfloat16)
        )


def taps(source, first, count, rate):
    tokens = source.shape[1]
    views = [
        source[pl.ds(DMAX + first + (tap - 1) * rate, count)].reshape(count * tokens, -1)
        for tap in range(3)
    ]
    return jnp.concatenate(views, axis=1)


def windows(source, rate, row_start, col_start, height, breadth):
    views = [
        source[
            pl.ds(row_start + DMAX + (tap // 3 - 1) * rate, height),
            pl.ds(col_start + DMAX + (tap % 3 - 1) * rate, breadth),
            :,
        ].reshape(height * breadth, -1)
        for tap in range(9)
    ]
    return jnp.concatenate(views, axis=1).astype(jnp.bfloat16)


def row_taps(strips, first, count, rate):
    views = [
        strips[tap, pl.ds(DMAX + first + ((tap - 1) * rate if tap != 1 else 0), count)]
        for tap in range(3)
    ]
    return views[0] + views[1] + views[2]


def clear_ends(strips, tokens):
    for tap in (0, 2):
        for rows in (slice(0, DMAX), slice(DMAX + tokens, 2 * DMAX + tokens)):
            strips[tap, rows] = jnp.zeros((DMAX,) + strips.shape[2:], jnp.float32)


def column_taps(source, weight, first, count, strips):
    tokens = source.shape[1]
    flat = source[pl.ds(DMAX + first, count)].reshape(count * tokens, -1)
    square = jnp.concatenate(
        [
            jnp.concatenate([weight(3 * row + col) for row in range(3)], axis=1)
            for col in range(3)
        ],
        axis=0,
    )
    result = matmul(flat, square)
    channels = strips.shape[3]
    for tap in range(3):
        strips[tap, pl.ds(DMAX + first, count)] = result[
            :, tap * channels : (tap + 1) * channels
        ].reshape(count, tokens, channels)


def lanes(step, size):
    return pl.ds(pl.multiple_of(step * size, size), size)


def clear_border(target, tokens):
    line, channels = target.shape[1], target.shape[2]
    border = jnp.zeros((DMAX, line, channels), target.dtype)
    rim = jnp.zeros((tokens, DMAX, channels), target.dtype)
    if target.shape[0] > tokens:
        target[0:DMAX] = border
        target[DMAX + tokens :] = border
    if line > tokens:
        rows = slice(target.shape[0] - tokens - DMAX, target.shape[0] - DMAX)
        if target.shape[0] == tokens:
            rows = slice(0, tokens)
        target[rows, 0:DMAX, :] = rim
        target[rows, DMAX + tokens :, :] = rim


def forward_kernel(
    plan,
    dilations,
    far,
    w_proj,
    w_gate,
    w_out,
    one,
    two,
    near_left,
    near_right,
    near_swapped,
    near_gating,
    near_contact,
    near_start,
    output,
    flipped,
    flipped_two,
    factor,
    mine,
    own_contact,
    far_left,
    right,
    swapped,
    far_gating,
    far_contact,
    far_start,
    turned_left,
    turned_right,
    products,
    normed,
    updated,
    field,
    wide,
    second,
    strips,
):
    _, _, height, breadth, tokens = plan
    hidden, channels = w_out.shape
    pixels = height * breadth
    chips = tokens // height // 2
    row_place, col_place = lax.axis_index("row"), lax.axis_index("col")
    core = row_place % 2
    rate_one, rate_two = dilations[0], dilations[1]
    inside = slice(DMAX, DMAX + tokens)
    for target in (field, second):
        clear_border(target, tokens)
    clear_ends(strips, tokens)

    right[core] = near_right[...]
    swapped[core] = near_swapped[...]
    project_half(
        plan,
        1 - core,
        far,
        w_proj,
        w_gate,
        far_left,
        right.at[1 - core],
        swapped.at[1 - core],
        far_gating,
        far_contact,
        far_start,
        (turned_left, turned_right),
    )

    lane = lax.broadcasted_iota(jnp.int32, (height, chips * tokens), 1)
    low = jnp.where(lane < tokens, 1.0, 0.0).astype(jnp.bfloat16)
    high = jnp.where(lane < tokens, 0.0, 1.0).astype(jnp.bfloat16)
    batch = 32
    pitch = 2 * height + PITCH

    def multiply(step, carry):
        for part in range(batch):
            h = step * batch + part
            ahead = [right[0, h], right[1, h]]
            back = [swapped[0, h], swapped[1, h]]
            strips = [strip * low for strip in ahead + back]
            strips += [strip * high for strip in back + ahead]
            mine = jnp.concatenate([near_left[h], far_left[h]], axis=0)
            products[pl.ds(pl.multiple_of(h * pitch, 8), 2 * height), :] = matmul_nt(
                mine, jnp.concatenate(strips, axis=0)
            )
        return carry

    lax.fori_loop(0, hidden // batch, multiply, 0)

    chunk = 8
    size = chunk * tokens

    halves = (
        (core, near_gating, near_contact, near_start),
        (1 - core, far_gating, far_contact, far_start),
    )
    parts = height // chunk

    def normalise(step):
        half, first = step // parts, step % parts * chunk
        for row in range(chunk):
            strip = products[pl.ds(half * height + first + row, hidden, stride=pitch), :]
            strip = layer_norm(strip, axis=0).astype(jnp.bfloat16).T
            for chip in range(chips):
                normed[step, chip, row] = strip[chip * tokens : (chip + 1) * tokens]

    def update(step):
        first = step % parts * chunk
        side, gating, contact, start = halves[step // parts]
        change = matmul(normed[step].reshape(chips * size, hidden), w_out[...])
        change = change.reshape(chips, chunk, tokens, channels)
        rows = pl.ds(first, chunk)
        fresh = start[:, rows].astype(jnp.float32) + gating[:, rows].astype(jnp.float32) * change
        fresh = fresh.astype(jnp.bfloat16).astype(jnp.float32)
        first_in = layer_norm(fresh) * contact[:, rows].astype(jnp.float32)
        for chip in range(chips):
            base = (chip * 2 + side) * height + first
            rows = pl.ds(base, chunk)
            updated[rows] = fresh[chip]
            field[rows, inside, :] = first_in[chip]
            spread(field, rows, 0, rate_one, wide)
            flipped[:, pl.ds(pl.multiple_of(base * tokens, size), size)] = (
                first_in[chip].reshape(size, channels).astype(jnp.bfloat16).T
            )

    def first_conv(step):
        side = halves[step // parts][0]
        for chip in range(chips):
            base = (chip * 2 + side) * height + step % parts * chunk
            column_taps(wide, lambda tap: one[tap], base, chunk, strips)

    count = 2 * parts
    for step in range(count + 2):
        if step < count:
            normalise(step)
        if 1 <= step <= count:
            update(step - 1)
        if step >= 2:
            first_conv(step - 2)

    def activate(step, carry):
        rows = pl.ds(step * chunk, chunk)
        pre = row_taps(strips, step * chunk, chunk, rate_one)
        sigma = sigmoid(pre)
        second_in = pre * sigma
        second[pl.ds(DMAX + step * chunk, chunk), inside, :] = second_in
        flipped_two[:, lanes(step, size)] = (
            second_in.reshape(size, channels).astype(jnp.bfloat16).T
        )
        factor[rows] = sigma * (1.0 + pre * (1.0 - sigma))
        return carry

    lax.fori_loop(0, tokens // chunk, activate, 0)

    row_start, col_start = row_place * height, col_place * breadth
    cols = pl.ds(pl.multiple_of(col_start, breadth), breadth)
    fresh = updated[pl.ds(row_start, height), cols, :].reshape(pixels, channels)
    mine[...] = fresh
    second_pre = matmul(
        windows(second, rate_two, row_start, col_start, height, breadth),
        two[...].reshape(9 * channels, channels),
    )
    output[...] = (fresh + second_pre).astype(jnp.bfloat16)
    marks = near_contact[row_place // 2].astype(jnp.float32)
    place_col = lax.broadcasted_iota(jnp.int32, (tokens, channels), 0) // breadth
    marks = jnp.where((place_col == col_place)[None], marks, 0.0)
    marks = marks.reshape(height, tokens // breadth, breadth, channels)
    own_contact[...] = jnp.sum(marks, axis=1).reshape(pixels, channels)


def backward_kernel(
    plan,
    dilations,
    cot_near,
    cot_far,
    one,
    two_t,
    flipped,
    flipped_two,
    factor,
    mine,
    own_contact,
    grad_pair,
    grad_one,
    grad_two,
    field,
    wide_cot,
    wide_pre,
    grad_pre,
    strips,
    sum_one,
    sum_two,
):
    _, cot_rounds, height, breadth, tokens = plan
    channels = one.shape[2]
    pixels = height * breadth
    row_place, col_place = lax.axis_index("row"), lax.axis_index("col")
    rate_one, rate_two = dilations[0], dilations[1]
    half = cot_far.shape[0]
    inside = slice(DMAX, DMAX + tokens)
    for target in (field, wide_cot, wide_pre, grad_pre):
        clear_border(target, tokens)
    clear_ends(strips, tokens)

    several = 4

    def place_cot(source, base):
        def body(step, carry):
            for i in range(several):
                slot = step * several + i
                row, col = place_of(base + slot, cot_rounds, row_place, col_place)
                cols = pl.ds(pl.multiple_of(DMAX + col * breadth, breadth), breadth)
                field[pl.ds(row * height, height), cols, :] = (
                    source[slot]
                    .astype(jnp.float32)
                    .reshape(height, breadth, channels)
                )
            return carry

        lax.fori_loop(0, half // several, body, 0)

    place_cot(cot_near, 0)
    place_cot(cot_far, half)

    chunk = 8
    size = chunk * tokens
    steps = tokens // chunk

    def spread_cot(step):
        spread(field, pl.ds(step * chunk, chunk), 0, -rate_two, wide_cot)

    def hidden_conv(step):
        column_taps(
            wide_cot,
            lambda tap: two_t[tap * channels : (tap + 1) * channels],
            step * chunk,
            chunk,
            strips,
        )

    def prepare(step, carry):
        hidden_conv(step - 1)
        spread_cot(step)
        return carry

    spread_cot(0)
    lax.fori_loop(1, steps, prepare, 0)
    hidden_conv(steps - 1)

    sum_two[...] = jnp.zeros_like(sum_two)

    def back_two(step, carry):
        first = step * chunk
        before = row_taps(strips, first, chunk, -rate_two) * factor[pl.ds(first, chunk)]
        grad_pre[pl.ds(DMAX + first, chunk), inside, :] = before.astype(jnp.bfloat16).astype(
            jnp.float32
        )
        spread(grad_pre, pl.ds(first, chunk), DMAX, -rate_one, wide_pre)
        sum_two[...] += matmul(
            flipped_two[:, lanes(step, size)], taps(wide_cot, first, chunk, -rate_two)
        )
        return carry

    lax.fori_loop(0, steps, back_two, 0)

    sum_one[...] = jnp.zeros_like(sum_one)

    def back_one(step, carry):
        sum_one[...] += matmul(
            flipped[:, lanes(step, size)], taps(wide_pre, step * chunk, chunk, -rate_one)
        )
        return carry

    lax.fori_loop(0, steps, back_one, 0)
    for tap in range(9):
        columns = slice(tap * channels, (tap + 1) * channels)
        grad_one[tap] = sum_one[:, columns] * (1.0 / tokens)
        grad_two[tap] = sum_two[:, columns] * (1.0 / tokens)

    one_rows = [one[tap] for tap in range(9)]
    grad_input = own_contact[...] * matmul_nt(
        windows(
            grad_pre, -rate_one, row_place * height, col_place * breadth, height, breadth
        ),
        jnp.concatenate(one_rows, axis=1),
    )
    centre = mine[...] - jnp.mean(mine[...], axis=-1, keepdims=True)
    inv_spread = lax.rsqrt(jnp.mean(centre * centre, axis=-1, keepdims=True) + EPSILON)
    scaled = centre * inv_spread
    grad_norm = inv_spread * (
        grad_input
        - jnp.mean(grad_input, axis=-1, keepdims=True)
        - scaled * jnp.mean(grad_input * scaled, axis=-1, keepdims=True)
    )
    grad_pair[...] = (cot_near[0].astype(jnp.float32) + grad_norm).astype(jnp.bfloat16)


def replicated(
    pair, pair_mask, contact_mask, dilations, w_proj, w_gate, w_out, conv_one, conv_two, cotangent
):
    height, breadth, channels = pair.shape
    hidden = w_out.shape[0]
    row_count, col_count = lax.axis_size("row"), lax.axis_size("col")
    tokens = height * row_count
    pixels = height * breadth
    rounds, cot_rounds = exchange_plan(row_count, col_count)
    f32, bf16 = jnp.float32, jnp.bfloat16
    plan = (rounds, cot_rounds, height, breadth, tokens)
    chips = row_count // 2
    line = tokens + 2 * DMAX
    in_vmem = pl.BlockSpec(memory_space=pltpu.VMEM)
    side = ((hidden, height, chips * tokens), bf16)
    rows = (chips, height, tokens, channels)
    halves = [side] * 3 + [(rows, bf16)] * 3
    turned = pltpu.VMEM((hidden * (height + PITCH), chips * tokens), f32)
    stat = ((pixels, channels), f32)

    def shapes(*entries):
        return [jax.ShapeDtypeStruct(shape, dtype) for shape, dtype in entries]

    in_smem = pl.BlockSpec(memory_space=pltpu.SMEM)
    spare = channels - 2 * height
    marks = jnp.pad(pair_mask.T, ((0, breadth), (0, height + spare))) + jnp.pad(
        contact_mask.T, ((0, breadth), (height, spare))
    )
    held = jnp.concatenate([pair.reshape(pixels, channels), marks.astype(bf16)], axis=0)[None]
    cot_held = jnp.maximum(cotangent.reshape(1, pixels, channels), jnp.finfo(bf16).min)
    rates = jnp.clip(dilations, 1, DMAX)
    cot_held, rates = lax.optimization_barrier((cot_held, rates))
    for step, (hop, cot_hop) in enumerate(zip(rounds[:-1], cot_rounds[:-1])):
        held = jnp.concatenate([held, exchange(held, hop)], axis=0)
        cot_other = exchange(cot_held, cot_hop)
        if step < len(rounds) - 2:
            cot_held = jnp.concatenate([cot_held, cot_other], axis=0)
    near, far = held, exchange(held, rounds[-1])
    *near_parts, two_t = pl.pallas_call(
        functools.partial(near_kernel, plan),
        in_specs=[in_vmem] * 4,
        out_specs=[in_vmem] * 7,
        out_shape=shapes(*halves, ((9 * channels, channels), bf16)),
        scratch_shapes=[turned] * 2,
        compiler_params=pltpu.CompilerParams(vmem_limit_bytes=VMEM_LIMIT // 3),
        cost_estimate=pl.CostEstimate(
            flops=tokens * tokens * channels * 5 * hidden,
            bytes_accessed=8 * tokens * tokens * channels,
            transcendentals=3 * tokens * tokens * channels // 2,
        ),
    )(near, w_proj, w_gate, conv_two)
    cot_other, two_t = lax.optimization_barrier((cot_other, two_t))
    cot_near = jnp.concatenate([cot_held, cot_other], axis=0)
    cot_far = exchange(cot_near, cot_rounds[-1])
    whole = pltpu.VMEM((tokens, tokens, channels), f32)
    padded = pltpu.VMEM((tokens, line, channels), f32)
    bordered = pltpu.VMEM((line, line, channels), f32)
    tripled = pltpu.VMEM((line, tokens, 3 * channels), bf16)
    both = pltpu.VMEM((2,) + side[0], bf16)
    alone = pltpu.VMEM(rows, bf16)
    banded = pltpu.VMEM((3, line, tokens, channels), f32)
    flat = ((channels, tokens * tokens), bf16)
    sums = pltpu.VMEM((channels, 9 * channels), f32)
    output, *held = pl.pallas_call(
        functools.partial(forward_kernel, plan),
        in_specs=[in_smem] + [in_vmem] * 12,
        out_specs=[in_vmem] * 6,
        out_shape=shapes(
            ((pixels, channels), bf16),
            flat,
            flat,
            ((tokens, tokens, channels), f32),
            stat,
            stat,
        ),
        scratch_shapes=[pltpu.VMEM(*side), both, both, alone, alone, alone]
        + [turned] * 2
        + [pltpu.VMEM((hidden * (2 * height + PITCH), chips * tokens), f32)]
        + [pltpu.VMEM((2 * height // 8, chips, 8, tokens, hidden), bf16)]
        + [whole, padded, tripled, bordered, banded],
        compiler_params=pltpu.CompilerParams(vmem_limit_bytes=FORWARD_VMEM),
        cost_estimate=pl.CostEstimate(
            flops=tokens * tokens * channels * 40 * hidden,
            bytes_accessed=40 * tokens * tokens * channels,
            transcendentals=4 * tokens * tokens * channels,
        ),
    )(
        rates,
        far,
        w_proj,
        w_gate,
        w_out,
        conv_one,
        conv_two,
        *near_parts,
    )
    grad_pair, grad_one, grad_two = pl.pallas_call(
        functools.partial(backward_kernel, plan),
        in_specs=[in_smem] + [in_vmem] * 9,
        out_specs=[in_vmem] * 3,
        out_shape=shapes(
            ((pixels, channels), bf16),
            ((9, channels, channels), f32),
            ((9, channels, channels), f32),
        ),
        scratch_shapes=[padded, tripled, tripled, bordered, banded, sums, sums],
        compiler_params=pltpu.CompilerParams(vmem_limit_bytes=BACKWARD_VMEM),
    )(
        rates,
        cot_near,
        cot_far,
        conv_one,
        two_t,
        *held,
    )
    block = (height, breadth, channels)
    return output.reshape(block), grad_pair.reshape(block), grad_one, grad_two


def fits(pair, w_out, row_count, col_count):
    height, breadth, channels = pair.shape
    tokens = height * row_count
    powers = all(count & (count - 1) == 0 for count in (row_count, col_count))
    whole = (tokens + 2 * DMAX) ** 2 * channels
    return (
        powers
        and row_count * col_count >= 8
        and height * breadth == channels == w_out.shape[0]
        and breadth == 8
        and row_count // 2 * tokens == channels
        and whole * 60 <= VMEM_LIMIT
    )


def local(*arguments):
    pair, w_out = arguments[0], arguments[6]
    if fits(pair, w_out, lax.axis_size("row"), lax.axis_size("col")):
        return replicated(*arguments)
    return sharded(*arguments)


def solution(mesh):
    in_specs = (
        P("row", "col", None),
        P("row", "col"),
        P("row", "col"),
        P(),
        P(),
        P(),
        P(),
        P(),
        P(),
        P("row", "col", None),
    )
    out_specs = (P("row", "col", None), P("row", "col", None), P(), P())
    return jax.shard_map(local, mesh=mesh, in_specs=in_specs, out_specs=out_specs, check_vma=False)
```

```python
import functools

import jax
import jax.numpy as jnp
from jax import lax
from jax.experimental import pallas as pl
from jax.experimental.pallas import tpu as pltpu
from jax.sharding import PartitionSpec as P

DMAX = 8
VMEM_LIMIT = 48 * 1024 * 1024
PITCH = 8
FORWARD_VMEM = 44 * 1024 * 1024
BACKWARD_VMEM = 28 * 1024 * 1024


EPSILON = 1e-05


def with_halo(block, sides, width):
    for axis, dim in sides:
        count = lax.axis_size(axis)
        forward = [(i, i + 1) for i in range(count - 1)]
        backward = [(target, source) for source, target in forward]
        low = lax.ppermute(
            lax.slice_in_dim(block, block.shape[dim] - width, None, axis=dim), axis, forward
        )
        high = lax.ppermute(lax.slice_in_dim(block, 0, width, axis=dim), axis, backward)
        block = jnp.concatenate([low, block, high], axis=dim)
    return block


def broadcast(x, axis, root):
    mine = lax.axis_index(axis) == root
    return lax.psum(jnp.where(mine, x, jnp.zeros_like(x)), axis)


def layer_norm(values, axis=-1):
    centre = values - jnp.mean(values, axis=axis, keepdims=True)
    spread = jnp.mean(centre * centre, axis=axis, keepdims=True)
    return centre * lax.rsqrt(spread + EPSILON)


def with_rim(field):
    return with_halo(field, (("row", 0), ("col", 1)), DMAX)


def gather_taps(padded, dilation, mirrored, height, breadth):
    windows = []
    for tap_index in range(9):
        row_tap = tap_index // 3
        col_tap = tap_index % 3
        if mirrored:
            row_tap = 2 - row_tap
            col_tap = 2 - col_tap
        row_start = DMAX + (row_tap - 1) * dilation
        col_start = DMAX + (col_tap - 1) * dilation
        windows.append(
            lax.dynamic_slice(
                padded, (row_start, col_start, jnp.int32(0)), (height, breadth, padded.shape[2])
            )
        )
    return jnp.concatenate(windows, axis=2).reshape(height * breadth, -1)


def sharded(
    pair, pair_mask, contact_mask, dilations, w_proj, w_gate, w_out, conv_one, conv_two, cotangent
):
    height, breadth, channels = pair.shape
    hidden = w_out.shape[0]
    row_count = lax.axis_size("row")
    col_count = lax.axis_size("col")
    ratio = col_count // row_count
    row_place = lax.axis_index("row")
    col_place = lax.axis_index("col")
    tokens = breadth * col_count
    pixels = height * breadth
    pair_flat = pair.astype(jnp.float32).reshape(pixels, channels)
    normed = layer_norm(pair_flat).astype(jnp.bfloat16)
    projected = jnp.dot(normed, w_proj, preferred_element_type=jnp.float32)
    mask_col = pair_mask.reshape(pixels, 1).astype(jnp.float32)
    left_side = (
        (mask_col * jax.nn.sigmoid(projected[:, hidden : 2 * hidden]) * projected[:, :hidden])
        .astype(jnp.bfloat16)
        .reshape(height, breadth, hidden)
    )
    right_side = (
        (
            mask_col
            * jax.nn.sigmoid(projected[:, 3 * hidden :])
            * projected[:, 2 * hidden : 3 * hidden]
        )
        .astype(jnp.bfloat16)
        .reshape(height, breadth, hidden)
    )
    right_all = lax.all_gather(right_side, "col", axis=1, tiled=True)
    offset = jnp.clip(col_place * breadth - row_place * height, 0, height - breadth)
    right_local = lax.dynamic_slice_in_dim(right_all, offset, breadth, 0)
    right_rows = broadcast(right_local, "row", col_place // ratio)
    products = jnp.einsum(
        "ikh,jkh->ijh",
        lax.all_gather(left_side, "col", axis=1, tiled=True),
        right_rows,
        preferred_element_type=jnp.float32,
    )
    product_norm = layer_norm(products.reshape(pixels, hidden)).astype(jnp.bfloat16)
    gating = jax.nn.sigmoid(jnp.dot(normed, w_gate, preferred_element_type=jnp.float32))
    updated = (
        pair_flat + gating * jnp.dot(product_norm, w_out, preferred_element_type=jnp.float32)
    ).astype(jnp.bfloat16)
    updated_f = updated.astype(jnp.float32)
    centre = updated_f - jnp.mean(updated_f, axis=-1, keepdims=True)
    inv_spread = lax.rsqrt(jnp.mean(centre * centre, axis=-1, keepdims=True) + EPSILON)
    scaled = centre * inv_spread
    contact = contact_mask.reshape(pixels, 1).astype(jnp.float32)
    first_in = (scaled * contact).astype(jnp.bfloat16).reshape(height, breadth, channels)
    rate_one = dilations[0]
    rate_two = dilations[1]
    first_taps = gather_taps(with_rim(first_in), rate_one, False, height, breadth)
    first_pre = jnp.dot(
        first_taps, conv_one.reshape(9 * channels, channels), preferred_element_type=jnp.float32
    )
    sigma = jax.nn.sigmoid(first_pre)
    second_in = (first_pre * sigma).astype(jnp.bfloat16).reshape(height, breadth, channels)
    second_taps = gather_taps(with_rim(second_in), rate_two, False, height, breadth)
    second_pre = jnp.dot(
        second_taps, conv_two.reshape(9 * channels, channels), preferred_element_type=jnp.float32
    )
    output = (updated_f + second_pre).astype(jnp.bfloat16).reshape(height, breadth, channels)
    cot_flat = cotangent.reshape(pixels, channels)
    grad_two = (
        lax.dot_general(
            second_taps, cot_flat, (((0,), (0,)), ((), ())), preferred_element_type=jnp.float32
        ).reshape(9, channels, channels)
        / tokens
    )
    cot_taps = gather_taps(with_rim(cotangent), rate_two, True, height, breadth)
    grad_hidden = jnp.dot(
        cot_taps,
        conv_two.transpose(0, 2, 1).reshape(9 * channels, channels),
        preferred_element_type=jnp.float32,
    )
    grad_pre = (grad_hidden * sigma * (1.0 + first_pre * (1.0 - sigma))).astype(jnp.bfloat16)
    grad_one = (
        lax.dot_general(
            first_taps, grad_pre, (((0,), (0,)), ((), ())), preferred_element_type=jnp.float32
        ).reshape(9, channels, channels)
        / tokens
    )
    grad_taps = gather_taps(
        with_rim(grad_pre.reshape(height, breadth, channels)), rate_one, True, height, breadth
    )
    grad_input = (
        jnp.dot(
            grad_taps,
            conv_one.transpose(0, 2, 1).reshape(9 * channels, channels),
            preferred_element_type=jnp.float32,
        )
        * contact
    )
    grad_norm = inv_spread * (
        grad_input
        - jnp.mean(grad_input, axis=-1, keepdims=True)
        - scaled * jnp.mean(grad_input * scaled, axis=-1, keepdims=True)
    )
    grad_pair = (
        (cot_flat.astype(jnp.float32) + grad_norm)
        .astype(jnp.bfloat16)
        .reshape(height, breadth, channels)
    )
    grad_one, grad_two = lax.psum((grad_one, grad_two), ("row", "col"))
    return (output, grad_pair, grad_one, grad_two)


def halvings(axis, count):
    return [(axis, count >> step) for step in range(1, count.bit_length())]


def exchange_plan(row_count, col_count):
    rows, cols = halvings("row", row_count), halvings("col", col_count)
    return cols + rows, cols[:-1] + rows[:-1] + cols[-1:] + rows[-1:]


def exchange(held, hop):
    axis, distance = hop
    return lax.ppermute(held, axis, [(i, i ^ distance) for i in range(lax.axis_size(axis))])


def place_of(position, rounds, row_place, col_place):
    row, col = row_place, col_place
    for step, (axis, distance) in enumerate(rounds):
        bit = ((position >> step) & 1) * distance
        if axis == "row":
            row = row ^ bit
        else:
            col = col ^ bit
    return row, col


def slot_of(row_change, col_change, rounds):
    slot = 0
    for step, (axis, distance) in enumerate(rounds[:-1]):
        change = row_change if axis == "row" else col_change
        slot = slot | (((change // distance) & 1) << step)
    return slot


def sigmoid(values):
    return 0.5 + 0.5 * jnp.tanh(0.5 * values)


def matmul(left, right):
    return jnp.dot(left, right, preferred_element_type=jnp.float32)


def matmul_nt(left, right):
    return lax.dot_general(
        left, right, (((1,), (1,)), ((), ())), preferred_element_type=jnp.float32
    )


def project_half(
    plan, core, pairs, w_proj, w_gate, left, right, swapped, gating, contact, start, turned
):
    rounds, _, height, breadth, tokens = plan
    channels, hidden = w_gate.shape[0], w_gate.shape[1]
    col_count, chips = tokens // breadth, tokens // height // 2
    row_place, col_place = lax.axis_index("row"), lax.axis_index("col")
    lane = lax.broadcasted_iota(jnp.int32, (height, breadth, channels), 2)
    place = lax.broadcasted_iota(jnp.int32, (height, breadth, channels), 0)
    own_lane = jnp.where((lane % height == place) & (lane < 2 * height), 1.0, 0.0)
    pick_lane = lax.broadcasted_iota(jnp.int32, (channels, 2 * channels), 0)
    pick_half = lax.broadcasted_iota(jnp.int32, (channels, 2 * channels), 1) // channels
    pick = jnp.where(pick_lane // height == pick_half, 1.0, 0.0).astype(jnp.bfloat16)
    pixels = height * breadth
    rows = 8
    for first in range(0, height, rows):
        values, masks = [], []
        for chip in range(chips):
            row_change = (chip * 2 + core) ^ row_place
            blocks, marks = [], []
            for col in range(col_count):
                col_change = col_place ^ col
                slot = slot_of(row_change, col_change, rounds)
                blocks.append(
                    pairs[slot, first * breadth : (first + rows) * breadth, :]
                    .astype(jnp.float32)
                    .reshape(rows, breadth, channels)
                )
                mark = pairs[slot, pixels:, :].astype(jnp.float32)[:breadth]
                marks.append(mark[None] * own_lane[first : first + rows])
            values.append(jnp.concatenate(blocks, axis=1).reshape(rows * tokens, channels))
            masks.append(jnp.concatenate(marks, axis=1).reshape(rows * tokens, channels))
        values = jnp.concatenate(values, axis=0)
        masks = matmul(jnp.concatenate(masks, axis=0).astype(jnp.bfloat16), pick)
        normed = layer_norm(values)
        gates = sigmoid(matmul(normed.astype(jnp.bfloat16), w_gate[...]))
        masked = (normed * masks[:, :channels]).astype(jnp.bfloat16)
        projected = matmul(masked, w_proj[...])
        sides = [
            sigmoid(projected[:, (2 * side + 1) * hidden : (2 * side + 2) * hidden])
            * projected[:, 2 * side * hidden : (2 * side + 1) * hidden]
            for side in range(2)
        ]
        for side, target in zip(sides, turned):
            side = side.reshape(chips, rows, tokens, hidden)
            for row in range(rows):
                strip = jnp.concatenate([side[chip, row] for chip in range(chips)], axis=0)
                target[pl.ds(first + row, hidden, stride=height + PITCH), :] = strip.T
        shape = (chips, rows, tokens, channels)
        span = slice(first, first + rows)
        gating[:, span] = gates.astype(jnp.bfloat16).reshape(shape)
        contact[:, span] = masks[:, channels:].astype(jnp.bfloat16).reshape(shape)
        start[:, span] = values.astype(jnp.bfloat16).reshape(shape)
    shape = (hidden, height + PITCH, chips * tokens)
    mine, other = turned[0][...], turned[1][...]
    for target, source in (
        (left, mine),
        (right, other),
        (swapped, pltpu.roll(other, tokens, 1)),
    ):
        target[...] = source.reshape(shape)[:, :height].astype(jnp.bfloat16)


def near_kernel(
    plan,
    near,
    w_proj,
    w_gate,
    two,
    left,
    right,
    swapped,
    gating,
    contact,
    start,
    two_t,
    turned_left,
    turned_right,
):
    core = lax.axis_index("row") % 2
    channels = two.shape[1]
    for tap in range(9):
        two_t[tap * channels : (tap + 1) * channels] = two[tap].T
    project_half(
        plan,
        core,
        near,
        w_proj,
        w_gate,
        left,
        right,
        swapped,
        gating,
        contact,
        start,
        (turned_left, turned_right),
    )


def spread(source, rows, pad, rate, target):
    tokens, channels = target.shape[1], source.shape[2]
    for tap in range(3):
        first = DMAX + (tap - 1) * rate if tap != 1 else DMAX
        moved = source[pl.ds(pad + rows.start, rows.size), pl.ds(first, tokens), :]
        target[pl.ds(DMAX + rows.start, rows.size), :, tap * channels : (tap + 1) * channels] = (
            moved.astype(jnp.bfloat16)
        )


def taps(source, first, count, rate):
    tokens = source.shape[1]
    views = [
        source[pl.ds(DMAX + first + (tap - 1) * rate, count)].reshape(count * tokens, -1)
        for tap in range(3)
    ]
    return jnp.concatenate(views, axis=1)


def windows(source, rate, row_start, col_start, height, breadth):
    views = [
        source[
            pl.ds(row_start + DMAX + (tap // 3 - 1) * rate, height),
            pl.ds(col_start + DMAX + (tap % 3 - 1) * rate, breadth),
            :,
        ].reshape(height * breadth, -1)
        for tap in range(9)
    ]
    return jnp.concatenate(views, axis=1).astype(jnp.bfloat16)


def row_taps(strips, first, count, rate):
    views = [
        strips[tap, pl.ds(DMAX + first + ((tap - 1) * rate if tap != 1 else 0), count)]
        for tap in range(3)
    ]
    return views[0] + views[1] + views[2]


def clear_ends(strips, tokens):
    for tap in (0, 2):
        for rows in (slice(0, DMAX), slice(DMAX + tokens, 2 * DMAX + tokens)):
            strips[tap, rows] = jnp.zeros((DMAX,) + strips.shape[2:], jnp.float32)


def column_taps(source, weight, first, count, strips):
    tokens = source.shape[1]
    flat = source[pl.ds(DMAX + first, count)].reshape(count * tokens, -1)
    square = jnp.concatenate(
        [
            jnp.concatenate([weight(3 * row + col) for row in range(3)], axis=1)
            for col in range(3)
        ],
        axis=0,
    )
    result = matmul(flat, square)
    channels = strips.shape[3]
    for tap in range(3):
        strips[tap, pl.ds(DMAX + first, count)] = result[
            :, tap * channels : (tap + 1) * channels
        ].reshape(count, tokens, channels)


def lanes(step, size):
    return pl.ds(pl.multiple_of(step * size, size), size)


def clear_border(target, tokens):
    line, channels = target.shape[1], target.shape[2]
    border = jnp.zeros((DMAX, line, channels), target.dtype)
    rim = jnp.zeros((tokens, DMAX, channels), target.dtype)
    if target.shape[0] > tokens:
        target[0:DMAX] = border
        target[DMAX + tokens :] = border
    if line > tokens:
        rows = slice(target.shape[0] - tokens - DMAX, target.shape[0] - DMAX)
        if target.shape[0] == tokens:
            rows = slice(0, tokens)
        target[rows, 0:DMAX, :] = rim
        target[rows, DMAX + tokens :, :] = rim


def forward_kernel(
    plan,
    dilations,
    far,
    w_proj,
    w_gate,
    w_out,
    one,
    two,
    near_left,
    near_right,
    near_swapped,
    near_gating,
    near_contact,
    near_start,
    output,
    flipped,
    flipped_two,
    factor,
    mine,
    own_contact,
    far_left,
    right,
    swapped,
    far_gating,
    far_contact,
    far_start,
    turned_left,
    turned_right,
    products,
    normed,
    updated,
    field,
    wide,
    second,
    strips,
):
    _, _, height, breadth, tokens = plan
    hidden, channels = w_out.shape
    pixels = height * breadth
    chips = tokens // height // 2
    row_place, col_place = lax.axis_index("row"), lax.axis_index("col")
    core = row_place % 2
    rate_one, rate_two = dilations[0], dilations[1]
    inside = slice(DMAX, DMAX + tokens)
    for target in (field, second):
        clear_border(target, tokens)
    clear_ends(strips, tokens)

    right[core] = near_right[...]
    swapped[core] = near_swapped[...]
    project_half(
        plan,
        1 - core,
        far,
        w_proj,
        w_gate,
        far_left,
        right.at[1 - core],
        swapped.at[1 - core],
        far_gating,
        far_contact,
        far_start,
        (turned_left, turned_right),
    )

    lane = lax.broadcasted_iota(jnp.int32, (height, chips * tokens), 1)
    low = jnp.where(lane < tokens, 1.0, 0.0).astype(jnp.bfloat16)
    high = jnp.where(lane < tokens, 0.0, 1.0).astype(jnp.bfloat16)
    batch = 32
    pitch = 2 * height + PITCH

    def multiply(step, carry):
        for part in range(batch):
            h = step * batch + part
            ahead = [right[0, h], right[1, h]]
            back = [swapped[0, h], swapped[1, h]]
            strips = [strip * low for strip in ahead + back]
            strips += [strip * high for strip in back + ahead]
            mine = jnp.concatenate([near_left[h], far_left[h]], axis=0)
            products[pl.ds(pl.multiple_of(h * pitch, 8), 2 * height), :] = matmul_nt(
                mine, jnp.concatenate(strips, axis=0)
            )
        return carry

    lax.fori_loop(0, hidden // batch, multiply, 0)

    chunk = 8
    size = chunk * tokens

    halves = (
        (core, near_gating, near_contact, near_start),
        (1 - core, far_gating, far_contact, far_start),
    )
    parts = height // chunk

    def normalise(step):
        half, first = step // parts, step % parts * chunk
        for row in range(chunk):
            strip = products[pl.ds(half * height + first + row, hidden, stride=pitch), :]
            strip = layer_norm(strip, axis=0).astype(jnp.bfloat16).T
            for chip in range(chips):
                normed[step, chip, row] = strip[chip * tokens : (chip + 1) * tokens]

    def update(step):
        first = step % parts * chunk
        side, gating, contact, start = halves[step // parts]
        change = matmul(normed[step].reshape(chips * size, hidden), w_out[...])
        change = change.reshape(chips, chunk, tokens, channels)
        rows = pl.ds(first, chunk)
        fresh = start[:, rows].astype(jnp.float32) + gating[:, rows].astype(jnp.float32) * change
        fresh = fresh.astype(jnp.bfloat16).astype(jnp.float32)
        first_in = layer_norm(fresh) * contact[:, rows].astype(jnp.float32)
        for chip in range(chips):
            base = (chip * 2 + side) * height + first
            rows = pl.ds(base, chunk)
            updated[rows] = fresh[chip]
            field[rows, inside, :] = first_in[chip]
            spread(field, rows, 0, rate_one, wide)
            flipped[:, pl.ds(pl.multiple_of(base * tokens, size), size)] = (
                first_in[chip].reshape(size, channels).astype(jnp.bfloat16).T
            )

    def first_conv(step):
        side = halves[step // parts][0]
        for chip in range(chips):
            base = (chip * 2 + side) * height + step % parts * chunk
            column_taps(wide, lambda tap: one[tap], base, chunk, strips)

    count = 2 * parts
    for step in range(count + 2):
        if step < count:
            normalise(step)
        if 1 <= step <= count:
            update(step - 1)
        if step >= 2:
            first_conv(step - 2)

    def activate(step, carry):
        rows = pl.ds(step * chunk, chunk)
        pre = row_taps(strips, step * chunk, chunk, rate_one)
        sigma = sigmoid(pre)
        second_in = pre * sigma
        second[pl.ds(DMAX + step * chunk, chunk), inside, :] = second_in
        flipped_two[:, lanes(step, size)] = (
            second_in.reshape(size, channels).astype(jnp.bfloat16).T
        )
        factor[rows] = sigma * (1.0 + pre * (1.0 - sigma))
        return carry

    lax.fori_loop(0, tokens // chunk, activate, 0)

    row_start, col_start = row_place * height, col_place * breadth
    cols = pl.ds(pl.multiple_of(col_start, breadth), breadth)
    fresh = updated[pl.ds(row_start, height), cols, :].reshape(pixels, channels)
    mine[...] = fresh
    second_pre = matmul(
        windows(second, rate_two, row_start, col_start, height, breadth),
        two[...].reshape(9 * channels, channels),
    )
    output[...] = (fresh + second_pre).astype(jnp.bfloat16)
    marks = near_contact[row_place // 2].astype(jnp.float32)
    place_col = lax.broadcasted_iota(jnp.int32, (tokens, channels), 0) // breadth
    marks = jnp.where((place_col == col_place)[None], marks, 0.0)
    marks = marks.reshape(height, tokens // breadth, breadth, channels)
    own_contact[...] = jnp.sum(marks, axis=1).reshape(pixels, channels)


def backward_kernel(
    plan,
    dilations,
    cot_near,
    cot_far,
    one,
    two_t,
    flipped,
    flipped_two,
    factor,
    mine,
    own_contact,
    grad_pair,
    grad_one,
    grad_two,
    field,
    wide_cot,
    wide_pre,
    grad_pre,
    sum_one,
    sum_two,
):
    _, cot_rounds, height, breadth, tokens = plan
    channels = one.shape[2]
    pixels = height * breadth
    row_place, col_place = lax.axis_index("row"), lax.axis_index("col")
    rate_one, rate_two = dilations[0], dilations[1]
    half = cot_far.shape[0]
    inside = slice(DMAX, DMAX + tokens)
    for target in (field, wide_cot, wide_pre, grad_pre):
        clear_border(target, tokens)

    several = 4

    def place_cot(source, base):
        def body(step, carry):
            for i in range(several):
                slot = step * several + i
                row, col = place_of(base + slot, cot_rounds, row_place, col_place)
                cols = pl.ds(pl.multiple_of(DMAX + col * breadth, breadth), breadth)
                field[pl.ds(row * height, height), cols, :] = (
                    source[slot]
                    .astype(jnp.float32)
                    .reshape(height, breadth, channels)
                )
            return carry

        lax.fori_loop(0, half // several, body, 0)

    place_cot(cot_near, 0)
    place_cot(cot_far, half)

    chunk = 8
    size = chunk * tokens
    steps = tokens // chunk

    def spread_cot(step, carry):
        spread(field, pl.ds(step * chunk, chunk), 0, -rate_two, wide_cot)
        return carry

    lax.fori_loop(0, steps, spread_cot, 0)

    sum_two[...] = jnp.zeros_like(sum_two)

    sum_one[...] = jnp.zeros_like(sum_one)

    def back_two(step):
        first = step * chunk
        shifted = taps(wide_cot, first, chunk, -rate_two)
        before = matmul(shifted, two_t[...]).reshape(chunk, tokens, channels)
        before = (before * factor[pl.ds(first, chunk)]).astype(jnp.bfloat16).astype(jnp.float32)
        grad_pre[pl.ds(DMAX + first, chunk), inside, :] = before
        sum_two[...] += matmul(flipped_two[:, lanes(step, size)], shifted)

    def spread_pre(step):
        spread(grad_pre, pl.ds(step * chunk, chunk), DMAX, -rate_one, wide_pre)

    def back_one(step):
        sum_one[...] += matmul(
            flipped[:, lanes(step, size)], taps(wide_pre, step * chunk, chunk, -rate_one)
        )

    def gradients(step, carry):
        back_one(step - 3)
        spread_pre(step - 1)
        back_two(step)
        return carry

    back_two(0)
    for step in (1, 2):
        spread_pre(step - 1)
        back_two(step)
    lax.fori_loop(3, steps, gradients, 0)
    spread_pre(steps - 1)
    lax.fori_loop(steps - 3, steps, lambda i, c: (back_one(i), c)[1], 0)
    for tap in range(9):
        columns = slice(tap * channels, (tap + 1) * channels)
        grad_one[tap] = sum_one[:, columns] * (1.0 / tokens)
        grad_two[tap] = sum_two[:, columns] * (1.0 / tokens)

    one_rows = [one[tap] for tap in range(9)]
    grad_input = own_contact[...] * matmul_nt(
        windows(
            grad_pre, -rate_one, row_place * height, col_place * breadth, height, breadth
        ),
        jnp.concatenate(one_rows, axis=1),
    )
    centre = mine[...] - jnp.mean(mine[...], axis=-1, keepdims=True)
    inv_spread = lax.rsqrt(jnp.mean(centre * centre, axis=-1, keepdims=True) + EPSILON)
    scaled = centre * inv_spread
    grad_norm = inv_spread * (
        grad_input
        - jnp.mean(grad_input, axis=-1, keepdims=True)
        - scaled * jnp.mean(grad_input * scaled, axis=-1, keepdims=True)
    )
    grad_pair[...] = (cot_near[0].astype(jnp.float32) + grad_norm).astype(jnp.bfloat16)


def replicated(
    pair, pair_mask, contact_mask, dilations, w_proj, w_gate, w_out, conv_one, conv_two, cotangent
):
    height, breadth, channels = pair.shape
    hidden = w_out.shape[0]
    row_count, col_count = lax.axis_size("row"), lax.axis_size("col")
    tokens = height * row_count
    pixels = height * breadth
    rounds, cot_rounds = exchange_plan(row_count, col_count)
    f32, bf16 = jnp.float32, jnp.bfloat16
    plan = (rounds, cot_rounds, height, breadth, tokens)
    chips = row_count // 2
    line = tokens + 2 * DMAX
    in_vmem = pl.BlockSpec(memory_space=pltpu.VMEM)
    side = ((hidden, height, chips * tokens), bf16)
    rows = (chips, height, tokens, channels)
    halves = [side] * 3 + [(rows, bf16)] * 3
    turned = pltpu.VMEM((hidden * (height + PITCH), chips * tokens), f32)
    stat = ((pixels, channels), f32)

    def shapes(*entries):
        return [jax.ShapeDtypeStruct(shape, dtype) for shape, dtype in entries]

    in_smem = pl.BlockSpec(memory_space=pltpu.SMEM)
    spare = channels - 2 * height
    marks = jnp.pad(pair_mask.T, ((pixels, breadth), (0, height + spare))) + jnp.pad(
        contact_mask.T, ((pixels, breadth), (height, spare))
    )
    block = pair.reshape(1, pixels, channels)
    mine = lax.optimization_barrier(jnp.maximum(block, jnp.finfo(bf16).min))
    above = jnp.pad(cotangent.reshape(pixels, channels), ((0, 2 * breadth), (0, 0)))
    cot_held = (above.astype(f32) + marks.astype(f32)).astype(bf16)[None]
    shared = len(halvings("col", col_count)) - 1

    def join(*parts, axis=0):
        return lax.optimization_barrier(jnp.concatenate(parts, axis=axis))

    held = join(mine, exchange(block, rounds[0]))
    cot_held = join(cot_held, exchange(cot_held, cot_rounds[0]))
    for hop in rounds[1:shared]:
        held = join(held, exchange(held, hop))
        cot_held = join(cot_held, exchange(cot_held, hop))
    held = join(held, cot_held[:, pixels:], axis=1)
    cot_held = cot_held[:, :pixels]
    rates = jnp.clip(dilations, 1, DMAX)
    for step in range(shared, len(rounds) - 1):
        other = exchange(held, rounds[step])
        cot_other = exchange(cot_held, cot_rounds[step])
        held = join(held, other)
        if step < len(rounds) - 2:
            cot_held, rates = lax.optimization_barrier(
                (jnp.concatenate([cot_held, cot_other], axis=0), rates)
            )
    near, far = held, exchange(held, rounds[-1])
    *near_parts, two_t = pl.pallas_call(
        functools.partial(near_kernel, plan),
        in_specs=[in_vmem] * 4,
        out_specs=[in_vmem] * 7,
        out_shape=shapes(*halves, ((9 * channels, channels), bf16)),
        scratch_shapes=[turned] * 2,
        compiler_params=pltpu.CompilerParams(vmem_limit_bytes=VMEM_LIMIT // 3),
        cost_estimate=pl.CostEstimate(
            flops=tokens * tokens * channels * 5 * hidden,
            bytes_accessed=8 * tokens * tokens * channels,
            transcendentals=3 * tokens * tokens * channels // 2,
        ),
    )(near, w_proj, w_gate, conv_two)
    cot_other, two_t = lax.optimization_barrier((cot_other, two_t))
    cot_near = jnp.concatenate([cot_held, cot_other], axis=0)
    cot_far = exchange(cot_near, cot_rounds[-1])
    whole = pltpu.VMEM((tokens, tokens, channels), f32)
    padded = pltpu.VMEM((tokens, line, channels), f32)
    bordered = pltpu.VMEM((line, line, channels), f32)
    tripled = pltpu.VMEM((line, tokens, 3 * channels), bf16)
    both = pltpu.VMEM((2,) + side[0], bf16)
    alone = pltpu.VMEM(rows, bf16)
    banded = pltpu.VMEM((3, line, tokens, channels), f32)
    flat = ((channels, tokens * tokens), bf16)
    sums = pltpu.VMEM((channels, 9 * channels), f32)
    output, *held = pl.pallas_call(
        functools.partial(forward_kernel, plan),
        in_specs=[in_smem] + [in_vmem] * 12,
        out_specs=[in_vmem] * 6,
        out_shape=shapes(
            ((pixels, channels), bf16),
            flat,
            flat,
            ((tokens, tokens, channels), f32),
            stat,
            stat,
        ),
        scratch_shapes=[pltpu.VMEM(*side), both, both, alone, alone, alone]
        + [turned] * 2
        + [pltpu.VMEM((hidden * (2 * height + PITCH), chips * tokens), f32)]
        + [pltpu.VMEM((2 * height // 8, chips, 8, tokens, hidden), bf16)]
        + [whole, padded, tripled, bordered, banded],
        compiler_params=pltpu.CompilerParams(vmem_limit_bytes=FORWARD_VMEM),
        cost_estimate=pl.CostEstimate(
            flops=tokens * tokens * channels * 40 * hidden,
            bytes_accessed=40 * tokens * tokens * channels,
            transcendentals=4 * tokens * tokens * channels,
        ),
    )(
        rates,
        far,
        w_proj,
        w_gate,
        w_out,
        conv_one,
        conv_two,
        *near_parts,
    )
    grad_pair, grad_one, grad_two = pl.pallas_call(
        functools.partial(backward_kernel, plan),
        in_specs=[in_smem] + [in_vmem] * 9,
        out_specs=[in_vmem] * 3,
        out_shape=shapes(
            ((pixels, channels), bf16),
            ((9, channels, channels), f32),
            ((9, channels, channels), f32),
        ),
        scratch_shapes=[padded, tripled, tripled, bordered, sums, sums],
        compiler_params=pltpu.CompilerParams(vmem_limit_bytes=BACKWARD_VMEM),
    )(
        rates,
        cot_near,
        cot_far,
        conv_one,
        two_t,
        *held,
    )
    block = (height, breadth, channels)
    return output.reshape(block), grad_pair.reshape(block), grad_one, grad_two


def fits(pair, w_out, row_count, col_count):
    height, breadth, channels = pair.shape
    tokens = height * row_count
    powers = all(count & (count - 1) == 0 for count in (row_count, col_count))
    whole = (tokens + 2 * DMAX) ** 2 * channels
    return (
        powers
        and row_count * col_count >= 8
        and height * breadth == channels == w_out.shape[0]
        and breadth == 8
        and row_count // 2 * tokens == channels
        and whole * 60 <= VMEM_LIMIT
    )


def local(*arguments):
    pair, w_out = arguments[0], arguments[6]
    if fits(pair, w_out, lax.axis_size("row"), lax.axis_size("col")):
        return replicated(*arguments)
    return sharded(*arguments)


def solution(mesh):
    in_specs = (
        P("row", "col", None),
        P("row", "col"),
        P("row", "col"),
        P(),
        P(),
        P(),
        P(),
        P(),
        P(),
        P("row", "col", None),
    )
    out_specs = (P("row", "col", None), P("row", "col", None), P(), P())
    return jax.shard_map(local, mesh=mesh, in_specs=in_specs, out_specs=out_specs, check_vma=False)
```

```python
import functools

import jax
import jax.numpy as jnp
from jax import lax
from jax.experimental import pallas as pl
from jax.experimental.pallas import tpu as pltpu
from jax.sharding import PartitionSpec as P

DMAX = 8
VMEM_LIMIT = 48 * 1024 * 1024
PITCH = 8
FORWARD_VMEM = 44 * 1024 * 1024
BACKWARD_VMEM = 36 * 1024 * 1024


EPSILON = 1e-05


def with_halo(block, sides, width):
    for axis, dim in sides:
        count = lax.axis_size(axis)
        forward = [(i, i + 1) for i in range(count - 1)]
        backward = [(target, source) for source, target in forward]
        low = lax.ppermute(
            lax.slice_in_dim(block, block.shape[dim] - width, None, axis=dim), axis, forward
        )
        high = lax.ppermute(lax.slice_in_dim(block, 0, width, axis=dim), axis, backward)
        block = jnp.concatenate([low, block, high], axis=dim)
    return block


def broadcast(x, axis, root):
    mine = lax.axis_index(axis) == root
    return lax.psum(jnp.where(mine, x, jnp.zeros_like(x)), axis)


def layer_norm(values, axis=-1):
    centre = values - jnp.mean(values, axis=axis, keepdims=True)
    spread = jnp.mean(centre * centre, axis=axis, keepdims=True)
    return centre * lax.rsqrt(spread + EPSILON)


def with_rim(field):
    return with_halo(field, (("row", 0), ("col", 1)), DMAX)


def gather_taps(padded, dilation, mirrored, height, breadth):
    windows = []
    for tap_index in range(9):
        row_tap = tap_index // 3
        col_tap = tap_index % 3
        if mirrored:
            row_tap = 2 - row_tap
            col_tap = 2 - col_tap
        row_start = DMAX + (row_tap - 1) * dilation
        col_start = DMAX + (col_tap - 1) * dilation
        windows.append(
            lax.dynamic_slice(
                padded, (row_start, col_start, jnp.int32(0)), (height, breadth, padded.shape[2])
            )
        )
    return jnp.concatenate(windows, axis=2).reshape(height * breadth, -1)


def sharded(
    pair, pair_mask, contact_mask, dilations, w_proj, w_gate, w_out, conv_one, conv_two, cotangent
):
    height, breadth, channels = pair.shape
    hidden = w_out.shape[0]
    row_count = lax.axis_size("row")
    col_count = lax.axis_size("col")
    ratio = col_count // row_count
    row_place = lax.axis_index("row")
    col_place = lax.axis_index("col")
    tokens = breadth * col_count
    pixels = height * breadth
    pair_flat = pair.astype(jnp.float32).reshape(pixels, channels)
    normed = layer_norm(pair_flat).astype(jnp.bfloat16)
    projected = jnp.dot(normed, w_proj, preferred_element_type=jnp.float32)
    mask_col = pair_mask.reshape(pixels, 1).astype(jnp.float32)
    left_side = (
        (mask_col * jax.nn.sigmoid(projected[:, hidden : 2 * hidden]) * projected[:, :hidden])
        .astype(jnp.bfloat16)
        .reshape(height, breadth, hidden)
    )
    right_side = (
        (
            mask_col
            * jax.nn.sigmoid(projected[:, 3 * hidden :])
            * projected[:, 2 * hidden : 3 * hidden]
        )
        .astype(jnp.bfloat16)
        .reshape(height, breadth, hidden)
    )
    right_all = lax.all_gather(right_side, "col", axis=1, tiled=True)
    offset = jnp.clip(col_place * breadth - row_place * height, 0, height - breadth)
    right_local = lax.dynamic_slice_in_dim(right_all, offset, breadth, 0)
    right_rows = broadcast(right_local, "row", col_place // ratio)
    products = jnp.einsum(
        "ikh,jkh->ijh",
        lax.all_gather(left_side, "col", axis=1, tiled=True),
        right_rows,
        preferred_element_type=jnp.float32,
    )
    product_norm = layer_norm(products.reshape(pixels, hidden)).astype(jnp.bfloat16)
    gating = jax.nn.sigmoid(jnp.dot(normed, w_gate, preferred_element_type=jnp.float32))
    updated = (
        pair_flat + gating * jnp.dot(product_norm, w_out, preferred_element_type=jnp.float32)
    ).astype(jnp.bfloat16)
    updated_f = updated.astype(jnp.float32)
    centre = updated_f - jnp.mean(updated_f, axis=-1, keepdims=True)
    inv_spread = lax.rsqrt(jnp.mean(centre * centre, axis=-1, keepdims=True) + EPSILON)
    scaled = centre * inv_spread
    contact = contact_mask.reshape(pixels, 1).astype(jnp.float32)
    first_in = (scaled * contact).astype(jnp.bfloat16).reshape(height, breadth, channels)
    rate_one = dilations[0]
    rate_two = dilations[1]
    first_taps = gather_taps(with_rim(first_in), rate_one, False, height, breadth)
    first_pre = jnp.dot(
        first_taps, conv_one.reshape(9 * channels, channels), preferred_element_type=jnp.float32
    )
    sigma = jax.nn.sigmoid(first_pre)
    second_in = (first_pre * sigma).astype(jnp.bfloat16).reshape(height, breadth, channels)
    second_taps = gather_taps(with_rim(second_in), rate_two, False, height, breadth)
    second_pre = jnp.dot(
        second_taps, conv_two.reshape(9 * channels, channels), preferred_element_type=jnp.float32
    )
    output = (updated_f + second_pre).astype(jnp.bfloat16).reshape(height, breadth, channels)
    cot_flat = cotangent.reshape(pixels, channels)
    grad_two = (
        lax.dot_general(
            second_taps, cot_flat, (((0,), (0,)), ((), ())), preferred_element_type=jnp.float32
        ).reshape(9, channels, channels)
        / tokens
    )
    cot_taps = gather_taps(with_rim(cotangent), rate_two, True, height, breadth)
    grad_hidden = jnp.dot(
        cot_taps,
        conv_two.transpose(0, 2, 1).reshape(9 * channels, channels),
        preferred_element_type=jnp.float32,
    )
    grad_pre = (grad_hidden * sigma * (1.0 + first_pre * (1.0 - sigma))).astype(jnp.bfloat16)
    grad_one = (
        lax.dot_general(
            first_taps, grad_pre, (((0,), (0,)), ((), ())), preferred_element_type=jnp.float32
        ).reshape(9, channels, channels)
        / tokens
    )
    grad_taps = gather_taps(
        with_rim(grad_pre.reshape(height, breadth, channels)), rate_one, True, height, breadth
    )
    grad_input = (
        jnp.dot(
            grad_taps,
            conv_one.transpose(0, 2, 1).reshape(9 * channels, channels),
            preferred_element_type=jnp.float32,
        )
        * contact
    )
    grad_norm = inv_spread * (
        grad_input
        - jnp.mean(grad_input, axis=-1, keepdims=True)
        - scaled * jnp.mean(grad_input * scaled, axis=-1, keepdims=True)
    )
    grad_pair = (
        (cot_flat.astype(jnp.float32) + grad_norm)
        .astype(jnp.bfloat16)
        .reshape(height, breadth, channels)
    )
    grad_one, grad_two = lax.psum((grad_one, grad_two), ("row", "col"))
    return (output, grad_pair, grad_one, grad_two)


def halvings(axis, count):
    return [(axis, count >> step) for step in range(1, count.bit_length())]


def exchange_plan(row_count, col_count):
    rows, cols = halvings("row", row_count), halvings("col", col_count)
    return cols + rows, rows[:-1] + cols + rows[-1:]


def exchange(held, hop):
    axis, distance = hop
    return lax.ppermute(held, axis, [(i, i ^ distance) for i in range(lax.axis_size(axis))])


def place_of(position, rounds, row_place, col_place):
    row, col = row_place, col_place
    for step, (axis, distance) in enumerate(rounds):
        bit = ((position >> step) & 1) * distance
        if axis == "row":
            row = row ^ bit
        else:
            col = col ^ bit
    return row, col


def slot_of(row_change, col_change, rounds):
    slot = 0
    for step, (axis, distance) in enumerate(rounds[:-1]):
        change = row_change if axis == "row" else col_change
        slot = slot | (((change // distance) & 1) << step)
    return slot


def sigmoid(values):
    return 0.5 + 0.5 * jnp.tanh(0.5 * values)


def matmul(left, right):
    return jnp.dot(left, right, preferred_element_type=jnp.float32)


def matmul_nt(left, right):
    return lax.dot_general(
        left, right, (((1,), (1,)), ((), ())), preferred_element_type=jnp.float32
    )


def project_half(
    plan, core, pairs, w_proj, w_gate, left, right, swapped, gating, contact, start, turned
):
    rounds, _, height, breadth, tokens = plan
    channels, hidden = w_gate.shape[0], w_gate.shape[1]
    col_count, chips = tokens // breadth, tokens // height // 2
    row_place, col_place = lax.axis_index("row"), lax.axis_index("col")
    lane = lax.broadcasted_iota(jnp.int32, (height, breadth, channels), 2)
    place = lax.broadcasted_iota(jnp.int32, (height, breadth, channels), 0)
    own_lane = jnp.where((lane % height == place) & (lane < 2 * height), 1.0, 0.0)
    pick_lane = lax.broadcasted_iota(jnp.int32, (channels, 2 * channels), 0)
    pick_half = lax.broadcasted_iota(jnp.int32, (channels, 2 * channels), 1) // channels
    pick = jnp.where(pick_lane // height == pick_half, 1.0, 0.0).astype(jnp.bfloat16)
    pixels = height * breadth
    rows = 8
    for first in range(0, height, rows):
        values, masks = [], []
        for chip in range(chips):
            row_change = (chip * 2 + core) ^ row_place
            blocks, marks = [], []
            for col in range(col_count):
                col_change = col_place ^ col
                slot = slot_of(row_change, col_change, rounds)
                blocks.append(
                    pairs[slot, first * breadth : (first + rows) * breadth, :]
                    .astype(jnp.float32)
                    .reshape(rows, breadth, channels)
                )
                mark = pairs[slot, pixels:, :].astype(jnp.float32)[:breadth]
                marks.append(mark[None] * own_lane[first : first + rows])
            values.append(jnp.concatenate(blocks, axis=1).reshape(rows * tokens, channels))
            masks.append(jnp.concatenate(marks, axis=1).reshape(rows * tokens, channels))
        values = jnp.concatenate(values, axis=0)
        masks = matmul(jnp.concatenate(masks, axis=0).astype(jnp.bfloat16), pick)
        normed = layer_norm(values)
        gates = sigmoid(matmul(normed.astype(jnp.bfloat16), w_gate[...]))
        masked = (normed * masks[:, :channels]).astype(jnp.bfloat16)
        projected = matmul(masked, w_proj[...])
        sides = [
            sigmoid(projected[:, (2 * side + 1) * hidden : (2 * side + 2) * hidden])
            * projected[:, 2 * side * hidden : (2 * side + 1) * hidden]
            for side in range(2)
        ]
        for side, target in zip(sides, turned):
            side = side.reshape(chips, rows, tokens, hidden)
            for row in range(rows):
                strip = jnp.concatenate([side[chip, row] for chip in range(chips)], axis=0)
                target[pl.ds(first + row, hidden, stride=height + PITCH), :] = strip.T
        shape = (chips, rows, tokens, channels)
        span = slice(first, first + rows)
        gating[:, span] = gates.astype(jnp.bfloat16).reshape(shape)
        contact[:, span] = masks[:, channels:].astype(jnp.bfloat16).reshape(shape)
        start[:, span] = values.astype(jnp.bfloat16).reshape(shape)
    shape = (hidden, height + PITCH, chips * tokens)
    mine, other = turned[0][...], turned[1][...]
    for target, source in (
        (left, mine),
        (right, other),
        (swapped, pltpu.roll(other, tokens, 1)),
    ):
        target[...] = source.reshape(shape)[:, :height].astype(jnp.bfloat16)


def near_kernel(
    plan,
    near,
    w_proj,
    w_gate,
    two,
    left,
    right,
    swapped,
    gating,
    contact,
    start,
    two_t,
    turned_left,
    turned_right,
):
    core = lax.axis_index("row") % 2
    channels = two.shape[1]
    for tap in range(9):
        two_t[tap * channels : (tap + 1) * channels] = two[tap].T
    project_half(
        plan,
        core,
        near,
        w_proj,
        w_gate,
        left,
        right,
        swapped,
        gating,
        contact,
        start,
        (turned_left, turned_right),
    )


def spread(source, rows, pad, rate, target):
    tokens, channels = target.shape[1], source.shape[2]
    for tap in range(3):
        first = DMAX + (tap - 1) * rate if tap != 1 else DMAX
        moved = source[pl.ds(pad + rows.start, rows.size), pl.ds(first, tokens), :]
        target[pl.ds(DMAX + rows.start, rows.size), :, tap * channels : (tap + 1) * channels] = (
            moved.astype(jnp.bfloat16)
        )


def taps(source, first, count, rate):
    tokens = source.shape[1]
    views = [
        source[pl.ds(DMAX + first + (tap - 1) * rate, count)].reshape(count * tokens, -1)
        for tap in range(3)
    ]
    return jnp.concatenate(views, axis=1)


def windows(source, rate, row_start, col_start, height, breadth):
    views = [
        source[
            pl.ds(row_start + DMAX + (tap // 3 - 1) * rate, height),
            pl.ds(col_start + DMAX + (tap % 3 - 1) * rate, breadth),
            :,
        ].reshape(height * breadth, -1)
        for tap in range(9)
    ]
    return jnp.concatenate(views, axis=1).astype(jnp.bfloat16)


def row_taps(strips, first, count, rate):
    views = [
        strips[tap, pl.ds(DMAX + first + ((tap - 1) * rate if tap != 1 else 0), count)]
        for tap in range(3)
    ]
    return views[0] + views[1] + views[2]


def clear_ends(strips, tokens):
    for tap in (0, 2):
        for rows in (slice(0, DMAX), slice(DMAX + tokens, 2 * DMAX + tokens)):
            strips[tap, rows] = jnp.zeros((DMAX,) + strips.shape[2:], jnp.float32)


def column_taps(source, weight, first, count, strips):
    tokens = source.shape[1]
    flat = source[pl.ds(DMAX + first, count)].reshape(count * tokens, -1)
    square = jnp.concatenate(
        [
            jnp.concatenate([weight(3 * row + col) for row in range(3)], axis=1)
            for col in range(3)
        ],
        axis=0,
    )
    result = matmul(flat, square)
    channels = strips.shape[3]
    for tap in range(3):
        strips[tap, pl.ds(DMAX + first, count)] = result[
            :, tap * channels : (tap + 1) * channels
        ].reshape(count, tokens, channels)


def lanes(step, size):
    return pl.ds(pl.multiple_of(step * size, size), size)


def clear_border(target, tokens):
    line, channels = target.shape[1], target.shape[2]
    border = jnp.zeros((DMAX, line, channels), target.dtype)
    rim = jnp.zeros((tokens, DMAX, channels), target.dtype)
    if target.shape[0] > tokens:
        target[0:DMAX] = border
        target[DMAX + tokens :] = border
    if line > tokens:
        rows = slice(target.shape[0] - tokens - DMAX, target.shape[0] - DMAX)
        if target.shape[0] == tokens:
            rows = slice(0, tokens)
        target[rows, 0:DMAX, :] = rim
        target[rows, DMAX + tokens :, :] = rim


def forward_kernel(
    plan,
    dilations,
    far,
    w_proj,
    w_gate,
    w_out,
    one,
    two,
    near_left,
    near_right,
    near_swapped,
    near_gating,
    near_contact,
    near_start,
    output,
    flipped,
    flipped_two,
    factor,
    mine,
    own_contact,
    far_left,
    right,
    swapped,
    far_gating,
    far_contact,
    far_start,
    turned_left,
    turned_right,
    products,
    normed,
    updated,
    field,
    wide,
    second,
    strips,
):
    _, _, height, breadth, tokens = plan
    hidden, channels = w_out.shape
    pixels = height * breadth
    chips = tokens // height // 2
    row_place, col_place = lax.axis_index("row"), lax.axis_index("col")
    core = row_place % 2
    rate_one, rate_two = dilations[0], dilations[1]
    inside = slice(DMAX, DMAX + tokens)
    for target in (field, second):
        clear_border(target, tokens)
    clear_ends(strips, tokens)

    right[core] = near_right[...]
    swapped[core] = near_swapped[...]
    project_half(
        plan,
        1 - core,
        far,
        w_proj,
        w_gate,
        far_left,
        right.at[1 - core],
        swapped.at[1 - core],
        far_gating,
        far_contact,
        far_start,
        (turned_left, turned_right),
    )

    lane = lax.broadcasted_iota(jnp.int32, (height, chips * tokens), 1)
    low = jnp.where(lane < tokens, 1.0, 0.0).astype(jnp.bfloat16)
    high = jnp.where(lane < tokens, 0.0, 1.0).astype(jnp.bfloat16)
    batch = 64
    pitch = 2 * height + PITCH

    def multiply(step, carry):
        for part in range(batch):
            h = step * batch + part
            ahead = [right[0, h], right[1, h]]
            back = [swapped[0, h], swapped[1, h]]
            strips = [strip * low for strip in ahead + back]
            strips += [strip * high for strip in back + ahead]
            mine = jnp.concatenate([near_left[h], far_left[h]], axis=0)
            products[pl.ds(pl.multiple_of(h * pitch, 8), 2 * height), :] = matmul_nt(
                mine, jnp.concatenate(strips, axis=0)
            )
        return carry

    lax.fori_loop(0, hidden // batch, multiply, 0)

    chunk = 8
    size = chunk * tokens

    halves = (
        (core, near_gating, near_contact, near_start),
        (1 - core, far_gating, far_contact, far_start),
    )
    parts = height // chunk

    def normalise(step):
        half, first = step // parts, step % parts * chunk
        for row in range(chunk):
            strip = products[pl.ds(half * height + first + row, hidden, stride=pitch), :]
            strip = layer_norm(strip, axis=0).astype(jnp.bfloat16).T
            for chip in range(chips):
                normed[step, chip, row] = strip[chip * tokens : (chip + 1) * tokens]

    def update(step):
        first = step % parts * chunk
        side, gating, contact, start = halves[step // parts]
        change = matmul(normed[step].reshape(chips * size, hidden), w_out[...])
        change = change.reshape(chips, chunk, tokens, channels)
        rows = pl.ds(first, chunk)
        fresh = start[:, rows].astype(jnp.float32) + gating[:, rows].astype(jnp.float32) * change
        fresh = fresh.astype(jnp.bfloat16).astype(jnp.float32)
        first_in = layer_norm(fresh) * contact[:, rows].astype(jnp.float32)
        for chip in range(chips):
            base = (chip * 2 + side) * height + first
            rows = pl.ds(base, chunk)
            updated[rows] = fresh[chip]
            field[rows, inside, :] = first_in[chip]
            spread(field, rows, 0, rate_one, wide)
            flipped[:, pl.ds(pl.multiple_of(base * tokens, size), size)] = (
                first_in[chip].reshape(size, channels).astype(jnp.bfloat16).T
            )

    def first_conv(step):
        side = halves[step // parts][0]
        for chip in range(chips):
            base = (chip * 2 + side) * height + step % parts * chunk
            column_taps(wide, lambda tap: one[tap], base, chunk, strips)

    count = 2 * parts
    for step in range(count + 2):
        if step < count:
            normalise(step)
        if 1 <= step <= count:
            update(step - 1)
        if step >= 2:
            first_conv(step - 2)

    deep = 2 * chunk

    def activate(step, carry):
        rows = pl.ds(step * deep, deep)
        pre = row_taps(strips, step * deep, deep, rate_one)
        sigma = sigmoid(pre)
        second_in = pre * sigma
        second[pl.ds(DMAX + step * deep, deep), inside, :] = second_in
        flipped_two[:, lanes(step, deep * tokens)] = (
            second_in.reshape(deep * tokens, channels).astype(jnp.bfloat16).T
        )
        factor[rows] = sigma * (1.0 + pre * (1.0 - sigma))
        return carry

    lax.fori_loop(0, tokens // deep, activate, 0)

    row_start, col_start = row_place * height, col_place * breadth
    cols = pl.ds(pl.multiple_of(col_start, breadth), breadth)
    fresh = updated[pl.ds(row_start, height), cols, :].reshape(pixels, channels)
    mine[...] = fresh
    second_pre = matmul(
        windows(second, rate_two, row_start, col_start, height, breadth),
        two[...].reshape(9 * channels, channels),
    )
    output[...] = (fresh + second_pre).astype(jnp.bfloat16)
    marks = near_contact[row_place // 2].astype(jnp.float32)
    place_col = lax.broadcasted_iota(jnp.int32, (tokens, channels), 0) // breadth
    marks = jnp.where((place_col == col_place)[None], marks, 0.0)
    marks = marks.reshape(height, tokens // breadth, breadth, channels)
    own_contact[...] = jnp.sum(marks, axis=1).reshape(pixels, channels)


def backward_kernel(
    plan,
    dilations,
    cot_near,
    cot_far,
    one,
    two_t,
    flipped,
    flipped_two,
    factor,
    mine,
    own_contact,
    grad_pair,
    grad_one,
    grad_two,
    field,
    wide_cot,
    wide_pre,
    grad_pre,
    sum_one,
    sum_two,
    scaled_one,
    scaled_two,
    sent,
):
    _, cot_rounds, height, breadth, tokens = plan
    channels = one.shape[2]
    pixels = height * breadth
    row_place, col_place = lax.axis_index("row"), lax.axis_index("col")
    rate_one, rate_two = dilations[0], dilations[1]
    half = cot_far.shape[0]
    inside = slice(DMAX, DMAX + tokens)
    for target in (field, wide_cot, wide_pre, grad_pre):
        clear_border(target, tokens)

    several = 8

    def place_cot(source, base):
        def body(step, carry):
            for i in range(several):
                slot = step * several + i
                row, col = place_of(base + slot, cot_rounds, row_place, col_place)
                cols = pl.ds(pl.multiple_of(DMAX + col * breadth, breadth), breadth)
                field[pl.ds(row * height, height), cols, :] = (
                    source[slot].astype(jnp.float32).reshape(height, breadth, channels)
                )
            return carry

        lax.fori_loop(0, half // several, body, 0)

    place_cot(cot_near, 0)
    place_cot(cot_far, half)
    chunk = 16
    size = chunk * tokens
    steps = tokens // chunk

    def spread_cot(step, carry):
        spread(field, pl.ds(step * chunk, chunk), 0, -rate_two, wide_cot)
        return carry

    lax.fori_loop(0, steps, spread_cot, 0)

    def back_two(step):
        first = step * chunk
        shifted = taps(wide_cot, first, chunk, -rate_two)
        before = matmul(shifted, two_t[...]).reshape(chunk, tokens, channels)
        before = (before * factor[pl.ds(first, chunk)]).astype(jnp.bfloat16).astype(jnp.float32)
        grad_pre[pl.ds(DMAX + first, chunk), inside, :] = before
        part = matmul(flipped_two[:, step * size : (step + 1) * size], shifted)
        sum_two[...] = part if step == 0 else sum_two[...] + part

    def spread_pre(step):
        spread(grad_pre, pl.ds(step * chunk, chunk), DMAX, -rate_one, wide_pre)

    def back_one(step):
        shifted = taps(wide_pre, step * chunk, chunk, -rate_one)
        part = matmul(flipped[:, step * size : (step + 1) * size], shifted)
        sum_one[...] = part if step == 0 else sum_one[...] + part

    def finish(total, scaled, target, place):
        for tap in range(9):
            columns = slice(tap * channels, (tap + 1) * channels)
            scaled[tap] = total[:, columns] * (1.0 / tokens)
        copy = pltpu.make_async_copy(scaled, target, sent.at[place])
        copy.start()
        return copy

    for step in range(steps):
        if step >= 3:
            back_one(step - 3)
        if step >= 1:
            spread_pre(step - 1)
        back_two(step)
    copies = [finish(sum_two, scaled_two, grad_two, 1)]
    spread_pre(steps - 1)
    for step in range(max(steps - 3, 0), steps):
        back_one(step)
    copies.append(finish(sum_one, scaled_one, grad_one, 0))

    one_rows = [one[tap] for tap in range(9)]
    grad_input = own_contact[...] * matmul_nt(
        windows(
            grad_pre, -rate_one, row_place * height, col_place * breadth, height, breadth
        ),
        jnp.concatenate(one_rows, axis=1),
    )
    centre = mine[...] - jnp.mean(mine[...], axis=-1, keepdims=True)
    inv_spread = lax.rsqrt(jnp.mean(centre * centre, axis=-1, keepdims=True) + EPSILON)
    scaled = centre * inv_spread
    grad_norm = inv_spread * (
        grad_input
        - jnp.mean(grad_input, axis=-1, keepdims=True)
        - scaled * jnp.mean(grad_input * scaled, axis=-1, keepdims=True)
    )
    grad_pair[...] = (cot_near[0].astype(jnp.float32) + grad_norm).astype(jnp.bfloat16)
    for copy in copies:
        copy.wait()


def replicated(
    pair, pair_mask, contact_mask, dilations, w_proj, w_gate, w_out, conv_one, conv_two, cotangent
):
    height, breadth, channels = pair.shape
    hidden = w_out.shape[0]
    row_count, col_count = lax.axis_size("row"), lax.axis_size("col")
    tokens = height * row_count
    pixels = height * breadth
    rounds, cot_rounds = exchange_plan(row_count, col_count)
    f32, bf16 = jnp.float32, jnp.bfloat16
    plan = (rounds, cot_rounds, height, breadth, tokens)
    chips = row_count // 2
    line = tokens + 2 * DMAX
    in_vmem = pl.BlockSpec(memory_space=pltpu.VMEM)
    side = ((hidden, height, chips * tokens), bf16)
    rows = (chips, height, tokens, channels)
    halves = [side] * 3 + [(rows, bf16)] * 3
    turned = pltpu.VMEM((hidden * (height + PITCH), chips * tokens), f32)
    stat = ((pixels, channels), f32)

    def shapes(*entries):
        return [jax.ShapeDtypeStruct(shape, dtype) for shape, dtype in entries]

    in_smem = pl.BlockSpec(memory_space=pltpu.SMEM)
    spare = channels - 2 * height
    marks = jnp.pad(pair_mask.T, ((pixels, breadth), (0, height + spare))) + jnp.pad(
        contact_mask.T, ((pixels, breadth), (height, spare))
    )
    above = jnp.pad(pair.reshape(pixels, channels), ((0, 2 * breadth), (0, 0)))
    held = (above.astype(f32) + marks.astype(f32)).astype(bf16)[None]
    block = cotangent.reshape(1, pixels, channels)
    cot_held = lax.optimization_barrier(jnp.maximum(block, jnp.finfo(bf16).min))
    rates = jnp.clip(dilations, 1, DMAX)
    for step in range(len(rounds) - 1):
        other = exchange(held, rounds[step])
        cot_other = exchange(cot_held if step else block, cot_rounds[step])
        held = lax.optimization_barrier(jnp.concatenate([held, other], axis=0))
        if step < len(rounds) - 2:
            cot_held = jnp.concatenate([cot_held, cot_other], axis=0)
            if step == len(rounds) - 3:
                cot_held, rates = lax.optimization_barrier((cot_held, rates))
            else:
                cot_held = lax.optimization_barrier(cot_held)
    near, far = held, exchange(held, rounds[-1])
    *near_parts, two_t = pl.pallas_call(
        functools.partial(near_kernel, plan),
        in_specs=[in_vmem] * 4,
        out_specs=[in_vmem] * 7,
        out_shape=shapes(*halves, ((9 * channels, channels), bf16)),
        scratch_shapes=[turned] * 2,
        compiler_params=pltpu.CompilerParams(vmem_limit_bytes=VMEM_LIMIT // 3),
        cost_estimate=pl.CostEstimate(
            flops=tokens * tokens * channels * 5 * hidden,
            bytes_accessed=8 * tokens * tokens * channels,
            transcendentals=3 * tokens * tokens * channels // 2,
        ),
    )(near, w_proj, w_gate, conv_two)
    cot_other, two_t = lax.optimization_barrier((cot_other, two_t))
    cot_near = jnp.concatenate([cot_held, cot_other], axis=0)
    cot_far = exchange(cot_near, cot_rounds[-1])
    whole = pltpu.VMEM((tokens, tokens, channels), f32)
    padded = pltpu.VMEM((tokens, line, channels), f32)
    bordered = pltpu.VMEM((line, line, channels), f32)
    tripled = pltpu.VMEM((line, tokens, 3 * channels), bf16)
    both = pltpu.VMEM((2,) + side[0], bf16)
    alone = pltpu.VMEM(rows, bf16)
    banded = pltpu.VMEM((3, line, tokens, channels), f32)
    flat = ((channels, tokens * tokens), bf16)
    sums = pltpu.VMEM((channels, 9 * channels), f32)
    output, *held = pl.pallas_call(
        functools.partial(forward_kernel, plan),
        in_specs=[in_smem] + [in_vmem] * 12,
        out_specs=[in_vmem] * 6,
        out_shape=shapes(
            ((pixels, channels), bf16),
            flat,
            flat,
            ((tokens, tokens, channels), f32),
            stat,
            stat,
        ),
        scratch_shapes=[pltpu.VMEM(*side), both, both, alone, alone, alone]
        + [turned] * 2
        + [pltpu.VMEM((hidden * (2 * height + PITCH), chips * tokens), f32)]
        + [pltpu.VMEM((2 * height // 8, chips, 8, tokens, hidden), bf16)]
        + [whole, padded, tripled, bordered, banded],
        compiler_params=pltpu.CompilerParams(vmem_limit_bytes=FORWARD_VMEM),
        cost_estimate=pl.CostEstimate(
            flops=tokens * tokens * channels * 40 * hidden,
            bytes_accessed=40 * tokens * tokens * channels,
            transcendentals=4 * tokens * tokens * channels,
        ),
    )(
        rates,
        far,
        w_proj,
        w_gate,
        w_out,
        conv_one,
        conv_two,
        *near_parts,
    )
    grad_pair, grad_one, grad_two = pl.pallas_call(
        functools.partial(backward_kernel, plan),
        in_specs=[in_smem] + [in_vmem] * 9,
        out_specs=[in_vmem] + [pl.BlockSpec(memory_space=pltpu.HBM)] * 2,
        out_shape=shapes(
            ((pixels, channels), bf16),
            ((9, channels, channels), f32),
            ((9, channels, channels), f32),
        ),
        scratch_shapes=[padded, tripled, tripled, bordered, sums, sums]
        + [pltpu.VMEM((9, channels, channels), f32)] * 2
        + [pltpu.SemaphoreType.DMA((2,))],
        compiler_params=pltpu.CompilerParams(vmem_limit_bytes=BACKWARD_VMEM),
    )(
        rates,
        cot_near,
        cot_far,
        conv_one,
        two_t,
        *held,
    )
    block = (height, breadth, channels)
    return output.reshape(block), grad_pair.reshape(block), grad_one, grad_two


def fits(pair, w_out, row_count, col_count):
    height, breadth, channels = pair.shape
    tokens = height * row_count
    powers = all(count & (count - 1) == 0 for count in (row_count, col_count))
    whole = (tokens + 2 * DMAX) ** 2 * channels
    return (
        powers
        and row_count * col_count >= 8
        and height * breadth == channels == w_out.shape[0]
        and breadth == 8
        and row_count // 2 * tokens == channels
        and whole * 60 <= VMEM_LIMIT
    )


def local(*arguments):
    pair, w_out = arguments[0], arguments[6]
    if fits(pair, w_out, lax.axis_size("row"), lax.axis_size("col")):
        return replicated(*arguments)
    return sharded(*arguments)


def solution(mesh):
    in_specs = (
        P("row", "col", None),
        P("row", "col"),
        P("row", "col"),
        P(),
        P(),
        P(),
        P(),
        P(),
        P(),
        P("row", "col", None),
    )
    out_specs = (P("row", "col", None), P("row", "col", None), P(), P())
    return jax.shard_map(local, mesh=mesh, in_specs=in_specs, out_specs=out_specs, check_vma=False)
```

```python
import functools

import jax
import jax.numpy as jnp
from jax import lax
from jax.experimental import pallas as pl
from jax.experimental.pallas import tpu as pltpu
from jax.sharding import PartitionSpec as P

DMAX = 8
VMEM_LIMIT = 48 * 1024 * 1024
PITCH = 8
FORWARD_VMEM = 44 * 1024 * 1024
BACKWARD_VMEM = 36 * 1024 * 1024


EPSILON = 1e-05


def with_halo(block, sides, width):
    for axis, dim in sides:
        count = lax.axis_size(axis)
        forward = [(i, i + 1) for i in range(count - 1)]
        backward = [(target, source) for source, target in forward]
        low = lax.ppermute(
            lax.slice_in_dim(block, block.shape[dim] - width, None, axis=dim), axis, forward
        )
        high = lax.ppermute(lax.slice_in_dim(block, 0, width, axis=dim), axis, backward)
        block = jnp.concatenate([low, block, high], axis=dim)
    return block


def broadcast(x, axis, root):
    mine = lax.axis_index(axis) == root
    return lax.psum(jnp.where(mine, x, jnp.zeros_like(x)), axis)


def layer_norm(values, axis=-1):
    centre = values - jnp.mean(values, axis=axis, keepdims=True)
    spread = jnp.mean(centre * centre, axis=axis, keepdims=True)
    return centre * lax.rsqrt(spread + EPSILON)


def with_rim(field):
    return with_halo(field, (("row", 0), ("col", 1)), DMAX)


def gather_taps(padded, dilation, mirrored, height, breadth):
    windows = []
    for tap_index in range(9):
        row_tap = tap_index // 3
        col_tap = tap_index % 3
        if mirrored:
            row_tap = 2 - row_tap
            col_tap = 2 - col_tap
        row_start = DMAX + (row_tap - 1) * dilation
        col_start = DMAX + (col_tap - 1) * dilation
        windows.append(
            lax.dynamic_slice(
                padded, (row_start, col_start, jnp.int32(0)), (height, breadth, padded.shape[2])
            )
        )
    return jnp.concatenate(windows, axis=2).reshape(height * breadth, -1)


def sharded(
    pair, pair_mask, contact_mask, dilations, w_proj, w_gate, w_out, conv_one, conv_two, cotangent
):
    height, breadth, channels = pair.shape
    hidden = w_out.shape[0]
    row_count = lax.axis_size("row")
    col_count = lax.axis_size("col")
    ratio = col_count // row_count
    row_place = lax.axis_index("row")
    col_place = lax.axis_index("col")
    tokens = breadth * col_count
    pixels = height * breadth
    pair_flat = pair.astype(jnp.float32).reshape(pixels, channels)
    normed = layer_norm(pair_flat).astype(jnp.bfloat16)
    projected = jnp.dot(normed, w_proj, preferred_element_type=jnp.float32)
    mask_col = pair_mask.reshape(pixels, 1).astype(jnp.float32)
    left_side = (
        (mask_col * jax.nn.sigmoid(projected[:, hidden : 2 * hidden]) * projected[:, :hidden])
        .astype(jnp.bfloat16)
        .reshape(height, breadth, hidden)
    )
    right_side = (
        (
            mask_col
            * jax.nn.sigmoid(projected[:, 3 * hidden :])
            * projected[:, 2 * hidden : 3 * hidden]
        )
        .astype(jnp.bfloat16)
        .reshape(height, breadth, hidden)
    )
    right_all = lax.all_gather(right_side, "col", axis=1, tiled=True)
    offset = jnp.clip(col_place * breadth - row_place * height, 0, height - breadth)
    right_local = lax.dynamic_slice_in_dim(right_all, offset, breadth, 0)
    right_rows = broadcast(right_local, "row", col_place // ratio)
    products = jnp.einsum(
        "ikh,jkh->ijh",
        lax.all_gather(left_side, "col", axis=1, tiled=True),
        right_rows,
        preferred_element_type=jnp.float32,
    )
    product_norm = layer_norm(products.reshape(pixels, hidden)).astype(jnp.bfloat16)
    gating = jax.nn.sigmoid(jnp.dot(normed, w_gate, preferred_element_type=jnp.float32))
    updated = (
        pair_flat + gating * jnp.dot(product_norm, w_out, preferred_element_type=jnp.float32)
    ).astype(jnp.bfloat16)
    updated_f = updated.astype(jnp.float32)
    centre = updated_f - jnp.mean(updated_f, axis=-1, keepdims=True)
    inv_spread = lax.rsqrt(jnp.mean(centre * centre, axis=-1, keepdims=True) + EPSILON)
    scaled = centre * inv_spread
    contact = contact_mask.reshape(pixels, 1).astype(jnp.float32)
    first_in = (scaled * contact).astype(jnp.bfloat16).reshape(height, breadth, channels)
    rate_one = dilations[0]
    rate_two = dilations[1]
    first_taps = gather_taps(with_rim(first_in), rate_one, False, height, breadth)
    first_pre = jnp.dot(
        first_taps, conv_one.reshape(9 * channels, channels), preferred_element_type=jnp.float32
    )
    sigma = jax.nn.sigmoid(first_pre)
    second_in = (first_pre * sigma).astype(jnp.bfloat16).reshape(height, breadth, channels)
    second_taps = gather_taps(with_rim(second_in), rate_two, False, height, breadth)
    second_pre = jnp.dot(
        second_taps, conv_two.reshape(9 * channels, channels), preferred_element_type=jnp.float32
    )
    output = (updated_f + second_pre).astype(jnp.bfloat16).reshape(height, breadth, channels)
    cot_flat = cotangent.reshape(pixels, channels)
    grad_two = (
        lax.dot_general(
            second_taps, cot_flat, (((0,), (0,)), ((), ())), preferred_element_type=jnp.float32
        ).reshape(9, channels, channels)
        / tokens
    )
    cot_taps = gather_taps(with_rim(cotangent), rate_two, True, height, breadth)
    grad_hidden = jnp.dot(
        cot_taps,
        conv_two.transpose(0, 2, 1).reshape(9 * channels, channels),
        preferred_element_type=jnp.float32,
    )
    grad_pre = (grad_hidden * sigma * (1.0 + first_pre * (1.0 - sigma))).astype(jnp.bfloat16)
    grad_one = (
        lax.dot_general(
            first_taps, grad_pre, (((0,), (0,)), ((), ())), preferred_element_type=jnp.float32
        ).reshape(9, channels, channels)
        / tokens
    )
    grad_taps = gather_taps(
        with_rim(grad_pre.reshape(height, breadth, channels)), rate_one, True, height, breadth
    )
    grad_input = (
        jnp.dot(
            grad_taps,
            conv_one.transpose(0, 2, 1).reshape(9 * channels, channels),
            preferred_element_type=jnp.float32,
        )
        * contact
    )
    grad_norm = inv_spread * (
        grad_input
        - jnp.mean(grad_input, axis=-1, keepdims=True)
        - scaled * jnp.mean(grad_input * scaled, axis=-1, keepdims=True)
    )
    grad_pair = (
        (cot_flat.astype(jnp.float32) + grad_norm)
        .astype(jnp.bfloat16)
        .reshape(height, breadth, channels)
    )
    grad_one, grad_two = lax.psum((grad_one, grad_two), ("row", "col"))
    return (output, grad_pair, grad_one, grad_two)


def halvings(axis, count):
    return [(axis, count >> step) for step in range(1, count.bit_length())]


def exchange_plan(row_count, col_count):
    rows, cols = halvings("row", row_count), halvings("col", col_count)
    return cols + rows, rows[:-1] + cols + rows[-1:]


def exchange(held, hop):
    axis, distance = hop
    return lax.ppermute(held, axis, [(i, i ^ distance) for i in range(lax.axis_size(axis))])


def place_of(position, rounds, row_place, col_place):
    row, col = row_place, col_place
    for step, (axis, distance) in enumerate(rounds):
        bit = ((position >> step) & 1) * distance
        if axis == "row":
            row = row ^ bit
        else:
            col = col ^ bit
    return row, col


def slot_of(row_change, col, col_count, row_rounds):
    slot = col
    for step, (_, distance) in enumerate(row_rounds[:-1]):
        slot = slot + ((row_change // distance) & 1) * (col_count << step)
    return slot


def sigmoid(values):
    return 0.5 + 0.5 * jnp.tanh(0.5 * values)


def matmul(left, right):
    return jnp.dot(left, right, preferred_element_type=jnp.float32)


def matmul_nt(left, right):
    return lax.dot_general(
        left, right, (((1,), (1,)), ((), ())), preferred_element_type=jnp.float32
    )


def project_half(
    plan, core, pairs, w_proj, w_gate, left, right, swapped, gating, contact, start, turned
):
    rounds, _, height, breadth, tokens = plan
    channels, hidden = w_gate.shape[0], w_gate.shape[1]
    col_count, chips = tokens // breadth, tokens // height // 2
    row_place = lax.axis_index("row")
    lane = lax.broadcasted_iota(jnp.int32, (height, breadth, channels), 2)
    place = lax.broadcasted_iota(jnp.int32, (height, breadth, channels), 0)
    own_lane = jnp.where((lane % height == place) & (lane < 2 * height), 1.0, 0.0)
    pick_lane = lax.broadcasted_iota(jnp.int32, (channels, 2 * channels), 0)
    pick_half = lax.broadcasted_iota(jnp.int32, (channels, 2 * channels), 1) // channels
    pick = jnp.where(pick_lane // height == pick_half, 1.0, 0.0).astype(jnp.bfloat16)
    pixels = height * breadth
    rows = 8
    for first in range(0, height, rows):
        values, masks = [], []
        for chip in range(chips):
            row_change = (chip * 2 + core) ^ row_place
            blocks, marks = [], []
            for col in range(col_count):
                slot = slot_of(row_change, col, col_count, rounds)
                blocks.append(
                    pairs[slot, first * breadth : (first + rows) * breadth, :]
                    .astype(jnp.float32)
                    .reshape(rows, breadth, channels)
                )
                mark = pairs[slot, pixels:, :].astype(jnp.float32)[:breadth]
                marks.append(mark[None] * own_lane[first : first + rows])
            values.append(jnp.concatenate(blocks, axis=1).reshape(rows * tokens, channels))
            masks.append(jnp.concatenate(marks, axis=1).reshape(rows * tokens, channels))
        values = jnp.concatenate(values, axis=0)
        masks = matmul(jnp.concatenate(masks, axis=0).astype(jnp.bfloat16), pick)
        normed = layer_norm(values)
        gates = sigmoid(matmul(normed.astype(jnp.bfloat16), w_gate[...]))
        masked = (normed * masks[:, :channels]).astype(jnp.bfloat16)
        projected = matmul(masked, w_proj[...])
        sides = [
            sigmoid(projected[:, (2 * side + 1) * hidden : (2 * side + 2) * hidden])
            * projected[:, 2 * side * hidden : (2 * side + 1) * hidden]
            for side in range(2)
        ]
        for side, target in zip(sides, turned):
            side = side.reshape(chips, rows, tokens, hidden)
            for row in range(rows):
                strip = jnp.concatenate([side[chip, row] for chip in range(chips)], axis=0)
                target[pl.ds(first + row, hidden, stride=height + PITCH), :] = strip.T
        shape = (chips, rows, tokens, channels)
        span = slice(first, first + rows)
        gating[:, span] = gates.astype(jnp.bfloat16).reshape(shape)
        contact[:, span] = masks[:, channels:].astype(jnp.bfloat16).reshape(shape)
        start[:, span] = values.astype(jnp.bfloat16).reshape(shape)
    shape = (hidden, height + PITCH, chips * tokens)
    mine, other = turned[0][...], turned[1][...]
    for target, source in (
        (left, mine),
        (right, other),
        (swapped, pltpu.roll(other, tokens, 1)),
    ):
        target[...] = source.reshape(shape)[:, :height].astype(jnp.bfloat16)


def near_kernel(
    plan,
    near,
    w_proj,
    w_gate,
    two,
    left,
    right,
    swapped,
    gating,
    contact,
    start,
    two_t,
    turned_left,
    turned_right,
):
    core = lax.axis_index("row") % 2
    channels = two.shape[1]
    for tap in range(9):
        two_t[tap * channels : (tap + 1) * channels] = two[tap].T
    project_half(
        plan,
        core,
        near,
        w_proj,
        w_gate,
        left,
        right,
        swapped,
        gating,
        contact,
        start,
        (turned_left, turned_right),
    )


def spread(source, rows, pad, rate, target):
    tokens, channels = target.shape[1], source.shape[2]
    for tap in range(3):
        first = DMAX + (tap - 1) * rate if tap != 1 else DMAX
        moved = source[pl.ds(pad + rows.start, rows.size), pl.ds(first, tokens), :]
        target[pl.ds(DMAX + rows.start, rows.size), :, tap * channels : (tap + 1) * channels] = (
            moved.astype(jnp.bfloat16)
        )


def taps(source, first, count, rate):
    tokens = source.shape[1]
    views = [
        source[pl.ds(DMAX + first + (tap - 1) * rate, count)].reshape(count * tokens, -1)
        for tap in range(3)
    ]
    return jnp.concatenate(views, axis=1)


def windows(source, rate, row_start, col_start, height, breadth):
    views = [
        source[
            pl.ds(row_start + DMAX + (tap // 3 - 1) * rate, height),
            pl.ds(col_start + DMAX + (tap % 3 - 1) * rate, breadth),
            :,
        ].reshape(height * breadth, -1)
        for tap in range(9)
    ]
    return jnp.concatenate(views, axis=1).astype(jnp.bfloat16)


def row_taps(strips, first, count, rate):
    views = [
        strips[tap, pl.ds(DMAX + first + ((tap - 1) * rate if tap != 1 else 0), count)]
        for tap in range(3)
    ]
    return views[0] + views[1] + views[2]


def clear_ends(strips, tokens):
    for tap in (0, 2):
        for rows in (slice(0, DMAX), slice(DMAX + tokens, 2 * DMAX + tokens)):
            strips[tap, rows] = jnp.zeros((DMAX,) + strips.shape[2:], jnp.float32)


def column_taps(source, weight, first, count, strips):
    tokens = source.shape[1]
    flat = source[pl.ds(DMAX + first, count)].reshape(count * tokens, -1)
    square = jnp.concatenate(
        [
            jnp.concatenate([weight(3 * row + col) for row in range(3)], axis=1)
            for col in range(3)
        ],
        axis=0,
    )
    result = matmul(flat, square)
    channels = strips.shape[3]
    for tap in range(3):
        strips[tap, pl.ds(DMAX + first, count)] = result[
            :, tap * channels : (tap + 1) * channels
        ].reshape(count, tokens, channels)


def lanes(step, size):
    return pl.ds(pl.multiple_of(step * size, size), size)


def clear_border(target, tokens):
    line, channels = target.shape[1], target.shape[2]
    border = jnp.zeros((DMAX, line, channels), target.dtype)
    rim = jnp.zeros((tokens, DMAX, channels), target.dtype)
    if target.shape[0] > tokens:
        target[0:DMAX] = border
        target[DMAX + tokens :] = border
    if line > tokens:
        rows = slice(target.shape[0] - tokens - DMAX, target.shape[0] - DMAX)
        if target.shape[0] == tokens:
            rows = slice(0, tokens)
        target[rows, 0:DMAX, :] = rim
        target[rows, DMAX + tokens :, :] = rim


def forward_kernel(
    plan,
    dilations,
    far,
    w_proj,
    w_gate,
    w_out,
    one,
    two,
    near_left,
    near_right,
    near_swapped,
    near_gating,
    near_contact,
    near_start,
    output,
    flipped,
    flipped_two,
    factor,
    mine,
    own_contact,
    far_left,
    right,
    swapped,
    far_gating,
    far_contact,
    far_start,
    turned_left,
    turned_right,
    products,
    normed,
    updated,
    field,
    wide,
    second,
    strips,
):
    _, _, height, breadth, tokens = plan
    hidden, channels = w_out.shape
    pixels = height * breadth
    chips = tokens // height // 2
    row_place, col_place = lax.axis_index("row"), lax.axis_index("col")
    core = row_place % 2
    rate_one, rate_two = dilations[0], dilations[1]
    inside = slice(DMAX, DMAX + tokens)
    for target in (field, second):
        clear_border(target, tokens)
    clear_ends(strips, tokens)

    right[core] = near_right[...]
    swapped[core] = near_swapped[...]
    project_half(
        plan,
        1 - core,
        far,
        w_proj,
        w_gate,
        far_left,
        right.at[1 - core],
        swapped.at[1 - core],
        far_gating,
        far_contact,
        far_start,
        (turned_left, turned_right),
    )

    lane = lax.broadcasted_iota(jnp.int32, (height, chips * tokens), 1)
    low = jnp.where(lane < tokens, 1.0, 0.0).astype(jnp.bfloat16)
    high = jnp.where(lane < tokens, 0.0, 1.0).astype(jnp.bfloat16)
    batch = 64
    pitch = 2 * height + PITCH

    def multiply(step, carry):
        for part in range(batch):
            h = step * batch + part
            ahead = [right[0, h], right[1, h]]
            back = [swapped[0, h], swapped[1, h]]
            strips = [strip * low for strip in ahead + back]
            strips += [strip * high for strip in back + ahead]
            mine = jnp.concatenate([near_left[h], far_left[h]], axis=0)
            products[pl.ds(pl.multiple_of(h * pitch, 8), 2 * height), :] = matmul_nt(
                mine, jnp.concatenate(strips, axis=0)
            )
        return carry

    lax.fori_loop(0, hidden // batch, multiply, 0)

    chunk = 8
    size = chunk * tokens

    halves = (
        (core, near_gating, near_contact, near_start),
        (1 - core, far_gating, far_contact, far_start),
    )
    parts = height // chunk

    def normalise(step):
        half, first = step // parts, step % parts * chunk
        for row in range(chunk):
            strip = products[pl.ds(half * height + first + row, hidden, stride=pitch), :]
            strip = layer_norm(strip, axis=0).astype(jnp.bfloat16).T
            for chip in range(chips):
                normed[step, chip, row] = strip[chip * tokens : (chip + 1) * tokens]

    def update(step):
        first = step % parts * chunk
        side, gating, contact, start = halves[step // parts]
        change = matmul(normed[step].reshape(chips * size, hidden), w_out[...])
        change = change.reshape(chips, chunk, tokens, channels)
        rows = pl.ds(first, chunk)
        fresh = start[:, rows].astype(jnp.float32) + gating[:, rows].astype(jnp.float32) * change
        fresh = fresh.astype(jnp.bfloat16).astype(jnp.float32)
        first_in = layer_norm(fresh) * contact[:, rows].astype(jnp.float32)
        for chip in range(chips):
            base = (chip * 2 + side) * height + first
            rows = pl.ds(base, chunk)
            updated[rows] = fresh[chip]
            field[rows, inside, :] = first_in[chip]
            spread(field, rows, 0, rate_one, wide)
            flipped[:, pl.ds(pl.multiple_of(base * tokens, size), size)] = (
                first_in[chip].reshape(size, channels).astype(jnp.bfloat16).T
            )

    def first_conv(step):
        side = halves[step // parts][0]
        for chip in range(chips):
            base = (chip * 2 + side) * height + step % parts * chunk
            column_taps(wide, lambda tap: one[tap], base, chunk, strips)

    count = 2 * parts
    for step in range(count + 2):
        if step < count:
            normalise(step)
        if 1 <= step <= count:
            update(step - 1)
        if step >= 2:
            first_conv(step - 2)

    deep = 2 * chunk

    def activate(step, carry):
        rows = pl.ds(step * deep, deep)
        pre = row_taps(strips, step * deep, deep, rate_one)
        sigma = sigmoid(pre)
        second_in = pre * sigma
        second[pl.ds(DMAX + step * deep, deep), inside, :] = second_in
        flipped_two[:, lanes(step, deep * tokens)] = (
            second_in.reshape(deep * tokens, channels).astype(jnp.bfloat16).T
        )
        factor[rows] = sigma * (1.0 + pre * (1.0 - sigma))
        return carry

    lax.fori_loop(0, tokens // deep, activate, 0)

    row_start, col_start = row_place * height, col_place * breadth
    cols = pl.ds(pl.multiple_of(col_start, breadth), breadth)
    fresh = updated[pl.ds(row_start, height), cols, :].reshape(pixels, channels)
    mine[...] = fresh
    second_pre = matmul(
        windows(second, rate_two, row_start, col_start, height, breadth),
        two[...].reshape(9 * channels, channels),
    )
    output[...] = (fresh + second_pre).astype(jnp.bfloat16)
    marks = near_contact[row_place // 2].astype(jnp.float32)
    place_col = lax.broadcasted_iota(jnp.int32, (tokens, channels), 0) // breadth
    marks = jnp.where((place_col == col_place)[None], marks, 0.0)
    marks = marks.reshape(height, tokens // breadth, breadth, channels)
    own_contact[...] = jnp.sum(marks, axis=1).reshape(pixels, channels)


def backward_kernel(
    plan,
    dilations,
    cot_near,
    cot_far,
    one,
    two_t,
    flipped,
    flipped_two,
    factor,
    mine,
    own_contact,
    grad_pair,
    grad_one,
    grad_two,
    field,
    wide_cot,
    wide_pre,
    grad_pre,
    sum_one,
    sum_two,
    scaled_one,
    scaled_two,
    sent,
):
    _, cot_rounds, height, breadth, tokens = plan
    channels = one.shape[2]
    pixels = height * breadth
    row_place, col_place = lax.axis_index("row"), lax.axis_index("col")
    rate_one, rate_two = dilations[0], dilations[1]
    half = cot_far.shape[0]
    inside = slice(DMAX, DMAX + tokens)
    for target in (field, wide_cot, wide_pre, grad_pre):
        clear_border(target, tokens)

    several = 8

    def place_cot(source, base):
        def body(step, carry):
            for i in range(several):
                slot = step * several + i
                row, col = place_of(base + slot, cot_rounds, row_place, col_place)
                cols = pl.ds(pl.multiple_of(DMAX + col * breadth, breadth), breadth)
                field[pl.ds(row * height, height), cols, :] = (
                    source[slot].astype(jnp.float32).reshape(height, breadth, channels)
                )
            return carry

        lax.fori_loop(0, half // several, body, 0)

    place_cot(cot_near, 0)
    place_cot(cot_far, half)
    chunk = 16
    size = chunk * tokens
    steps = tokens // chunk

    def spread_cot(step, carry):
        spread(field, pl.ds(step * chunk, chunk), 0, -rate_two, wide_cot)
        return carry

    lax.fori_loop(0, steps, spread_cot, 0)

    def back_two(step):
        first = step * chunk
        shifted = taps(wide_cot, first, chunk, -rate_two)
        before = matmul(shifted, two_t[...]).reshape(chunk, tokens, channels)
        before = (before * factor[pl.ds(first, chunk)]).astype(jnp.bfloat16).astype(jnp.float32)
        grad_pre[pl.ds(DMAX + first, chunk), inside, :] = before
        part = matmul(flipped_two[:, step * size : (step + 1) * size], shifted)
        sum_two[...] = part if step == 0 else sum_two[...] + part

    def spread_pre(step):
        spread(grad_pre, pl.ds(step * chunk, chunk), DMAX, -rate_one, wide_pre)

    def back_one(step):
        shifted = taps(wide_pre, step * chunk, chunk, -rate_one)
        part = matmul(flipped[:, step * size : (step + 1) * size], shifted)
        sum_one[...] = part if step == 0 else sum_one[...] + part

    def finish(total, scaled, target, place):
        for tap in range(9):
            columns = slice(tap * channels, (tap + 1) * channels)
            scaled[tap] = total[:, columns] * (1.0 / tokens)
        copy = pltpu.make_async_copy(scaled, target, sent.at[place])
        copy.start()
        return copy

    for step in range(steps):
        if step >= 3:
            back_one(step - 3)
        if step >= 1:
            spread_pre(step - 1)
        back_two(step)
    copies = [finish(sum_two, scaled_two, grad_two, 1)]
    spread_pre(steps - 1)
    for step in range(max(steps - 3, 0), steps):
        back_one(step)
    copies.append(finish(sum_one, scaled_one, grad_one, 0))

    one_rows = [one[tap] for tap in range(9)]
    grad_input = own_contact[...] * matmul_nt(
        windows(
            grad_pre, -rate_one, row_place * height, col_place * breadth, height, breadth
        ),
        jnp.concatenate(one_rows, axis=1),
    )
    centre = mine[...] - jnp.mean(mine[...], axis=-1, keepdims=True)
    inv_spread = lax.rsqrt(jnp.mean(centre * centre, axis=-1, keepdims=True) + EPSILON)
    scaled = centre * inv_spread
    grad_norm = inv_spread * (
        grad_input
        - jnp.mean(grad_input, axis=-1, keepdims=True)
        - scaled * jnp.mean(grad_input * scaled, axis=-1, keepdims=True)
    )
    grad_pair[...] = (cot_near[0].astype(jnp.float32) + grad_norm).astype(jnp.bfloat16)
    for copy in copies:
        copy.wait()


def replicated(
    pair, pair_mask, contact_mask, dilations, w_proj, w_gate, w_out, conv_one, conv_two, cotangent
):
    height, breadth, channels = pair.shape
    hidden = w_out.shape[0]
    row_count, col_count = lax.axis_size("row"), lax.axis_size("col")
    tokens = height * row_count
    pixels = height * breadth
    rounds, cot_rounds = exchange_plan(row_count, col_count)
    f32, bf16 = jnp.float32, jnp.bfloat16
    plan = (halvings("row", row_count), cot_rounds, height, breadth, tokens)
    chips = row_count // 2
    line = tokens + 2 * DMAX
    in_vmem = pl.BlockSpec(memory_space=pltpu.VMEM)
    side = ((hidden, height, chips * tokens), bf16)
    rows = (chips, height, tokens, channels)
    halves = [side] * 3 + [(rows, bf16)] * 3
    turned = pltpu.VMEM((hidden * (height + PITCH), chips * tokens), f32)
    stat = ((pixels, channels), f32)

    def shapes(*entries):
        return [jax.ShapeDtypeStruct(shape, dtype) for shape, dtype in entries]

    in_smem = pl.BlockSpec(memory_space=pltpu.SMEM)
    spare = channels - 2 * height
    marks = jnp.pad(pair_mask.T, ((pixels, breadth), (0, height + spare))) + jnp.pad(
        contact_mask.T, ((pixels, breadth), (height, spare))
    )
    above = jnp.pad(pair.reshape(pixels, channels), ((0, 2 * breadth), (0, 0)))
    held = (above.astype(f32) + marks.astype(f32)).astype(bf16)[None]
    block = cotangent.reshape(1, pixels, channels)
    cot_held = lax.optimization_barrier(jnp.maximum(block, jnp.finfo(bf16).min))
    rates = jnp.clip(dilations, 1, DMAX)
    for step in range(len(cot_rounds) - 1):
        cot_other = exchange(cot_held if step else block, cot_rounds[step])
        if step < len(rounds) - 2:
            cot_held = jnp.concatenate([cot_held, cot_other], axis=0)
            if step == len(rounds) - 3:
                cot_held, rates = lax.optimization_barrier((cot_held, rates))
            else:
                cot_held = lax.optimization_barrier(cot_held)
    held = lax.all_to_all(
        jnp.broadcast_to(held, (col_count,) + held.shape[1:]), "col", 0, 0, tiled=True
    )
    for hop in halvings("row", row_count)[:-1]:
        held = lax.optimization_barrier(jnp.concatenate([held, exchange(held, hop)], axis=0))
    near, far = held, exchange(held, rounds[-1])
    *near_parts, two_t = pl.pallas_call(
        functools.partial(near_kernel, plan),
        in_specs=[in_vmem] * 4,
        out_specs=[in_vmem] * 7,
        out_shape=shapes(*halves, ((9 * channels, channels), bf16)),
        scratch_shapes=[turned] * 2,
        compiler_params=pltpu.CompilerParams(vmem_limit_bytes=VMEM_LIMIT // 3),
        cost_estimate=pl.CostEstimate(
            flops=tokens * tokens * channels * 5 * hidden,
            bytes_accessed=8 * tokens * tokens * channels,
            transcendentals=3 * tokens * tokens * channels // 2,
        ),
    )(near, w_proj, w_gate, conv_two)
    cot_other, two_t = lax.optimization_barrier((cot_other, two_t))
    cot_near = jnp.concatenate([cot_held, cot_other], axis=0)
    cot_far = exchange(cot_near, cot_rounds[-1])
    whole = pltpu.VMEM((tokens, tokens, channels), f32)
    padded = pltpu.VMEM((tokens, line, channels), f32)
    bordered = pltpu.VMEM((line, line, channels), f32)
    tripled = pltpu.VMEM((line, tokens, 3 * channels), bf16)
    both = pltpu.VMEM((2,) + side[0], bf16)
    alone = pltpu.VMEM(rows, bf16)
    banded = pltpu.VMEM((3, line, tokens, channels), f32)
    flat = ((channels, tokens * tokens), bf16)
    sums = pltpu.VMEM((channels, 9 * channels), f32)
    output, *held = pl.pallas_call(
        functools.partial(forward_kernel, plan),
        in_specs=[in_smem] + [in_vmem] * 12,
        out_specs=[in_vmem] * 6,
        out_shape=shapes(
            ((pixels, channels), bf16),
            flat,
            flat,
            ((tokens, tokens, channels), f32),
            stat,
            stat,
        ),
        scratch_shapes=[pltpu.VMEM(*side), both, both, alone, alone, alone]
        + [turned] * 2
        + [pltpu.VMEM((hidden * (2 * height + PITCH), chips * tokens), f32)]
        + [pltpu.VMEM((2 * height // 8, chips, 8, tokens, hidden), bf16)]
        + [whole, padded, tripled, bordered, banded],
        compiler_params=pltpu.CompilerParams(vmem_limit_bytes=FORWARD_VMEM),
        cost_estimate=pl.CostEstimate(
            flops=tokens * tokens * channels * 40 * hidden,
            bytes_accessed=40 * tokens * tokens * channels,
            transcendentals=4 * tokens * tokens * channels,
        ),
    )(
        rates,
        far,
        w_proj,
        w_gate,
        w_out,
        conv_one,
        conv_two,
        *near_parts,
    )
    grad_pair, grad_one, grad_two = pl.pallas_call(
        functools.partial(backward_kernel, plan),
        in_specs=[in_smem] + [in_vmem] * 9,
        out_specs=[in_vmem] + [pl.BlockSpec(memory_space=pltpu.HBM)] * 2,
        out_shape=shapes(
            ((pixels, channels), bf16),
            ((9, channels, channels), f32),
            ((9, channels, channels), f32),
        ),
        scratch_shapes=[padded, tripled, tripled, bordered, sums, sums]
        + [pltpu.VMEM((9, channels, channels), f32)] * 2
        + [pltpu.SemaphoreType.DMA((2,))],
        compiler_params=pltpu.CompilerParams(vmem_limit_bytes=BACKWARD_VMEM),
    )(
        rates,
        cot_near,
        cot_far,
        conv_one,
        two_t,
        *held,
    )
    block = (height, breadth, channels)
    return output.reshape(block), grad_pair.reshape(block), grad_one, grad_two


def fits(pair, w_out, row_count, col_count):
    height, breadth, channels = pair.shape
    tokens = height * row_count
    powers = all(count & (count - 1) == 0 for count in (row_count, col_count))
    whole = (tokens + 2 * DMAX) ** 2 * channels
    return (
        powers
        and row_count * col_count >= 8
        and height * breadth == channels == w_out.shape[0]
        and breadth == 8
        and row_count // 2 * tokens == channels
        and whole * 60 <= VMEM_LIMIT
    )


def local(*arguments):
    pair, w_out = arguments[0], arguments[6]
    if fits(pair, w_out, lax.axis_size("row"), lax.axis_size("col")):
        return replicated(*arguments)
    return sharded(*arguments)


def solution(mesh):
    in_specs = (
        P("row", "col", None),
        P("row", "col"),
        P("row", "col"),
        P(),
        P(),
        P(),
        P(),
        P(),
        P(),
        P("row", "col", None),
    )
    out_specs = (P("row", "col", None), P("row", "col", None), P(), P())
    return jax.shard_map(local, mesh=mesh, in_specs=in_specs, out_specs=out_specs, check_vma=False)
```

```python
import functools

import jax
import jax.numpy as jnp
from jax import lax
from jax.experimental import pallas as pl
from jax.experimental.pallas import tpu as pltpu
from jax.sharding import PartitionSpec as P

DMAX = 8
VMEM_LIMIT = 48 * 1024 * 1024
PITCH = 8
FORWARD_VMEM = 44 * 1024 * 1024
BACKWARD_VMEM = 36 * 1024 * 1024


EPSILON = 1e-05


def with_halo(block, sides, width):
    for axis, dim in sides:
        count = lax.axis_size(axis)
        forward = [(i, i + 1) for i in range(count - 1)]
        backward = [(target, source) for source, target in forward]
        low = lax.ppermute(
            lax.slice_in_dim(block, block.shape[dim] - width, None, axis=dim), axis, forward
        )
        high = lax.ppermute(lax.slice_in_dim(block, 0, width, axis=dim), axis, backward)
        block = jnp.concatenate([low, block, high], axis=dim)
    return block


def broadcast(x, axis, root):
    mine = lax.axis_index(axis) == root
    return lax.psum(jnp.where(mine, x, jnp.zeros_like(x)), axis)


def layer_norm(values, axis=-1):
    centre = values - jnp.mean(values, axis=axis, keepdims=True)
    spread = jnp.mean(centre * centre, axis=axis, keepdims=True)
    return centre * lax.rsqrt(spread + EPSILON)


def with_rim(field):
    return with_halo(field, (("row", 0), ("col", 1)), DMAX)


def gather_taps(padded, dilation, mirrored, height, breadth):
    windows = []
    for tap_index in range(9):
        row_tap = tap_index // 3
        col_tap = tap_index % 3
        if mirrored:
            row_tap = 2 - row_tap
            col_tap = 2 - col_tap
        row_start = DMAX + (row_tap - 1) * dilation
        col_start = DMAX + (col_tap - 1) * dilation
        windows.append(
            lax.dynamic_slice(
                padded, (row_start, col_start, jnp.int32(0)), (height, breadth, padded.shape[2])
            )
        )
    return jnp.concatenate(windows, axis=2).reshape(height * breadth, -1)


def sharded(
    pair, pair_mask, contact_mask, dilations, w_proj, w_gate, w_out, conv_one, conv_two, cotangent
):
    height, breadth, channels = pair.shape
    hidden = w_out.shape[0]
    row_count = lax.axis_size("row")
    col_count = lax.axis_size("col")
    ratio = col_count // row_count
    row_place = lax.axis_index("row")
    col_place = lax.axis_index("col")
    tokens = breadth * col_count
    pixels = height * breadth
    pair_flat = pair.astype(jnp.float32).reshape(pixels, channels)
    normed = layer_norm(pair_flat).astype(jnp.bfloat16)
    projected = jnp.dot(normed, w_proj, preferred_element_type=jnp.float32)
    mask_col = pair_mask.reshape(pixels, 1).astype(jnp.float32)
    left_side = (
        (mask_col * jax.nn.sigmoid(projected[:, hidden : 2 * hidden]) * projected[:, :hidden])
        .astype(jnp.bfloat16)
        .reshape(height, breadth, hidden)
    )
    right_side = (
        (
            mask_col
            * jax.nn.sigmoid(projected[:, 3 * hidden :])
            * projected[:, 2 * hidden : 3 * hidden]
        )
        .astype(jnp.bfloat16)
        .reshape(height, breadth, hidden)
    )
    right_all = lax.all_gather(right_side, "col", axis=1, tiled=True)
    offset = jnp.clip(col_place * breadth - row_place * height, 0, height - breadth)
    right_local = lax.dynamic_slice_in_dim(right_all, offset, breadth, 0)
    right_rows = broadcast(right_local, "row", col_place // ratio)
    products = jnp.einsum(
        "ikh,jkh->ijh",
        lax.all_gather(left_side, "col", axis=1, tiled=True),
        right_rows,
        preferred_element_type=jnp.float32,
    )
    product_norm = layer_norm(products.reshape(pixels, hidden)).astype(jnp.bfloat16)
    gating = jax.nn.sigmoid(jnp.dot(normed, w_gate, preferred_element_type=jnp.float32))
    updated = (
        pair_flat + gating * jnp.dot(product_norm, w_out, preferred_element_type=jnp.float32)
    ).astype(jnp.bfloat16)
    updated_f = updated.astype(jnp.float32)
    centre = updated_f - jnp.mean(updated_f, axis=-1, keepdims=True)
    inv_spread = lax.rsqrt(jnp.mean(centre * centre, axis=-1, keepdims=True) + EPSILON)
    scaled = centre * inv_spread
    contact = contact_mask.reshape(pixels, 1).astype(jnp.float32)
    first_in = (scaled * contact).astype(jnp.bfloat16).reshape(height, breadth, channels)
    rate_one = dilations[0]
    rate_two = dilations[1]
    first_taps = gather_taps(with_rim(first_in), rate_one, False, height, breadth)
    first_pre = jnp.dot(
        first_taps, conv_one.reshape(9 * channels, channels), preferred_element_type=jnp.float32
    )
    sigma = jax.nn.sigmoid(first_pre)
    second_in = (first_pre * sigma).astype(jnp.bfloat16).reshape(height, breadth, channels)
    second_taps = gather_taps(with_rim(second_in), rate_two, False, height, breadth)
    second_pre = jnp.dot(
        second_taps, conv_two.reshape(9 * channels, channels), preferred_element_type=jnp.float32
    )
    output = (updated_f + second_pre).astype(jnp.bfloat16).reshape(height, breadth, channels)
    cot_flat = cotangent.reshape(pixels, channels)
    grad_two = (
        lax.dot_general(
            second_taps, cot_flat, (((0,), (0,)), ((), ())), preferred_element_type=jnp.float32
        ).reshape(9, channels, channels)
        / tokens
    )
    cot_taps = gather_taps(with_rim(cotangent), rate_two, True, height, breadth)
    grad_hidden = jnp.dot(
        cot_taps,
        conv_two.transpose(0, 2, 1).reshape(9 * channels, channels),
        preferred_element_type=jnp.float32,
    )
    grad_pre = (grad_hidden * sigma * (1.0 + first_pre * (1.0 - sigma))).astype(jnp.bfloat16)
    grad_one = (
        lax.dot_general(
            first_taps, grad_pre, (((0,), (0,)), ((), ())), preferred_element_type=jnp.float32
        ).reshape(9, channels, channels)
        / tokens
    )
    grad_taps = gather_taps(
        with_rim(grad_pre.reshape(height, breadth, channels)), rate_one, True, height, breadth
    )
    grad_input = (
        jnp.dot(
            grad_taps,
            conv_one.transpose(0, 2, 1).reshape(9 * channels, channels),
            preferred_element_type=jnp.float32,
        )
        * contact
    )
    grad_norm = inv_spread * (
        grad_input
        - jnp.mean(grad_input, axis=-1, keepdims=True)
        - scaled * jnp.mean(grad_input * scaled, axis=-1, keepdims=True)
    )
    grad_pair = (
        (cot_flat.astype(jnp.float32) + grad_norm)
        .astype(jnp.bfloat16)
        .reshape(height, breadth, channels)
    )
    grad_one, grad_two = lax.psum((grad_one, grad_two), ("row", "col"))
    return (output, grad_pair, grad_one, grad_two)


def halvings(axis, count):
    return [(axis, count >> step) for step in range(1, count.bit_length())]


def exchange_plan(row_count, col_count):
    rows, cols = halvings("row", row_count), halvings("col", col_count)
    return cols + rows, rows[:-1] + cols + rows[-1:]


def exchange(held, hop):
    axis, distance = hop
    return lax.ppermute(held, axis, [(i, i ^ distance) for i in range(lax.axis_size(axis))])


def place_of(position, rounds, row_place, col_place):
    row, col = row_place, col_place
    for step, (axis, distance) in enumerate(rounds):
        bit = ((position >> step) & 1) * distance
        if axis == "row":
            row = row ^ bit
        else:
            col = col ^ bit
    return row, col


def slot_of(row_change, col_change, rounds):
    slot = 0
    for step, (axis, distance) in enumerate(rounds[:-1]):
        change = row_change if axis == "row" else col_change
        slot = slot | (((change // distance) & 1) << step)
    return slot


def sigmoid(values):
    return 0.5 + 0.5 * jnp.tanh(0.5 * values)


def matmul(left, right):
    return jnp.dot(left, right, preferred_element_type=jnp.float32)


def matmul_by_rows(left, right):
    rows = 256
    return jnp.concatenate(
        [matmul(left[i : i + rows], right) for i in range(0, left.shape[0], rows)], axis=0
    )


def matmul_nt(left, right):
    return lax.dot_general(
        left, right, (((1,), (1,)), ((), ())), preferred_element_type=jnp.float32
    )


def project_half(
    plan, core, pairs, w_proj, w_gate, left, right, swapped, gating, contact, start, turned
):
    rounds, _, height, breadth, tokens = plan
    channels, hidden = w_gate.shape[0], w_gate.shape[1]
    col_count, chips = tokens // breadth, tokens // height // 2
    row_place, col_place = lax.axis_index("row"), lax.axis_index("col")
    lane = lax.broadcasted_iota(jnp.int32, (height, breadth, channels), 2)
    place = lax.broadcasted_iota(jnp.int32, (height, breadth, channels), 0)
    own_lane = jnp.where((lane % height == place) & (lane < 2 * height), 1.0, 0.0)
    pick_lane = lax.broadcasted_iota(jnp.int32, (channels, 2 * channels), 0)
    pick_half = lax.broadcasted_iota(jnp.int32, (channels, 2 * channels), 1) // channels
    pick = jnp.where(pick_lane // height == pick_half, 1.0, 0.0).astype(jnp.bfloat16)
    pixels = height * breadth
    rows = 8
    for first in range(0, height, rows):
        values, masks = [], []
        for chip in range(chips):
            row_change = (chip * 2 + core) ^ row_place
            blocks, marks = [], []
            for col in range(col_count):
                col_change = col_place ^ col
                slot = slot_of(row_change, col_change, rounds)
                blocks.append(
                    pairs[slot, first * breadth : (first + rows) * breadth, :]
                    .astype(jnp.float32)
                    .reshape(rows, breadth, channels)
                )
                mark = pairs[slot, pixels:, :].astype(jnp.float32)[:breadth]
                marks.append(mark[None] * own_lane[first : first + rows])
            values.append(jnp.concatenate(blocks, axis=1).reshape(rows * tokens, channels))
            masks.append(jnp.concatenate(marks, axis=1).reshape(rows * tokens, channels))
        values = jnp.concatenate(values, axis=0)
        masks = matmul(jnp.concatenate(masks, axis=0).astype(jnp.bfloat16), pick)
        normed = layer_norm(values)
        gates = sigmoid(matmul(normed.astype(jnp.bfloat16), w_gate[...]))
        masked = (normed * masks[:, :channels]).astype(jnp.bfloat16)
        projected = matmul(masked, w_proj[...])
        sides = [
            sigmoid(projected[:, (2 * side + 1) * hidden : (2 * side + 2) * hidden])
            * projected[:, 2 * side * hidden : (2 * side + 1) * hidden]
            for side in range(2)
        ]
        for side, target in zip(sides, turned):
            side = side.reshape(chips, rows, tokens, hidden)
            for row in range(rows):
                strip = jnp.concatenate([side[chip, row] for chip in range(chips)], axis=0)
                target[pl.ds(first + row, hidden, stride=height + PITCH), :] = strip.T
        shape = (chips, rows, tokens, channels)
        span = slice(first, first + rows)
        gating[:, span] = gates.astype(jnp.bfloat16).reshape(shape)
        contact[:, span] = masks[:, channels:].astype(jnp.bfloat16).reshape(shape)
        start[:, span] = values.astype(jnp.bfloat16).reshape(shape)
    shape = (hidden, height + PITCH, chips * tokens)
    mine, other = turned[0][...], turned[1][...]
    for target, source in (
        (left, mine),
        (right, other),
        (swapped, pltpu.roll(other, tokens, 1)),
    ):
        target[...] = source.reshape(shape)[:, :height].astype(jnp.bfloat16)


def near_kernel(
    plan,
    near,
    w_proj,
    w_gate,
    two,
    left,
    right,
    swapped,
    gating,
    contact,
    start,
    two_t,
    turned_left,
    turned_right,
):
    core = lax.axis_index("row") % 2
    channels = two.shape[1]
    for tap in range(9):
        two_t[tap * channels : (tap + 1) * channels] = two[tap].T
    project_half(
        plan,
        core,
        near,
        w_proj,
        w_gate,
        left,
        right,
        swapped,
        gating,
        contact,
        start,
        (turned_left, turned_right),
    )


def spread(source, rows, pad, rate, target):
    tokens, channels = target.shape[1], source.shape[2]
    for tap in range(3):
        first = DMAX + (tap - 1) * rate if tap != 1 else DMAX
        moved = source[pl.ds(pad + rows.start, rows.size), pl.ds(first, tokens), :]
        target[pl.ds(DMAX + rows.start, rows.size), :, tap * channels : (tap + 1) * channels] = (
            moved.astype(jnp.bfloat16)
        )


def taps(source, first, count, rate):
    tokens = source.shape[1]
    views = [
        source[pl.ds(DMAX + first + (tap - 1) * rate, count)].reshape(count * tokens, -1)
        for tap in range(3)
    ]
    return jnp.concatenate(views, axis=1)


def windows(source, rate, row_start, col_start, height, breadth):
    views = [
        source[
            pl.ds(row_start + DMAX + (tap // 3 - 1) * rate, height),
            pl.ds(col_start + DMAX + (tap % 3 - 1) * rate, breadth),
            :,
        ].reshape(height * breadth, -1)
        for tap in range(9)
    ]
    return jnp.concatenate(views, axis=1).astype(jnp.bfloat16)


def row_taps(strips, first, count, rate):
    views = [
        strips[tap, pl.ds(DMAX + first + ((tap - 1) * rate if tap != 1 else 0), count)]
        for tap in range(3)
    ]
    return views[0] + views[1] + views[2]


def clear_ends(strips, tokens):
    for tap in (0, 2):
        for rows in (slice(0, DMAX), slice(DMAX + tokens, 2 * DMAX + tokens)):
            strips[tap, rows] = jnp.zeros((DMAX,) + strips.shape[2:], jnp.float32)


def column_taps(source, weight, first, count, strips):
    tokens = source.shape[1]
    flat = source[pl.ds(DMAX + first, count)].reshape(count * tokens, -1)
    square = jnp.concatenate(
        [
            jnp.concatenate([weight(3 * row + col) for row in range(3)], axis=1)
            for col in range(3)
        ],
        axis=0,
    )
    result = matmul_by_rows(flat, square)
    channels = strips.shape[3]
    for tap in range(3):
        strips[tap, pl.ds(DMAX + first, count)] = result[
            :, tap * channels : (tap + 1) * channels
        ].reshape(count, tokens, channels)


def lanes(step, size):
    return pl.ds(pl.multiple_of(step * size, size), size)


def clear_border(target, tokens):
    line, channels = target.shape[1], target.shape[2]
    border = jnp.zeros((DMAX, line, channels), target.dtype)
    rim = jnp.zeros((tokens, DMAX, channels), target.dtype)
    if target.shape[0] > tokens:
        target[0:DMAX] = border
        target[DMAX + tokens :] = border
    if line > tokens:
        rows = slice(target.shape[0] - tokens - DMAX, target.shape[0] - DMAX)
        if target.shape[0] == tokens:
            rows = slice(0, tokens)
        target[rows, 0:DMAX, :] = rim
        target[rows, DMAX + tokens :, :] = rim


def forward_kernel(
    plan,
    dilations,
    far,
    w_proj,
    w_gate,
    w_out,
    one,
    two,
    near_left,
    near_right,
    near_swapped,
    near_gating,
    near_contact,
    near_start,
    output,
    flipped,
    flipped_two,
    factor,
    mine,
    own_contact,
    far_left,
    right,
    swapped,
    far_gating,
    far_contact,
    far_start,
    turned_left,
    turned_right,
    products,
    normed,
    updated,
    field,
    wide,
    second,
    strips,
):
    _, _, height, breadth, tokens = plan
    hidden, channels = w_out.shape
    pixels = height * breadth
    chips = tokens // height // 2
    row_place, col_place = lax.axis_index("row"), lax.axis_index("col")
    core = row_place % 2
    rate_one, rate_two = dilations[0], dilations[1]
    inside = slice(DMAX, DMAX + tokens)
    for target in (field, second):
        clear_border(target, tokens)
    clear_ends(strips, tokens)

    right[core] = near_right[...]
    swapped[core] = near_swapped[...]
    project_half(
        plan,
        1 - core,
        far,
        w_proj,
        w_gate,
        far_left,
        right.at[1 - core],
        swapped.at[1 - core],
        far_gating,
        far_contact,
        far_start,
        (turned_left, turned_right),
    )

    lane = lax.broadcasted_iota(jnp.int32, (height, chips * tokens), 1)
    low = jnp.where(lane < tokens, 1.0, 0.0).astype(jnp.bfloat16)
    high = jnp.where(lane < tokens, 0.0, 1.0).astype(jnp.bfloat16)
    batch = 64
    pitch = 2 * height + PITCH

    def multiply(step, carry):
        for part in range(batch):
            h = step * batch + part
            ahead = [right[0, h], right[1, h]]
            back = [swapped[0, h], swapped[1, h]]
            strips = [strip * low for strip in ahead + back]
            strips += [strip * high for strip in back + ahead]
            mine = jnp.concatenate([near_left[h], far_left[h]], axis=0)
            products[pl.ds(pl.multiple_of(h * pitch, 8), 2 * height), :] = matmul_nt(
                mine, jnp.concatenate(strips, axis=0)
            )
        return carry

    lax.fori_loop(0, hidden // batch, multiply, 0)

    chunk = 8
    size = chunk * tokens

    halves = (
        (core, near_gating, near_contact, near_start),
        (1 - core, far_gating, far_contact, far_start),
    )
    parts = height // chunk

    def normalise(step):
        half, first = step // parts, step % parts * chunk
        for row in range(chunk):
            strip = products[pl.ds(half * height + first + row, hidden, stride=pitch), :]
            strip = layer_norm(strip, axis=0).astype(jnp.bfloat16).T
            for chip in range(chips):
                normed[step, chip, row] = strip[chip * tokens : (chip + 1) * tokens]

    def update(step):
        first = step % parts * chunk
        side, gating, contact, start = halves[step // parts]
        change = matmul(normed[step].reshape(chips * size, hidden), w_out[...])
        change = change.reshape(chips, chunk, tokens, channels)
        rows = pl.ds(first, chunk)
        fresh = start[:, rows].astype(jnp.float32) + gating[:, rows].astype(jnp.float32) * change
        fresh = fresh.astype(jnp.bfloat16).astype(jnp.float32)
        first_in = layer_norm(fresh) * contact[:, rows].astype(jnp.float32)
        for chip in range(chips):
            base = (chip * 2 + side) * height + first
            rows = pl.ds(base, chunk)
            updated[rows] = fresh[chip]
            field[rows, inside, :] = first_in[chip]
            spread(field, rows, 0, rate_one, wide)
            flipped[:, pl.ds(pl.multiple_of(base * tokens, size), size)] = (
                first_in[chip].reshape(size, channels).astype(jnp.bfloat16).T
            )

    def first_conv(step):
        side = halves[step // parts][0]
        for chip in range(chips):
            base = (chip * 2 + side) * height + step % parts * chunk
            column_taps(wide, lambda tap: one[tap], base, chunk, strips)

    count = 2 * parts
    for step in range(count + 2):
        if step < count:
            normalise(step)
        if 1 <= step <= count:
            update(step - 1)
        if step >= 2:
            first_conv(step - 2)

    deep = 2 * chunk

    def activate(step, carry):
        rows = pl.ds(step * deep, deep)
        pre = row_taps(strips, step * deep, deep, rate_one)
        sigma = sigmoid(pre)
        second_in = pre * sigma
        second[pl.ds(DMAX + step * deep, deep), inside, :] = second_in
        flipped_two[:, lanes(step, deep * tokens)] = (
            second_in.reshape(deep * tokens, channels).astype(jnp.bfloat16).T
        )
        factor[rows] = sigma * (1.0 + pre * (1.0 - sigma))
        return carry

    lax.fori_loop(0, tokens // deep, activate, 0)

    row_start, col_start = row_place * height, col_place * breadth
    cols = pl.ds(pl.multiple_of(col_start, breadth), breadth)
    fresh = updated[pl.ds(row_start, height), cols, :].reshape(pixels, channels)
    mine[...] = fresh
    second_pre = matmul(
        windows(second, rate_two, row_start, col_start, height, breadth),
        two[...].reshape(9 * channels, channels),
    )
    output[...] = (fresh + second_pre).astype(jnp.bfloat16)
    marks = near_contact[row_place // 2].astype(jnp.float32)
    place_col = lax.broadcasted_iota(jnp.int32, (tokens, channels), 0) // breadth
    marks = jnp.where((place_col == col_place)[None], marks, 0.0)
    marks = marks.reshape(height, tokens // breadth, breadth, channels)
    own_contact[...] = jnp.sum(marks, axis=1).reshape(pixels, channels)


def backward_kernel(
    plan,
    dilations,
    cot_near,
    cot_far,
    one,
    two_t,
    flipped,
    flipped_two,
    factor,
    mine,
    own_contact,
    grad_pair,
    grad_one,
    grad_two,
    field,
    wide_cot,
    wide_pre,
    grad_pre,
    sum_one,
    sum_two,
    scaled_one,
    scaled_two,
    sent,
):
    _, cot_rounds, height, breadth, tokens = plan
    channels = one.shape[2]
    pixels = height * breadth
    row_place, col_place = lax.axis_index("row"), lax.axis_index("col")
    rate_one, rate_two = dilations[0], dilations[1]
    half = cot_far.shape[0]
    inside = slice(DMAX, DMAX + tokens)
    for target in (field, wide_cot, wide_pre, grad_pre):
        clear_border(target, tokens)

    several = 8

    def place_cot(source, base):
        def body(step, carry):
            for i in range(several):
                slot = step * several + i
                row, col = place_of(base + slot, cot_rounds, row_place, col_place)
                cols = pl.ds(pl.multiple_of(DMAX + col * breadth, breadth), breadth)
                field[pl.ds(row * height, height), cols, :] = (
                    source[slot].astype(jnp.float32).reshape(height, breadth, channels)
                )
            return carry

        lax.fori_loop(0, half // several, body, 0)

    place_cot(cot_near, 0)
    place_cot(cot_far, half)
    chunk = 16
    size = chunk * tokens
    steps = tokens // chunk

    def spread_cot(step, carry):
        spread(field, pl.ds(step * chunk, chunk), 0, -rate_two, wide_cot)
        return carry

    lax.fori_loop(0, steps, spread_cot, 0)

    def back_two(step):
        first = step * chunk
        shifted = taps(wide_cot, first, chunk, -rate_two)
        before = matmul_by_rows(shifted, two_t[...]).reshape(chunk, tokens, channels)
        before = (before * factor[pl.ds(first, chunk)]).astype(jnp.bfloat16).astype(jnp.float32)
        grad_pre[pl.ds(DMAX + first, chunk), inside, :] = before
        part = matmul(flipped_two[:, step * size : (step + 1) * size], shifted)
        sum_two[...] = part if step == 0 else sum_two[...] + part

    def spread_pre(step):
        spread(grad_pre, pl.ds(step * chunk, chunk), DMAX, -rate_one, wide_pre)

    def back_one(step):
        shifted = taps(wide_pre, step * chunk, chunk, -rate_one)
        part = matmul(flipped[:, step * size : (step + 1) * size], shifted)
        sum_one[...] = part if step == 0 else sum_one[...] + part

    def finish(total, scaled, target, row):
        for tap in range(3 * row, 3 * row + 3):
            columns = slice(tap * channels, (tap + 1) * channels)
            scaled[tap] = total[:, columns] * (1.0 / tokens)
        taps_done = pl.ds(3 * row, 3)
        copy = pltpu.make_async_copy(
            scaled.at[taps_done], target.at[taps_done], sent.at[len(copies)]
        )
        copy.start()
        copies.append(copy)

    copies = []
    for step in range(steps):
        if step >= 3:
            back_one(step - 3)
        if step >= 1:
            spread_pre(step - 1)
        back_two(step)
    spread_pre(steps - 1)
    for row in range(3):
        finish(sum_two, scaled_two, grad_two, row)
    for step in range(max(steps - 3, 0), steps - 1):
        back_one(step)

    one_rows = [one[tap] for tap in range(9)]
    grad_input = own_contact[...] * matmul_nt(
        windows(
            grad_pre, -rate_one, row_place * height, col_place * breadth, height, breadth
        ),
        jnp.concatenate(one_rows, axis=1),
    )
    centre = mine[...] - jnp.mean(mine[...], axis=-1, keepdims=True)
    inv_spread = lax.rsqrt(jnp.mean(centre * centre, axis=-1, keepdims=True) + EPSILON)
    scaled = centre * inv_spread
    grad_norm = inv_spread * (
        grad_input
        - jnp.mean(grad_input, axis=-1, keepdims=True)
        - scaled * jnp.mean(grad_input * scaled, axis=-1, keepdims=True)
    )
    grad_pair[...] = (cot_near[0].astype(jnp.float32) + grad_norm).astype(jnp.bfloat16)

    last = steps - 1
    for row in range(3):
        columns = slice(3 * row * channels, 3 * (row + 1) * channels)
        moved = pl.ds(DMAX + last * chunk - (row - 1) * rate_one, chunk)
        sum_one[:, columns] += matmul(
            flipped[:, last * size : (last + 1) * size], wide_pre[moved].reshape(size, -1)
        )
        finish(sum_one, scaled_one, grad_one, row)
    for copy in copies:
        copy.wait()


def replicated(
    pair, pair_mask, contact_mask, dilations, w_proj, w_gate, w_out, conv_one, conv_two, cotangent
):
    height, breadth, channels = pair.shape
    hidden = w_out.shape[0]
    row_count, col_count = lax.axis_size("row"), lax.axis_size("col")
    tokens = height * row_count
    pixels = height * breadth
    rounds, cot_rounds = exchange_plan(row_count, col_count)
    f32, bf16 = jnp.float32, jnp.bfloat16
    plan = (rounds, cot_rounds, height, breadth, tokens)
    chips = row_count // 2
    line = tokens + 2 * DMAX
    in_vmem = pl.BlockSpec(memory_space=pltpu.VMEM)
    side = ((hidden, height, chips * tokens), bf16)
    rows = (chips, height, tokens, channels)
    halves = [side] * 3 + [(rows, bf16)] * 3
    turned = pltpu.VMEM((hidden * (height + PITCH), chips * tokens), f32)
    stat = ((pixels, channels), f32)

    def shapes(*entries):
        return [jax.ShapeDtypeStruct(shape, dtype) for shape, dtype in entries]

    in_smem = pl.BlockSpec(memory_space=pltpu.SMEM)
    spare = channels - 2 * height
    marks = jnp.pad(pair_mask.T, ((pixels, breadth), (0, height + spare))) + jnp.pad(
        contact_mask.T, ((pixels, breadth), (height, spare))
    )
    above = jnp.pad(pair.reshape(pixels, channels), ((0, 2 * breadth), (0, 0)))
    held = (above.astype(f32) + marks.astype(f32)).astype(bf16)[None]
    block = cotangent.reshape(1, pixels, channels)
    cot_held = lax.optimization_barrier(jnp.maximum(block, jnp.finfo(bf16).min))
    rates = jnp.clip(dilations, 1, DMAX)
    for step in range(len(rounds) - 1):
        other = exchange(held, rounds[step])
        cot_other = exchange(cot_held if step else block, cot_rounds[step])
        held = lax.optimization_barrier(jnp.concatenate([held, other], axis=0))
        if step < len(rounds) - 2:
            cot_held = jnp.concatenate([cot_held, cot_other], axis=0)
            if step == len(rounds) - 3:
                cot_held, rates = lax.optimization_barrier((cot_held, rates))
            else:
                cot_held = lax.optimization_barrier(cot_held)
    near, far = held, exchange(held, rounds[-1])
    *near_parts, two_t = pl.pallas_call(
        functools.partial(near_kernel, plan),
        in_specs=[in_vmem] * 4,
        out_specs=[in_vmem] * 7,
        out_shape=shapes(*halves, ((9 * channels, channels), bf16)),
        scratch_shapes=[turned] * 2,
        compiler_params=pltpu.CompilerParams(vmem_limit_bytes=VMEM_LIMIT // 3),
        cost_estimate=pl.CostEstimate(
            flops=tokens * tokens * channels * 5 * hidden,
            bytes_accessed=8 * tokens * tokens * channels,
            transcendentals=3 * tokens * tokens * channels // 2,
        ),
    )(near, w_proj, w_gate, conv_two)
    cot_other, two_t = lax.optimization_barrier((cot_other, two_t))
    cot_near = jnp.concatenate([cot_held, cot_other], axis=0)
    cot_far = exchange(cot_near, cot_rounds[-1])
    whole = pltpu.VMEM((tokens, tokens, channels), f32)
    padded = pltpu.VMEM((tokens, line, channels), f32)
    bordered = pltpu.VMEM((line, line, channels), f32)
    tripled = pltpu.VMEM((line, tokens, 3 * channels), bf16)
    both = pltpu.VMEM((2,) + side[0], bf16)
    alone = pltpu.VMEM(rows, bf16)
    banded = pltpu.VMEM((3, line, tokens, channels), f32)
    flat = ((channels, tokens * tokens), bf16)
    sums = pltpu.VMEM((channels, 9 * channels), f32)
    output, *held = pl.pallas_call(
        functools.partial(forward_kernel, plan),
        in_specs=[in_smem] + [in_vmem] * 12,
        out_specs=[in_vmem] * 6,
        out_shape=shapes(
            ((pixels, channels), bf16),
            flat,
            flat,
            ((tokens, tokens, channels), f32),
            stat,
            stat,
        ),
        scratch_shapes=[pltpu.VMEM(*side), both, both, alone, alone, alone]
        + [turned] * 2
        + [pltpu.VMEM((hidden * (2 * height + PITCH), chips * tokens), f32)]
        + [pltpu.VMEM((2 * height // 8, chips, 8, tokens, hidden), bf16)]
        + [whole, padded, tripled, bordered, banded],
        compiler_params=pltpu.CompilerParams(vmem_limit_bytes=FORWARD_VMEM),
        cost_estimate=pl.CostEstimate(
            flops=tokens * tokens * channels * 40 * hidden,
            bytes_accessed=40 * tokens * tokens * channels,
            transcendentals=4 * tokens * tokens * channels,
        ),
    )(
        rates,
        far,
        w_proj,
        w_gate,
        w_out,
        conv_one,
        conv_two,
        *near_parts,
    )
    grad_pair, grad_one, grad_two = pl.pallas_call(
        functools.partial(backward_kernel, plan),
        in_specs=[in_smem] + [in_vmem] * 9,
        out_specs=[in_vmem] + [pl.BlockSpec(memory_space=pltpu.HBM)] * 2,
        out_shape=shapes(
            ((pixels, channels), bf16),
            ((9, channels, channels), f32),
            ((9, channels, channels), f32),
        ),
        scratch_shapes=[padded, tripled, tripled, bordered, sums, sums]
        + [pltpu.VMEM((9, channels, channels), f32)] * 2
        + [pltpu.SemaphoreType.DMA((6,))],
        compiler_params=pltpu.CompilerParams(vmem_limit_bytes=BACKWARD_VMEM),
    )(
        rates,
        cot_near,
        cot_far,
        conv_one,
        two_t,
        *held,
    )
    block = (height, breadth, channels)
    return output.reshape(block), grad_pair.reshape(block), grad_one, grad_two


def fits(pair, w_out, row_count, col_count):
    height, breadth, channels = pair.shape
    tokens = height * row_count
    powers = all(count & (count - 1) == 0 for count in (row_count, col_count))
    whole = (tokens + 2 * DMAX) ** 2 * channels
    return (
        powers
        and row_count * col_count >= 8
        and height * breadth == channels == w_out.shape[0]
        and breadth == 8
        and row_count // 2 * tokens == channels
        and whole * 60 <= VMEM_LIMIT
    )


def local(*arguments):
    pair, w_out = arguments[0], arguments[6]
    if fits(pair, w_out, lax.axis_size("row"), lax.axis_size("col")):
        return replicated(*arguments)
    return sharded(*arguments)


def solution(mesh):
    in_specs = (
        P("row", "col", None),
        P("row", "col"),
        P("row", "col"),
        P(),
        P(),
        P(),
        P(),
        P(),
        P(),
        P("row", "col", None),
    )
    out_specs = (P("row", "col", None), P("row", "col", None), P(), P())
    return jax.shard_map(local, mesh=mesh, in_specs=in_specs, out_specs=out_specs, check_vma=False)
```

```python
import functools

import jax
import jax.numpy as jnp
from jax import lax
from jax.experimental import pallas as pl
from jax.experimental.pallas import tpu as pltpu
from jax.sharding import PartitionSpec as P

DMAX = 8
VMEM_LIMIT = 48 * 1024 * 1024
PITCH = 8
FORWARD_VMEM = 32 * 1024 * 1024
BACKWARD_VMEM = 36 * 1024 * 1024


EPSILON = 1e-05


def with_halo(block, sides, width):
    for axis, dim in sides:
        count = lax.axis_size(axis)
        forward = [(i, i + 1) for i in range(count - 1)]
        backward = [(target, source) for source, target in forward]
        low = lax.ppermute(
            lax.slice_in_dim(block, block.shape[dim] - width, None, axis=dim), axis, forward
        )
        high = lax.ppermute(lax.slice_in_dim(block, 0, width, axis=dim), axis, backward)
        block = jnp.concatenate([low, block, high], axis=dim)
    return block


def broadcast(x, axis, root):
    mine = lax.axis_index(axis) == root
    return lax.psum(jnp.where(mine, x, jnp.zeros_like(x)), axis)


def layer_norm(values, axis=-1):
    centre = values - jnp.mean(values, axis=axis, keepdims=True)
    spread = jnp.mean(centre * centre, axis=axis, keepdims=True)
    return centre * lax.rsqrt(spread + EPSILON)


def with_rim(field):
    return with_halo(field, (("row", 0), ("col", 1)), DMAX)


def gather_taps(padded, dilation, mirrored, height, breadth):
    windows = []
    for tap_index in range(9):
        row_tap = tap_index // 3
        col_tap = tap_index % 3
        if mirrored:
            row_tap = 2 - row_tap
            col_tap = 2 - col_tap
        row_start = DMAX + (row_tap - 1) * dilation
        col_start = DMAX + (col_tap - 1) * dilation
        windows.append(
            lax.dynamic_slice(
                padded, (row_start, col_start, jnp.int32(0)), (height, breadth, padded.shape[2])
            )
        )
    return jnp.concatenate(windows, axis=2).reshape(height * breadth, -1)


def sharded(
    pair, pair_mask, contact_mask, dilations, w_proj, w_gate, w_out, conv_one, conv_two, cotangent
):
    height, breadth, channels = pair.shape
    hidden = w_out.shape[0]
    row_count = lax.axis_size("row")
    col_count = lax.axis_size("col")
    ratio = col_count // row_count
    row_place = lax.axis_index("row")
    col_place = lax.axis_index("col")
    tokens = breadth * col_count
    pixels = height * breadth
    pair_flat = pair.astype(jnp.float32).reshape(pixels, channels)
    normed = layer_norm(pair_flat).astype(jnp.bfloat16)
    projected = jnp.dot(normed, w_proj, preferred_element_type=jnp.float32)
    mask_col = pair_mask.reshape(pixels, 1).astype(jnp.float32)
    left_side = (
        (mask_col * jax.nn.sigmoid(projected[:, hidden : 2 * hidden]) * projected[:, :hidden])
        .astype(jnp.bfloat16)
        .reshape(height, breadth, hidden)
    )
    right_side = (
        (
            mask_col
            * jax.nn.sigmoid(projected[:, 3 * hidden :])
            * projected[:, 2 * hidden : 3 * hidden]
        )
        .astype(jnp.bfloat16)
        .reshape(height, breadth, hidden)
    )
    right_all = lax.all_gather(right_side, "col", axis=1, tiled=True)
    offset = jnp.clip(col_place * breadth - row_place * height, 0, height - breadth)
    right_local = lax.dynamic_slice_in_dim(right_all, offset, breadth, 0)
    right_rows = broadcast(right_local, "row", col_place // ratio)
    products = jnp.einsum(
        "ikh,jkh->ijh",
        lax.all_gather(left_side, "col", axis=1, tiled=True),
        right_rows,
        preferred_element_type=jnp.float32,
    )
    product_norm = layer_norm(products.reshape(pixels, hidden)).astype(jnp.bfloat16)
    gating = jax.nn.sigmoid(jnp.dot(normed, w_gate, preferred_element_type=jnp.float32))
    updated = (
        pair_flat + gating * jnp.dot(product_norm, w_out, preferred_element_type=jnp.float32)
    ).astype(jnp.bfloat16)
    updated_f = updated.astype(jnp.float32)
    centre = updated_f - jnp.mean(updated_f, axis=-1, keepdims=True)
    inv_spread = lax.rsqrt(jnp.mean(centre * centre, axis=-1, keepdims=True) + EPSILON)
    scaled = centre * inv_spread
    contact = contact_mask.reshape(pixels, 1).astype(jnp.float32)
    first_in = (scaled * contact).astype(jnp.bfloat16).reshape(height, breadth, channels)
    rate_one = dilations[0]
    rate_two = dilations[1]
    first_taps = gather_taps(with_rim(first_in), rate_one, False, height, breadth)
    first_pre = jnp.dot(
        first_taps, conv_one.reshape(9 * channels, channels), preferred_element_type=jnp.float32
    )
    sigma = jax.nn.sigmoid(first_pre)
    second_in = (first_pre * sigma).astype(jnp.bfloat16).reshape(height, breadth, channels)
    second_taps = gather_taps(with_rim(second_in), rate_two, False, height, breadth)
    second_pre = jnp.dot(
        second_taps, conv_two.reshape(9 * channels, channels), preferred_element_type=jnp.float32
    )
    output = (updated_f + second_pre).astype(jnp.bfloat16).reshape(height, breadth, channels)
    cot_flat = cotangent.reshape(pixels, channels)
    grad_two = (
        lax.dot_general(
            second_taps, cot_flat, (((0,), (0,)), ((), ())), preferred_element_type=jnp.float32
        ).reshape(9, channels, channels)
        / tokens
    )
    cot_taps = gather_taps(with_rim(cotangent), rate_two, True, height, breadth)
    grad_hidden = jnp.dot(
        cot_taps,
        conv_two.transpose(0, 2, 1).reshape(9 * channels, channels),
        preferred_element_type=jnp.float32,
    )
    grad_pre = (grad_hidden * sigma * (1.0 + first_pre * (1.0 - sigma))).astype(jnp.bfloat16)
    grad_one = (
        lax.dot_general(
            first_taps, grad_pre, (((0,), (0,)), ((), ())), preferred_element_type=jnp.float32
        ).reshape(9, channels, channels)
        / tokens
    )
    grad_taps = gather_taps(
        with_rim(grad_pre.reshape(height, breadth, channels)), rate_one, True, height, breadth
    )
    grad_input = (
        jnp.dot(
            grad_taps,
            conv_one.transpose(0, 2, 1).reshape(9 * channels, channels),
            preferred_element_type=jnp.float32,
        )
        * contact
    )
    grad_norm = inv_spread * (
        grad_input
        - jnp.mean(grad_input, axis=-1, keepdims=True)
        - scaled * jnp.mean(grad_input * scaled, axis=-1, keepdims=True)
    )
    grad_pair = (
        (cot_flat.astype(jnp.float32) + grad_norm)
        .astype(jnp.bfloat16)
        .reshape(height, breadth, channels)
    )
    grad_one, grad_two = lax.psum((grad_one, grad_two), ("row", "col"))
    return (output, grad_pair, grad_one, grad_two)


def halvings(axis, count):
    return [(axis, count >> step) for step in range(1, count.bit_length())]


def exchange_plan(row_count, col_count):
    rows, cols = halvings("row", row_count), halvings("col", col_count)
    return cols + rows, rows[:-1] + cols + rows[-1:]


def exchange(held, hop):
    axis, distance = hop
    return lax.ppermute(held, axis, [(i, i ^ distance) for i in range(lax.axis_size(axis))])


def place_of(position, rounds, row_place, col_place):
    row, col = row_place, col_place
    for step, (axis, distance) in enumerate(rounds):
        bit = ((position >> step) & 1) * distance
        if axis == "row":
            row = row ^ bit
        else:
            col = col ^ bit
    return row, col


def slot_of(row_change, col_change, rounds):
    slot = 0
    for step, (axis, distance) in enumerate(rounds[:-1]):
        change = row_change if axis == "row" else col_change
        slot = slot | (((change // distance) & 1) << step)
    return slot


def sigmoid(values):
    return 0.5 + 0.5 * jnp.tanh(0.5 * values)


def matmul(left, right):
    return jnp.dot(left, right, preferred_element_type=jnp.float32)


def matmul_by_rows(left, right):
    rows = 256
    return jnp.concatenate(
        [matmul(left[i : i + rows], right) for i in range(0, left.shape[0], rows)], axis=0
    )


def matmul_nt(left, right):
    return lax.dot_general(
        left, right, (((1,), (1,)), ((), ())), preferred_element_type=jnp.float32
    )


def project_half(
    plan, core, pairs, w_proj, w_gate, left, right, swapped, gating, contact, start, turned
):
    rounds, _, height, breadth, tokens = plan
    channels, hidden = w_gate.shape[0], w_gate.shape[1]
    col_count, chips = tokens // breadth, tokens // height // 2
    row_place, col_place = lax.axis_index("row"), lax.axis_index("col")
    lane = lax.broadcasted_iota(jnp.int32, (height, breadth, channels), 2)
    place = lax.broadcasted_iota(jnp.int32, (height, breadth, channels), 0)
    own_lane = jnp.where((lane % height == place) & (lane < 2 * height), 1.0, 0.0)
    pick_lane = lax.broadcasted_iota(jnp.int32, (channels, 2 * channels), 0)
    pick_half = lax.broadcasted_iota(jnp.int32, (channels, 2 * channels), 1) // channels
    pick = jnp.where(pick_lane // height == pick_half, 1.0, 0.0).astype(jnp.bfloat16)
    pixels = height * breadth
    rows = 8
    for first in range(0, height, rows):
        values, masks = [], []
        for chip in range(chips):
            row_change = (chip * 2 + core) ^ row_place
            blocks, marks = [], []
            for col in range(col_count):
                col_change = col_place ^ col
                slot = slot_of(row_change, col_change, rounds)
                blocks.append(
                    pairs[slot, first * breadth : (first + rows) * breadth, :]
                    .astype(jnp.float32)
                    .reshape(rows, breadth, channels)
                )
                mark = pairs[slot, pixels:, :].astype(jnp.float32)[:breadth]
                marks.append(mark[None] * own_lane[first : first + rows])
            values.append(jnp.concatenate(blocks, axis=1).reshape(rows * tokens, channels))
            masks.append(jnp.concatenate(marks, axis=1).reshape(rows * tokens, channels))
        values = jnp.concatenate(values, axis=0)
        masks = matmul(jnp.concatenate(masks, axis=0).astype(jnp.bfloat16), pick)
        normed = layer_norm(values)
        gates = sigmoid(matmul(normed.astype(jnp.bfloat16), w_gate[...]))
        masked = (normed * masks[:, :channels]).astype(jnp.bfloat16)
        projected = matmul(masked, w_proj[...])
        sides = [
            sigmoid(projected[:, (2 * side + 1) * hidden : (2 * side + 2) * hidden])
            * projected[:, 2 * side * hidden : (2 * side + 1) * hidden]
            for side in range(2)
        ]
        for side, target in zip(sides, turned):
            side = side.reshape(chips, rows, tokens, hidden)
            for row in range(rows):
                strip = jnp.concatenate([side[chip, row] for chip in range(chips)], axis=0)
                target[pl.ds(first + row, hidden, stride=height + PITCH), :] = strip.T
        shape = (chips, rows, tokens, channels)
        span = slice(first, first + rows)
        gating[:, span] = gates.astype(jnp.bfloat16).reshape(shape)
        contact[:, span] = masks[:, channels:].astype(jnp.bfloat16).reshape(shape)
        start[:, span] = values.astype(jnp.bfloat16).reshape(shape)
    shape = (hidden, height + PITCH, chips * tokens)
    mine, other = turned[0][...], turned[1][...]
    for target, source in (
        (left, mine),
        (right, other),
        (swapped, pltpu.roll(other, tokens, 1)),
    ):
        target[...] = source.reshape(shape)[:, :height].astype(jnp.bfloat16)


def near_kernel(
    plan,
    near,
    w_proj,
    w_gate,
    two,
    left,
    right,
    swapped,
    gating,
    contact,
    start,
    two_t,
    turned_left,
    turned_right,
):
    core = lax.axis_index("row") % 2
    channels = two.shape[1]
    for tap in range(9):
        two_t[tap * channels : (tap + 1) * channels] = two[tap].T
    project_half(
        plan,
        core,
        near,
        w_proj,
        w_gate,
        left,
        right,
        swapped,
        gating,
        contact,
        start,
        (turned_left, turned_right),
    )


def spread(source, rows, pad, rate, target):
    tokens, channels = target.shape[1], source.shape[2]
    for tap in range(3):
        first = DMAX + (tap - 1) * rate if tap != 1 else DMAX
        moved = source[pl.ds(pad + rows.start, rows.size), pl.ds(first, tokens), :]
        target[pl.ds(DMAX + rows.start, rows.size), :, tap * channels : (tap + 1) * channels] = (
            moved.astype(jnp.bfloat16)
        )


def taps(source, first, count, rate):
    tokens = source.shape[1]
    views = [
        source[pl.ds(DMAX + first + (tap - 1) * rate, count)].reshape(count * tokens, -1)
        for tap in range(3)
    ]
    return jnp.concatenate(views, axis=1)


def windows(source, rate, row_start, col_start, height, breadth):
    views = [
        source[
            pl.ds(row_start + DMAX + (tap // 3 - 1) * rate, height),
            pl.ds(col_start + DMAX + (tap % 3 - 1) * rate, breadth),
            :,
        ].reshape(height * breadth, -1)
        for tap in range(9)
    ]
    return jnp.concatenate(views, axis=1).astype(jnp.bfloat16)


def row_taps(strips, first, count, rate):
    views = [
        strips[tap, pl.ds(DMAX + first + ((tap - 1) * rate if tap != 1 else 0), count)]
        for tap in range(3)
    ]
    return views[0] + views[1] + views[2]


def clear_ends(strips, tokens):
    for tap in (0, 2):
        for rows in (slice(0, DMAX), slice(DMAX + tokens, 2 * DMAX + tokens)):
            strips[tap, rows] = jnp.zeros((DMAX,) + strips.shape[2:], jnp.float32)


def column_taps(source, weight, rate, first, count, strips):
    tokens = strips.shape[2]
    columns = [DMAX - rate, DMAX, DMAX + rate]
    flat = jnp.concatenate(
        [
            source[pl.ds(first, count), pl.ds(column, tokens), :].reshape(count * tokens, -1)
            for column in columns
        ],
        axis=1,
    ).astype(jnp.bfloat16)
    square = jnp.concatenate(
        [
            jnp.concatenate([weight(3 * row + col) for row in range(3)], axis=1)
            for col in range(3)
        ],
        axis=0,
    )
    result = matmul_by_rows(flat, square)
    channels = strips.shape[3]
    for tap in range(3):
        strips[tap, pl.ds(DMAX + first, count)] = result[
            :, tap * channels : (tap + 1) * channels
        ].reshape(count, tokens, channels)


def lanes(step, size):
    return pl.ds(pl.multiple_of(step * size, size), size)


def clear_border(target, tokens):
    line, channels = target.shape[1], target.shape[2]
    border = jnp.zeros((DMAX, line, channels), target.dtype)
    rim = jnp.zeros((tokens, DMAX, channels), target.dtype)
    if target.shape[0] > tokens:
        target[0:DMAX] = border
        target[DMAX + tokens :] = border
    if line > tokens:
        rows = slice(target.shape[0] - tokens - DMAX, target.shape[0] - DMAX)
        if target.shape[0] == tokens:
            rows = slice(0, tokens)
        target[rows, 0:DMAX, :] = rim
        target[rows, DMAX + tokens :, :] = rim


def forward_kernel(
    plan,
    dilations,
    far,
    w_proj,
    w_gate,
    w_out,
    one,
    near_left,
    near_right,
    near_swapped,
    near_gating,
    near_contact,
    near_start,
    strips,
    flipped,
    mine,
    own_contact,
    far_left,
    right,
    swapped,
    far_gating,
    far_contact,
    far_start,
    turned_left,
    turned_right,
    products,
    normed,
    updated,
    field,
):
    _, _, height, breadth, tokens = plan
    hidden, channels = w_out.shape
    pixels = height * breadth
    chips = tokens // height // 2
    row_place, col_place = lax.axis_index("row"), lax.axis_index("col")
    core = row_place % 2
    rate_one = dilations[0]
    inside = slice(DMAX, DMAX + tokens)
    clear_border(field, tokens)
    clear_ends(strips, tokens)

    right[core] = near_right[...]
    swapped[core] = near_swapped[...]
    project_half(
        plan,
        1 - core,
        far,
        w_proj,
        w_gate,
        far_left,
        right.at[1 - core],
        swapped.at[1 - core],
        far_gating,
        far_contact,
        far_start,
        (turned_left, turned_right),
    )

    lane = lax.broadcasted_iota(jnp.int32, (height, chips * tokens), 1)
    low = jnp.where(lane < tokens, 1.0, 0.0).astype(jnp.bfloat16)
    high = jnp.where(lane < tokens, 0.0, 1.0).astype(jnp.bfloat16)
    batch = 64
    pitch = 2 * height + PITCH

    def multiply(step, carry):
        for part in range(batch):
            h = step * batch + part
            ahead = [right[0, h], right[1, h]]
            back = [swapped[0, h], swapped[1, h]]
            strips = [strip * low for strip in ahead + back]
            strips += [strip * high for strip in back + ahead]
            mine = jnp.concatenate([near_left[h], far_left[h]], axis=0)
            products[pl.ds(pl.multiple_of(h * pitch, 8), 2 * height), :] = matmul_nt(
                mine, jnp.concatenate(strips, axis=0)
            )
        return carry

    lax.fori_loop(0, hidden // batch, multiply, 0)

    chunk = 8
    size = chunk * tokens

    halves = (
        (core, near_gating, near_contact, near_start),
        (1 - core, far_gating, far_contact, far_start),
    )
    parts = height // chunk

    def normalise(step):
        half, first = step // parts, step % parts * chunk
        for row in range(chunk):
            strip = products[pl.ds(half * height + first + row, hidden, stride=pitch), :]
            strip = layer_norm(strip, axis=0).astype(jnp.bfloat16).T
            for chip in range(chips):
                normed[step, chip, row] = strip[chip * tokens : (chip + 1) * tokens]

    def update(step):
        first = step % parts * chunk
        side, gating, contact, start = halves[step // parts]
        change = matmul(normed[step].reshape(chips * size, hidden), w_out[...])
        change = change.reshape(chips, chunk, tokens, channels)
        rows = pl.ds(first, chunk)
        fresh = start[:, rows].astype(jnp.float32) + gating[:, rows].astype(jnp.float32) * change
        fresh = fresh.astype(jnp.bfloat16).astype(jnp.float32)
        first_in = layer_norm(fresh) * contact[:, rows].astype(jnp.float32)
        if step < parts:
            updated[:, rows] = fresh
        for chip in range(chips):
            base = (chip * 2 + side) * height + first
            field[pl.ds(base, chunk), inside, :] = first_in[chip]
            flipped[:, pl.ds(pl.multiple_of(base * tokens, size), size)] = (
                first_in[chip].reshape(size, channels).astype(jnp.bfloat16).T
            )

    def first_conv(step):
        side = halves[step // parts][0]
        for chip in range(chips):
            base = (chip * 2 + side) * height + step % parts * chunk
            column_taps(field, lambda tap: one[tap], rate_one, base, chunk, strips)

    count = 2 * parts
    for step in range(count + 2):
        if step < count:
            normalise(step)
        if 1 <= step <= count:
            update(step - 1)
        if step >= 2:
            first_conv(step - 2)

    cols = pl.ds(pl.multiple_of(col_place * breadth, breadth), breadth)
    mine[...] = updated[row_place // 2, :, cols, :].reshape(pixels, channels)
    marks = near_contact[row_place // 2].astype(jnp.float32)
    place_col = lax.broadcasted_iota(jnp.int32, (tokens, channels), 0) // breadth
    marks = jnp.where((place_col == col_place)[None], marks, 0.0)
    marks = marks.reshape(height, tokens // breadth, breadth, channels)
    own_contact[...] = jnp.sum(marks, axis=1).reshape(pixels, channels)


def backward_kernel(
    plan,
    dilations,
    cot_near,
    cot_far,
    one,
    two,
    two_t,
    strips,
    flipped,
    mine,
    own_contact,
    output,
    grad_pair,
    grad_one,
    grad_two,
    field,
    wide_cot,
    wide_pre,
    grad_pre,
    second,
    sum_one,
    sum_two,
    scaled_one,
    scaled_two,
    sent,
):
    _, cot_rounds, height, breadth, tokens = plan
    channels = one.shape[2]
    pixels = height * breadth
    row_place, col_place = lax.axis_index("row"), lax.axis_index("col")
    rate_one, rate_two = dilations[0], dilations[1]
    half = cot_far.shape[0]
    inside = slice(DMAX, DMAX + tokens)
    for target in (field, wide_cot, wide_pre, grad_pre, second):
        clear_border(target, tokens)

    several = 8

    def place_cot(source, base):
        def body(step, carry):
            for i in range(several):
                slot = step * several + i
                row, col = place_of(base + slot, cot_rounds, row_place, col_place)
                cols = pl.ds(pl.multiple_of(DMAX + col * breadth, breadth), breadth)
                field[pl.ds(row * height, height), cols, :] = (
                    source[slot].astype(jnp.float32).reshape(height, breadth, channels)
                )
            return carry

        lax.fori_loop(0, half // several, body, 0)

    place_cot(cot_near, 0)
    place_cot(cot_far, half)
    chunk = 16
    size = chunk * tokens
    steps = tokens // chunk

    def spread_cot(step, carry):
        spread(field, pl.ds(step * chunk, chunk), 0, -rate_two, wide_cot)
        return carry

    lax.fori_loop(0, steps, spread_cot, 0)

    def back_two(step):
        first = step * chunk
        rows = pl.ds(DMAX + first, chunk)
        pre = row_taps(strips, first, chunk, rate_one)
        sigma = sigmoid(pre)
        second_in = pre * sigma
        second[rows, inside, :] = second_in
        factor = sigma * (1.0 + pre * (1.0 - sigma))
        turned = second_in.reshape(size, channels).astype(jnp.bfloat16).T
        shifted = taps(wide_cot, first, chunk, -rate_two)
        before = matmul_by_rows(shifted, two_t[...]).reshape(chunk, tokens, channels)
        grad_pre[rows, inside, :] = (before * factor).astype(jnp.bfloat16).astype(jnp.float32)
        part = matmul(turned, shifted)
        sum_two[...] = part if step == 0 else sum_two[...] + part

    def spread_pre(step):
        spread(grad_pre, pl.ds(step * chunk, chunk), DMAX, -rate_one, wide_pre)

    def back_one(step):
        shifted = taps(wide_pre, step * chunk, chunk, -rate_one)
        part = matmul(flipped[:, step * size : (step + 1) * size], shifted)
        sum_one[...] = part if step == 0 else sum_one[...] + part

    def finish(total, scaled, target, row):
        for tap in range(3 * row, 3 * row + 3):
            columns = slice(tap * channels, (tap + 1) * channels)
            scaled[tap] = total[:, columns] * (1.0 / tokens)
        taps_done = pl.ds(3 * row, 3)
        copy = pltpu.make_async_copy(
            scaled.at[taps_done], target.at[taps_done], sent.at[len(copies)]
        )
        copy.start()
        copies.append(copy)

    copies = []
    for step in range(steps):
        if step >= 3:
            back_one(step - 3)
        if step >= 1:
            spread_pre(step - 1)
        back_two(step)
    spread_pre(steps - 1)
    for row in range(3):
        finish(sum_two, scaled_two, grad_two, row)
    for step in range(max(steps - 3, 0), steps - 1):
        back_one(step)

    spot = (row_place * height, col_place * breadth, height, breadth)
    second_pre = matmul(
        windows(second, rate_two, *spot), two[...].reshape(9 * channels, channels)
    )
    output[...] = (mine[...] + second_pre).astype(jnp.bfloat16)
    one_rows = [one[tap] for tap in range(9)]
    grad_input = own_contact[...] * matmul_nt(
        windows(grad_pre, -rate_one, *spot),
        jnp.concatenate(one_rows, axis=1),
    )
    centre = mine[...] - jnp.mean(mine[...], axis=-1, keepdims=True)
    inv_spread = lax.rsqrt(jnp.mean(centre * centre, axis=-1, keepdims=True) + EPSILON)
    scaled = centre * inv_spread
    grad_norm = inv_spread * (
        grad_input
        - jnp.mean(grad_input, axis=-1, keepdims=True)
        - scaled * jnp.mean(grad_input * scaled, axis=-1, keepdims=True)
    )
    grad_pair[...] = (cot_near[0].astype(jnp.float32) + grad_norm).astype(jnp.bfloat16)

    last = steps - 1
    for row in range(3):
        columns = slice(3 * row * channels, 3 * (row + 1) * channels)
        moved = pl.ds(DMAX + last * chunk - (row - 1) * rate_one, chunk)
        sum_one[:, columns] += matmul(
            flipped[:, last * size : (last + 1) * size], wide_pre[moved].reshape(size, -1)
        )
        finish(sum_one, scaled_one, grad_one, row)
    for copy in copies:
        copy.wait()


def replicated(
    pair, pair_mask, contact_mask, dilations, w_proj, w_gate, w_out, conv_one, conv_two, cotangent
):
    height, breadth, channels = pair.shape
    hidden = w_out.shape[0]
    row_count, col_count = lax.axis_size("row"), lax.axis_size("col")
    tokens = height * row_count
    pixels = height * breadth
    rounds, cot_rounds = exchange_plan(row_count, col_count)
    f32, bf16 = jnp.float32, jnp.bfloat16
    plan = (rounds, cot_rounds, height, breadth, tokens)
    chips = row_count // 2
    line = tokens + 2 * DMAX
    in_vmem = pl.BlockSpec(memory_space=pltpu.VMEM)
    side = ((hidden, height, chips * tokens), bf16)
    rows = (chips, height, tokens, channels)
    halves = [side] * 3 + [(rows, bf16)] * 3
    turned = pltpu.VMEM((hidden * (height + PITCH), chips * tokens), f32)
    stat = ((pixels, channels), f32)

    def shapes(*entries):
        return [jax.ShapeDtypeStruct(shape, dtype) for shape, dtype in entries]

    in_smem = pl.BlockSpec(memory_space=pltpu.SMEM)
    spare = channels - 2 * height
    marks = jnp.pad(pair_mask.T, ((pixels, breadth), (0, height + spare))) + jnp.pad(
        contact_mask.T, ((pixels, breadth), (height, spare))
    )
    above = jnp.pad(pair.reshape(pixels, channels), ((0, 2 * breadth), (0, 0)))
    held = (above.astype(f32) + marks.astype(f32)).astype(bf16)[None]
    block = cotangent.reshape(1, pixels, channels)
    cot_held = lax.optimization_barrier(jnp.maximum(block, jnp.finfo(bf16).min))
    rates = jnp.clip(dilations, 1, DMAX)
    for step in range(len(rounds) - 1):
        other = exchange(held, rounds[step])
        cot_other = exchange(cot_held if step else block, cot_rounds[step])
        held = lax.optimization_barrier(jnp.concatenate([held, other], axis=0))
        if step < len(rounds) - 2:
            cot_held = jnp.concatenate([cot_held, cot_other], axis=0)
            if step == len(rounds) - 3:
                cot_held, rates = lax.optimization_barrier((cot_held, rates))
            else:
                cot_held = lax.optimization_barrier(cot_held)
    near, far = held, exchange(held, rounds[-1])
    *near_parts, two_t = pl.pallas_call(
        functools.partial(near_kernel, plan),
        in_specs=[in_vmem] * 4,
        out_specs=[in_vmem] * 7,
        out_shape=shapes(*halves, ((9 * channels, channels), bf16)),
        scratch_shapes=[turned] * 2,
        compiler_params=pltpu.CompilerParams(vmem_limit_bytes=VMEM_LIMIT // 3),
        cost_estimate=pl.CostEstimate(
            flops=tokens * tokens * channels * 5 * hidden,
            bytes_accessed=8 * tokens * tokens * channels,
            transcendentals=3 * tokens * tokens * channels // 2,
        ),
    )(near, w_proj, w_gate, conv_two)
    cot_other, two_t = lax.optimization_barrier((cot_other, two_t))
    cot_near = jnp.concatenate([cot_held, cot_other], axis=0)
    cot_far = exchange(cot_near, cot_rounds[-1])
    padded = pltpu.VMEM((tokens, line, channels), f32)
    bordered = pltpu.VMEM((line, line, channels), f32)
    tripled = pltpu.VMEM((line, tokens, 3 * channels), bf16)
    both = pltpu.VMEM((2,) + side[0], bf16)
    alone = pltpu.VMEM(rows, bf16)
    flat = ((channels, tokens * tokens), bf16)
    sums = pltpu.VMEM((channels, 9 * channels), f32)
    held = pl.pallas_call(
        functools.partial(forward_kernel, plan),
        in_specs=[in_smem] + [in_vmem] * 11,
        out_specs=[in_vmem] * 4,
        out_shape=shapes(((3, line, tokens, channels), f32), flat, stat, stat),
        scratch_shapes=[pltpu.VMEM(*side), both, both, alone, alone, alone]
        + [turned] * 2
        + [pltpu.VMEM((hidden * (2 * height + PITCH), chips * tokens), f32)]
        + [pltpu.VMEM((2 * height // 8, chips, 8, tokens, hidden), bf16)]
        + [pltpu.VMEM(rows, f32), padded],
        compiler_params=pltpu.CompilerParams(vmem_limit_bytes=FORWARD_VMEM),
        cost_estimate=pl.CostEstimate(
            flops=tokens * tokens * channels * 30 * hidden,
            bytes_accessed=40 * tokens * tokens * channels,
            transcendentals=2 * tokens * tokens * channels,
        ),
    )(
        rates,
        far,
        w_proj,
        w_gate,
        w_out,
        conv_one,
        *near_parts,
    )
    output, grad_pair, grad_one, grad_two = pl.pallas_call(
        functools.partial(backward_kernel, plan),
        in_specs=[in_smem] + [in_vmem] * 9,
        out_specs=[in_vmem] * 2 + [pl.BlockSpec(memory_space=pltpu.HBM)] * 2,
        out_shape=shapes(
            ((pixels, channels), bf16),
            ((pixels, channels), bf16),
            ((9, channels, channels), f32),
            ((9, channels, channels), f32),
        ),
        scratch_shapes=[padded, tripled, tripled, bordered, bordered, sums, sums]
        + [pltpu.VMEM((9, channels, channels), f32)] * 2
        + [pltpu.SemaphoreType.DMA((6,))],
        compiler_params=pltpu.CompilerParams(vmem_limit_bytes=BACKWARD_VMEM),
    )(
        rates,
        cot_near,
        cot_far,
        conv_one,
        conv_two,
        two_t,
        *held,
    )
    block = (height, breadth, channels)
    return output.reshape(block), grad_pair.reshape(block), grad_one, grad_two


def fits(pair, w_out, row_count, col_count):
    height, breadth, channels = pair.shape
    tokens = height * row_count
    powers = all(count & (count - 1) == 0 for count in (row_count, col_count))
    whole = (tokens + 2 * DMAX) ** 2 * channels
    return (
        powers
        and row_count * col_count >= 8
        and height * breadth == channels == w_out.shape[0]
        and breadth == 8
        and row_count // 2 * tokens == channels
        and whole * 60 <= VMEM_LIMIT
    )


def local(*arguments):
    pair, w_out = arguments[0], arguments[6]
    if fits(pair, w_out, lax.axis_size("row"), lax.axis_size("col")):
        return replicated(*arguments)
    return sharded(*arguments)


def solution(mesh):
    in_specs = (
        P("row", "col", None),
        P("row", "col"),
        P("row", "col"),
        P(),
        P(),
        P(),
        P(),
        P(),
        P(),
        P("row", "col", None),
    )
    out_specs = (P("row", "col", None), P("row", "col", None), P(), P())
    return jax.shard_map(local, mesh=mesh, in_specs=in_specs, out_specs=out_specs, check_vma=False)
```

```python
import functools

import jax
import jax.numpy as jnp
from jax import lax
from jax.experimental import pallas as pl
from jax.experimental.pallas import tpu as pltpu
from jax.sharding import PartitionSpec as P

DMAX = 8
VMEM_LIMIT = 48 * 1024 * 1024
PITCH = 8
FORWARD_VMEM = 32 * 1024 * 1024
BACKWARD_VMEM = 36 * 1024 * 1024


EPSILON = 1e-05


def with_halo(block, sides, width):
    for axis, dim in sides:
        count = lax.axis_size(axis)
        forward = [(i, i + 1) for i in range(count - 1)]
        backward = [(target, source) for source, target in forward]
        low = lax.ppermute(
            lax.slice_in_dim(block, block.shape[dim] - width, None, axis=dim), axis, forward
        )
        high = lax.ppermute(lax.slice_in_dim(block, 0, width, axis=dim), axis, backward)
        block = jnp.concatenate([low, block, high], axis=dim)
    return block


def broadcast(x, axis, root):
    mine = lax.axis_index(axis) == root
    return lax.psum(jnp.where(mine, x, jnp.zeros_like(x)), axis)


def layer_norm(values, axis=-1):
    centre = values - jnp.mean(values, axis=axis, keepdims=True)
    spread = jnp.mean(centre * centre, axis=axis, keepdims=True)
    return centre * lax.rsqrt(spread + EPSILON)


def with_rim(field):
    return with_halo(field, (("row", 0), ("col", 1)), DMAX)


def gather_taps(padded, dilation, mirrored, height, breadth):
    windows = []
    for tap_index in range(9):
        row_tap = tap_index // 3
        col_tap = tap_index % 3
        if mirrored:
            row_tap = 2 - row_tap
            col_tap = 2 - col_tap
        row_start = DMAX + (row_tap - 1) * dilation
        col_start = DMAX + (col_tap - 1) * dilation
        windows.append(
            lax.dynamic_slice(
                padded, (row_start, col_start, jnp.int32(0)), (height, breadth, padded.shape[2])
            )
        )
    return jnp.concatenate(windows, axis=2).reshape(height * breadth, -1)


def sharded(
    pair, pair_mask, contact_mask, dilations, w_proj, w_gate, w_out, conv_one, conv_two, cotangent
):
    height, breadth, channels = pair.shape
    hidden = w_out.shape[0]
    row_count = lax.axis_size("row")
    col_count = lax.axis_size("col")
    ratio = col_count // row_count
    row_place = lax.axis_index("row")
    col_place = lax.axis_index("col")
    tokens = breadth * col_count
    pixels = height * breadth
    pair_flat = pair.astype(jnp.float32).reshape(pixels, channels)
    normed = layer_norm(pair_flat).astype(jnp.bfloat16)
    projected = jnp.dot(normed, w_proj, preferred_element_type=jnp.float32)
    mask_col = pair_mask.reshape(pixels, 1).astype(jnp.float32)
    left_side = (
        (mask_col * jax.nn.sigmoid(projected[:, hidden : 2 * hidden]) * projected[:, :hidden])
        .astype(jnp.bfloat16)
        .reshape(height, breadth, hidden)
    )
    right_side = (
        (
            mask_col
            * jax.nn.sigmoid(projected[:, 3 * hidden :])
            * projected[:, 2 * hidden : 3 * hidden]
        )
        .astype(jnp.bfloat16)
        .reshape(height, breadth, hidden)
    )
    right_all = lax.all_gather(right_side, "col", axis=1, tiled=True)
    offset = jnp.clip(col_place * breadth - row_place * height, 0, height - breadth)
    right_local = lax.dynamic_slice_in_dim(right_all, offset, breadth, 0)
    right_rows = broadcast(right_local, "row", col_place // ratio)
    products = jnp.einsum(
        "ikh,jkh->ijh",
        lax.all_gather(left_side, "col", axis=1, tiled=True),
        right_rows,
        preferred_element_type=jnp.float32,
    )
    product_norm = layer_norm(products.reshape(pixels, hidden)).astype(jnp.bfloat16)
    gating = jax.nn.sigmoid(jnp.dot(normed, w_gate, preferred_element_type=jnp.float32))
    updated = (
        pair_flat + gating * jnp.dot(product_norm, w_out, preferred_element_type=jnp.float32)
    ).astype(jnp.bfloat16)
    updated_f = updated.astype(jnp.float32)
    centre = updated_f - jnp.mean(updated_f, axis=-1, keepdims=True)
    inv_spread = lax.rsqrt(jnp.mean(centre * centre, axis=-1, keepdims=True) + EPSILON)
    scaled = centre * inv_spread
    contact = contact_mask.reshape(pixels, 1).astype(jnp.float32)
    first_in = (scaled * contact).astype(jnp.bfloat16).reshape(height, breadth, channels)
    rate_one = dilations[0]
    rate_two = dilations[1]
    first_taps = gather_taps(with_rim(first_in), rate_one, False, height, breadth)
    first_pre = jnp.dot(
        first_taps, conv_one.reshape(9 * channels, channels), preferred_element_type=jnp.float32
    )
    sigma = jax.nn.sigmoid(first_pre)
    second_in = (first_pre * sigma).astype(jnp.bfloat16).reshape(height, breadth, channels)
    second_taps = gather_taps(with_rim(second_in), rate_two, False, height, breadth)
    second_pre = jnp.dot(
        second_taps, conv_two.reshape(9 * channels, channels), preferred_element_type=jnp.float32
    )
    output = (updated_f + second_pre).astype(jnp.bfloat16).reshape(height, breadth, channels)
    cot_flat = cotangent.reshape(pixels, channels)
    grad_two = (
        lax.dot_general(
            second_taps, cot_flat, (((0,), (0,)), ((), ())), preferred_element_type=jnp.float32
        ).reshape(9, channels, channels)
        / tokens
    )
    cot_taps = gather_taps(with_rim(cotangent), rate_two, True, height, breadth)
    grad_hidden = jnp.dot(
        cot_taps,
        conv_two.transpose(0, 2, 1).reshape(9 * channels, channels),
        preferred_element_type=jnp.float32,
    )
    grad_pre = (grad_hidden * sigma * (1.0 + first_pre * (1.0 - sigma))).astype(jnp.bfloat16)
    grad_one = (
        lax.dot_general(
            first_taps, grad_pre, (((0,), (0,)), ((), ())), preferred_element_type=jnp.float32
        ).reshape(9, channels, channels)
        / tokens
    )
    grad_taps = gather_taps(
        with_rim(grad_pre.reshape(height, breadth, channels)), rate_one, True, height, breadth
    )
    grad_input = (
        jnp.dot(
            grad_taps,
            conv_one.transpose(0, 2, 1).reshape(9 * channels, channels),
            preferred_element_type=jnp.float32,
        )
        * contact
    )
    grad_norm = inv_spread * (
        grad_input
        - jnp.mean(grad_input, axis=-1, keepdims=True)
        - scaled * jnp.mean(grad_input * scaled, axis=-1, keepdims=True)
    )
    grad_pair = (
        (cot_flat.astype(jnp.float32) + grad_norm)
        .astype(jnp.bfloat16)
        .reshape(height, breadth, channels)
    )
    grad_one, grad_two = lax.psum((grad_one, grad_two), ("row", "col"))
    return (output, grad_pair, grad_one, grad_two)


def halvings(axis, count):
    return [(axis, count >> step) for step in range(1, count.bit_length())]


def exchange_plan(row_count, col_count):
    rows, cols = halvings("row", row_count), halvings("col", col_count)
    return cols + rows, rows[:-1] + cols + rows[-1:]


def exchange(held, hop):
    axis, distance = hop
    return lax.ppermute(held, axis, [(i, i ^ distance) for i in range(lax.axis_size(axis))])


def place_of(position, rounds, row_place, col_place):
    row, col = row_place, col_place
    for step, (axis, distance) in enumerate(rounds):
        bit = ((position >> step) & 1) * distance
        if axis == "row":
            row = row ^ bit
        else:
            col = col ^ bit
    return row, col


def slot_of(row_change, col_change, rounds):
    slot = 0
    for step, (axis, distance) in enumerate(rounds[:-1]):
        change = row_change if axis == "row" else col_change
        slot = slot | (((change // distance) & 1) << step)
    return slot


def sigmoid(values):
    return 0.5 + 0.5 * jnp.tanh(0.5 * values)


def matmul(left, right):
    return jnp.dot(left, right, preferred_element_type=jnp.float32)


def matmul_by_rows(left, right):
    rows = 256
    return jnp.concatenate(
        [matmul(left[i : i + rows], right) for i in range(0, left.shape[0], rows)], axis=0
    )


def matmul_nt(left, right):
    return lax.dot_general(
        left, right, (((1,), (1,)), ((), ())), preferred_element_type=jnp.float32
    )


def project_half(
    plan, core, pairs, w_proj, w_gate, left, right, swapped, gating, contact, start, turned
):
    rounds, _, height, breadth, tokens = plan
    channels, hidden = w_gate.shape[0], w_gate.shape[1]
    col_count, chips = tokens // breadth, tokens // height // 2
    row_place, col_place = lax.axis_index("row"), lax.axis_index("col")
    lane = lax.broadcasted_iota(jnp.int32, (height, breadth, channels), 2)
    place = lax.broadcasted_iota(jnp.int32, (height, breadth, channels), 0)
    own_lane = jnp.where((lane % height == place) & (lane < 2 * height), 1.0, 0.0)
    pick_lane = lax.broadcasted_iota(jnp.int32, (channels, 2 * channels), 0)
    pick_half = lax.broadcasted_iota(jnp.int32, (channels, 2 * channels), 1) // channels
    pick = jnp.where(pick_lane // height == pick_half, 1.0, 0.0).astype(jnp.bfloat16)
    pixels = height * breadth
    rows = 8
    for first in range(0, height, rows):
        values, masks = [], []
        for chip in range(chips):
            row_change = (chip * 2 + core) ^ row_place
            blocks, marks = [], []
            for col in range(col_count):
                col_change = col_place ^ col
                slot = slot_of(row_change, col_change, rounds)
                blocks.append(
                    pairs[slot, first * breadth : (first + rows) * breadth, :]
                    .astype(jnp.float32)
                    .reshape(rows, breadth, channels)
                )
                mark = pairs[slot, pixels:, :].astype(jnp.float32)[:breadth]
                marks.append(mark[None] * own_lane[first : first + rows])
            values.append(jnp.concatenate(blocks, axis=1).reshape(rows * tokens, channels))
            masks.append(jnp.concatenate(marks, axis=1).reshape(rows * tokens, channels))
        values = jnp.concatenate(values, axis=0)
        masks = matmul(jnp.concatenate(masks, axis=0).astype(jnp.bfloat16), pick)
        normed = layer_norm(values)
        gates = sigmoid(matmul(normed.astype(jnp.bfloat16), w_gate[...]))
        masked = (normed * masks[:, :channels]).astype(jnp.bfloat16)
        projected = matmul(masked, w_proj[...])
        sides = [
            sigmoid(projected[:, (2 * side + 1) * hidden : (2 * side + 2) * hidden])
            * projected[:, 2 * side * hidden : (2 * side + 1) * hidden]
            for side in range(2)
        ]
        for side, target in zip(sides, turned):
            side = side.reshape(chips, rows, tokens, hidden)
            for row in range(rows):
                strip = jnp.concatenate([side[chip, row] for chip in range(chips)], axis=0)
                target[pl.ds(first + row, hidden, stride=height + PITCH), :] = strip.T
        shape = (chips, rows, tokens, channels)
        span = slice(first, first + rows)
        gating[:, span] = gates.astype(jnp.bfloat16).reshape(shape)
        contact[:, span] = masks[:, channels:].astype(jnp.bfloat16).reshape(shape)
        start[:, span] = values.astype(jnp.bfloat16).reshape(shape)
    shape = (hidden, height + PITCH, chips * tokens)
    mine, other = turned[0][...], turned[1][...]
    for target, source in (
        (left, mine),
        (right, other),
        (swapped, pltpu.roll(other, tokens, 1)),
    ):
        target[...] = source.reshape(shape)[:, :height].astype(jnp.bfloat16)


def near_kernel(
    plan,
    near,
    w_proj,
    w_gate,
    two,
    left,
    right,
    swapped,
    gating,
    contact,
    start,
    two_t,
    two_copy,
    turned_left,
    turned_right,
):
    core = lax.axis_index("row") % 2
    two_copy[...] = two[...]
    channels = two.shape[1]
    for tap in range(9):
        two_t[tap * channels : (tap + 1) * channels] = two[tap].T
    project_half(
        plan,
        core,
        near,
        w_proj,
        w_gate,
        left,
        right,
        swapped,
        gating,
        contact,
        start,
        (turned_left, turned_right),
    )


def spread(source, rows, pad, rate, target):
    tokens, channels = target.shape[1], source.shape[2]
    for tap in range(3):
        first = DMAX + (tap - 1) * rate if tap != 1 else DMAX
        moved = source[pl.ds(pad + rows.start, rows.size), pl.ds(first, tokens), :]
        target[pl.ds(DMAX + rows.start, rows.size), :, tap * channels : (tap + 1) * channels] = (
            moved.astype(jnp.bfloat16)
        )


def taps(source, first, count, rate):
    tokens = source.shape[1]
    views = [
        source[pl.ds(DMAX + first + (tap - 1) * rate, count)].reshape(count * tokens, -1)
        for tap in range(3)
    ]
    return jnp.concatenate(views, axis=1)


def windows(source, rate, row_start, col_start, height, breadth):
    views = [
        source[
            pl.ds(row_start + DMAX + (tap // 3 - 1) * rate, height),
            pl.ds(col_start + DMAX + (tap % 3 - 1) * rate, breadth),
            :,
        ].reshape(height * breadth, -1)
        for tap in range(9)
    ]
    return jnp.concatenate(views, axis=1).astype(jnp.bfloat16)


def row_taps(strips, first, count, rate):
    views = [
        strips[tap, pl.ds(DMAX + first + ((tap - 1) * rate if tap != 1 else 0), count)]
        for tap in range(3)
    ]
    return views[0] + views[1] + views[2]


def clear_ends(strips, tokens):
    for tap in (0, 2):
        for rows in (slice(0, DMAX), slice(DMAX + tokens, 2 * DMAX + tokens)):
            strips[tap, rows] = jnp.zeros((DMAX,) + strips.shape[2:], jnp.float32)


def column_taps(source, weight, rate, first, count, strips):
    tokens = strips.shape[2]
    columns = [DMAX - rate, DMAX, DMAX + rate]
    flat = jnp.concatenate(
        [
            source[pl.ds(first, count), pl.ds(column, tokens), :].reshape(count * tokens, -1)
            for column in columns
        ],
        axis=1,
    ).astype(jnp.bfloat16)
    square = jnp.concatenate(
        [
            jnp.concatenate([weight(3 * row + col) for row in range(3)], axis=1)
            for col in range(3)
        ],
        axis=0,
    )
    result = matmul_by_rows(flat, square)
    channels = strips.shape[3]
    for tap in range(3):
        strips[tap, pl.ds(DMAX + first, count)] = result[
            :, tap * channels : (tap + 1) * channels
        ].reshape(count, tokens, channels)


def lanes(step, size):
    return pl.ds(pl.multiple_of(step * size, size), size)


def clear_border(target, tokens):
    line, channels = target.shape[1], target.shape[2]
    border = jnp.zeros((DMAX, line, channels), target.dtype)
    rim = jnp.zeros((tokens, DMAX, channels), target.dtype)
    if target.shape[0] > tokens:
        target[0:DMAX] = border
        target[DMAX + tokens :] = border
    if line > tokens:
        rows = slice(target.shape[0] - tokens - DMAX, target.shape[0] - DMAX)
        if target.shape[0] == tokens:
            rows = slice(0, tokens)
        target[rows, 0:DMAX, :] = rim
        target[rows, DMAX + tokens :, :] = rim


def forward_kernel(
    plan,
    dilations,
    far,
    w_proj,
    w_gate,
    w_out,
    one,
    near_left,
    near_right,
    near_swapped,
    near_gating,
    near_contact,
    near_start,
    strips,
    flipped,
    mine,
    own_contact,
    far_left,
    right,
    swapped,
    far_gating,
    far_contact,
    far_start,
    turned_left,
    turned_right,
    products,
    normed,
    updated,
    field,
):
    _, _, height, breadth, tokens = plan
    hidden, channels = w_out.shape
    pixels = height * breadth
    chips = tokens // height // 2
    row_place, col_place = lax.axis_index("row"), lax.axis_index("col")
    core = row_place % 2
    rate_one = dilations[0]
    inside = slice(DMAX, DMAX + tokens)
    clear_border(field, tokens)
    clear_ends(strips, tokens)

    right[core] = near_right[...]
    swapped[core] = near_swapped[...]
    project_half(
        plan,
        1 - core,
        far,
        w_proj,
        w_gate,
        far_left,
        right.at[1 - core],
        swapped.at[1 - core],
        far_gating,
        far_contact,
        far_start,
        (turned_left, turned_right),
    )

    lane = lax.broadcasted_iota(jnp.int32, (height, chips * tokens), 1)
    low = jnp.where(lane < tokens, 1.0, 0.0).astype(jnp.bfloat16)
    high = jnp.where(lane < tokens, 0.0, 1.0).astype(jnp.bfloat16)
    batch = 64
    pitch = 2 * height + PITCH

    def multiply(step, carry):
        for part in range(batch):
            h = step * batch + part
            ahead = [right[0, h], right[1, h]]
            back = [swapped[0, h], swapped[1, h]]
            strips = [strip * low for strip in ahead + back]
            strips += [strip * high for strip in back + ahead]
            mine = jnp.concatenate([near_left[h], far_left[h]], axis=0)
            products[pl.ds(pl.multiple_of(h * pitch, 8), 2 * height), :] = matmul_nt(
                mine, jnp.concatenate(strips, axis=0)
            )
        return carry

    lax.fori_loop(0, hidden // batch, multiply, 0)

    chunk = 8
    size = chunk * tokens

    halves = (
        (core, near_gating, near_contact, near_start),
        (1 - core, far_gating, far_contact, far_start),
    )
    parts = height // chunk

    def normalise(step):
        half, first = step // parts, step % parts * chunk
        for row in range(chunk):
            strip = products[pl.ds(half * height + first + row, hidden, stride=pitch), :]
            strip = layer_norm(strip, axis=0).astype(jnp.bfloat16).T
            for chip in range(chips):
                normed[step, chip, row] = strip[chip * tokens : (chip + 1) * tokens]

    def update(step):
        first = step % parts * chunk
        side, gating, contact, start = halves[step // parts]
        change = matmul(normed[step].reshape(chips * size, hidden), w_out[...])
        change = change.reshape(chips, chunk, tokens, channels)
        rows = pl.ds(first, chunk)
        fresh = start[:, rows].astype(jnp.float32) + gating[:, rows].astype(jnp.float32) * change
        fresh = fresh.astype(jnp.bfloat16).astype(jnp.float32)
        first_in = layer_norm(fresh) * contact[:, rows].astype(jnp.float32)
        if step < parts:
            updated[:, rows] = fresh
        for chip in range(chips):
            base = (chip * 2 + side) * height + first
            field[pl.ds(base, chunk), inside, :] = first_in[chip]
            flipped[:, pl.ds(pl.multiple_of(base * tokens, size), size)] = (
                first_in[chip].reshape(size, channels).astype(jnp.bfloat16).T
            )

    def first_conv(step):
        side = halves[step // parts][0]
        for chip in range(chips):
            base = (chip * 2 + side) * height + step % parts * chunk
            column_taps(field, lambda tap: one[tap], rate_one, base, chunk, strips)

    count = 2 * parts
    for step in range(count + 2):
        if step < count:
            normalise(step)
        if 1 <= step <= count:
            update(step - 1)
        if step >= 2:
            first_conv(step - 2)

    cols = pl.ds(pl.multiple_of(col_place * breadth, breadth), breadth)
    mine[...] = updated[row_place // 2, :, cols, :].reshape(pixels, channels)
    marks = near_contact[row_place // 2].astype(jnp.float32)
    place_col = lax.broadcasted_iota(jnp.int32, (tokens, channels), 0) // breadth
    marks = jnp.where((place_col == col_place)[None], marks, 0.0)
    marks = marks.reshape(height, tokens // breadth, breadth, channels)
    own_contact[...] = jnp.sum(marks, axis=1).reshape(pixels, channels)


def backward_kernel(
    plan,
    dilations,
    cot_near,
    cot_far,
    one,
    two,
    two_t,
    strips,
    flipped,
    mine,
    own_contact,
    output,
    grad_pair,
    grad_one,
    grad_two,
    field,
    wide_cot,
    wide_pre,
    grad_pre,
    second,
    sum_one,
    sum_two,
    scaled_one,
    scaled_two,
    sent,
):
    _, cot_rounds, height, breadth, tokens = plan
    channels = one.shape[2]
    pixels = height * breadth
    row_place, col_place = lax.axis_index("row"), lax.axis_index("col")
    rate_one, rate_two = dilations[0], dilations[1]
    half = cot_far.shape[0]
    inside = slice(DMAX, DMAX + tokens)
    for target in (field, wide_cot, wide_pre, grad_pre, second):
        clear_border(target, tokens)

    several = 8

    def place_cot(source, base):
        def body(step, carry):
            for i in range(several):
                slot = step * several + i
                row, col = place_of(base + slot, cot_rounds, row_place, col_place)
                cols = pl.ds(pl.multiple_of(DMAX + col * breadth, breadth), breadth)
                field[pl.ds(row * height, height), cols, :] = (
                    source[slot].astype(jnp.float32).reshape(height, breadth, channels)
                )
            return carry

        lax.fori_loop(0, half // several, body, 0)

    place_cot(cot_near, 0)
    place_cot(cot_far, half)
    chunk = 16
    size = chunk * tokens
    steps = tokens // chunk

    def spread_cot(step, carry):
        spread(field, pl.ds(step * chunk, chunk), 0, -rate_two, wide_cot)
        return carry

    lax.fori_loop(0, steps, spread_cot, 0)

    def back_two(step):
        first = step * chunk
        rows = pl.ds(DMAX + first, chunk)
        pre = row_taps(strips, first, chunk, rate_one)
        sigma = sigmoid(pre)
        second_in = pre * sigma
        second[rows, inside, :] = second_in
        factor = sigma * (1.0 + pre * (1.0 - sigma))
        turned = second_in.reshape(size, channels).astype(jnp.bfloat16).T
        shifted = taps(wide_cot, first, chunk, -rate_two)
        before = matmul_by_rows(shifted, two_t[...]).reshape(chunk, tokens, channels)
        grad_pre[rows, inside, :] = (before * factor).astype(jnp.bfloat16).astype(jnp.float32)
        part = matmul(turned, shifted)
        sum_two[...] = part if step == 0 else sum_two[...] + part

    def spread_pre(step):
        spread(grad_pre, pl.ds(step * chunk, chunk), DMAX, -rate_one, wide_pre)

    def back_one(step):
        shifted = taps(wide_pre, step * chunk, chunk, -rate_one)
        part = matmul(flipped[:, step * size : (step + 1) * size], shifted)
        sum_one[...] = part if step == 0 else sum_one[...] + part

    def finish(total, scaled, target, row):
        for tap in range(3 * row, 3 * row + 3):
            columns = slice(tap * channels, (tap + 1) * channels)
            scaled[tap] = total[:, columns] * (1.0 / tokens)
        taps_done = pl.ds(3 * row, 3)
        copy = pltpu.make_async_copy(
            scaled.at[taps_done], target.at[taps_done], sent.at[len(copies)]
        )
        copy.start()
        copies.append(copy)

    copies = []
    for step in range(steps):
        if step >= 3:
            back_one(step - 3)
        if step >= 1:
            spread_pre(step - 1)
        back_two(step)
    spread_pre(steps - 1)
    for row in range(3):
        finish(sum_two, scaled_two, grad_two, row)
    for step in range(max(steps - 3, 0), steps - 1):
        back_one(step)

    spot = (row_place * height, col_place * breadth, height, breadth)
    second_pre = matmul(
        windows(second, rate_two, *spot), two[...].reshape(9 * channels, channels)
    )
    output[...] = (mine[...] + second_pre).astype(jnp.bfloat16)
    one_rows = [one[tap] for tap in range(9)]
    grad_input = own_contact[...] * matmul_nt(
        windows(grad_pre, -rate_one, *spot),
        jnp.concatenate(one_rows, axis=1),
    )
    centre = mine[...] - jnp.mean(mine[...], axis=-1, keepdims=True)
    inv_spread = lax.rsqrt(jnp.mean(centre * centre, axis=-1, keepdims=True) + EPSILON)
    scaled = centre * inv_spread
    grad_norm = inv_spread * (
        grad_input
        - jnp.mean(grad_input, axis=-1, keepdims=True)
        - scaled * jnp.mean(grad_input * scaled, axis=-1, keepdims=True)
    )
    grad_pair[...] = (cot_near[0].astype(jnp.float32) + grad_norm).astype(jnp.bfloat16)

    last = steps - 1
    for row in range(3):
        columns = slice(3 * row * channels, 3 * (row + 1) * channels)
        moved = pl.ds(DMAX + last * chunk - (row - 1) * rate_one, chunk)
        sum_one[:, columns] += matmul(
            flipped[:, last * size : (last + 1) * size], wide_pre[moved].reshape(size, -1)
        )
        finish(sum_one, scaled_one, grad_one, row)
    for copy in copies:
        copy.wait()


def replicated(
    pair, pair_mask, contact_mask, dilations, w_proj, w_gate, w_out, conv_one, conv_two, cotangent
):
    height, breadth, channels = pair.shape
    hidden = w_out.shape[0]
    row_count, col_count = lax.axis_size("row"), lax.axis_size("col")
    tokens = height * row_count
    pixels = height * breadth
    rounds, cot_rounds = exchange_plan(row_count, col_count)
    f32, bf16 = jnp.float32, jnp.bfloat16
    plan = (rounds, cot_rounds, height, breadth, tokens)
    chips = row_count // 2
    line = tokens + 2 * DMAX
    in_vmem = pl.BlockSpec(memory_space=pltpu.VMEM)
    side = ((hidden, height, chips * tokens), bf16)
    rows = (chips, height, tokens, channels)
    halves = [side] * 3 + [(rows, bf16)] * 3
    turned = pltpu.VMEM((hidden * (height + PITCH), chips * tokens), f32)
    stat = ((pixels, channels), f32)

    def shapes(*entries):
        return [jax.ShapeDtypeStruct(shape, dtype) for shape, dtype in entries]

    in_smem = pl.BlockSpec(memory_space=pltpu.SMEM)
    spare = channels - 2 * height
    marks = jnp.pad(pair_mask.T, ((pixels, breadth), (0, height + spare))) + jnp.pad(
        contact_mask.T, ((pixels, breadth), (height, spare))
    )
    above = jnp.pad(pair.reshape(pixels, channels), ((0, 2 * breadth), (0, 0)))
    held = (above.astype(f32) + marks.astype(f32)).astype(bf16)[None]
    block = cotangent.reshape(1, pixels, channels)
    cot_held = lax.optimization_barrier(jnp.maximum(block, jnp.finfo(bf16).min))
    def read(*weights):
        return [jnp.maximum(weight, jnp.finfo(bf16).min) for weight in weights]

    dense, kernels = (dilations, w_proj, w_gate, w_out), (conv_one, conv_two)
    for step in range(len(rounds) - 1):
        other = exchange(held, rounds[step])
        cot_other = exchange(cot_held if step else block, cot_rounds[step])
        held = jnp.concatenate([held, other], axis=0)
        if step == len(rounds) - 4:
            cot_other, dense = lax.optimization_barrier((cot_other, dense))
            rates = jnp.clip(dense[0], 1, DMAX)
            dense = read(*dense[1:])
        if step == len(rounds) - 3:
            cot_other, kernels = lax.optimization_barrier((cot_other, kernels))
            kernels = read(*kernels)
        if step < len(rounds) - 2:
            held = lax.optimization_barrier(held)
            cot_held = lax.optimization_barrier(jnp.concatenate([cot_held, cot_other], axis=0))
        else:
            held, rates, dense, kernels = lax.optimization_barrier((held, rates, dense, kernels))
    w_proj, w_gate, w_out = dense
    conv_one, conv_two = kernels
    near, far = held, exchange(held, rounds[-1])
    *near_parts, two_t, two = pl.pallas_call(
        functools.partial(near_kernel, plan),
        in_specs=[in_vmem] * 4,
        out_specs=[in_vmem] * 8,
        out_shape=shapes(
            *halves, ((9 * channels, channels), bf16), ((9, channels, channels), bf16)
        ),
        scratch_shapes=[turned] * 2,
        compiler_params=pltpu.CompilerParams(vmem_limit_bytes=VMEM_LIMIT // 3),
        cost_estimate=pl.CostEstimate(
            flops=tokens * tokens * channels * 5 * hidden,
            bytes_accessed=8 * tokens * tokens * channels,
            transcendentals=3 * tokens * tokens * channels // 2,
        ),
    )(near, w_proj, w_gate, conv_two)
    cot_other, two_t = lax.optimization_barrier((cot_other, two_t))
    cot_near = jnp.concatenate([cot_held, cot_other], axis=0)
    cot_far = exchange(cot_near, cot_rounds[-1])
    padded = pltpu.VMEM((tokens, line, channels), f32)
    bordered = pltpu.VMEM((line, line, channels), f32)
    tripled = pltpu.VMEM((line, tokens, 3 * channels), bf16)
    both = pltpu.VMEM((2,) + side[0], bf16)
    alone = pltpu.VMEM(rows, bf16)
    flat = ((channels, tokens * tokens), bf16)
    sums = pltpu.VMEM((channels, 9 * channels), f32)
    held = pl.pallas_call(
        functools.partial(forward_kernel, plan),
        in_specs=[in_smem] + [in_vmem] * 11,
        out_specs=[in_vmem] * 4,
        out_shape=shapes(((3, line, tokens, channels), f32), flat, stat, stat),
        scratch_shapes=[pltpu.VMEM(*side), both, both, alone, alone, alone]
        + [turned] * 2
        + [pltpu.VMEM((hidden * (2 * height + PITCH), chips * tokens), f32)]
        + [pltpu.VMEM((2 * height // 8, chips, 8, tokens, hidden), bf16)]
        + [pltpu.VMEM(rows, f32), padded],
        compiler_params=pltpu.CompilerParams(vmem_limit_bytes=FORWARD_VMEM),
        cost_estimate=pl.CostEstimate(
            flops=tokens * tokens * channels * 40 * hidden,
            bytes_accessed=40 * tokens * tokens * channels,
            transcendentals=4 * tokens * tokens * channels,
        ),
    )(
        rates,
        far,
        w_proj,
        w_gate,
        w_out,
        conv_one,
        *near_parts,
    )
    output, grad_pair, grad_one, grad_two = pl.pallas_call(
        functools.partial(backward_kernel, plan),
        in_specs=[in_smem] + [in_vmem] * 9,
        out_specs=[in_vmem] * 2 + [pl.BlockSpec(memory_space=pltpu.HBM)] * 2,
        out_shape=shapes(
            ((pixels, channels), bf16),
            ((pixels, channels), bf16),
            ((9, channels, channels), f32),
            ((9, channels, channels), f32),
        ),
        scratch_shapes=[padded, tripled, tripled, bordered, bordered, sums, sums]
        + [pltpu.VMEM((9, channels, channels), f32)] * 2
        + [pltpu.SemaphoreType.DMA((6,))],
        compiler_params=pltpu.CompilerParams(vmem_limit_bytes=BACKWARD_VMEM),
    )(
        rates,
        cot_near,
        cot_far,
        conv_one,
        two,
        two_t,
        *held,
    )
    block = (height, breadth, channels)
    return output.reshape(block), grad_pair.reshape(block), grad_one, grad_two


def fits(pair, w_out, row_count, col_count):
    height, breadth, channels = pair.shape
    tokens = height * row_count
    powers = all(count & (count - 1) == 0 for count in (row_count, col_count))
    whole = (tokens + 2 * DMAX) ** 2 * channels
    return (
        powers
        and row_count * col_count >= 16
        and height * breadth == channels == w_out.shape[0]
        and breadth == 8
        and row_count // 2 * tokens == channels
        and whole * 60 <= VMEM_LIMIT
    )


def local(*arguments):
    pair, w_out = arguments[0], arguments[6]
    if fits(pair, w_out, lax.axis_size("row"), lax.axis_size("col")):
        return replicated(*arguments)
    return sharded(*arguments)


def solution(mesh):
    in_specs = (
        P("row", "col", None),
        P("row", "col"),
        P("row", "col"),
        P(),
        P(),
        P(),
        P(),
        P(),
        P(),
        P("row", "col", None),
    )
    out_specs = (P("row", "col", None), P("row", "col", None), P(), P())
    return jax.shard_map(local, mesh=mesh, in_specs=in_specs, out_specs=out_specs, check_vma=False)
```

```python
import functools

import jax
import jax.numpy as jnp
from jax import lax
from jax.experimental import pallas as pl
from jax.experimental.pallas import tpu as pltpu
from jax.sharding import PartitionSpec as P

DMAX = 8
VMEM_LIMIT = 48 * 1024 * 1024
PITCH = 8
FORWARD_VMEM = 32 * 1024 * 1024
BACKWARD_VMEM = 36 * 1024 * 1024


EPSILON = 1e-05


def with_halo(block, sides, width):
    for axis, dim in sides:
        count = lax.axis_size(axis)
        forward = [(i, i + 1) for i in range(count - 1)]
        backward = [(target, source) for source, target in forward]
        low = lax.ppermute(
            lax.slice_in_dim(block, block.shape[dim] - width, None, axis=dim), axis, forward
        )
        high = lax.ppermute(lax.slice_in_dim(block, 0, width, axis=dim), axis, backward)
        block = jnp.concatenate([low, block, high], axis=dim)
    return block


def broadcast(x, axis, root):
    mine = lax.axis_index(axis) == root
    return lax.psum(jnp.where(mine, x, jnp.zeros_like(x)), axis)


def layer_norm(values, axis=-1):
    centre = values - jnp.mean(values, axis=axis, keepdims=True)
    spread = jnp.mean(centre * centre, axis=axis, keepdims=True)
    return centre * lax.rsqrt(spread + EPSILON)


def with_rim(field):
    return with_halo(field, (("row", 0), ("col", 1)), DMAX)


def gather_taps(padded, dilation, mirrored, height, breadth):
    windows = []
    for tap_index in range(9):
        row_tap = tap_index // 3
        col_tap = tap_index % 3
        if mirrored:
            row_tap = 2 - row_tap
            col_tap = 2 - col_tap
        row_start = DMAX + (row_tap - 1) * dilation
        col_start = DMAX + (col_tap - 1) * dilation
        windows.append(
            lax.dynamic_slice(
                padded, (row_start, col_start, jnp.int32(0)), (height, breadth, padded.shape[2])
            )
        )
    return jnp.concatenate(windows, axis=2).reshape(height * breadth, -1)


def sharded(
    pair, pair_mask, contact_mask, dilations, w_proj, w_gate, w_out, conv_one, conv_two, cotangent
):
    height, breadth, channels = pair.shape
    hidden = w_out.shape[0]
    row_count = lax.axis_size("row")
    col_count = lax.axis_size("col")
    ratio = col_count // row_count
    row_place = lax.axis_index("row")
    col_place = lax.axis_index("col")
    tokens = breadth * col_count
    pixels = height * breadth
    pair_flat = pair.astype(jnp.float32).reshape(pixels, channels)
    normed = layer_norm(pair_flat).astype(jnp.bfloat16)
    projected = jnp.dot(normed, w_proj, preferred_element_type=jnp.float32)
    mask_col = pair_mask.reshape(pixels, 1).astype(jnp.float32)
    left_side = (
        (mask_col * jax.nn.sigmoid(projected[:, hidden : 2 * hidden]) * projected[:, :hidden])
        .astype(jnp.bfloat16)
        .reshape(height, breadth, hidden)
    )
    right_side = (
        (
            mask_col
            * jax.nn.sigmoid(projected[:, 3 * hidden :])
            * projected[:, 2 * hidden : 3 * hidden]
        )
        .astype(jnp.bfloat16)
        .reshape(height, breadth, hidden)
    )
    right_all = lax.all_gather(right_side, "col", axis=1, tiled=True)
    offset = jnp.clip(col_place * breadth - row_place * height, 0, height - breadth)
    right_local = lax.dynamic_slice_in_dim(right_all, offset, breadth, 0)
    right_rows = broadcast(right_local, "row", col_place // ratio)
    products = jnp.einsum(
        "ikh,jkh->ijh",
        lax.all_gather(left_side, "col", axis=1, tiled=True),
        right_rows,
        preferred_element_type=jnp.float32,
    )
    product_norm = layer_norm(products.reshape(pixels, hidden)).astype(jnp.bfloat16)
    gating = jax.nn.sigmoid(jnp.dot(normed, w_gate, preferred_element_type=jnp.float32))
    updated = (
        pair_flat + gating * jnp.dot(product_norm, w_out, preferred_element_type=jnp.float32)
    ).astype(jnp.bfloat16)
    updated_f = updated.astype(jnp.float32)
    centre = updated_f - jnp.mean(updated_f, axis=-1, keepdims=True)
    inv_spread = lax.rsqrt(jnp.mean(centre * centre, axis=-1, keepdims=True) + EPSILON)
    scaled = centre * inv_spread
    contact = contact_mask.reshape(pixels, 1).astype(jnp.float32)
    first_in = (scaled * contact).astype(jnp.bfloat16).reshape(height, breadth, channels)
    rate_one = dilations[0]
    rate_two = dilations[1]
    first_taps = gather_taps(with_rim(first_in), rate_one, False, height, breadth)
    first_pre = jnp.dot(
        first_taps, conv_one.reshape(9 * channels, channels), preferred_element_type=jnp.float32
    )
    sigma = jax.nn.sigmoid(first_pre)
    second_in = (first_pre * sigma).astype(jnp.bfloat16).reshape(height, breadth, channels)
    second_taps = gather_taps(with_rim(second_in), rate_two, False, height, breadth)
    second_pre = jnp.dot(
        second_taps, conv_two.reshape(9 * channels, channels), preferred_element_type=jnp.float32
    )
    output = (updated_f + second_pre).astype(jnp.bfloat16).reshape(height, breadth, channels)
    cot_flat = cotangent.reshape(pixels, channels)
    grad_two = (
        lax.dot_general(
            second_taps, cot_flat, (((0,), (0,)), ((), ())), preferred_element_type=jnp.float32
        ).reshape(9, channels, channels)
        / tokens
    )
    cot_taps = gather_taps(with_rim(cotangent), rate_two, True, height, breadth)
    grad_hidden = jnp.dot(
        cot_taps,
        conv_two.transpose(0, 2, 1).reshape(9 * channels, channels),
        preferred_element_type=jnp.float32,
    )
    grad_pre = (grad_hidden * sigma * (1.0 + first_pre * (1.0 - sigma))).astype(jnp.bfloat16)
    grad_one = (
        lax.dot_general(
            first_taps, grad_pre, (((0,), (0,)), ((), ())), preferred_element_type=jnp.float32
        ).reshape(9, channels, channels)
        / tokens
    )
    grad_taps = gather_taps(
        with_rim(grad_pre.reshape(height, breadth, channels)), rate_one, True, height, breadth
    )
    grad_input = (
        jnp.dot(
            grad_taps,
            conv_one.transpose(0, 2, 1).reshape(9 * channels, channels),
            preferred_element_type=jnp.float32,
        )
        * contact
    )
    grad_norm = inv_spread * (
        grad_input
        - jnp.mean(grad_input, axis=-1, keepdims=True)
        - scaled * jnp.mean(grad_input * scaled, axis=-1, keepdims=True)
    )
    grad_pair = (
        (cot_flat.astype(jnp.float32) + grad_norm)
        .astype(jnp.bfloat16)
        .reshape(height, breadth, channels)
    )
    grad_one, grad_two = lax.psum((grad_one, grad_two), ("row", "col"))
    return (output, grad_pair, grad_one, grad_two)


def halvings(axis, count):
    return [(axis, count >> step) for step in range(1, count.bit_length())]


def exchange_plan(row_count, col_count):
    rows, cols = halvings("row", row_count), halvings("col", col_count)
    return cols + rows, rows[:-1] + cols + rows[-1:]


def exchange(held, hop):
    axis, distance = hop
    return lax.ppermute(held, axis, [(i, i ^ distance) for i in range(lax.axis_size(axis))])


def place_of(position, rounds, row_place, col_place):
    row, col = row_place, col_place
    for step, (axis, distance) in enumerate(rounds):
        bit = ((position >> step) & 1) * distance
        if axis == "row":
            row = row ^ bit
        else:
            col = col ^ bit
    return row, col


def slot_of(row_change, col_change, rounds):
    slot = 0
    for step, (axis, distance) in enumerate(rounds[:-1]):
        change = row_change if axis == "row" else col_change
        slot = slot | (((change // distance) & 1) << step)
    return slot


def sigmoid(values):
    return 0.5 + 0.5 * jnp.tanh(0.5 * values)


def matmul(left, right):
    return jnp.dot(left, right, preferred_element_type=jnp.float32)


def matmul_by_rows(left, right):
    rows = 256
    return jnp.concatenate(
        [matmul(left[i : i + rows], right) for i in range(0, left.shape[0], rows)], axis=0
    )


def matmul_nt(left, right):
    return lax.dot_general(
        left, right, (((1,), (1,)), ((), ())), preferred_element_type=jnp.float32
    )


def project_half(
    plan, core, pairs, w_proj, w_gate, left, right, swapped, gating, contact, start, turned
):
    rounds, _, height, breadth, tokens = plan
    channels, hidden = w_gate.shape[0], w_gate.shape[1]
    col_count, chips = tokens // breadth, tokens // height // 2
    row_place, col_place = lax.axis_index("row"), lax.axis_index("col")
    lane = lax.broadcasted_iota(jnp.int32, (height, breadth, channels), 2)
    place = lax.broadcasted_iota(jnp.int32, (height, breadth, channels), 0)
    own_lane = jnp.where((lane % height == place) & (lane < 2 * height), 1.0, 0.0)
    pick_lane = lax.broadcasted_iota(jnp.int32, (channels, 2 * channels), 0)
    pick_half = lax.broadcasted_iota(jnp.int32, (channels, 2 * channels), 1) // channels
    pick = jnp.where(pick_lane // height == pick_half, 1.0, 0.0).astype(jnp.bfloat16)
    pixels = height * breadth
    rows = 8
    for first in range(0, height, rows):
        values, masks = [], []
        for chip in range(chips):
            row_change = (chip * 2 + core) ^ row_place
            blocks, marks = [], []
            for col in range(col_count):
                col_change = col_place ^ col
                slot = slot_of(row_change, col_change, rounds)
                blocks.append(
                    pairs[slot, first * breadth : (first + rows) * breadth, :]
                    .astype(jnp.float32)
                    .reshape(rows, breadth, channels)
                )
                mark = pairs[slot, pixels:, :].astype(jnp.float32)[:breadth]
                marks.append(mark[None] * own_lane[first : first + rows])
            values.append(jnp.concatenate(blocks, axis=1).reshape(rows * tokens, channels))
            masks.append(jnp.concatenate(marks, axis=1).reshape(rows * tokens, channels))
        values = jnp.concatenate(values, axis=0)
        masks = matmul(jnp.concatenate(masks, axis=0).astype(jnp.bfloat16), pick)
        normed = layer_norm(values)
        gates = sigmoid(matmul(normed.astype(jnp.bfloat16), w_gate[...]))
        masked = (normed * masks[:, :channels]).astype(jnp.bfloat16)
        projected = matmul(masked, w_proj[...])
        sides = [
            sigmoid(projected[:, (2 * side + 1) * hidden : (2 * side + 2) * hidden])
            * projected[:, 2 * side * hidden : (2 * side + 1) * hidden]
            for side in range(2)
        ]
        for side, target in zip(sides, turned):
            side = side.reshape(chips, rows, tokens, hidden)
            for row in range(rows):
                strip = jnp.concatenate([side[chip, row] for chip in range(chips)], axis=0)
                target[pl.ds(first + row, hidden, stride=height + PITCH), :] = strip.T
        shape = (chips, rows, tokens, channels)
        span = slice(first, first + rows)
        gating[:, span] = gates.astype(jnp.bfloat16).reshape(shape)
        contact[:, span] = masks[:, channels:].astype(jnp.bfloat16).reshape(shape)
        start[:, span] = values.astype(jnp.bfloat16).reshape(shape)
    shape = (hidden, height + PITCH, chips * tokens)
    mine, other = turned[0][...], turned[1][...]
    for target, source in (
        (left, mine),
        (right, other),
        (swapped, pltpu.roll(other, tokens, 1)),
    ):
        target[...] = source.reshape(shape)[:, :height].astype(jnp.bfloat16)


def near_kernel(
    plan,
    near,
    w_proj,
    w_gate,
    two,
    left,
    right,
    swapped,
    gating,
    contact,
    start,
    two_t,
    two_copy,
    turned_left,
    turned_right,
):
    core = lax.axis_index("row") % 2
    two_copy[...] = two[...]
    channels = two.shape[1]
    for tap in range(9):
        two_t[tap * channels : (tap + 1) * channels] = two[tap].T
    project_half(
        plan,
        core,
        near,
        w_proj,
        w_gate,
        left,
        right,
        swapped,
        gating,
        contact,
        start,
        (turned_left, turned_right),
    )


def spread(source, rows, pad, rate, target):
    tokens, channels = target.shape[1], source.shape[2]
    for tap in range(3):
        first = DMAX + (tap - 1) * rate if tap != 1 else DMAX
        moved = source[pl.ds(pad + rows.start, rows.size), pl.ds(first, tokens), :]
        target[pl.ds(DMAX + rows.start, rows.size), :, tap * channels : (tap + 1) * channels] = (
            moved.astype(jnp.bfloat16)
        )


def taps(source, first, count, rate):
    tokens = source.shape[1]
    views = [
        source[pl.ds(DMAX + first + (tap - 1) * rate, count)].reshape(count * tokens, -1)
        for tap in range(3)
    ]
    return jnp.concatenate(views, axis=1)


def windows(source, rate, row_start, col_start, height, breadth):
    views = [
        source[
            pl.ds(row_start + DMAX + (tap // 3 - 1) * rate, height),
            pl.ds(col_start + DMAX + (tap % 3 - 1) * rate, breadth),
            :,
        ].reshape(height * breadth, -1)
        for tap in range(9)
    ]
    return jnp.concatenate(views, axis=1).astype(jnp.bfloat16)


def row_taps(strips, first, count, rate):
    views = [
        strips[tap, pl.ds(DMAX + first + ((tap - 1) * rate if tap != 1 else 0), count)]
        for tap in range(3)
    ]
    return views[0] + views[1] + views[2]


def clear_ends(strips, tokens):
    for tap in (0, 2):
        for rows in (slice(0, DMAX), slice(DMAX + tokens, 2 * DMAX + tokens)):
            strips[tap, rows] = jnp.zeros((DMAX,) + strips.shape[2:], jnp.float32)


def column_taps(source, weight, rate, first, count, strips):
    tokens = strips.shape[2]
    columns = [DMAX - rate, DMAX, DMAX + rate]
    flat = jnp.concatenate(
        [
            source[pl.ds(first, count), pl.ds(column, tokens), :].reshape(count * tokens, -1)
            for column in columns
        ],
        axis=1,
    ).astype(jnp.bfloat16)
    square = jnp.concatenate(
        [
            jnp.concatenate([weight(3 * row + col) for row in range(3)], axis=1)
            for col in range(3)
        ],
        axis=0,
    )
    result = matmul_by_rows(flat, square)
    channels = strips.shape[3]
    for tap in range(3):
        strips[tap, pl.ds(DMAX + first, count)] = result[
            :, tap * channels : (tap + 1) * channels
        ].reshape(count, tokens, channels)


def lanes(step, size):
    return pl.ds(pl.multiple_of(step * size, size), size)


def clear_border(target, tokens):
    line, channels = target.shape[1], target.shape[2]
    border = jnp.zeros((DMAX, line, channels), target.dtype)
    rim = jnp.zeros((tokens, DMAX, channels), target.dtype)
    if target.shape[0] > tokens:
        target[0:DMAX] = border
        target[DMAX + tokens :] = border
    if line > tokens:
        rows = slice(target.shape[0] - tokens - DMAX, target.shape[0] - DMAX)
        if target.shape[0] == tokens:
            rows = slice(0, tokens)
        target[rows, 0:DMAX, :] = rim
        target[rows, DMAX + tokens :, :] = rim


def forward_kernel(
    plan,
    dilations,
    far,
    w_proj,
    w_gate,
    w_out,
    one,
    near_left,
    near_right,
    near_swapped,
    near_gating,
    near_contact,
    near_start,
    pre,
    flipped,
    mine,
    own_contact,
    far_left,
    right,
    swapped,
    far_gating,
    far_contact,
    far_start,
    turned_left,
    turned_right,
    products,
    normed,
    updated,
    field,
    strips,
):
    _, _, height, breadth, tokens = plan
    hidden, channels = w_out.shape
    pixels = height * breadth
    chips = tokens // height // 2
    row_place, col_place = lax.axis_index("row"), lax.axis_index("col")
    core = row_place % 2
    rate_one = dilations[0]
    inside = slice(DMAX, DMAX + tokens)
    clear_border(field, tokens)
    clear_ends(strips, tokens)

    right[core] = near_right[...]
    swapped[core] = near_swapped[...]
    project_half(
        plan,
        1 - core,
        far,
        w_proj,
        w_gate,
        far_left,
        right.at[1 - core],
        swapped.at[1 - core],
        far_gating,
        far_contact,
        far_start,
        (turned_left, turned_right),
    )

    lane = lax.broadcasted_iota(jnp.int32, (height, chips * tokens), 1)
    low = jnp.where(lane < tokens, 1.0, 0.0).astype(jnp.bfloat16)
    high = jnp.where(lane < tokens, 0.0, 1.0).astype(jnp.bfloat16)
    batch = 64
    pitch = 2 * height + PITCH

    def multiply(step, carry):
        for part in range(batch):
            h = step * batch + part
            ahead = [right[0, h], right[1, h]]
            back = [swapped[0, h], swapped[1, h]]
            strips = [strip * low for strip in ahead + back]
            strips += [strip * high for strip in back + ahead]
            mine = jnp.concatenate([near_left[h], far_left[h]], axis=0)
            products[pl.ds(pl.multiple_of(h * pitch, 8), 2 * height), :] = matmul_nt(
                mine, jnp.concatenate(strips, axis=0)
            )
        return carry

    lax.fori_loop(0, hidden // batch, multiply, 0)

    chunk = 8
    size = chunk * tokens

    halves = (
        (core, near_gating, near_contact, near_start),
        (1 - core, far_gating, far_contact, far_start),
    )
    parts = height // chunk

    def normalise(step):
        half, first = step // parts, step % parts * chunk
        for row in range(chunk):
            strip = products[pl.ds(half * height + first + row, hidden, stride=pitch), :]
            strip = layer_norm(strip, axis=0).astype(jnp.bfloat16).T
            for chip in range(chips):
                normed[step, chip, row] = strip[chip * tokens : (chip + 1) * tokens]

    def update(step):
        first = step % parts * chunk
        side, gating, contact, start = halves[step // parts]
        change = matmul(normed[step].reshape(chips * size, hidden), w_out[...])
        change = change.reshape(chips, chunk, tokens, channels)
        rows = pl.ds(first, chunk)
        fresh = start[:, rows].astype(jnp.float32) + gating[:, rows].astype(jnp.float32) * change
        fresh = fresh.astype(jnp.bfloat16).astype(jnp.float32)
        first_in = layer_norm(fresh) * contact[:, rows].astype(jnp.float32)
        if step < parts:
            updated[:, rows] = fresh
        for chip in range(chips):
            base = (chip * 2 + side) * height + first
            field[pl.ds(base, chunk), inside, :] = first_in[chip]
            flipped[:, pl.ds(pl.multiple_of(base * tokens, size), size)] = (
                first_in[chip].reshape(size, channels).astype(jnp.bfloat16).T
            )

    def first_conv(step):
        side = halves[step // parts][0]
        for chip in range(chips):
            base = (chip * 2 + side) * height + step % parts * chunk
            column_taps(field, lambda tap: one[tap], rate_one, base, chunk, strips)

    count = 2 * parts
    for step in range(count + 2):
        if step < count:
            normalise(step)
        if 1 <= step <= count:
            update(step - 1)
        if step >= 2:
            first_conv(step - 2)

    def add_taps(step, carry):
        pre[pl.ds(step * chunk, chunk)] = row_taps(strips, step * chunk, chunk, rate_one)
        return carry

    lax.fori_loop(0, tokens // chunk, add_taps, 0)

    cols = pl.ds(pl.multiple_of(col_place * breadth, breadth), breadth)
    mine[...] = updated[row_place // 2, :, cols, :].reshape(pixels, channels)
    marks = near_contact[row_place // 2].astype(jnp.float32)
    place_col = lax.broadcasted_iota(jnp.int32, (tokens, channels), 0) // breadth
    marks = jnp.where((place_col == col_place)[None], marks, 0.0)
    marks = marks.reshape(height, tokens // breadth, breadth, channels)
    own_contact[...] = jnp.sum(marks, axis=1).reshape(pixels, channels)


def backward_kernel(
    plan,
    dilations,
    cot_near,
    cot_far,
    one,
    two,
    two_t,
    pre,
    flipped,
    mine,
    own_contact,
    output,
    grad_pair,
    grad_one,
    grad_two,
    field,
    wide_cot,
    wide_pre,
    grad_pre,
    second,
    sum_one,
    sum_two,
    scaled_one,
    scaled_two,
    sent,
):
    _, cot_rounds, height, breadth, tokens = plan
    channels = one.shape[2]
    pixels = height * breadth
    row_place, col_place = lax.axis_index("row"), lax.axis_index("col")
    rate_one, rate_two = dilations[0], dilations[1]
    half = cot_far.shape[0]
    inside = slice(DMAX, DMAX + tokens)
    for target in (field, wide_cot, wide_pre, grad_pre, second):
        clear_border(target, tokens)

    several = 8

    def place_cot(source, base):
        def body(step, carry):
            for i in range(several):
                slot = step * several + i
                row, col = place_of(base + slot, cot_rounds, row_place, col_place)
                cols = pl.ds(pl.multiple_of(DMAX + col * breadth, breadth), breadth)
                field[pl.ds(row * height, height), cols, :] = (
                    source[slot].astype(jnp.float32).reshape(height, breadth, channels)
                )
            return carry

        lax.fori_loop(0, half // several, body, 0)

    place_cot(cot_near, 0)
    place_cot(cot_far, half)
    chunk = 16
    size = chunk * tokens
    steps = tokens // chunk

    def spread_cot(step, carry):
        spread(field, pl.ds(step * chunk, chunk), 0, -rate_two, wide_cot)
        return carry

    lax.fori_loop(0, steps, spread_cot, 0)

    def back_two(step):
        first = step * chunk
        rows = pl.ds(DMAX + first, chunk)
        before_act = pre[pl.ds(first, chunk)]
        sigma = sigmoid(before_act)
        second_in = before_act * sigma
        second[rows, inside, :] = second_in
        factor = sigma * (1.0 + before_act * (1.0 - sigma))
        turned = second_in.reshape(size, channels).astype(jnp.bfloat16).T
        shifted = taps(wide_cot, first, chunk, -rate_two)
        before = matmul_by_rows(shifted, two_t[...]).reshape(chunk, tokens, channels)
        grad_pre[rows, inside, :] = (before * factor).astype(jnp.bfloat16).astype(jnp.float32)
        part = matmul(turned, shifted)
        sum_two[...] = part if step == 0 else sum_two[...] + part

    def spread_pre(step):
        spread(grad_pre, pl.ds(step * chunk, chunk), DMAX, -rate_one, wide_pre)

    def back_one(step):
        shifted = taps(wide_pre, step * chunk, chunk, -rate_one)
        part = matmul(flipped[:, step * size : (step + 1) * size], shifted)
        sum_one[...] = part if step == 0 else sum_one[...] + part

    def finish(total, scaled, target, row):
        for tap in range(3 * row, 3 * row + 3):
            columns = slice(tap * channels, (tap + 1) * channels)
            scaled[tap] = total[:, columns] * (1.0 / tokens)
        taps_done = pl.ds(3 * row, 3)
        copy = pltpu.make_async_copy(
            scaled.at[taps_done], target.at[taps_done], sent.at[len(copies)]
        )
        copy.start()
        copies.append(copy)

    copies = []
    for step in range(steps):
        if step >= 3:
            back_one(step - 3)
        if step >= 1:
            spread_pre(step - 1)
        back_two(step)
    spread_pre(steps - 1)
    for row in range(3):
        finish(sum_two, scaled_two, grad_two, row)
    for step in range(max(steps - 3, 0), steps - 1):
        back_one(step)

    spot = (row_place * height, col_place * breadth, height, breadth)
    second_pre = matmul(
        windows(second, rate_two, *spot), two[...].reshape(9 * channels, channels)
    )
    output[...] = (mine[...] + second_pre).astype(jnp.bfloat16)
    one_rows = [one[tap] for tap in range(9)]
    grad_input = own_contact[...] * matmul_nt(
        windows(grad_pre, -rate_one, *spot),
        jnp.concatenate(one_rows, axis=1),
    )
    centre = mine[...] - jnp.mean(mine[...], axis=-1, keepdims=True)
    inv_spread = lax.rsqrt(jnp.mean(centre * centre, axis=-1, keepdims=True) + EPSILON)
    scaled = centre * inv_spread
    grad_norm = inv_spread * (
        grad_input
        - jnp.mean(grad_input, axis=-1, keepdims=True)
        - scaled * jnp.mean(grad_input * scaled, axis=-1, keepdims=True)
    )
    grad_pair[...] = (cot_near[0].astype(jnp.float32) + grad_norm).astype(jnp.bfloat16)

    last = steps - 1
    for row in range(3):
        columns = slice(3 * row * channels, 3 * (row + 1) * channels)
        moved = pl.ds(DMAX + last * chunk - (row - 1) * rate_one, chunk)
        sum_one[:, columns] += matmul(
            flipped[:, last * size : (last + 1) * size], wide_pre[moved].reshape(size, -1)
        )
        finish(sum_one, scaled_one, grad_one, row)
    for copy in copies:
        copy.wait()


def replicated(
    pair, pair_mask, contact_mask, dilations, w_proj, w_gate, w_out, conv_one, conv_two, cotangent
):
    height, breadth, channels = pair.shape
    hidden = w_out.shape[0]
    row_count, col_count = lax.axis_size("row"), lax.axis_size("col")
    tokens = height * row_count
    pixels = height * breadth
    rounds, cot_rounds = exchange_plan(row_count, col_count)
    f32, bf16 = jnp.float32, jnp.bfloat16
    plan = (rounds, cot_rounds, height, breadth, tokens)
    chips = row_count // 2
    line = tokens + 2 * DMAX
    in_vmem = pl.BlockSpec(memory_space=pltpu.VMEM)
    side = ((hidden, height, chips * tokens), bf16)
    rows = (chips, height, tokens, channels)
    halves = [side] * 3 + [(rows, bf16)] * 3
    turned = pltpu.VMEM((hidden * (height + PITCH), chips * tokens), f32)
    stat = ((pixels, channels), f32)

    def shapes(*entries):
        return [jax.ShapeDtypeStruct(shape, dtype) for shape, dtype in entries]

    in_smem = pl.BlockSpec(memory_space=pltpu.SMEM)
    spare = channels - 2 * height
    marks = jnp.pad(pair_mask.T, ((pixels, breadth), (0, height + spare))) + jnp.pad(
        contact_mask.T, ((pixels, breadth), (height, spare))
    )
    above = jnp.pad(pair.reshape(pixels, channels), ((0, 2 * breadth), (0, 0)))
    held = (above.astype(f32) + marks.astype(f32)).astype(bf16)[None]
    block = cotangent.reshape(1, pixels, channels)
    cot_held = lax.optimization_barrier(jnp.maximum(block, jnp.finfo(bf16).min))
    rates = jnp.clip(dilations, 1, DMAX)
    for step in range(len(rounds) - 1):
        other = exchange(held, rounds[step])
        cot_other = exchange(cot_held if step else block, cot_rounds[step])
        held = lax.optimization_barrier(jnp.concatenate([held, other], axis=0))
        if step < len(rounds) - 2:
            cot_held = jnp.concatenate([cot_held, cot_other], axis=0)
            if step == len(rounds) - 3:
                cot_held, rates = lax.optimization_barrier((cot_held, rates))
            else:
                cot_held = lax.optimization_barrier(cot_held)
    near, far = held, exchange(held, rounds[-1])
    *near_parts, two_t, two = pl.pallas_call(
        functools.partial(near_kernel, plan),
        in_specs=[in_vmem] * 4,
        out_specs=[in_vmem] * 8,
        out_shape=shapes(
            *halves, ((9 * channels, channels), bf16), ((9, channels, channels), bf16)
        ),
        scratch_shapes=[turned] * 2,
        compiler_params=pltpu.CompilerParams(vmem_limit_bytes=VMEM_LIMIT // 3),
        cost_estimate=pl.CostEstimate(
            flops=tokens * tokens * channels * 5 * hidden,
            bytes_accessed=8 * tokens * tokens * channels,
            transcendentals=3 * tokens * tokens * channels // 2,
        ),
    )(near, w_proj, w_gate, conv_two)
    cot_other, two_t = lax.optimization_barrier((cot_other, two_t))
    cot_near = jnp.concatenate([cot_held, cot_other], axis=0)
    cot_far = exchange(cot_near, cot_rounds[-1])
    padded = pltpu.VMEM((tokens, line, channels), f32)
    bordered = pltpu.VMEM((line, line, channels), f32)
    tripled = pltpu.VMEM((line, tokens, 3 * channels), bf16)
    both = pltpu.VMEM((2,) + side[0], bf16)
    alone = pltpu.VMEM(rows, bf16)
    flat = ((channels, tokens * tokens), bf16)
    sums = pltpu.VMEM((channels, 9 * channels), f32)
    held = pl.pallas_call(
        functools.partial(forward_kernel, plan),
        in_specs=[in_smem] + [in_vmem] * 11,
        out_specs=[in_vmem] * 4,
        out_shape=shapes(((tokens, tokens, channels), f32), flat, stat, stat),
        scratch_shapes=[pltpu.VMEM(*side), both, both, alone, alone, alone]
        + [turned] * 2
        + [pltpu.VMEM((hidden * (2 * height + PITCH), chips * tokens), f32)]
        + [pltpu.VMEM((2 * height // 8, chips, 8, tokens, hidden), bf16)]
        + [pltpu.VMEM(rows, f32), padded]
        + [pltpu.VMEM((3, line, tokens, channels), f32)],
        compiler_params=pltpu.CompilerParams(vmem_limit_bytes=FORWARD_VMEM),
        cost_estimate=pl.CostEstimate(
            flops=tokens * tokens * channels * 40 * hidden,
            bytes_accessed=40 * tokens * tokens * channels,
            transcendentals=4 * tokens * tokens * channels,
        ),
    )(
        rates,
        far,
        w_proj,
        w_gate,
        w_out,
        conv_one,
        *near_parts,
    )
    output, grad_pair, grad_one, grad_two = pl.pallas_call(
        functools.partial(backward_kernel, plan),
        in_specs=[in_smem] + [in_vmem] * 9,
        out_specs=[in_vmem] * 2 + [pl.BlockSpec(memory_space=pltpu.HBM)] * 2,
        out_shape=shapes(
            ((pixels, channels), bf16),
            ((pixels, channels), bf16),
            ((9, channels, channels), f32),
            ((9, channels, channels), f32),
        ),
        scratch_shapes=[padded, tripled, tripled, bordered, bordered, sums, sums]
        + [pltpu.VMEM((9, channels, channels), f32)] * 2
        + [pltpu.SemaphoreType.DMA((6,))],
        compiler_params=pltpu.CompilerParams(vmem_limit_bytes=BACKWARD_VMEM),
    )(
        rates,
        cot_near,
        cot_far,
        conv_one,
        two,
        two_t,
        *held,
    )
    block = (height, breadth, channels)
    return output.reshape(block), grad_pair.reshape(block), grad_one, grad_two


def fits(pair, w_out, row_count, col_count):
    height, breadth, channels = pair.shape
    tokens = height * row_count
    powers = all(count & (count - 1) == 0 for count in (row_count, col_count))
    whole = (tokens + 2 * DMAX) ** 2 * channels
    return (
        powers
        and row_count * col_count >= 8
        and height * breadth == channels == w_out.shape[0]
        and breadth == 8
        and row_count // 2 * tokens == channels
        and whole * 60 <= VMEM_LIMIT
    )


def local(*arguments):
    pair, w_out = arguments[0], arguments[6]
    if fits(pair, w_out, lax.axis_size("row"), lax.axis_size("col")):
        return replicated(*arguments)
    return sharded(*arguments)


def solution(mesh):
    in_specs = (
        P("row", "col", None),
        P("row", "col"),
        P("row", "col"),
        P(),
        P(),
        P(),
        P(),
        P(),
        P(),
        P("row", "col", None),
    )
    out_specs = (P("row", "col", None), P("row", "col", None), P(), P())
    return jax.shard_map(local, mesh=mesh, in_specs=in_specs, out_specs=out_specs, check_vma=False)
```

```python
import functools

import jax
import jax.numpy as jnp
from jax import lax
from jax.experimental import pallas as pl
from jax.experimental.pallas import tpu as pltpu
from jax.sharding import PartitionSpec as P

DMAX = 8
VMEM_LIMIT = 48 * 1024 * 1024
PITCH = 8
FORWARD_VMEM = 32 * 1024 * 1024
BACKWARD_VMEM = 36 * 1024 * 1024


EPSILON = 1e-05


def with_halo(block, sides, width):
    for axis, dim in sides:
        count = lax.axis_size(axis)
        forward = [(i, i + 1) for i in range(count - 1)]
        backward = [(target, source) for source, target in forward]
        low = lax.ppermute(
            lax.slice_in_dim(block, block.shape[dim] - width, None, axis=dim), axis, forward
        )
        high = lax.ppermute(lax.slice_in_dim(block, 0, width, axis=dim), axis, backward)
        block = jnp.concatenate([low, block, high], axis=dim)
    return block


def broadcast(x, axis, root):
    mine = lax.axis_index(axis) == root
    return lax.psum(jnp.where(mine, x, jnp.zeros_like(x)), axis)


def layer_norm(values, axis=-1):
    centre = values - jnp.mean(values, axis=axis, keepdims=True)
    spread = jnp.mean(centre * centre, axis=axis, keepdims=True)
    return centre * lax.rsqrt(spread + EPSILON)


def with_rim(field):
    return with_halo(field, (("row", 0), ("col", 1)), DMAX)


def gather_taps(padded, dilation, mirrored, height, breadth):
    windows = []
    for tap_index in range(9):
        row_tap = tap_index // 3
        col_tap = tap_index % 3
        if mirrored:
            row_tap = 2 - row_tap
            col_tap = 2 - col_tap
        row_start = DMAX + (row_tap - 1) * dilation
        col_start = DMAX + (col_tap - 1) * dilation
        windows.append(
            lax.dynamic_slice(
                padded, (row_start, col_start, jnp.int32(0)), (height, breadth, padded.shape[2])
            )
        )
    return jnp.concatenate(windows, axis=2).reshape(height * breadth, -1)


def sharded(
    pair, pair_mask, contact_mask, dilations, w_proj, w_gate, w_out, conv_one, conv_two, cotangent
):
    height, breadth, channels = pair.shape
    hidden = w_out.shape[0]
    row_count = lax.axis_size("row")
    col_count = lax.axis_size("col")
    ratio = col_count // row_count
    row_place = lax.axis_index("row")
    col_place = lax.axis_index("col")
    tokens = breadth * col_count
    pixels = height * breadth
    pair_flat = pair.astype(jnp.float32).reshape(pixels, channels)
    normed = layer_norm(pair_flat).astype(jnp.bfloat16)
    projected = jnp.dot(normed, w_proj, preferred_element_type=jnp.float32)
    mask_col = pair_mask.reshape(pixels, 1).astype(jnp.float32)
    left_side = (
        (mask_col * jax.nn.sigmoid(projected[:, hidden : 2 * hidden]) * projected[:, :hidden])
        .astype(jnp.bfloat16)
        .reshape(height, breadth, hidden)
    )
    right_side = (
        (
            mask_col
            * jax.nn.sigmoid(projected[:, 3 * hidden :])
            * projected[:, 2 * hidden : 3 * hidden]
        )
        .astype(jnp.bfloat16)
        .reshape(height, breadth, hidden)
    )
    right_all = lax.all_gather(right_side, "col", axis=1, tiled=True)
    offset = jnp.clip(col_place * breadth - row_place * height, 0, height - breadth)
    right_local = lax.dynamic_slice_in_dim(right_all, offset, breadth, 0)
    right_rows = broadcast(right_local, "row", col_place // ratio)
    products = jnp.einsum(
        "ikh,jkh->ijh",
        lax.all_gather(left_side, "col", axis=1, tiled=True),
        right_rows,
        preferred_element_type=jnp.float32,
    )
    product_norm = layer_norm(products.reshape(pixels, hidden)).astype(jnp.bfloat16)
    gating = jax.nn.sigmoid(jnp.dot(normed, w_gate, preferred_element_type=jnp.float32))
    updated = (
        pair_flat + gating * jnp.dot(product_norm, w_out, preferred_element_type=jnp.float32)
    ).astype(jnp.bfloat16)
    updated_f = updated.astype(jnp.float32)
    centre = updated_f - jnp.mean(updated_f, axis=-1, keepdims=True)
    inv_spread = lax.rsqrt(jnp.mean(centre * centre, axis=-1, keepdims=True) + EPSILON)
    scaled = centre * inv_spread
    contact = contact_mask.reshape(pixels, 1).astype(jnp.float32)
    first_in = (scaled * contact).astype(jnp.bfloat16).reshape(height, breadth, channels)
    rate_one = dilations[0]
    rate_two = dilations[1]
    first_taps = gather_taps(with_rim(first_in), rate_one, False, height, breadth)
    first_pre = jnp.dot(
        first_taps, conv_one.reshape(9 * channels, channels), preferred_element_type=jnp.float32
    )
    sigma = jax.nn.sigmoid(first_pre)
    second_in = (first_pre * sigma).astype(jnp.bfloat16).reshape(height, breadth, channels)
    second_taps = gather_taps(with_rim(second_in), rate_two, False, height, breadth)
    second_pre = jnp.dot(
        second_taps, conv_two.reshape(9 * channels, channels), preferred_element_type=jnp.float32
    )
    output = (updated_f + second_pre).astype(jnp.bfloat16).reshape(height, breadth, channels)
    cot_flat = cotangent.reshape(pixels, channels)
    grad_two = (
        lax.dot_general(
            second_taps, cot_flat, (((0,), (0,)), ((), ())), preferred_element_type=jnp.float32
        ).reshape(9, channels, channels)
        / tokens
    )
    cot_taps = gather_taps(with_rim(cotangent), rate_two, True, height, breadth)
    grad_hidden = jnp.dot(
        cot_taps,
        conv_two.transpose(0, 2, 1).reshape(9 * channels, channels),
        preferred_element_type=jnp.float32,
    )
    grad_pre = (grad_hidden * sigma * (1.0 + first_pre * (1.0 - sigma))).astype(jnp.bfloat16)
    grad_one = (
        lax.dot_general(
            first_taps, grad_pre, (((0,), (0,)), ((), ())), preferred_element_type=jnp.float32
        ).reshape(9, channels, channels)
        / tokens
    )
    grad_taps = gather_taps(
        with_rim(grad_pre.reshape(height, breadth, channels)), rate_one, True, height, breadth
    )
    grad_input = (
        jnp.dot(
            grad_taps,
            conv_one.transpose(0, 2, 1).reshape(9 * channels, channels),
            preferred_element_type=jnp.float32,
        )
        * contact
    )
    grad_norm = inv_spread * (
        grad_input
        - jnp.mean(grad_input, axis=-1, keepdims=True)
        - scaled * jnp.mean(grad_input * scaled, axis=-1, keepdims=True)
    )
    grad_pair = (
        (cot_flat.astype(jnp.float32) + grad_norm)
        .astype(jnp.bfloat16)
        .reshape(height, breadth, channels)
    )
    grad_one, grad_two = lax.psum((grad_one, grad_two), ("row", "col"))
    return (output, grad_pair, grad_one, grad_two)


def halvings(axis, count):
    return [(axis, count >> step) for step in range(1, count.bit_length())]


def exchange_plan(row_count, col_count):
    rows, cols = halvings("row", row_count), halvings("col", col_count)
    return cols + rows, rows[:-1] + cols + rows[-1:]


def exchange(held, hop):
    axis, distance = hop
    return lax.ppermute(held, axis, [(i, i ^ distance) for i in range(lax.axis_size(axis))])


def place_of(position, rounds, row_place, col_place):
    row, col = row_place, col_place
    for step, (axis, distance) in enumerate(rounds):
        bit = ((position >> step) & 1) * distance
        if axis == "row":
            row = row ^ bit
        else:
            col = col ^ bit
    return row, col


def slot_of(row_change, col_change, rounds):
    slot = 0
    for step, (axis, distance) in enumerate(rounds[:-1]):
        change = row_change if axis == "row" else col_change
        slot = slot | (((change // distance) & 1) << step)
    return slot


def sigmoid(values):
    return 0.5 + 0.5 * jnp.tanh(0.5 * values)


def matmul(left, right):
    return jnp.dot(left, right, preferred_element_type=jnp.float32)


def matmul_by_rows(left, right):
    rows = 256
    return jnp.concatenate(
        [matmul(left[i : i + rows], right) for i in range(0, left.shape[0], rows)], axis=0
    )


def matmul_nt(left, right):
    return lax.dot_general(
        left, right, (((1,), (1,)), ((), ())), preferred_element_type=jnp.float32
    )


def project_half(
    plan, core, pairs, w_proj, w_gate, left, right, swapped, gating, contact, start, turned
):
    rounds, _, height, breadth, tokens = plan
    channels, hidden = w_gate.shape[0], w_gate.shape[1]
    col_count, chips = tokens // breadth, tokens // height // 2
    row_place, col_place = lax.axis_index("row"), lax.axis_index("col")
    lane = lax.broadcasted_iota(jnp.int32, (height, breadth, channels), 2)
    place = lax.broadcasted_iota(jnp.int32, (height, breadth, channels), 0)
    own_lane = jnp.where((lane % height == place) & (lane < 2 * height), 1.0, 0.0)
    pick_lane = lax.broadcasted_iota(jnp.int32, (channels, 2 * channels), 0)
    pick_half = lax.broadcasted_iota(jnp.int32, (channels, 2 * channels), 1) // channels
    pick = jnp.where(pick_lane // height == pick_half, 1.0, 0.0).astype(jnp.bfloat16)
    pixels = height * breadth
    rows = 8
    for first in range(0, height, rows):
        values, masks = [], []
        for chip in range(chips):
            row_change = (chip * 2 + core) ^ row_place
            blocks, marks = [], []
            for col in range(col_count):
                col_change = col_place ^ col
                slot = slot_of(row_change, col_change, rounds)
                blocks.append(
                    pairs[slot, first * breadth : (first + rows) * breadth, :]
                    .astype(jnp.float32)
                    .reshape(rows, breadth, channels)
                )
                mark = pairs[slot, pixels:, :].astype(jnp.float32)[:breadth]
                marks.append(mark[None] * own_lane[first : first + rows])
            values.append(jnp.concatenate(blocks, axis=1).reshape(rows * tokens, channels))
            masks.append(jnp.concatenate(marks, axis=1).reshape(rows * tokens, channels))
        values = jnp.concatenate(values, axis=0)
        masks = matmul(jnp.concatenate(masks, axis=0).astype(jnp.bfloat16), pick)
        normed = layer_norm(values)
        gates = sigmoid(matmul(normed.astype(jnp.bfloat16), w_gate[...]))
        masked = (normed * masks[:, :channels]).astype(jnp.bfloat16)
        projected = matmul(masked, w_proj[...])
        sides = [
            sigmoid(projected[:, (2 * side + 1) * hidden : (2 * side + 2) * hidden])
            * projected[:, 2 * side * hidden : (2 * side + 1) * hidden]
            for side in range(2)
        ]
        for side, target in zip(sides, turned):
            side = side.reshape(chips, rows, tokens, hidden)
            for row in range(rows):
                strip = jnp.concatenate([side[chip, row] for chip in range(chips)], axis=0)
                target[pl.ds(first + row, hidden, stride=height + PITCH), :] = strip.T
        shape = (chips, rows, tokens, channels)
        span = slice(first, first + rows)
        gating[:, span] = gates.astype(jnp.bfloat16).reshape(shape)
        contact[:, span] = masks[:, channels:].astype(jnp.bfloat16).reshape(shape)
        start[:, span] = values.astype(jnp.bfloat16).reshape(shape)
    shape = (hidden, height + PITCH, chips * tokens)
    mine, other = turned[0][...], turned[1][...]
    for target, source in (
        (left, mine),
        (right, other),
        (swapped, pltpu.roll(other, tokens, 1)),
    ):
        target[...] = source.reshape(shape)[:, :height].astype(jnp.bfloat16)


def near_kernel(
    plan,
    near,
    w_proj,
    w_gate,
    two,
    left,
    right,
    swapped,
    gating,
    contact,
    start,
    two_t,
    two_copy,
    turned_left,
    turned_right,
):
    core = lax.axis_index("row") % 2
    two_copy[...] = two[...]
    channels = two.shape[1]
    for tap in range(9):
        two_t[tap * channels : (tap + 1) * channels] = two[tap].T
    project_half(
        plan,
        core,
        near,
        w_proj,
        w_gate,
        left,
        right,
        swapped,
        gating,
        contact,
        start,
        (turned_left, turned_right),
    )


def spread(source, rows, pad, rate, target):
    tokens, channels = target.shape[1], source.shape[2]
    for tap in range(3):
        first = DMAX + (tap - 1) * rate if tap != 1 else DMAX
        moved = source[pl.ds(pad + rows.start, rows.size), pl.ds(first, tokens), :]
        target[pl.ds(DMAX + rows.start, rows.size), :, tap * channels : (tap + 1) * channels] = (
            moved.astype(jnp.bfloat16)
        )


def taps(source, first, count, rate):
    tokens = source.shape[1]
    views = [
        source[pl.ds(DMAX + first + (tap - 1) * rate, count)].reshape(count * tokens, -1)
        for tap in range(3)
    ]
    return jnp.concatenate(views, axis=1)


def windows(source, rate, row_start, col_start, height, breadth):
    views = [
        source[
            pl.ds(row_start + DMAX + (tap // 3 - 1) * rate, height),
            pl.ds(col_start + DMAX + (tap % 3 - 1) * rate, breadth),
            :,
        ].reshape(height * breadth, -1)
        for tap in range(9)
    ]
    return jnp.concatenate(views, axis=1).astype(jnp.bfloat16)


def row_taps(strips, first, count, rate):
    views = [
        strips[tap, pl.ds(DMAX + first + ((tap - 1) * rate if tap != 1 else 0), count)]
        for tap in range(3)
    ]
    return views[0] + views[1] + views[2]


def clear_ends(strips, tokens):
    for tap in (0, 2):
        for rows in (slice(0, DMAX), slice(DMAX + tokens, 2 * DMAX + tokens)):
            strips[tap, rows] = jnp.zeros((DMAX,) + strips.shape[2:], jnp.float32)


def column_taps(source, weight, rate, first, count, strips):
    tokens = strips.shape[2]
    columns = [DMAX - rate, DMAX, DMAX + rate]
    flat = jnp.concatenate(
        [
            source[pl.ds(first, count), pl.ds(column, tokens), :].reshape(count * tokens, -1)
            for column in columns
        ],
        axis=1,
    ).astype(jnp.bfloat16)
    square = jnp.concatenate(
        [
            jnp.concatenate([weight(3 * row + col) for row in range(3)], axis=1)
            for col in range(3)
        ],
        axis=0,
    )
    result = matmul_by_rows(flat, square)
    channels = strips.shape[3]
    for tap in range(3):
        strips[tap, pl.ds(DMAX + first, count)] = result[
            :, tap * channels : (tap + 1) * channels
        ].reshape(count, tokens, channels)


def lanes(step, size):
    return pl.ds(pl.multiple_of(step * size, size), size)


def clear_border(target, tokens):
    line, channels = target.shape[1], target.shape[2]
    border = jnp.zeros((DMAX, line, channels), target.dtype)
    rim = jnp.zeros((tokens, DMAX, channels), target.dtype)
    if target.shape[0] > tokens:
        target[0:DMAX] = border
        target[DMAX + tokens :] = border
    if line > tokens:
        rows = slice(target.shape[0] - tokens - DMAX, target.shape[0] - DMAX)
        if target.shape[0] == tokens:
            rows = slice(0, tokens)
        target[rows, 0:DMAX, :] = rim
        target[rows, DMAX + tokens :, :] = rim


def forward_kernel(
    plan,
    dilations,
    far,
    w_proj,
    w_gate,
    w_out,
    one,
    near_left,
    near_right,
    near_swapped,
    near_gating,
    near_contact,
    near_start,
    pre,
    flipped,
    mine,
    own_contact,
    far_left,
    right,
    swapped,
    far_gating,
    far_contact,
    far_start,
    turned_left,
    turned_right,
    products,
    normed,
    updated,
    field,
    strips,
):
    _, _, height, breadth, tokens = plan
    hidden, channels = w_out.shape
    pixels = height * breadth
    chips = tokens // height // 2
    row_place, col_place = lax.axis_index("row"), lax.axis_index("col")
    core = row_place % 2
    rate_one = dilations[0]
    inside = slice(DMAX, DMAX + tokens)
    clear_border(field, tokens)
    clear_ends(strips, tokens)

    right[core] = near_right[...]
    swapped[core] = near_swapped[...]
    project_half(
        plan,
        1 - core,
        far,
        w_proj,
        w_gate,
        far_left,
        right.at[1 - core],
        swapped.at[1 - core],
        far_gating,
        far_contact,
        far_start,
        (turned_left, turned_right),
    )

    lane = lax.broadcasted_iota(jnp.int32, (height, chips * tokens), 1)
    low = jnp.where(lane < tokens, 1.0, 0.0).astype(jnp.bfloat16)
    high = jnp.where(lane < tokens, 0.0, 1.0).astype(jnp.bfloat16)
    batch = 128
    pitch = 2 * height + PITCH

    def multiply(step, carry):
        for part in range(batch):
            h = step * batch + part
            ahead = [right[0, h], right[1, h]]
            back = [swapped[0, h], swapped[1, h]]
            strips = [strip * low for strip in ahead + back]
            strips += [strip * high for strip in back + ahead]
            mine = jnp.concatenate([near_left[h], far_left[h]], axis=0)
            products[pl.ds(pl.multiple_of(h * pitch, 8), 2 * height), :] = matmul_nt(
                mine, jnp.concatenate(strips, axis=0)
            )
        return carry

    lax.fori_loop(0, hidden // batch, multiply, 0)

    chunk = 8
    size = chunk * tokens

    halves = (
        (core, near_gating, near_contact, near_start),
        (1 - core, far_gating, far_contact, far_start),
    )
    parts = height // chunk

    def normalise(step):
        half, first = step // parts, step % parts * chunk
        for row in range(chunk):
            strip = products[pl.ds(half * height + first + row, hidden, stride=pitch), :]
            strip = layer_norm(strip, axis=0).astype(jnp.bfloat16).T
            for chip in range(chips):
                normed[step, chip, row] = strip[chip * tokens : (chip + 1) * tokens]

    def update(step):
        first = step % parts * chunk
        side, gating, contact, start = halves[step // parts]
        change = matmul(normed[step].reshape(chips * size, hidden), w_out[...])
        change = change.reshape(chips, chunk, tokens, channels)
        rows = pl.ds(first, chunk)
        fresh = start[:, rows].astype(jnp.float32) + gating[:, rows].astype(jnp.float32) * change
        fresh = fresh.astype(jnp.bfloat16).astype(jnp.float32)
        first_in = layer_norm(fresh) * contact[:, rows].astype(jnp.float32)
        if step < parts:
            updated[:, rows] = fresh
        for chip in range(chips):
            base = (chip * 2 + side) * height + first
            field[pl.ds(base, chunk), inside, :] = first_in[chip]
            flipped[:, pl.ds(pl.multiple_of(base * tokens, size), size)] = (
                first_in[chip].reshape(size, channels).astype(jnp.bfloat16).T
            )

    def first_conv(step):
        side = halves[step // parts][0]
        for chip in range(chips):
            base = (chip * 2 + side) * height + step % parts * chunk
            column_taps(field, lambda tap: one[tap], rate_one, base, chunk, strips)

    count = 2 * parts
    for step in range(count + 2):
        if step >= 2:
            first_conv(step - 2)
        if step < count:
            normalise(step)
        if 1 <= step <= count:
            update(step - 1)

    for first in range(0, tokens, chunk):
        pre[pl.ds(first, chunk)] = row_taps(strips, first, chunk, rate_one)

    cols = pl.ds(pl.multiple_of(col_place * breadth, breadth), breadth)
    mine[...] = updated[row_place // 2, :, cols, :].reshape(pixels, channels)
    marks = near_contact[row_place // 2].astype(jnp.float32)
    place_col = lax.broadcasted_iota(jnp.int32, (tokens, channels), 0) // breadth
    marks = jnp.where((place_col == col_place)[None], marks, 0.0)
    marks = marks.reshape(height, tokens // breadth, breadth, channels)
    own_contact[...] = jnp.sum(marks, axis=1).reshape(pixels, channels)


def backward_kernel(
    plan,
    dilations,
    cot_near,
    cot_far,
    one,
    two,
    two_t,
    pre,
    flipped,
    mine,
    own_contact,
    output,
    grad_pair,
    grad_one,
    grad_two,
    field,
    wide_cot,
    wide_pre,
    grad_pre,
    second,
    sum_one,
    sum_two,
    scaled_one,
    scaled_two,
    sent,
):
    _, cot_rounds, height, breadth, tokens = plan
    channels = one.shape[2]
    pixels = height * breadth
    row_place, col_place = lax.axis_index("row"), lax.axis_index("col")
    rate_one, rate_two = dilations[0], dilations[1]
    half = cot_far.shape[0]
    inside = slice(DMAX, DMAX + tokens)
    for target in (field, wide_cot, wide_pre, grad_pre, second):
        clear_border(target, tokens)

    several = 8

    def place_cot(source, base):
        def body(step, carry):
            for i in range(several):
                slot = step * several + i
                row, col = place_of(base + slot, cot_rounds, row_place, col_place)
                cols = pl.ds(pl.multiple_of(DMAX + col * breadth, breadth), breadth)
                field[pl.ds(row * height, height), cols, :] = (
                    source[slot].astype(jnp.float32).reshape(height, breadth, channels)
                )
            return carry

        lax.fori_loop(0, half // several, body, 0)

    place_cot(cot_near, 0)
    place_cot(cot_far, half)
    chunk = 16
    size = chunk * tokens
    steps = tokens // chunk

    def spread_cot(step, carry):
        spread(field, pl.ds(step * chunk, chunk), 0, -rate_two, wide_cot)
        return carry

    lax.fori_loop(0, steps, spread_cot, 0)

    def back_two(step):
        first = step * chunk
        rows = pl.ds(DMAX + first, chunk)
        before_act = pre[pl.ds(first, chunk)]
        sigma = sigmoid(before_act)
        second_in = before_act * sigma
        second[rows, inside, :] = second_in
        factor = sigma * (1.0 + before_act * (1.0 - sigma))
        turned = second_in.reshape(size, channels).astype(jnp.bfloat16).T
        shifted = taps(wide_cot, first, chunk, -rate_two)
        before = matmul_by_rows(shifted, two_t[...]).reshape(chunk, tokens, channels)
        grad_pre[rows, inside, :] = (before * factor).astype(jnp.bfloat16).astype(jnp.float32)
        part = matmul(turned, shifted)
        sum_two[...] = part if step == 0 else sum_two[...] + part

    def spread_pre(step):
        spread(grad_pre, pl.ds(step * chunk, chunk), DMAX, -rate_one, wide_pre)

    def back_one(step):
        shifted = taps(wide_pre, step * chunk, chunk, -rate_one)
        part = matmul(flipped[:, step * size : (step + 1) * size], shifted)
        sum_one[...] = part if step == 0 else sum_one[...] + part

    def finish(total, scaled, target, row):
        for tap in range(3 * row, 3 * row + 3):
            columns = slice(tap * channels, (tap + 1) * channels)
            scaled[tap] = total[:, columns] * (1.0 / tokens)
        taps_done = pl.ds(3 * row, 3)
        copy = pltpu.make_async_copy(
            scaled.at[taps_done], target.at[taps_done], sent.at[len(copies)]
        )
        copy.start()
        copies.append(copy)

    copies = []
    for step in range(steps):
        if step >= 3:
            back_one(step - 3)
        if step >= 1:
            spread_pre(step - 1)
        back_two(step)
    for row in range(3):
        finish(sum_two, scaled_two, grad_two, row)
    for step in range(max(steps - 3, 0), steps - 2):
        back_one(step)
    spread_pre(steps - 1)
    back_one(steps - 2)

    spot = (row_place * height, col_place * breadth, height, breadth)
    second_pre = matmul(
        windows(second, rate_two, *spot), two[...].reshape(9 * channels, channels)
    )
    output[...] = (mine[...] + second_pre).astype(jnp.bfloat16)
    one_rows = [one[tap] for tap in range(9)]
    grad_input = own_contact[...] * matmul_nt(
        windows(grad_pre, -rate_one, *spot),
        jnp.concatenate(one_rows, axis=1),
    )
    centre = mine[...] - jnp.mean(mine[...], axis=-1, keepdims=True)
    inv_spread = lax.rsqrt(jnp.mean(centre * centre, axis=-1, keepdims=True) + EPSILON)
    scaled = centre * inv_spread
    grad_norm = inv_spread * (
        grad_input
        - jnp.mean(grad_input, axis=-1, keepdims=True)
        - scaled * jnp.mean(grad_input * scaled, axis=-1, keepdims=True)
    )
    grad_pair[...] = (cot_near[0].astype(jnp.float32) + grad_norm).astype(jnp.bfloat16)

    last = steps - 1
    for row in range(3):
        columns = slice(3 * row * channels, 3 * (row + 1) * channels)
        moved = pl.ds(DMAX + last * chunk - (row - 1) * rate_one, chunk)
        sum_one[:, columns] += matmul(
            flipped[:, last * size : (last + 1) * size], wide_pre[moved].reshape(size, -1)
        )
        finish(sum_one, scaled_one, grad_one, row)
    for copy in copies:
        copy.wait()


def replicated(
    pair, pair_mask, contact_mask, dilations, w_proj, w_gate, w_out, conv_one, conv_two, cotangent
):
    height, breadth, channels = pair.shape
    hidden = w_out.shape[0]
    row_count, col_count = lax.axis_size("row"), lax.axis_size("col")
    tokens = height * row_count
    pixels = height * breadth
    rounds, cot_rounds = exchange_plan(row_count, col_count)
    f32, bf16 = jnp.float32, jnp.bfloat16
    plan = (rounds, cot_rounds, height, breadth, tokens)
    chips = row_count // 2
    line = tokens + 2 * DMAX
    in_vmem = pl.BlockSpec(memory_space=pltpu.VMEM)
    side = ((hidden, height, chips * tokens), bf16)
    rows = (chips, height, tokens, channels)
    halves = [side] * 3 + [(rows, bf16)] * 3
    turned = pltpu.VMEM((hidden * (height + PITCH), chips * tokens), f32)
    stat = ((pixels, channels), f32)

    def shapes(*entries):
        return [jax.ShapeDtypeStruct(shape, dtype) for shape, dtype in entries]

    in_smem = pl.BlockSpec(memory_space=pltpu.SMEM)
    spare = channels - 2 * height
    marks = jnp.pad(pair_mask.T, ((pixels, breadth), (0, height + spare))) + jnp.pad(
        contact_mask.T, ((pixels, breadth), (height, spare))
    )
    above = jnp.pad(pair.reshape(pixels, channels), ((0, 2 * breadth), (0, 0)))
    held = (above.astype(f32) + marks.astype(f32)).astype(bf16)[None]
    block = cotangent.reshape(1, pixels, channels)
    cot_held = lax.optimization_barrier(jnp.maximum(block, jnp.finfo(bf16).min))
    rates = jnp.clip(dilations, 1, DMAX)
    for step in range(len(rounds) - 1):
        other = exchange(held, rounds[step])
        cot_other = exchange(cot_held if step else block, cot_rounds[step])
        held = lax.optimization_barrier(jnp.concatenate([held, other], axis=0))
        if step < len(rounds) - 2:
            cot_held = jnp.concatenate([cot_held, cot_other], axis=0)
            if step == len(rounds) - 3:
                cot_held, rates = lax.optimization_barrier((cot_held, rates))
            else:
                cot_held = lax.optimization_barrier(cot_held)
    near, far = held, exchange(held, rounds[-1])
    *near_parts, two_t, two = pl.pallas_call(
        functools.partial(near_kernel, plan),
        in_specs=[in_vmem] * 4,
        out_specs=[in_vmem] * 8,
        out_shape=shapes(
            *halves, ((9 * channels, channels), bf16), ((9, channels, channels), bf16)
        ),
        scratch_shapes=[turned] * 2,
        compiler_params=pltpu.CompilerParams(vmem_limit_bytes=VMEM_LIMIT // 3),
        cost_estimate=pl.CostEstimate(
            flops=tokens * tokens * channels * 5 * hidden,
            bytes_accessed=8 * tokens * tokens * channels,
            transcendentals=3 * tokens * tokens * channels // 2,
        ),
    )(near, w_proj, w_gate, conv_two)
    cot_other, two_t = lax.optimization_barrier((cot_other, two_t))
    cot_near = jnp.concatenate([cot_held, cot_other], axis=0)
    cot_far = exchange(cot_near, cot_rounds[-1])
    padded = pltpu.VMEM((tokens, line, channels), f32)
    bordered = pltpu.VMEM((line, line, channels), f32)
    tripled = pltpu.VMEM((line, tokens, 3 * channels), bf16)
    both = pltpu.VMEM((2,) + side[0], bf16)
    alone = pltpu.VMEM(rows, bf16)
    flat = ((channels, tokens * tokens), bf16)
    sums = pltpu.VMEM((channels, 9 * channels), f32)
    held = pl.pallas_call(
        functools.partial(forward_kernel, plan),
        in_specs=[in_smem] + [in_vmem] * 11,
        out_specs=[in_vmem] * 4,
        out_shape=shapes(((tokens, tokens, channels), f32), flat, stat, stat),
        scratch_shapes=[pltpu.VMEM(*side), both, both, alone, alone, alone]
        + [turned] * 2
        + [pltpu.VMEM((hidden * (2 * height + PITCH), chips * tokens), f32)]
        + [pltpu.VMEM((2 * height // 8, chips, 8, tokens, hidden), bf16)]
        + [pltpu.VMEM(rows, f32), padded]
        + [pltpu.VMEM((3, line, tokens, channels), f32)],
        compiler_params=pltpu.CompilerParams(vmem_limit_bytes=FORWARD_VMEM),
        cost_estimate=pl.CostEstimate(
            flops=tokens * tokens * channels * 40 * hidden,
            bytes_accessed=40 * tokens * tokens * channels,
            transcendentals=4 * tokens * tokens * channels,
        ),
    )(
        rates,
        far,
        w_proj,
        w_gate,
        w_out,
        conv_one,
        *near_parts,
    )
    output, grad_pair, grad_one, grad_two = pl.pallas_call(
        functools.partial(backward_kernel, plan),
        in_specs=[in_smem] + [in_vmem] * 9,
        out_specs=[in_vmem] * 2 + [pl.BlockSpec(memory_space=pltpu.HBM)] * 2,
        out_shape=shapes(
            ((pixels, channels), bf16),
            ((pixels, channels), bf16),
            ((9, channels, channels), f32),
            ((9, channels, channels), f32),
        ),
        scratch_shapes=[padded, tripled, tripled, bordered, bordered, sums, sums]
        + [pltpu.VMEM((9, channels, channels), f32)] * 2
        + [pltpu.SemaphoreType.DMA((6,))],
        compiler_params=pltpu.CompilerParams(vmem_limit_bytes=BACKWARD_VMEM),
    )(
        rates,
        cot_near,
        cot_far,
        conv_one,
        two,
        two_t,
        *held,
    )
    block = (height, breadth, channels)
    return output.reshape(block), grad_pair.reshape(block), grad_one, grad_two


def fits(pair, w_out, row_count, col_count):
    height, breadth, channels = pair.shape
    tokens = height * row_count
    powers = all(count & (count - 1) == 0 for count in (row_count, col_count))
    whole = (tokens + 2 * DMAX) ** 2 * channels
    return (
        powers
        and row_count * col_count >= 8
        and height * breadth == channels == w_out.shape[0]
        and breadth == 8
        and row_count // 2 * tokens == channels
        and whole * 60 <= VMEM_LIMIT
    )


def local(*arguments):
    pair, w_out = arguments[0], arguments[6]
    if fits(pair, w_out, lax.axis_size("row"), lax.axis_size("col")):
        return replicated(*arguments)
    return sharded(*arguments)


def solution(mesh):
    in_specs = (
        P("row", "col", None),
        P("row", "col"),
        P("row", "col"),
        P(),
        P(),
        P(),
        P(),
        P(),
        P(),
        P("row", "col", None),
    )
    out_specs = (P("row", "col", None), P("row", "col", None), P(), P())
    return jax.shard_map(local, mesh=mesh, in_specs=in_specs, out_specs=out_specs, check_vma=False)
```

```python
import functools

import jax
import jax.numpy as jnp
from jax import lax
from jax.experimental import pallas as pl
from jax.experimental.pallas import tpu as pltpu
from jax.sharding import PartitionSpec as P

DMAX = 8
VMEM_LIMIT = 48 * 1024 * 1024
PITCH = 8
FORWARD_VMEM = 32 * 1024 * 1024
BACKWARD_VMEM = 36 * 1024 * 1024


EPSILON = 1e-05


def with_halo(block, sides, width):
    for axis, dim in sides:
        count = lax.axis_size(axis)
        forward = [(i, i + 1) for i in range(count - 1)]
        backward = [(target, source) for source, target in forward]
        low = lax.ppermute(
            lax.slice_in_dim(block, block.shape[dim] - width, None, axis=dim), axis, forward
        )
        high = lax.ppermute(lax.slice_in_dim(block, 0, width, axis=dim), axis, backward)
        block = jnp.concatenate([low, block, high], axis=dim)
    return block


def broadcast(x, axis, root):
    mine = lax.axis_index(axis) == root
    return lax.psum(jnp.where(mine, x, jnp.zeros_like(x)), axis)


def layer_norm(values, axis=-1):
    centre = values - jnp.mean(values, axis=axis, keepdims=True)
    spread = jnp.mean(centre * centre, axis=axis, keepdims=True)
    return centre * lax.rsqrt(spread + EPSILON)


def with_rim(field):
    return with_halo(field, (("row", 0), ("col", 1)), DMAX)


def gather_taps(padded, dilation, mirrored, height, breadth):
    windows = []
    for tap_index in range(9):
        row_tap = tap_index // 3
        col_tap = tap_index % 3
        if mirrored:
            row_tap = 2 - row_tap
            col_tap = 2 - col_tap
        row_start = DMAX + (row_tap - 1) * dilation
        col_start = DMAX + (col_tap - 1) * dilation
        windows.append(
            lax.dynamic_slice(
                padded, (row_start, col_start, jnp.int32(0)), (height, breadth, padded.shape[2])
            )
        )
    return jnp.concatenate(windows, axis=2).reshape(height * breadth, -1)


def sharded(
    pair, pair_mask, contact_mask, dilations, w_proj, w_gate, w_out, conv_one, conv_two, cotangent
):
    height, breadth, channels = pair.shape
    hidden = w_out.shape[0]
    row_count = lax.axis_size("row")
    col_count = lax.axis_size("col")
    ratio = col_count // row_count
    row_place = lax.axis_index("row")
    col_place = lax.axis_index("col")
    tokens = breadth * col_count
    pixels = height * breadth
    pair_flat = pair.astype(jnp.float32).reshape(pixels, channels)
    normed = layer_norm(pair_flat).astype(jnp.bfloat16)
    projected = jnp.dot(normed, w_proj, preferred_element_type=jnp.float32)
    mask_col = pair_mask.reshape(pixels, 1).astype(jnp.float32)
    left_side = (
        (mask_col * jax.nn.sigmoid(projected[:, hidden : 2 * hidden]) * projected[:, :hidden])
        .astype(jnp.bfloat16)
        .reshape(height, breadth, hidden)
    )
    right_side = (
        (
            mask_col
            * jax.nn.sigmoid(projected[:, 3 * hidden :])
            * projected[:, 2 * hidden : 3 * hidden]
        )
        .astype(jnp.bfloat16)
        .reshape(height, breadth, hidden)
    )
    right_all = lax.all_gather(right_side, "col", axis=1, tiled=True)
    offset = jnp.clip(col_place * breadth - row_place * height, 0, height - breadth)
    right_local = lax.dynamic_slice_in_dim(right_all, offset, breadth, 0)
    right_rows = broadcast(right_local, "row", col_place // ratio)
    products = jnp.einsum(
        "ikh,jkh->ijh",
        lax.all_gather(left_side, "col", axis=1, tiled=True),
        right_rows,
        preferred_element_type=jnp.float32,
    )
    product_norm = layer_norm(products.reshape(pixels, hidden)).astype(jnp.bfloat16)
    gating = jax.nn.sigmoid(jnp.dot(normed, w_gate, preferred_element_type=jnp.float32))
    updated = (
        pair_flat + gating * jnp.dot(product_norm, w_out, preferred_element_type=jnp.float32)
    ).astype(jnp.bfloat16)
    updated_f = updated.astype(jnp.float32)
    centre = updated_f - jnp.mean(updated_f, axis=-1, keepdims=True)
    inv_spread = lax.rsqrt(jnp.mean(centre * centre, axis=-1, keepdims=True) + EPSILON)
    scaled = centre * inv_spread
    contact = contact_mask.reshape(pixels, 1).astype(jnp.float32)
    first_in = (scaled * contact).astype(jnp.bfloat16).reshape(height, breadth, channels)
    rate_one = dilations[0]
    rate_two = dilations[1]
    first_taps = gather_taps(with_rim(first_in), rate_one, False, height, breadth)
    first_pre = jnp.dot(
        first_taps, conv_one.reshape(9 * channels, channels), preferred_element_type=jnp.float32
    )
    sigma = jax.nn.sigmoid(first_pre)
    second_in = (first_pre * sigma).astype(jnp.bfloat16).reshape(height, breadth, channels)
    second_taps = gather_taps(with_rim(second_in), rate_two, False, height, breadth)
    second_pre = jnp.dot(
        second_taps, conv_two.reshape(9 * channels, channels), preferred_element_type=jnp.float32
    )
    output = (updated_f + second_pre).astype(jnp.bfloat16).reshape(height, breadth, channels)
    cot_flat = cotangent.reshape(pixels, channels)
    grad_two = (
        lax.dot_general(
            second_taps, cot_flat, (((0,), (0,)), ((), ())), preferred_element_type=jnp.float32
        ).reshape(9, channels, channels)
        / tokens
    )
    cot_taps = gather_taps(with_rim(cotangent), rate_two, True, height, breadth)
    grad_hidden = jnp.dot(
        cot_taps,
        conv_two.transpose(0, 2, 1).reshape(9 * channels, channels),
        preferred_element_type=jnp.float32,
    )
    grad_pre = (grad_hidden * sigma * (1.0 + first_pre * (1.0 - sigma))).astype(jnp.bfloat16)
    grad_one = (
        lax.dot_general(
            first_taps, grad_pre, (((0,), (0,)), ((), ())), preferred_element_type=jnp.float32
        ).reshape(9, channels, channels)
        / tokens
    )
    grad_taps = gather_taps(
        with_rim(grad_pre.reshape(height, breadth, channels)), rate_one, True, height, breadth
    )
    grad_input = (
        jnp.dot(
            grad_taps,
            conv_one.transpose(0, 2, 1).reshape(9 * channels, channels),
            preferred_element_type=jnp.float32,
        )
        * contact
    )
    grad_norm = inv_spread * (
        grad_input
        - jnp.mean(grad_input, axis=-1, keepdims=True)
        - scaled * jnp.mean(grad_input * scaled, axis=-1, keepdims=True)
    )
    grad_pair = (
        (cot_flat.astype(jnp.float32) + grad_norm)
        .astype(jnp.bfloat16)
        .reshape(height, breadth, channels)
    )
    grad_one, grad_two = lax.psum((grad_one, grad_two), ("row", "col"))
    return (output, grad_pair, grad_one, grad_two)


def halvings(axis, count):
    return [(axis, count >> step) for step in range(1, count.bit_length())]


def exchange_plan(row_count, col_count):
    rows, cols = halvings("row", row_count), halvings("col", col_count)
    return cols + rows, rows[:-1] + cols + rows[-1:]


def exchange(held, hop):
    axis, distance = hop
    return lax.ppermute(held, axis, [(i, i ^ distance) for i in range(lax.axis_size(axis))])


def place_of(position, rounds, row_place, col_place):
    row, col = row_place, col_place
    for step, (axis, distance) in enumerate(rounds):
        bit = ((position >> step) & 1) * distance
        if axis == "row":
            row = row ^ bit
        else:
            col = col ^ bit
    return row, col


def slot_of(row_change, col_change, rounds):
    slot = 0
    for step, (axis, distance) in enumerate(rounds[:-1]):
        change = row_change if axis == "row" else col_change
        slot = slot | (((change // distance) & 1) << step)
    return slot


def sigmoid(values):
    return 0.5 + 0.5 * jnp.tanh(0.5 * values)


def matmul(left, right):
    return jnp.dot(left, right, preferred_element_type=jnp.float32)


def matmul_by_rows(left, right):
    rows = 256
    return jnp.concatenate(
        [matmul(left[i : i + rows], right) for i in range(0, left.shape[0], rows)], axis=0
    )


def matmul_nt(left, right):
    return lax.dot_general(
        left, right, (((1,), (1,)), ((), ())), preferred_element_type=jnp.float32
    )


def project_half(
    plan, core, pairs, w_proj, w_gate, left, right, swapped, gating, contact, start, turned
):
    rounds, _, height, breadth, tokens = plan
    channels, hidden = w_gate.shape[0], w_gate.shape[1]
    col_count, chips = tokens // breadth, tokens // height // 2
    row_place, col_place = lax.axis_index("row"), lax.axis_index("col")
    lane = lax.broadcasted_iota(jnp.int32, (height, breadth, channels), 2)
    place = lax.broadcasted_iota(jnp.int32, (height, breadth, channels), 0)
    own_lane = jnp.where((lane % height == place) & (lane < 2 * height), 1.0, 0.0)
    pick_lane = lax.broadcasted_iota(jnp.int32, (channels, 2 * channels), 0)
    pick_half = lax.broadcasted_iota(jnp.int32, (channels, 2 * channels), 1) // channels
    pick = jnp.where(pick_lane // height == pick_half, 1.0, 0.0).astype(jnp.bfloat16)
    pixels = height * breadth
    rows = 8
    for first in range(0, height, rows):
        values, masks = [], []
        for chip in range(chips):
            row_change = (chip * 2 + core) ^ row_place
            blocks, marks = [], []
            for col in range(col_count):
                col_change = col_place ^ col
                slot = slot_of(row_change, col_change, rounds)
                blocks.append(
                    pairs[slot, first * breadth : (first + rows) * breadth, :]
                    .astype(jnp.float32)
                    .reshape(rows, breadth, channels)
                )
                mark = pairs[slot, pixels:, :].astype(jnp.float32)[:breadth]
                marks.append(mark[None] * own_lane[first : first + rows])
            values.append(jnp.concatenate(blocks, axis=1).reshape(rows * tokens, channels))
            masks.append(jnp.concatenate(marks, axis=1).reshape(rows * tokens, channels))
        values = jnp.concatenate(values, axis=0)
        masks = matmul(jnp.concatenate(masks, axis=0).astype(jnp.bfloat16), pick)
        normed = layer_norm(values)
        gates = sigmoid(matmul(normed.astype(jnp.bfloat16), w_gate[...]))
        masked = (normed * masks[:, :channels]).astype(jnp.bfloat16)
        projected = matmul(masked, w_proj[...])
        sides = [
            sigmoid(projected[:, (2 * side + 1) * hidden : (2 * side + 2) * hidden])
            * projected[:, 2 * side * hidden : (2 * side + 1) * hidden]
            for side in range(2)
        ]
        for side, target in zip(sides, turned):
            side = side.reshape(chips, rows, tokens, hidden)
            for row in range(rows):
                strip = jnp.concatenate([side[chip, row] for chip in range(chips)], axis=0)
                target[pl.ds(first + row, hidden, stride=height + PITCH), :] = strip.T
        shape = (chips, rows, tokens, channels)
        span = slice(first, first + rows)
        gating[:, span] = gates.astype(jnp.bfloat16).reshape(shape)
        contact[:, span] = masks[:, channels:].astype(jnp.bfloat16).reshape(shape)
        start[:, span] = values.astype(jnp.bfloat16).reshape(shape)
    shape = (hidden, height + PITCH, chips * tokens)
    mine, other = turned[0][...], turned[1][...]
    for target, source in (
        (left, mine),
        (right, other),
        (swapped, pltpu.roll(other, tokens, 1)),
    ):
        target[...] = source.reshape(shape)[:, :height].astype(jnp.bfloat16)


def near_kernel(
    plan,
    near,
    w_proj,
    w_gate,
    two,
    left,
    right,
    swapped,
    gating,
    contact,
    start,
    two_t,
    two_copy,
    turned_left,
    turned_right,
):
    core = lax.axis_index("row") % 2
    two_copy[...] = two[...]
    channels = two.shape[1]
    for tap in range(9):
        two_t[tap * channels : (tap + 1) * channels] = two[tap].T
    project_half(
        plan,
        core,
        near,
        w_proj,
        w_gate,
        left,
        right,
        swapped,
        gating,
        contact,
        start,
        (turned_left, turned_right),
    )


def spread(source, rows, pad, rate, target):
    tokens, channels = target.shape[1], source.shape[2]
    for tap in range(3):
        first = DMAX + (tap - 1) * rate if tap != 1 else DMAX
        moved = source[pl.ds(pad + rows.start, rows.size), pl.ds(first, tokens), :]
        target[pl.ds(DMAX + rows.start, rows.size), :, tap * channels : (tap + 1) * channels] = (
            moved.astype(jnp.bfloat16)
        )


def taps(source, first, count, rate):
    tokens = source.shape[1]
    views = [
        source[pl.ds(DMAX + first + (tap - 1) * rate, count)].reshape(count * tokens, -1)
        for tap in range(3)
    ]
    return jnp.concatenate(views, axis=1)


def silu(values):
    return values * sigmoid(values)


def windows(source, rate, row_start, col_start, height, breadth, change=lambda values: values):
    views = [
        change(
            source[
                pl.ds(row_start + DMAX + (tap // 3 - 1) * rate, height),
                pl.ds(col_start + DMAX + (tap % 3 - 1) * rate, breadth),
                :,
            ]
        ).reshape(height * breadth, -1)
        for tap in range(9)
    ]
    return jnp.concatenate(views, axis=1).astype(jnp.bfloat16)


def row_taps(strips, first, count, rate):
    views = [
        strips[tap, pl.ds(DMAX + first + ((tap - 1) * rate if tap != 1 else 0), count)].astype(
            jnp.float32
        )
        for tap in range(3)
    ]
    return views[0] + views[1] + views[2]


def clear_ends(strips, tokens):
    for tap in (0, 2):
        for rows in (slice(0, DMAX), slice(DMAX + tokens, 2 * DMAX + tokens)):
            strips[tap, rows] = jnp.zeros((DMAX,) + strips.shape[2:], strips.dtype)


def column_taps(source, weight, rate, first, count, strips):
    tokens = strips.shape[2]
    columns = [DMAX - rate, DMAX, DMAX + rate]
    flat = jnp.concatenate(
        [
            source[pl.ds(first, count), pl.ds(column, tokens), :].reshape(count * tokens, -1)
            for column in columns
        ],
        axis=1,
    ).astype(jnp.bfloat16)
    square = jnp.concatenate(
        [
            jnp.concatenate([weight(3 * row + col) for row in range(3)], axis=1)
            for col in range(3)
        ],
        axis=0,
    )
    result = matmul_by_rows(flat, square)
    channels = strips.shape[3]
    for tap in range(3):
        strips[tap, pl.ds(DMAX + first, count)] = result[
            :, tap * channels : (tap + 1) * channels
        ].reshape(count, tokens, channels).astype(strips.dtype)


def clear_around(target, row_start, col_start, height, breadth):
    shape = (height + 2 * DMAX, breadth + 2 * DMAX, target.shape[2])
    cols = pl.ds(pl.multiple_of(col_start, 8), shape[1])
    target[pl.ds(row_start, shape[0]), cols, :] = jnp.zeros(shape, target.dtype)


def lanes(step, size):
    return pl.ds(pl.multiple_of(step * size, size), size)


def clear_border(target, tokens):
    line, channels = target.shape[1], target.shape[2]
    border = jnp.zeros((DMAX, line, channels), target.dtype)
    rim = jnp.zeros((tokens, DMAX, channels), target.dtype)
    if target.shape[0] > tokens:
        target[0:DMAX] = border
        target[DMAX + tokens :] = border
    if line > tokens:
        rows = slice(target.shape[0] - tokens - DMAX, target.shape[0] - DMAX)
        if target.shape[0] == tokens:
            rows = slice(0, tokens)
        target[rows, 0:DMAX, :] = rim
        target[rows, DMAX + tokens :, :] = rim


def forward_kernel(
    plan,
    dilations,
    far,
    w_proj,
    w_gate,
    w_out,
    one,
    near_left,
    near_right,
    near_swapped,
    near_gating,
    near_contact,
    near_start,
    pre,
    flipped,
    mine,
    own_contact,
    far_left,
    right,
    swapped,
    far_gating,
    far_contact,
    far_start,
    turned_left,
    turned_right,
    products,
    normed,
    updated,
    field,
    strips,
):
    _, _, height, breadth, tokens = plan
    hidden, channels = w_out.shape
    pixels = height * breadth
    chips = tokens // height // 2
    row_place, col_place = lax.axis_index("row"), lax.axis_index("col")
    core = row_place % 2
    rate_one = dilations[0]
    inside = slice(DMAX, DMAX + tokens)
    clear_border(field, tokens)
    clear_ends(strips, tokens)

    right[core] = near_right[...]
    swapped[core] = near_swapped[...]
    project_half(
        plan,
        1 - core,
        far,
        w_proj,
        w_gate,
        far_left,
        right.at[1 - core],
        swapped.at[1 - core],
        far_gating,
        far_contact,
        far_start,
        (turned_left, turned_right),
    )

    lane = lax.broadcasted_iota(jnp.int32, (height, chips * tokens), 1)
    low = jnp.where(lane < tokens, 1.0, 0.0).astype(jnp.bfloat16)
    high = jnp.where(lane < tokens, 0.0, 1.0).astype(jnp.bfloat16)
    batch = 128
    pitch = 2 * height + PITCH

    def multiply(step, carry):
        for part in range(batch):
            h = step * batch + part
            ahead = [right[0, h], right[1, h]]
            back = [swapped[0, h], swapped[1, h]]
            strips = [strip * low for strip in ahead + back]
            strips += [strip * high for strip in back + ahead]
            mine = jnp.concatenate([near_left[h], far_left[h]], axis=0)
            products[pl.ds(pl.multiple_of(h * pitch, 8), 2 * height), :] = matmul_nt(
                mine, jnp.concatenate(strips, axis=0)
            )
        return carry

    lax.fori_loop(0, hidden // batch, multiply, 0)

    chunk = 8
    size = chunk * tokens

    halves = (
        (core, near_gating, near_contact, near_start),
        (1 - core, far_gating, far_contact, far_start),
    )
    parts = height // chunk

    def normalise(step):
        half, first = step // parts, step % parts * chunk
        for row in range(chunk):
            strip = products[pl.ds(half * height + first + row, hidden, stride=pitch), :]
            strip = layer_norm(strip, axis=0).astype(jnp.bfloat16).T
            for chip in range(chips):
                normed[step, chip, row] = strip[chip * tokens : (chip + 1) * tokens]

    def update(step):
        first = step % parts * chunk
        side, gating, contact, start = halves[step // parts]
        change = matmul(normed[step].reshape(chips * size, hidden), w_out[...])
        change = change.reshape(chips, chunk, tokens, channels)
        rows = pl.ds(first, chunk)
        fresh = start[:, rows].astype(jnp.float32) + gating[:, rows].astype(jnp.float32) * change
        fresh = fresh.astype(jnp.bfloat16).astype(jnp.float32)
        first_in = layer_norm(fresh) * contact[:, rows].astype(jnp.float32)
        if step < parts:
            updated[:, rows] = fresh
        for chip in range(chips):
            base = (chip * 2 + side) * height + first
            field[pl.ds(base, chunk), inside, :] = first_in[chip]
            flipped[:, pl.ds(pl.multiple_of(base * tokens, size), size)] = (
                first_in[chip].reshape(size, channels).astype(jnp.bfloat16).T
            )

    def first_conv(step):
        side = halves[step // parts][0]
        for chip in range(chips):
            base = (chip * 2 + side) * height + step % parts * chunk
            column_taps(field, lambda tap: one[tap], rate_one, base, chunk, strips)

    count = 2 * parts
    for step in range(count + 2):
        if step >= 2:
            first_conv(step - 2)
        if step < count:
            normalise(step)
        if 1 <= step <= count:
            update(step - 1)

    clear_around(pre, row_place * height, col_place * breadth, height, breadth)
    for first in range(0, tokens, chunk):
        pre[pl.ds(DMAX + first, chunk), inside, :] = row_taps(strips, first, chunk, rate_one)

    cols = pl.ds(pl.multiple_of(col_place * breadth, breadth), breadth)
    mine[...] = updated[row_place // 2, :, cols, :].reshape(pixels, channels)
    marks = near_contact[row_place // 2].astype(jnp.float32)
    place_col = lax.broadcasted_iota(jnp.int32, (tokens, channels), 0) // breadth
    marks = jnp.where((place_col == col_place)[None], marks, 0.0)
    marks = marks.reshape(height, tokens // breadth, breadth, channels)
    own_contact[...] = jnp.sum(marks, axis=1).reshape(pixels, channels)


def backward_kernel(
    plan,
    dilations,
    cot_near,
    cot_far,
    one,
    two,
    two_t,
    pre,
    flipped,
    mine,
    own_contact,
    output,
    grad_pair,
    grad_one,
    grad_two,
    field,
    wide_cot,
    wide_pre,
    grad_pre,
    sum_one,
    sum_two,
    scaled_one,
    scaled_two,
    sent,
):
    _, cot_rounds, height, breadth, tokens = plan
    channels = one.shape[2]
    pixels = height * breadth
    row_place, col_place = lax.axis_index("row"), lax.axis_index("col")
    rate_one, rate_two = dilations[0], dilations[1]
    half = cot_far.shape[0]
    inside = slice(DMAX, DMAX + tokens)
    for target in (field, wide_cot, wide_pre, grad_pre):
        clear_border(target, tokens)

    several = 8

    def place_cot(source, base):
        def body(step, carry):
            for i in range(several):
                slot = step * several + i
                row, col = place_of(base + slot, cot_rounds, row_place, col_place)
                cols = pl.ds(pl.multiple_of(DMAX + col * breadth, breadth), breadth)
                field[pl.ds(row * height, height), cols, :] = (
                    source[slot].astype(jnp.float32).reshape(height, breadth, channels)
                )
            return carry

        lax.fori_loop(0, half // several, body, 0)

    place_cot(cot_near, 0)
    place_cot(cot_far, half)
    chunk = 16
    size = chunk * tokens
    steps = tokens // chunk

    def spread_cot(step, carry):
        spread(field, pl.ds(step * chunk, chunk), 0, -rate_two, wide_cot)
        return carry

    lax.fori_loop(0, steps, spread_cot, 0)

    def back_two(step):
        first = step * chunk
        rows = pl.ds(DMAX + first, chunk)
        before_act = pre[rows, inside, :]
        sigma = sigmoid(before_act)
        second_in = before_act * sigma
        factor = sigma * (1.0 + before_act * (1.0 - sigma))
        turned = second_in.reshape(size, channels).astype(jnp.bfloat16).T
        shifted = taps(wide_cot, first, chunk, -rate_two)
        before = matmul_by_rows(shifted, two_t[...]).reshape(chunk, tokens, channels)
        grad_pre[rows, inside, :] = (before * factor).astype(jnp.bfloat16).astype(jnp.float32)
        part = matmul(turned, shifted)
        sum_two[...] = part if step == 0 else sum_two[...] + part

    def spread_pre(step):
        spread(grad_pre, pl.ds(step * chunk, chunk), DMAX, -rate_one, wide_pre)

    def back_one(step):
        shifted = taps(wide_pre, step * chunk, chunk, -rate_one)
        part = matmul(flipped[:, step * size : (step + 1) * size], shifted)
        sum_one[...] = part if step == 0 else sum_one[...] + part

    def finish(total, scaled, target, row):
        for tap in range(3 * row, 3 * row + 3):
            columns = slice(tap * channels, (tap + 1) * channels)
            scaled[tap] = total[:, columns] * (1.0 / tokens)
        taps_done = pl.ds(3 * row, 3)
        copy = pltpu.make_async_copy(
            scaled.at[taps_done], target.at[taps_done], sent.at[len(copies)]
        )
        copy.start()
        copies.append(copy)

    copies = []
    for step in range(steps):
        if step >= 3:
            back_one(step - 3)
        if step >= 1:
            spread_pre(step - 1)
        back_two(step)
    spread_pre(steps - 1)
    for row in range(3):
        finish(sum_two, scaled_two, grad_two, row)
    for step in range(max(steps - 3, 0), steps - 1):
        back_one(step)

    spot = (row_place * height, col_place * breadth, height, breadth)
    second_pre = matmul(
        windows(pre, rate_two, *spot, silu), two[...].reshape(9 * channels, channels)
    )
    output[...] = (mine[...] + second_pre).astype(jnp.bfloat16)
    one_rows = [one[tap] for tap in range(9)]
    grad_input = own_contact[...] * matmul_nt(
        windows(grad_pre, -rate_one, *spot),
        jnp.concatenate(one_rows, axis=1),
    )
    centre = mine[...] - jnp.mean(mine[...], axis=-1, keepdims=True)
    inv_spread = lax.rsqrt(jnp.mean(centre * centre, axis=-1, keepdims=True) + EPSILON)
    scaled = centre * inv_spread
    grad_norm = inv_spread * (
        grad_input
        - jnp.mean(grad_input, axis=-1, keepdims=True)
        - scaled * jnp.mean(grad_input * scaled, axis=-1, keepdims=True)
    )
    grad_pair[...] = (cot_near[0].astype(jnp.float32) + grad_norm).astype(jnp.bfloat16)

    last = steps - 1
    for row in range(3):
        columns = slice(3 * row * channels, 3 * (row + 1) * channels)
        moved = pl.ds(DMAX + last * chunk - (row - 1) * rate_one, chunk)
        sum_one[:, columns] += matmul(
            flipped[:, last * size : (last + 1) * size], wide_pre[moved].reshape(size, -1)
        )
        finish(sum_one, scaled_one, grad_one, row)
    for copy in copies:
        copy.wait()


def replicated(
    pair, pair_mask, contact_mask, dilations, w_proj, w_gate, w_out, conv_one, conv_two, cotangent
):
    height, breadth, channels = pair.shape
    hidden = w_out.shape[0]
    row_count, col_count = lax.axis_size("row"), lax.axis_size("col")
    tokens = height * row_count
    pixels = height * breadth
    rounds, cot_rounds = exchange_plan(row_count, col_count)
    f32, bf16 = jnp.float32, jnp.bfloat16
    plan = (rounds, cot_rounds, height, breadth, tokens)
    chips = row_count // 2
    line = tokens + 2 * DMAX
    in_vmem = pl.BlockSpec(memory_space=pltpu.VMEM)
    side = ((hidden, height, chips * tokens), bf16)
    rows = (chips, height, tokens, channels)
    halves = [side] * 3 + [(rows, bf16)] * 3
    turned = pltpu.VMEM((hidden * (height + PITCH), chips * tokens), f32)
    stat = ((pixels, channels), f32)

    def shapes(*entries):
        return [jax.ShapeDtypeStruct(shape, dtype) for shape, dtype in entries]

    in_smem = pl.BlockSpec(memory_space=pltpu.SMEM)
    spare = channels - 2 * height
    marks = jnp.pad(pair_mask.T, ((pixels, breadth), (0, height + spare))) + jnp.pad(
        contact_mask.T, ((pixels, breadth), (height, spare))
    )
    above = jnp.pad(pair.reshape(pixels, channels), ((0, 2 * breadth), (0, 0)))
    held = (above.astype(f32) + marks.astype(f32)).astype(bf16)[None]
    block = cotangent.reshape(1, pixels, channels)
    cot_held = lax.optimization_barrier(jnp.maximum(block, jnp.finfo(bf16).min))
    rates = jnp.clip(dilations, 1, DMAX)
    for step in range(len(rounds) - 1):
        other = exchange(held, rounds[step])
        cot_other = exchange(cot_held if step else block, cot_rounds[step])
        held = lax.optimization_barrier(jnp.concatenate([held, other], axis=0))
        if step < len(rounds) - 2:
            cot_held = jnp.concatenate([cot_held, cot_other], axis=0)
            if step == len(rounds) - 3:
                cot_held, rates = lax.optimization_barrier((cot_held, rates))
            else:
                cot_held = lax.optimization_barrier(cot_held)
    near, far = held, exchange(held, rounds[-1])
    *near_parts, two_t, two = pl.pallas_call(
        functools.partial(near_kernel, plan),
        in_specs=[in_vmem] * 4,
        out_specs=[in_vmem] * 8,
        out_shape=shapes(
            *halves, ((9 * channels, channels), bf16), ((9, channels, channels), bf16)
        ),
        scratch_shapes=[turned] * 2,
        compiler_params=pltpu.CompilerParams(vmem_limit_bytes=VMEM_LIMIT // 3),
        cost_estimate=pl.CostEstimate(
            flops=tokens * tokens * channels * 5 * hidden,
            bytes_accessed=8 * tokens * tokens * channels,
            transcendentals=3 * tokens * tokens * channels // 2,
        ),
    )(near, w_proj, w_gate, conv_two)
    cot_other, two_t = lax.optimization_barrier((cot_other, two_t))
    cot_near = jnp.concatenate([cot_held, cot_other], axis=0)
    cot_far = exchange(cot_near, cot_rounds[-1])
    padded = pltpu.VMEM((tokens, line, channels), f32)
    bordered = pltpu.VMEM((line, line, channels), f32)
    tripled = pltpu.VMEM((line, tokens, 3 * channels), bf16)
    both = pltpu.VMEM((2,) + side[0], bf16)
    alone = pltpu.VMEM(rows, bf16)
    flat = ((channels, tokens * tokens), bf16)
    sums = pltpu.VMEM((channels, 9 * channels), f32)
    held = pl.pallas_call(
        functools.partial(forward_kernel, plan),
        in_specs=[in_smem] + [in_vmem] * 11,
        out_specs=[in_vmem] * 4,
        out_shape=shapes(((line, line, channels), f32), flat, stat, stat),
        scratch_shapes=[pltpu.VMEM(*side), both, both, alone, alone, alone]
        + [turned] * 2
        + [pltpu.VMEM((hidden * (2 * height + PITCH), chips * tokens), f32)]
        + [pltpu.VMEM((2 * height // 8, chips, 8, tokens, hidden), bf16)]
        + [pltpu.VMEM(rows, f32), padded]
        + [pltpu.VMEM((3, line, tokens, channels), bf16)],
        compiler_params=pltpu.CompilerParams(vmem_limit_bytes=FORWARD_VMEM),
        cost_estimate=pl.CostEstimate(
            flops=tokens * tokens * channels * 40 * hidden,
            bytes_accessed=40 * tokens * tokens * channels,
            transcendentals=4 * tokens * tokens * channels,
        ),
    )(
        rates,
        far,
        w_proj,
        w_gate,
        w_out,
        conv_one,
        *near_parts,
    )
    output, grad_pair, grad_one, grad_two = pl.pallas_call(
        functools.partial(backward_kernel, plan),
        in_specs=[in_smem] + [in_vmem] * 9,
        out_specs=[in_vmem] * 2 + [pl.BlockSpec(memory_space=pltpu.HBM)] * 2,
        out_shape=shapes(
            ((pixels, channels), bf16),
            ((pixels, channels), bf16),
            ((9, channels, channels), f32),
            ((9, channels, channels), f32),
        ),
        scratch_shapes=[padded, tripled, tripled, bordered, sums, sums]
        + [pltpu.VMEM((9, channels, channels), f32)] * 2
        + [pltpu.SemaphoreType.DMA((6,))],
        compiler_params=pltpu.CompilerParams(vmem_limit_bytes=BACKWARD_VMEM),
    )(
        rates,
        cot_near,
        cot_far,
        conv_one,
        two,
        two_t,
        *held,
    )
    block = (height, breadth, channels)
    return output.reshape(block), grad_pair.reshape(block), grad_one, grad_two


def fits(pair, w_out, row_count, col_count):
    height, breadth, channels = pair.shape
    tokens = height * row_count
    powers = all(count & (count - 1) == 0 for count in (row_count, col_count))
    whole = (tokens + 2 * DMAX) ** 2 * channels
    return (
        powers
        and row_count * col_count >= 8
        and height * breadth == channels == w_out.shape[0]
        and breadth == 8
        and row_count // 2 * tokens == channels
        and whole * 60 <= VMEM_LIMIT
    )


def local(*arguments):
    pair, w_out = arguments[0], arguments[6]
    if fits(pair, w_out, lax.axis_size("row"), lax.axis_size("col")):
        return replicated(*arguments)
    return sharded(*arguments)


def solution(mesh):
    in_specs = (
        P("row", "col", None),
        P("row", "col"),
        P("row", "col"),
        P(),
        P(),
        P(),
        P(),
        P(),
        P(),
        P("row", "col", None),
    )
    out_specs = (P("row", "col", None), P("row", "col", None), P(), P())
    return jax.shard_map(local, mesh=mesh, in_specs=in_specs, out_specs=out_specs, check_vma=False)
```

```python
import functools

import jax
import jax.numpy as jnp
from jax import lax
from jax.experimental import pallas as pl
from jax.experimental.pallas import tpu as pltpu
from jax.sharding import PartitionSpec as P

DMAX = 8
VMEM_LIMIT = 48 * 1024 * 1024
PITCH = 8
FORWARD_VMEM = 32 * 1024 * 1024
BACKWARD_VMEM = 36 * 1024 * 1024


EPSILON = 1e-05


def with_halo(block, sides, width):
    for axis, dim in sides:
        count = lax.axis_size(axis)
        forward = [(i, i + 1) for i in range(count - 1)]
        backward = [(target, source) for source, target in forward]
        low = lax.ppermute(
            lax.slice_in_dim(block, block.shape[dim] - width, None, axis=dim), axis, forward
        )
        high = lax.ppermute(lax.slice_in_dim(block, 0, width, axis=dim), axis, backward)
        block = jnp.concatenate([low, block, high], axis=dim)
    return block


def broadcast(x, axis, root):
    mine = lax.axis_index(axis) == root
    return lax.psum(jnp.where(mine, x, jnp.zeros_like(x)), axis)


def layer_norm(values, axis=-1):
    centre = values - jnp.mean(values, axis=axis, keepdims=True)
    spread = jnp.mean(centre * centre, axis=axis, keepdims=True)
    return centre * lax.rsqrt(spread + EPSILON)


def with_rim(field):
    return with_halo(field, (("row", 0), ("col", 1)), DMAX)


def gather_taps(padded, dilation, mirrored, height, breadth):
    windows = []
    for tap_index in range(9):
        row_tap = tap_index // 3
        col_tap = tap_index % 3
        if mirrored:
            row_tap = 2 - row_tap
            col_tap = 2 - col_tap
        row_start = DMAX + (row_tap - 1) * dilation
        col_start = DMAX + (col_tap - 1) * dilation
        windows.append(
            lax.dynamic_slice(
                padded, (row_start, col_start, jnp.int32(0)), (height, breadth, padded.shape[2])
            )
        )
    return jnp.concatenate(windows, axis=2).reshape(height * breadth, -1)


def sharded(
    pair, pair_mask, contact_mask, dilations, w_proj, w_gate, w_out, conv_one, conv_two, cotangent
):
    height, breadth, channels = pair.shape
    hidden = w_out.shape[0]
    row_count = lax.axis_size("row")
    col_count = lax.axis_size("col")
    ratio = col_count // row_count
    row_place = lax.axis_index("row")
    col_place = lax.axis_index("col")
    tokens = breadth * col_count
    pixels = height * breadth
    pair_flat = pair.astype(jnp.float32).reshape(pixels, channels)
    normed = layer_norm(pair_flat).astype(jnp.bfloat16)
    projected = jnp.dot(normed, w_proj, preferred_element_type=jnp.float32)
    mask_col = pair_mask.reshape(pixels, 1).astype(jnp.float32)
    left_side = (
        (mask_col * jax.nn.sigmoid(projected[:, hidden : 2 * hidden]) * projected[:, :hidden])
        .astype(jnp.bfloat16)
        .reshape(height, breadth, hidden)
    )
    right_side = (
        (
            mask_col
            * jax.nn.sigmoid(projected[:, 3 * hidden :])
            * projected[:, 2 * hidden : 3 * hidden]
        )
        .astype(jnp.bfloat16)
        .reshape(height, breadth, hidden)
    )
    right_all = lax.all_gather(right_side, "col", axis=1, tiled=True)
    offset = jnp.clip(col_place * breadth - row_place * height, 0, height - breadth)
    right_local = lax.dynamic_slice_in_dim(right_all, offset, breadth, 0)
    right_rows = broadcast(right_local, "row", col_place // ratio)
    products = jnp.einsum(
        "ikh,jkh->ijh",
        lax.all_gather(left_side, "col", axis=1, tiled=True),
        right_rows,
        preferred_element_type=jnp.float32,
    )
    product_norm = layer_norm(products.reshape(pixels, hidden)).astype(jnp.bfloat16)
    gating = jax.nn.sigmoid(jnp.dot(normed, w_gate, preferred_element_type=jnp.float32))
    updated = (
        pair_flat + gating * jnp.dot(product_norm, w_out, preferred_element_type=jnp.float32)
    ).astype(jnp.bfloat16)
    updated_f = updated.astype(jnp.float32)
    centre = updated_f - jnp.mean(updated_f, axis=-1, keepdims=True)
    inv_spread = lax.rsqrt(jnp.mean(centre * centre, axis=-1, keepdims=True) + EPSILON)
    scaled = centre * inv_spread
    contact = contact_mask.reshape(pixels, 1).astype(jnp.float32)
    first_in = (scaled * contact).astype(jnp.bfloat16).reshape(height, breadth, channels)
    rate_one = dilations[0]
    rate_two = dilations[1]
    first_taps = gather_taps(with_rim(first_in), rate_one, False, height, breadth)
    first_pre = jnp.dot(
        first_taps, conv_one.reshape(9 * channels, channels), preferred_element_type=jnp.float32
    )
    sigma = jax.nn.sigmoid(first_pre)
    second_in = (first_pre * sigma).astype(jnp.bfloat16).reshape(height, breadth, channels)
    second_taps = gather_taps(with_rim(second_in), rate_two, False, height, breadth)
    second_pre = jnp.dot(
        second_taps, conv_two.reshape(9 * channels, channels), preferred_element_type=jnp.float32
    )
    output = (updated_f + second_pre).astype(jnp.bfloat16).reshape(height, breadth, channels)
    cot_flat = cotangent.reshape(pixels, channels)
    grad_two = (
        lax.dot_general(
            second_taps, cot_flat, (((0,), (0,)), ((), ())), preferred_element_type=jnp.float32
        ).reshape(9, channels, channels)
        / tokens
    )
    cot_taps = gather_taps(with_rim(cotangent), rate_two, True, height, breadth)
    grad_hidden = jnp.dot(
        cot_taps,
        conv_two.transpose(0, 2, 1).reshape(9 * channels, channels),
        preferred_element_type=jnp.float32,
    )
    grad_pre = (grad_hidden * sigma * (1.0 + first_pre * (1.0 - sigma))).astype(jnp.bfloat16)
    grad_one = (
        lax.dot_general(
            first_taps, grad_pre, (((0,), (0,)), ((), ())), preferred_element_type=jnp.float32
        ).reshape(9, channels, channels)
        / tokens
    )
    grad_taps = gather_taps(
        with_rim(grad_pre.reshape(height, breadth, channels)), rate_one, True, height, breadth
    )
    grad_input = (
        jnp.dot(
            grad_taps,
            conv_one.transpose(0, 2, 1).reshape(9 * channels, channels),
            preferred_element_type=jnp.float32,
        )
        * contact
    )
    grad_norm = inv_spread * (
        grad_input
        - jnp.mean(grad_input, axis=-1, keepdims=True)
        - scaled * jnp.mean(grad_input * scaled, axis=-1, keepdims=True)
    )
    grad_pair = (
        (cot_flat.astype(jnp.float32) + grad_norm)
        .astype(jnp.bfloat16)
        .reshape(height, breadth, channels)
    )
    grad_one, grad_two = lax.psum((grad_one, grad_two), ("row", "col"))
    return (output, grad_pair, grad_one, grad_two)


def halvings(axis, count):
    return [(axis, count >> step) for step in range(1, count.bit_length())]


def exchange_plan(row_count, col_count):
    rows, cols = halvings("row", row_count), halvings("col", col_count)
    return cols + rows, rows[:-1] + cols + rows[-1:]


def exchange(held, hop):
    axis, distance = hop
    return lax.ppermute(held, axis, [(i, i ^ distance) for i in range(lax.axis_size(axis))])


def place_of(position, rounds, row_place, col_place):
    row, col = row_place, col_place
    for step, (axis, distance) in enumerate(rounds):
        bit = ((position >> step) & 1) * distance
        if axis == "row":
            row = row ^ bit
        else:
            col = col ^ bit
    return row, col


def slot_of(row_change, col_change, rounds):
    slot = 0
    for step, (axis, distance) in enumerate(rounds[:-1]):
        change = row_change if axis == "row" else col_change
        slot = slot | (((change // distance) & 1) << step)
    return slot


def sigmoid(values):
    return 0.5 + 0.5 * jnp.tanh(0.5 * values)


def matmul(left, right):
    return jnp.dot(left, right, preferred_element_type=jnp.float32)


def matmul_by_rows(left, right):
    rows = 256
    return jnp.concatenate(
        [matmul(left[i : i + rows], right) for i in range(0, left.shape[0], rows)], axis=0
    )


def matmul_nt(left, right):
    return lax.dot_general(
        left, right, (((1,), (1,)), ((), ())), preferred_element_type=jnp.float32
    )


def project_half(
    plan, core, pairs, w_proj, w_gate, left, right, swapped, gating, contact, start, turned
):
    rounds, _, height, breadth, tokens = plan
    channels, hidden = w_gate.shape[0], w_gate.shape[1]
    col_count, chips = tokens // breadth, tokens // height // 2
    row_place, col_place = lax.axis_index("row"), lax.axis_index("col")
    lane = lax.broadcasted_iota(jnp.int32, (height, breadth, channels), 2)
    place = lax.broadcasted_iota(jnp.int32, (height, breadth, channels), 0)
    own_lane = jnp.where((lane % height == place) & (lane < 2 * height), 1.0, 0.0)
    pick_lane = lax.broadcasted_iota(jnp.int32, (channels, 2 * channels), 0)
    pick_half = lax.broadcasted_iota(jnp.int32, (channels, 2 * channels), 1) // channels
    pick = jnp.where(pick_lane // height == pick_half, 1.0, 0.0).astype(jnp.bfloat16)
    pixels = height * breadth
    rows = 8
    for first in range(0, height, rows):
        values, masks = [], []
        for chip in range(chips):
            row_change = (chip * 2 + core) ^ row_place
            blocks, marks = [], []
            for col in range(col_count):
                col_change = col_place ^ col
                slot = slot_of(row_change, col_change, rounds)
                blocks.append(
                    pairs[slot, first * breadth : (first + rows) * breadth, :]
                    .astype(jnp.float32)
                    .reshape(rows, breadth, channels)
                )
                mark = pairs[slot, pixels:, :].astype(jnp.float32)[:breadth]
                marks.append(mark[None] * own_lane[first : first + rows])
            values.append(jnp.concatenate(blocks, axis=1).reshape(rows * tokens, channels))
            masks.append(jnp.concatenate(marks, axis=1).reshape(rows * tokens, channels))
        values = jnp.concatenate(values, axis=0)
        masks = matmul(jnp.concatenate(masks, axis=0).astype(jnp.bfloat16), pick)
        normed = layer_norm(values)
        gates = sigmoid(matmul(normed.astype(jnp.bfloat16), w_gate[...]))
        masked = (normed * masks[:, :channels]).astype(jnp.bfloat16)
        projected = matmul(masked, w_proj[...])
        sides = [
            sigmoid(projected[:, (2 * side + 1) * hidden : (2 * side + 2) * hidden])
            * projected[:, 2 * side * hidden : (2 * side + 1) * hidden]
            for side in range(2)
        ]
        for side, target in zip(sides, turned):
            side = side.reshape(chips, rows, tokens, hidden)
            for row in range(rows):
                strip = jnp.concatenate([side[chip, row] for chip in range(chips)], axis=0)
                target[pl.ds(first + row, hidden, stride=height + PITCH), :] = strip.T
        shape = (chips, rows, tokens, channels)
        span = slice(first, first + rows)
        gating[:, span] = gates.astype(jnp.bfloat16).reshape(shape)
        contact[:, span] = masks[:, channels:].astype(jnp.bfloat16).reshape(shape)
        start[:, span] = values.astype(jnp.bfloat16).reshape(shape)
    shape = (hidden, height + PITCH, chips * tokens)
    mine, other = turned[0][...], turned[1][...]
    for target, source in (
        (left, mine),
        (right, other),
        (swapped, pltpu.roll(other, tokens, 1)),
    ):
        target[...] = source.reshape(shape)[:, :height].astype(jnp.bfloat16)


def near_kernel(
    plan,
    near,
    w_proj,
    w_gate,
    two,
    left,
    right,
    swapped,
    gating,
    contact,
    start,
    two_t,
    two_copy,
    turned_left,
    turned_right,
):
    core = lax.axis_index("row") % 2
    two_copy[...] = two[...]
    channels = two.shape[1]
    for tap in range(9):
        two_t[tap * channels : (tap + 1) * channels] = two[tap].T
    project_half(
        plan,
        core,
        near,
        w_proj,
        w_gate,
        left,
        right,
        swapped,
        gating,
        contact,
        start,
        (turned_left, turned_right),
    )


def spread(source, rows, pad, rate, target):
    tokens, channels = target.shape[1], source.shape[2]
    for tap in range(3):
        first = DMAX + (tap - 1) * rate if tap != 1 else DMAX
        moved = source[pl.ds(pad + rows.start, rows.size), pl.ds(first, tokens), :]
        target[pl.ds(DMAX + rows.start, rows.size), :, tap * channels : (tap + 1) * channels] = (
            moved.astype(jnp.bfloat16)
        )


def taps(source, first, count, rate):
    tokens = source.shape[1]
    views = [
        source[pl.ds(DMAX + first + (tap - 1) * rate, count)].reshape(count * tokens, -1)
        for tap in range(3)
    ]
    return jnp.concatenate(views, axis=1)


def windows(source, rate, row_start, col_start, height, breadth):
    views = [
        source[
            pl.ds(row_start + DMAX + (tap // 3 - 1) * rate, height),
            pl.ds(col_start + DMAX + (tap % 3 - 1) * rate, breadth),
            :,
        ].reshape(height * breadth, -1)
        for tap in range(9)
    ]
    return jnp.concatenate(views, axis=1).astype(jnp.bfloat16)


def row_taps(strips, first, count, rate):
    views = [
        strips[tap, pl.ds(DMAX + first + ((tap - 1) * rate if tap != 1 else 0), count)]
        for tap in range(3)
    ]
    return views[0] + views[1] + views[2]


def clear_ends(strips, tokens):
    for tap in (0, 2):
        for rows in (slice(0, DMAX), slice(DMAX + tokens, 2 * DMAX + tokens)):
            strips[tap, rows] = jnp.zeros((DMAX,) + strips.shape[2:], jnp.float32)


def column_taps(source, weight, rate, first, count, strips):
    tokens = strips.shape[2]
    columns = [DMAX - rate, DMAX, DMAX + rate]
    flat = jnp.concatenate(
        [
            source[pl.ds(first, count), pl.ds(column, tokens), :].reshape(count * tokens, -1)
            for column in columns
        ],
        axis=1,
    ).astype(jnp.bfloat16)
    square = jnp.concatenate(
        [
            jnp.concatenate([weight(3 * row + col) for row in range(3)], axis=1)
            for col in range(3)
        ],
        axis=0,
    )
    result = matmul_by_rows(flat, square)
    channels = strips.shape[3]
    for tap in range(3):
        strips[tap, pl.ds(DMAX + first, count)] = result[
            :, tap * channels : (tap + 1) * channels
        ].reshape(count, tokens, channels)


def lanes(step, size):
    return pl.ds(pl.multiple_of(step * size, size), size)


def clear_border(target, tokens):
    line, channels = target.shape[1], target.shape[2]
    border = jnp.zeros((DMAX, line, channels), target.dtype)
    rim = jnp.zeros((tokens, DMAX, channels), target.dtype)
    if target.shape[0] > tokens:
        target[0:DMAX] = border
        target[DMAX + tokens :] = border
    if line > tokens:
        rows = slice(target.shape[0] - tokens - DMAX, target.shape[0] - DMAX)
        if target.shape[0] == tokens:
            rows = slice(0, tokens)
        target[rows, 0:DMAX, :] = rim
        target[rows, DMAX + tokens :, :] = rim


def forward_kernel(
    plan,
    dilations,
    far,
    w_proj,
    w_gate,
    w_out,
    one,
    near_left,
    near_right,
    near_swapped,
    near_gating,
    near_contact,
    near_start,
    pre,
    flipped,
    mine,
    own_contact,
    far_left,
    right,
    swapped,
    far_gating,
    far_contact,
    far_start,
    turned_left,
    turned_right,
    products,
    normed,
    updated,
    field,
    strips,
):
    _, _, height, breadth, tokens = plan
    hidden, channels = w_out.shape
    pixels = height * breadth
    chips = tokens // height // 2
    row_place, col_place = lax.axis_index("row"), lax.axis_index("col")
    core = row_place % 2
    rate_one = dilations[0]
    inside = slice(DMAX, DMAX + tokens)
    clear_border(field, tokens)
    clear_ends(strips, tokens)

    right[core] = near_right[...]
    swapped[core] = near_swapped[...]
    project_half(
        plan,
        1 - core,
        far,
        w_proj,
        w_gate,
        far_left,
        right.at[1 - core],
        swapped.at[1 - core],
        far_gating,
        far_contact,
        far_start,
        (turned_left, turned_right),
    )

    lane = lax.broadcasted_iota(jnp.int32, (height, chips * tokens), 1)
    low = jnp.where(lane < tokens, 1.0, 0.0).astype(jnp.bfloat16)
    high = jnp.where(lane < tokens, 0.0, 1.0).astype(jnp.bfloat16)
    batch = 128
    pitch = 2 * height + PITCH

    def multiply(step, carry):
        for part in range(batch):
            h = step * batch + part
            ahead = [right[0, h], right[1, h]]
            back = [swapped[0, h], swapped[1, h]]
            strips = [strip * low for strip in ahead + back]
            strips += [strip * high for strip in back + ahead]
            mine = jnp.concatenate([near_left[h], far_left[h]], axis=0)
            products[pl.ds(pl.multiple_of(h * pitch, 8), 2 * height), :] = matmul_nt(
                mine, jnp.concatenate(strips, axis=0)
            )
        return carry

    lax.fori_loop(0, hidden // batch, multiply, 0)

    chunk = 8
    size = chunk * tokens

    halves = (
        (core, near_gating, near_contact, near_start),
        (1 - core, far_gating, far_contact, far_start),
    )
    parts = height // chunk

    def normalise(step):
        half, first = step // parts, step % parts * chunk
        for row in range(chunk):
            strip = products[pl.ds(half * height + first + row, hidden, stride=pitch), :]
            strip = layer_norm(strip, axis=0).astype(jnp.bfloat16).T
            for chip in range(chips):
                normed[step, chip, row] = strip[chip * tokens : (chip + 1) * tokens]

    def update(step):
        first = step % parts * chunk
        side, gating, contact, start = halves[step // parts]
        change = matmul(normed[step].reshape(chips * size, hidden), w_out[...])
        change = change.reshape(chips, chunk, tokens, channels)
        rows = pl.ds(first, chunk)
        fresh = start[:, rows].astype(jnp.float32) + gating[:, rows].astype(jnp.float32) * change
        fresh = fresh.astype(jnp.bfloat16).astype(jnp.float32)
        first_in = layer_norm(fresh) * contact[:, rows].astype(jnp.float32)
        if step < parts:
            updated[:, rows] = fresh
        for chip in range(chips):
            base = (chip * 2 + side) * height + first
            field[pl.ds(base, chunk), inside, :] = first_in[chip]
            flipped[:, pl.ds(pl.multiple_of(base * tokens, size), size)] = (
                first_in[chip].reshape(size, channels).astype(jnp.bfloat16).T
            )

    def first_conv(step):
        side = halves[step // parts][0]
        for chip in range(chips):
            base = (chip * 2 + side) * height + step % parts * chunk
            column_taps(field, lambda tap: one[tap], rate_one, base, chunk, strips)

    count = 2 * parts
    for step in range(count + 2):
        if step >= 2:
            first_conv(step - 2)
        if step < count:
            normalise(step)
        if 1 <= step <= count:
            update(step - 1)

    for first in range(0, tokens, chunk):
        pre[pl.ds(first, chunk)] = row_taps(strips, first, chunk, rate_one)

    cols = pl.ds(pl.multiple_of(col_place * breadth, breadth), breadth)
    mine[...] = updated[row_place // 2, :, cols, :].reshape(pixels, channels)
    marks = near_contact[row_place // 2].astype(jnp.float32)
    place_col = lax.broadcasted_iota(jnp.int32, (tokens, channels), 0) // breadth
    marks = jnp.where((place_col == col_place)[None], marks, 0.0)
    marks = marks.reshape(height, tokens // breadth, breadth, channels)
    own_contact[...] = jnp.sum(marks, axis=1).reshape(pixels, channels)


def backward_kernel(
    plan,
    dilations,
    cot_near,
    cot_far,
    one,
    two,
    two_t,
    pre,
    flipped,
    mine,
    own_contact,
    output,
    grad_pair,
    grad_one,
    grad_two,
    field,
    wide_cot,
    wide_pre,
    grad_pre,
    second,
    sum_one,
    sum_two,
    scaled_one,
    scaled_two,
    sent,
):
    _, cot_rounds, height, breadth, tokens = plan
    channels = one.shape[2]
    pixels = height * breadth
    row_place, col_place = lax.axis_index("row"), lax.axis_index("col")
    rate_one, rate_two = dilations[0], dilations[1]
    half = cot_far.shape[0]
    inside = slice(DMAX, DMAX + tokens)
    for target in (field, wide_cot, wide_pre, grad_pre, second):
        clear_border(target, tokens)

    several = 8

    def place_cot(source, base):
        def body(step, carry):
            for i in range(several):
                slot = step * several + i
                row, col = place_of(base + slot, cot_rounds, row_place, col_place)
                cols = pl.ds(pl.multiple_of(DMAX + col * breadth, breadth), breadth)
                field[pl.ds(row * height, height), cols, :] = (
                    source[slot].astype(jnp.float32).reshape(height, breadth, channels)
                )
            return carry

        lax.fori_loop(0, half // several, body, 0)

    place_cot(cot_near, 0)
    place_cot(cot_far, half)
    chunk = 16
    size = chunk * tokens
    steps = tokens // chunk

    def spread_cot(step):
        spread(field, pl.ds(step * chunk, chunk), 0, -rate_two, wide_cot)

    def back_two(step):
        first = step * chunk
        rows = pl.ds(DMAX + first, chunk)
        before_act = pre[pl.ds(first, chunk)]
        sigma = sigmoid(before_act)
        second_in = before_act * sigma
        second[rows, inside, :] = second_in
        factor = sigma * (1.0 + before_act * (1.0 - sigma))
        turned = second_in.reshape(size, channels).astype(jnp.bfloat16).T
        shifted = taps(wide_cot, first, chunk, -rate_two)
        before = matmul_by_rows(shifted, two_t[...]).reshape(chunk, tokens, channels)
        grad_pre[rows, inside, :] = (before * factor).astype(jnp.bfloat16).astype(jnp.float32)
        part = matmul(turned, shifted)
        sum_two[...] = part if step == 0 else sum_two[...] + part

    def spread_pre(step):
        spread(grad_pre, pl.ds(step * chunk, chunk), DMAX, -rate_one, wide_pre)

    def back_one(step):
        shifted = taps(wide_pre, step * chunk, chunk, -rate_one)
        part = matmul(flipped[:, step * size : (step + 1) * size], shifted)
        sum_one[...] = part if step == 0 else sum_one[...] + part

    def finish(total, scaled, target, row):
        for tap in range(3 * row, 3 * row + 3):
            columns = slice(tap * channels, (tap + 1) * channels)
            scaled[tap] = total[:, columns] * (1.0 / tokens)
        taps_done = pl.ds(3 * row, 3)
        copy = pltpu.make_async_copy(
            scaled.at[taps_done], target.at[taps_done], sent.at[len(copies)]
        )
        copy.start()
        copies.append(copy)

    copies = []
    for step in range(min(2, steps)):
        spread_cot(step)
    for step in range(steps):
        if step >= 3:
            back_one(step - 3)
        if step >= 1:
            spread_pre(step - 1)
        back_two(step)
        if step + 2 < steps:
            spread_cot(step + 2)
    spread_pre(steps - 1)
    for row in range(3):
        finish(sum_two, scaled_two, grad_two, row)
    for step in range(max(steps - 3, 0), steps - 1):
        back_one(step)

    spot = (row_place * height, col_place * breadth, height, breadth)
    second_pre = matmul(
        windows(second, rate_two, *spot), two[...].reshape(9 * channels, channels)
    )
    output[...] = (mine[...] + second_pre).astype(jnp.bfloat16)
    one_rows = [one[tap] for tap in range(9)]
    grad_input = own_contact[...] * matmul_nt(
        windows(grad_pre, -rate_one, *spot),
        jnp.concatenate(one_rows, axis=1),
    )
    centre = mine[...] - jnp.mean(mine[...], axis=-1, keepdims=True)
    inv_spread = lax.rsqrt(jnp.mean(centre * centre, axis=-1, keepdims=True) + EPSILON)
    scaled = centre * inv_spread
    grad_norm = inv_spread * (
        grad_input
        - jnp.mean(grad_input, axis=-1, keepdims=True)
        - scaled * jnp.mean(grad_input * scaled, axis=-1, keepdims=True)
    )
    grad_pair[...] = (cot_near[0].astype(jnp.float32) + grad_norm).astype(jnp.bfloat16)

    last = steps - 1
    for row in range(3):
        columns = slice(3 * row * channels, 3 * (row + 1) * channels)
        moved = pl.ds(DMAX + last * chunk - (row - 1) * rate_one, chunk)
        sum_one[:, columns] += matmul(
            flipped[:, last * size : (last + 1) * size], wide_pre[moved].reshape(size, -1)
        )
        finish(sum_one, scaled_one, grad_one, row)
    for copy in copies:
        copy.wait()


def replicated(
    pair, pair_mask, contact_mask, dilations, w_proj, w_gate, w_out, conv_one, conv_two, cotangent
):
    height, breadth, channels = pair.shape
    hidden = w_out.shape[0]
    row_count, col_count = lax.axis_size("row"), lax.axis_size("col")
    tokens = height * row_count
    pixels = height * breadth
    rounds, cot_rounds = exchange_plan(row_count, col_count)
    f32, bf16 = jnp.float32, jnp.bfloat16
    plan = (rounds, cot_rounds, height, breadth, tokens)
    chips = row_count // 2
    line = tokens + 2 * DMAX
    in_vmem = pl.BlockSpec(memory_space=pltpu.VMEM)
    side = ((hidden, height, chips * tokens), bf16)
    rows = (chips, height, tokens, channels)
    halves = [side] * 3 + [(rows, bf16)] * 3
    turned = pltpu.VMEM((hidden * (height + PITCH), chips * tokens), f32)
    stat = ((pixels, channels), f32)

    def shapes(*entries):
        return [jax.ShapeDtypeStruct(shape, dtype) for shape, dtype in entries]

    in_smem = pl.BlockSpec(memory_space=pltpu.SMEM)
    spare = channels - 2 * height
    marks = jnp.pad(pair_mask.T, ((pixels, breadth), (0, height + spare))) + jnp.pad(
        contact_mask.T, ((pixels, breadth), (height, spare))
    )
    above = jnp.pad(pair.reshape(pixels, channels), ((0, 2 * breadth), (0, 0)))
    held = (above.astype(f32) + marks.astype(f32)).astype(bf16)[None]
    block = cotangent.reshape(1, pixels, channels)
    cot_held = lax.optimization_barrier(jnp.maximum(block, jnp.finfo(bf16).min))
    rates = jnp.clip(dilations, 1, DMAX)
    for step in range(len(rounds) - 1):
        other = exchange(held, rounds[step])
        cot_other = exchange(cot_held if step else block, cot_rounds[step])
        held = lax.optimization_barrier(jnp.concatenate([held, other], axis=0))
        if step < len(rounds) - 2:
            cot_held = jnp.concatenate([cot_held, cot_other], axis=0)
            if step == len(rounds) - 3:
                cot_held, rates = lax.optimization_barrier((cot_held, rates))
            else:
                cot_held = lax.optimization_barrier(cot_held)
    near, far = held, exchange(held, rounds[-1])
    *near_parts, two_t, two = pl.pallas_call(
        functools.partial(near_kernel, plan),
        in_specs=[in_vmem] * 4,
        out_specs=[in_vmem] * 8,
        out_shape=shapes(
            *halves, ((9 * channels, channels), bf16), ((9, channels, channels), bf16)
        ),
        scratch_shapes=[turned] * 2,
        compiler_params=pltpu.CompilerParams(vmem_limit_bytes=VMEM_LIMIT // 3),
        cost_estimate=pl.CostEstimate(
            flops=tokens * tokens * channels * 5 * hidden,
            bytes_accessed=8 * tokens * tokens * channels,
            transcendentals=3 * tokens * tokens * channels // 2,
        ),
    )(near, w_proj, w_gate, conv_two)
    cot_other, two_t = lax.optimization_barrier((cot_other, two_t))
    cot_near = jnp.concatenate([cot_held, cot_other], axis=0)
    cot_far = exchange(cot_near, cot_rounds[-1])
    padded = pltpu.VMEM((tokens, line, channels), f32)
    bordered = pltpu.VMEM((line, line, channels), f32)
    tripled = pltpu.VMEM((line, tokens, 3 * channels), bf16)
    both = pltpu.VMEM((2,) + side[0], bf16)
    alone = pltpu.VMEM(rows, bf16)
    flat = ((channels, tokens * tokens), bf16)
    sums = pltpu.VMEM((channels, 9 * channels), f32)
    held = pl.pallas_call(
        functools.partial(forward_kernel, plan),
        in_specs=[in_smem] + [in_vmem] * 11,
        out_specs=[in_vmem] * 4,
        out_shape=shapes(((tokens, tokens, channels), f32), flat, stat, stat),
        scratch_shapes=[pltpu.VMEM(*side), both, both, alone, alone, alone]
        + [turned] * 2
        + [pltpu.VMEM((hidden * (2 * height + PITCH), chips * tokens), f32)]
        + [pltpu.VMEM((2 * height // 8, chips, 8, tokens, hidden), bf16)]
        + [pltpu.VMEM(rows, f32), padded]
        + [pltpu.VMEM((3, line, tokens, channels), f32)],
        compiler_params=pltpu.CompilerParams(vmem_limit_bytes=FORWARD_VMEM),
        cost_estimate=pl.CostEstimate(
            flops=tokens * tokens * channels * 40 * hidden,
            bytes_accessed=40 * tokens * tokens * channels,
            transcendentals=4 * tokens * tokens * channels,
        ),
    )(
        rates,
        far,
        w_proj,
        w_gate,
        w_out,
        conv_one,
        *near_parts,
    )
    output, grad_pair, grad_one, grad_two = pl.pallas_call(
        functools.partial(backward_kernel, plan),
        in_specs=[in_smem] + [in_vmem] * 9,
        out_specs=[in_vmem] * 2 + [pl.BlockSpec(memory_space=pltpu.HBM)] * 2,
        out_shape=shapes(
            ((pixels, channels), bf16),
            ((pixels, channels), bf16),
            ((9, channels, channels), f32),
            ((9, channels, channels), f32),
        ),
        scratch_shapes=[padded, tripled, tripled, bordered, bordered, sums, sums]
        + [pltpu.VMEM((9, channels, channels), f32)] * 2
        + [pltpu.SemaphoreType.DMA((6,))],
        compiler_params=pltpu.CompilerParams(vmem_limit_bytes=BACKWARD_VMEM),
    )(
        rates,
        cot_near,
        cot_far,
        conv_one,
        two,
        two_t,
        *held,
    )
    block = (height, breadth, channels)
    return output.reshape(block), grad_pair.reshape(block), grad_one, grad_two


def fits(pair, w_out, row_count, col_count):
    height, breadth, channels = pair.shape
    tokens = height * row_count
    powers = all(count & (count - 1) == 0 for count in (row_count, col_count))
    whole = (tokens + 2 * DMAX) ** 2 * channels
    return (
        powers
        and row_count * col_count >= 8
        and height * breadth == channels == w_out.shape[0]
        and breadth == 8
        and row_count // 2 * tokens == channels
        and whole * 60 <= VMEM_LIMIT
    )


def local(*arguments):
    pair, w_out = arguments[0], arguments[6]
    if fits(pair, w_out, lax.axis_size("row"), lax.axis_size("col")):
        return replicated(*arguments)
    return sharded(*arguments)


def solution(mesh):
    in_specs = (
        P("row", "col", None),
        P("row", "col"),
        P("row", "col"),
        P(),
        P(),
        P(),
        P(),
        P(),
        P(),
        P("row", "col", None),
    )
    out_specs = (P("row", "col", None), P("row", "col", None), P(), P())
    return jax.shard_map(local, mesh=mesh, in_specs=in_specs, out_specs=out_specs, check_vma=False)
```
